128 devices in a mesh: section: 2 (over z_lo), dp: 4 (over z_hi, core), tensor: 16 (over y, x).
Axes of the slice: x: 4, y: 4, z: 4 (z_hi: 2, z_lo: 2; z = z_hi * 2 + z_lo), core: 2. Of those that a mesh axis runs over, the one named last changes fastest.
Arguments:
- encoder_tokens: bfloat16 [8, 1280, 1024], P('dp', 'tensor'), may hold values from -6 to 6
- encoder_segments: int32 [8, 1280], P('dp'), may hold values from 0 to 3, as said below
- decoder_tokens: bfloat16 [8, 128, 1024], P('dp', 'tensor'), may hold values from -6 to 6
- decoder_segments: int32 [8, 128], P('dp'), may hold values from 0 to 3, as said below
- cotangent: bfloat16 [8, 128, 1024], P('dp', 'tensor'), may hold values from -6 to 6
- attention_weight: bfloat16 [2, 6, 1024, 1024], P('section', None, None, 'tensor'), may hold values from -2 to 2
- feedforward_weight: bfloat16 [2, 2, 1024, 4096], P('section', None, None, 'tensor'), may hold values from -0.1875 to 0.1875
- norm_gain: float32 [2, 3, 1024], P('section'), may hold values from 0.5 to 1.5
- norm_shift: float32 [2, 3, 1024], P('section'), may hold values from -1.5 to 1.5
Outputs:
- decoder_output: bfloat16 [8, 128, 1024], P('dp', 'tensor', 'section')
- encoder_grad: float32 [8, 1280, 1024], P('dp', 'tensor', 'section')
- decoder_grad: float32 [8, 128, 1024], P('dp', 'tensor', 'section')
- attention_grad: float32 [2, 6, 1024, 1024], P('section', None, None, 'tensor')
- feedforward_grad: float32 [2, 2, 1024, 4096], P('section', None, None, 'tensor')
- gain_grad: float32 [2, 3, 1024], P('section')
- shift_grad: float32 [2, 3, 1024], P('section')
The draws below stay inside these ranges and needn't reach their ends.
Inputs may be any that keep to these rules, and one draw needn't show every extreme that they name: In each pack the ids start at 0, never fall and rise by at most one from token to token; decoder_segments of a pack hold exactly the ids of encoder_segments of that pack, each at least once; among the 2 packs of each index of dp one holds a single item, and some pack holds four items. `decoder_segments`: ids as in encoder_segments, with the same items per pack.
All inputs are finite; a program needn't handle non-finite values.
Results may differ from the reference program's by a relative error of at most 0.034.
Values may be sent and summed in bfloat16 or wider, within the bound.
A program may use at most 128 MiB of HBM per device.

```python
import math
import jax
import jax.numpy as jnp
from jax import lax

D = 1024
HEAD = 64
FF = 4096
ENC_LEN = 1280
DEC_LEN = 128
MICRO = 2
PACKS = 8
N_DP = 4


def item_counts(key):
    drawn = jax.random.randint(jax.random.fold_in(key, 11), (PACKS,), 2, 5)
    single = jax.random.randint(jax.random.fold_in(key, 12), (N_DP,), 0, MICRO)
    pack_index = jnp.arange(PACKS)
    micro_index = pack_index % MICRO
    shard_index = pack_index // MICRO
    alone = micro_index == single[shard_index]
    fullest = (shard_index == 0) & (micro_index == (single[0] + 1) % MICRO)
    return jnp.where(alone, 1, jnp.where(fullest, 4, drawn)).astype(jnp.int32)


def segment_ids(key, counts, length):
    position = jnp.arange(length)

    def one_pack(pack_index, item_count):
        cut_points = jax.random.permutation(jax.random.fold_in(key, pack_index), length - 1)[:3] + 1
        is_live = jnp.arange(3) < item_count - 1
        is_after = is_live[None, :] & (position[:, None] >= cut_points[None, :])
        return jnp.sum(is_after.astype(jnp.int32), axis=1)
    return jax.vmap(one_pack)(jnp.arange(PACKS), counts).astype(jnp.int32)


def draw_encoder_segments(key, part):
    counts = item_counts(key)
    key = jax.random.fold_in(key, 3)
    return segment_ids(key, counts, ENC_LEN)


def draw_decoder_segments(key, part):
    counts = item_counts(key)
    key = jax.random.fold_in(key, 4)
    return segment_ids(key, counts, DEC_LEN)


def draw_attention_weight(key, part):
    key = jax.random.fold_in(key, 5)
    shape = (2, 6, D, D)
    raw = jnp.clip(jax.random.normal(key, shape, jnp.float32), -4.0, 4.0)
    section_index = jnp.arange(2)[:, None]
    slot_index = jnp.arange(6)[None, :]
    output_slot = (slot_index == 3) | (section_index == 1) & (slot_index == 5)
    factor = jnp.where(output_slot, 8.0, 1.0) / math.sqrt(D)
    return jnp.clip(raw * factor[:, :, None, None], -2.0, 2.0).astype(jnp.bfloat16)


def levels(stream_key, dims, pieces, smallest, largest):
    level = 1.0
    for dim, parts in pieces:
        draws = jax.random.uniform(jax.random.fold_in(jax.random.fold_in(stream_key, 6), dim), (parts,), jnp.float32, smallest / len(pieces), largest / len(pieces))
        level = level * jnp.repeat(jnp.exp(draws), dims[dim] // parts).reshape((-1,) + (1,) * (len(dims) - 1 - dim))
    return level


def gaussian(rng, shape, spread, most, split=(), dtype=jnp.bfloat16):
    values = jax.random.normal(rng, shape, jnp.float32) * spread
    if len(split) > 0:
        values = levels(rng, shape, split, -0.22, 0.18) * values
    return jnp.clip(values, min=-most, max=most).astype(dtype)


def setup_inputs(seed: int = 0) -> dict:
    keys = jax.random.split(jax.random.key(seed), 10)
    return {
        "encoder_tokens": gaussian(keys[0], (PACKS, ENC_LEN, D), 1.0, 6.0, ((0, 4), (1, 16))),
        "encoder_segments": draw_encoder_segments(jax.random.fold_in(keys[9], 71), 0),
        "decoder_tokens": gaussian(keys[2], (PACKS, DEC_LEN, D), 1.0, 6.0, ((0, 4), (1, 16))),
        "decoder_segments": draw_decoder_segments(jax.random.fold_in(keys[9], 71), 0),
        "cotangent": gaussian(keys[4], (PACKS, DEC_LEN, D), 1.0, 6.0, ((0, 4), (1, 16))),
        "attention_weight": draw_attention_weight(jax.random.fold_in(keys[9], 71), 0),
        "feedforward_weight": gaussian(keys[6], (2, 2, D, FF), D ** -0.5, 0.1875, ((0, 2), (3, 16))),
        "norm_gain": jnp.clip(1.0 + 0.1 * jax.random.normal(keys[7], (2, 3, D), jnp.float32), 0.5, 1.5),
        "norm_shift": gaussian(keys[8], (2, 3, D), 0.3, 1.5, ((0, 2),), jnp.float32),
    }


EPSILON = 1e-05
MASKED = -1000000000.0
HIGHEST = lax.Precision.HIGHEST

@jax.custom_vjp
def low(v):
    return lax.optimization_barrier(v.astype(jnp.bfloat16)).astype(jnp.float32)

@jax.custom_vjp
def low_back(v):
    return v

def low_keep(v):
    return (low(v), None)

def low_pass(kept, grad):
    return (grad,)

def back_keep(v):
    return (v, None)

def back_low(kept, grad):
    return (low(grad),)
low.defvjp(low_keep, low_pass)
low_back.defvjp(back_keep, back_low)

def norm_rows(values, gains, shifts):
    center = values - lax.optimization_barrier(jnp.mean(values, -1, keepdims=True))
    variance = lax.optimization_barrier(jnp.mean(center * center, -1, keepdims=True))
    return center * lax.rsqrt(variance + EPSILON) * gains + shifts

def dense(values, matrix):
    return jnp.dot(values, matrix, precision=HIGHEST)

def dense_back(values, matrix):
    return jnp.dot(values, matrix.T, precision=HIGHEST)

def projected(values, matrix):
    return low_back(low(dense(values, matrix)))

def by_head(values):
    return values.reshape(values.shape[0], -1, HEAD)

def attention(queries, key_rows, value_rows, allowed):
    scores = jnp.einsum('qhd,khd->hqk', by_head(queries), by_head(key_rows), precision=HIGHEST)
    scores = low_back(jnp.where(allowed[None], scores * HEAD ** (-0.5), MASKED))
    probs = low(jax.nn.softmax(scores, axis=-1))
    attended = jnp.einsum('hqk,khd->qhd', probs, by_head(value_rows), precision=HIGHEST)
    return low_back(low(attended.reshape(queries.shape[0], -1)))

def feedforward(normed, ffn_mats):
    hidden = low(jax.nn.gelu(low_back(dense(low(normed), ffn_mats[0])), approximate=False))
    return low_back(dense_back(hidden, ffn_mats[1]))

def encoder_layer(weights, ffn_mats, gains, shifts, tokens, segment):
    normed_zero = norm_rows(tokens, gains[0], shifts[0])
    full_zero = low(normed_zero)
    allowed = segment[:, None] == segment[None, :]
    attended = attention(projected(full_zero, weights[0]), projected(full_zero, weights[1]), projected(full_zero, weights[2]), allowed)
    normed_one = norm_rows(normed_zero + low_back(dense_back(attended, weights[3])), gains[1], shifts[1])
    memory = norm_rows(normed_one + feedforward(normed_one, ffn_mats), gains[2], shifts[2])
    full_two = low(memory)
    return (projected(full_two, weights[4]), projected(full_two, weights[5]))

def decoder_layer(weights, ffn_mats, gains, shifts, tokens, segment, enc_segment, cross_keys, cross_values):
    full_in = low(tokens)
    position = jnp.arange(segment.shape[0])
    allowed = (segment[:, None] == segment[None, :]) & (position[:, None] >= position[None, :])
    attended = attention(projected(full_in, weights[0]), projected(full_in, weights[1]), projected(full_in, weights[2]), allowed)
    normed_zero = norm_rows(tokens + low_back(dense_back(attended, weights[3])), gains[0], shifts[0])
    cross_allowed = segment[:, None] == enc_segment[None, :]
    crossed = attention(projected(low(normed_zero), weights[4]), cross_keys, cross_values, cross_allowed)
    normed_one = norm_rows(normed_zero + low_back(dense_back(crossed, weights[5])), gains[1], shifts[1])
    return norm_rows(normed_one + feedforward(normed_one, ffn_mats), gains[2], shifts[2])

def layer_pair(params, enc_tokens, dec_tokens, enc_segment, dec_segment):
    weights, ffn_mats, gains, shifts = params
    cross_keys, cross_values = encoder_layer(weights[0], ffn_mats[0], gains[0], shifts[0], enc_tokens, enc_segment)
    return decoder_layer(weights[1], ffn_mats[1], gains[1], shifts[1], dec_tokens, dec_segment, enc_segment, cross_keys, cross_values)

def reference(encoder_tokens, encoder_segments, decoder_tokens, decoder_segments, cotangent, attention_weight, feedforward_weight, norm_gain, norm_shift):
    params = (attention_weight.astype(jnp.float32), feedforward_weight.astype(jnp.float32), norm_gain.astype(jnp.float32), norm_shift.astype(jnp.float32))

    def step(totals, sliced):
        enc_tokens, enc_segment, dec_tokens, dec_segment, ahead = sliced

        def forward(values, enc_rows, dec_rows):
            return layer_pair(values, enc_rows, dec_rows, enc_segment, dec_segment)
        result, pull = jax.vjp(forward, params, enc_tokens.astype(jnp.float32), dec_tokens.astype(jnp.float32))
        grads, enc_grad, dec_grad = pull(ahead.astype(jnp.float32))
        totals = jax.tree.map(jnp.add, totals, grads)
        return (totals, (result.astype(jnp.bfloat16), enc_grad, dec_grad))
    zero_totals = jax.tree.map(jnp.zeros_like, params)
    totals, outputs = lax.scan(step, zero_totals, (encoder_tokens, encoder_segments, decoder_tokens, decoder_segments, cotangent))
    return (outputs[0], outputs[1], outputs[2], totals[0], totals[1], totals[2], totals[3])
```

```python
import jax
import jax.numpy as jnp
from jax import lax
from jax.sharding import PartitionSpec as P

HEAD = 64
EPSILON = 1e-05
MASKED = -1000000000.0
F32 = jnp.float32
BF16 = jnp.bfloat16


def swapped(value, axis):
    return lax.ppermute(value, axis, [(0, 1), (1, 0)])


def norm_parts(values):
    center = values - jnp.mean(values, -1, keepdims=True)
    scale = lax.rsqrt(jnp.mean(center * center, -1, keepdims=True) + EPSILON)
    return center * scale, scale


def norm_back(grad, unit, scale, gains):
    inner = grad * gains
    back = scale * (
        inner
        - jnp.mean(inner, -1, keepdims=True)
        - unit * jnp.mean(inner * unit, -1, keepdims=True)
    )
    return back, jnp.sum(grad * unit, 0), jnp.sum(grad, 0)


def gelu_exact(values):
    return jax.nn.gelu(values, approximate=False)


def gather_rows(values):
    return lax.all_gather(values.astype(BF16), "tensor", axis=0, tiled=True)


def sum_rows(values):
    return lax.psum_scatter(
        values.astype(BF16), "tensor", scatter_dimension=0, tiled=True
    ).astype(F32)


def gather_both(enc, dec):
    size, ra, rb = lax.axis_size("tensor"), enc.shape[0], dec.shape[0]
    full = gather_rows(jnp.concatenate([enc, dec], 0)).reshape(size, ra + rb, -1)
    return full[:, :ra].reshape(size * ra, -1), full[:, ra:].reshape(size * rb, -1)


def sum_both(enc, dec):
    size = lax.axis_size("tensor")
    ra, rb = enc.shape[0] // size, dec.shape[0] // size
    both = jnp.concatenate(
        [enc.astype(BF16).reshape(size, ra, -1), dec.astype(BF16).reshape(size, rb, -1)], 1
    )
    mine = sum_rows(both.reshape(size * (ra + rb), -1))
    return mine[:ra], mine[ra:]


def dot(a, b):
    return jnp.dot(a, b, preferred_element_type=F32)


def dot_t(a, b):
    return lax.dot_general(a, b, (((1,), (1,)), ((), ())), preferred_element_type=F32)


def t_dot(a, b):
    return lax.dot_general(a, b, (((0,), (0,)), ((), ())), preferred_element_type=F32)


def scores_of(queries, key_rows, allowed):
    return jnp.where(allowed, dot_t(queries, key_rows) * HEAD ** (-0.5), MASKED)


def attend(queries, key_rows, value_rows, allowed):
    scores = scores_of(queries, key_rows, allowed)
    row_max = jnp.max(scores, -1, keepdims=True)
    exponent = jnp.exp(scores - row_max)
    row_sum = jnp.sum(exponent, -1, keepdims=True)
    probs_low = (exponent / row_sum).astype(BF16)
    return dot(probs_low, value_rows).astype(BF16), row_max + jnp.log(row_sum)


def attend_back(queries, key_rows, value_rows, log_total, allowed, attended_grad):
    scores = scores_of(queries, key_rows, allowed)
    probs = jnp.exp(scores - log_total)
    value_grad = t_dot(probs.astype(BF16), attended_grad)
    probs_grad = dot_t(attended_grad, value_rows)
    scores_grad = (probs * (probs_grad - jnp.sum(probs * probs_grad, -1, keepdims=True))).astype(
        BF16
    )
    query_grad = dot(scores_grad, key_rows) * HEAD ** (-0.5)
    key_grad = t_dot(scores_grad, queries) * HEAD ** (-0.5)
    return query_grad.astype(BF16), key_grad.astype(BF16), value_grad.astype(BF16)


def feedforward_back(full_back, full_in, up, down):
    hidden_raw, gelu_pull = jax.vjp(gelu_exact, dot(full_in, up))
    hidden = hidden_raw.astype(BF16)
    down_grad = t_dot(full_back, hidden)
    pre_grad = gelu_pull(dot(full_back, down))[0].astype(BF16)
    up_grad = t_dot(full_in, pre_grad)
    return pre_grad, up_grad, down_grad


def slot(weights, first, last):
    return weights[:, first * HEAD : last * HEAD]


def on_device(
    encoder_tokens,
    encoder_segments,
    decoder_tokens,
    decoder_segments,
    cotangent,
    attention_weight,
    feedforward_weight,
    norm_gain,
    norm_shift,
):
    section = lax.axis_index("section")
    on_encoder = section == 0
    mine = lambda a: lax.dynamic_index_in_dim(a, section, 0, keepdims=False)

    def layers(own):
        other = swapped(own, "section")
        return jnp.where(on_encoder, own, other), jnp.where(on_encoder, other, own)

    own_attention = jnp.concatenate([attention_weight[0, j] for j in range(6)], 1)
    we, wd = layers(own_attention)
    fe, fd = layers(feedforward_weight[0])
    ge, gd = layers(norm_gain[0])
    se, sd = layers(norm_shift[0])

    x = mine(encoder_tokens).astype(F32)
    y = mine(decoder_tokens).astype(F32)
    cot = mine(cotangent).astype(F32)
    e = mine(encoder_segments)
    c = mine(decoder_segments)
    position = jnp.arange(c.shape[0])
    allow_e = e[:, None] == e[None, :]
    allow_d = (c[:, None] == c[None, :]) & (position[:, None] >= position[None, :])
    allow_c = c[:, None] == e[None, :]

    unit0, scale0 = norm_parts(x)
    h0 = unit0 * ge[0] + se[0]
    full_h0, full_y = gather_both(h0, y)
    qkv = dot(full_h0, slot(we, 0, 3)).astype(BF16)
    q, k, v = (slot(qkv, j, j + 1) for j in range(3))
    att_e, log_e = attend(q, k, v, allow_e)
    dqkv = dot(full_y, slot(wd, 0, 3)).astype(BF16)
    sq, sk, sv = (slot(dqkv, j, j + 1) for j in range(3))
    att_d, log_d = attend(sq, sk, sv, allow_d)
    part_e, part_d = sum_both(dot_t(att_e, slot(we, 3, 4)), dot_t(att_d, slot(wd, 3, 4)))
    unit1, scale1 = norm_parts(h0 + part_e)
    h1 = unit1 * ge[1] + se[1]
    dunit0, dscale0 = norm_parts(y + part_d)
    d1 = dunit0 * gd[0] + sd[0]
    full_h1, full_d1 = gather_both(h1, d1)
    hidden = gelu_exact(dot(full_h1, fe[0])).astype(BF16)
    cq = dot(full_d1, slot(wd, 4, 5)).astype(BF16)
    unit2, scale2 = norm_parts(h1 + sum_rows(dot_t(hidden, fe[1])))
    full_m = gather_rows(unit2 * ge[2] + se[2])
    kvc = dot(full_m, slot(we, 4, 6)).astype(BF16)
    kc, vc = slot(kvc, 0, 1), slot(kvc, 1, 2)

    att_c, log_c = attend(cq, kc, vc, allow_c)
    dunit1, dscale1 = norm_parts(d1 + sum_rows(dot_t(att_c, slot(wd, 5, 6))))
    d2 = dunit1 * gd[1] + sd[1]
    full_d2 = gather_rows(d2)
    dhidden = gelu_exact(dot(full_d2, fd[0])).astype(BF16)
    dunit2, dscale2 = norm_parts(d2 + sum_rows(dot_t(dhidden, fd[1])))
    d3 = dunit2 * gd[2] + sd[2]
    dback2, dgain2, dshift2 = norm_back(cot, dunit2, dscale2, gd[2])
    full_db2 = gather_rows(dback2)
    dpre, dup, ddown = feedforward_back(full_db2, full_d2, fd[0], fd[1])
    dback1, dgain1, dshift1 = norm_back(
        dback2 + sum_rows(dot_t(dpre, fd[0])), dunit1, dscale1, gd[1]
    )
    full_db1 = gather_rows(dback1)
    att_c_grad = dot(full_db1, slot(wd, 5, 6)).astype(BF16)
    d_w5 = t_dot(full_db1, att_c)
    cq_grad, kc_grad, vc_grad = attend_back(cq, kc, vc, log_c, allow_c, att_c_grad)
    kvc_grad = jnp.concatenate([kc_grad, vc_grad], 1)
    d_w4 = t_dot(full_d1, cq_grad)
    e_w45 = t_dot(full_m, kvc_grad)

    mem_grad, d1_grad = sum_both(
        dot_t(kvc_grad, slot(we, 4, 6)), dot_t(cq_grad, slot(wd, 4, 5))
    )
    back2, gain2, shift2 = norm_back(mem_grad, unit2, scale2, ge[2])
    dback0, dgain0, dshift0 = norm_back(dback1 + d1_grad, dunit0, dscale0, gd[0])
    full_b2, full_db0 = gather_both(back2, dback0)
    pre, up, down = feedforward_back(full_b2, full_h1, fe[0], fe[1])
    att_d_grad = dot(full_db0, slot(wd, 3, 4)).astype(BF16)
    d_w3 = t_dot(full_db0, att_d)
    dqkv_grad = jnp.concatenate(attend_back(sq, sk, sv, log_d, allow_d, att_d_grad), 1)
    d_w012 = t_dot(full_y, dqkv_grad)
    part_e, part_d = sum_both(dot_t(pre, fe[0]), dot_t(dqkv_grad, slot(wd, 0, 3)))
    dec_grad = dback0 + part_d
    back1, gain1, shift1 = norm_back(back2 + part_e, unit1, scale1, ge[1])
    full_b1 = gather_rows(back1)
    att_e_grad = dot(full_b1, slot(we, 3, 4)).astype(BF16)
    e_w3 = t_dot(full_b1, att_e)
    qkv_grad = jnp.concatenate(attend_back(q, k, v, log_e, allow_e, att_e_grad), 1)
    e_w012 = t_dot(full_h0, qkv_grad)
    enc_grad, gain0, shift0 = norm_back(
        back1 + sum_rows(dot_t(qkv_grad, slot(we, 0, 3))), unit0, scale0, ge[0]
    )

    att_grads = jnp.stack(
        [jnp.concatenate([e_w012, e_w3, e_w45], 1), jnp.concatenate([d_w012, d_w3, d_w4, d_w5], 1)]
    ).astype(BF16)
    ffn_grads = jnp.stack([jnp.stack([up, down]), jnp.stack([dup, ddown])]).astype(BF16)
    small = jnp.stack(
        [
            jnp.stack([gain0, gain1, gain2, shift0, shift1, shift2]),
            jnp.stack([dgain0, dgain1, dgain2, dshift0, dshift1, dshift2]),
        ]
    )

    def own_layer(both):
        own = lax.dynamic_index_in_dim(both, section, 0, keepdims=False)
        other = lax.dynamic_index_in_dim(both, 1 - section, 0, keepdims=False)
        return own + swapped(other, "section")

    att_sum = lax.psum(own_layer(att_grads), "dp").astype(F32)
    ffn_sum = lax.psum(own_layer(ffn_grads), "dp").astype(F32)
    small_sum = lax.psum(own_layer(small), ("dp", "tensor"))

    half = x.shape[1] // 2

    def both_packs(rows, kind):
        halves = rows.reshape(rows.shape[0], 2, half)
        keep = lax.dynamic_index_in_dim(halves, section, 1, keepdims=False)
        give = lax.dynamic_index_in_dim(halves, 1 - section, 1, keepdims=False)
        got = swapped(give.astype(BF16), "section").astype(kind)
        keep = keep.astype(kind)
        return jnp.where(on_encoder, jnp.stack([keep, got]), jnp.stack([got, keep]))

    att_out = jnp.stack([slot(att_sum, j, j + 1) for j in range(6)])
    return (
        both_packs(d3, BF16),
        both_packs(enc_grad, F32),
        both_packs(dec_grad, F32),
        att_out[None],
        ffn_sum[None],
        small_sum[None, :3],
        small_sum[None, 3:],
    )


def solution(mesh):
    in_specs = (
        P("dp", "tensor", None),
        P("dp", None),
        P("dp", "tensor", None),
        P("dp", None),
        P("dp", "tensor", None),
        P("section", None, None, "tensor"),
        P("section", None, None, "tensor"),
        P("section", None, None),
        P("section", None, None),
    )
    out_specs = (
        P("dp", "tensor", "section"),
        P("dp", "tensor", "section"),
        P("dp", "tensor", "section"),
        P("section", None, None, "tensor"),
        P("section", None, None, "tensor"),
        P("section", None, None),
        P("section", None, None),
    )
    return jax.shard_map(
        on_device, mesh=mesh, in_specs=in_specs, out_specs=out_specs, check_vma=False
    )
```

```python
import jax
import jax.numpy as jnp
from jax import lax
from jax.experimental import pallas as pl
from jax.experimental.pallas import tpu as pltpu
from jax.sharding import PartitionSpec as P

HEAD = 64
EPSILON = 1e-05
MASKED = -1000000000.0

F32 = jnp.float32
BF16 = jnp.bfloat16
SIDE = 4
UP = (0, 2)
DOWN = (1, 3)
GATHER_COPIES = 32
SUM_COPIES = 32


def at_grid():
    index = lax.axis_index("tensor")
    return lax.div(index, SIDE), lax.rem(index, SIDE)


def moved(place, axis, steps):
    y, x = place
    if axis == 0:
        return lax.rem(y + steps % SIDE, SIDE), x
    return y, lax.rem(x + steps % SIDE, SIDE)


def greet(place):
    barrier = pltpu.get_barrier_semaphore()
    for axis in range(2):
        for steps in (1, -1):
            y, x = moved(place, axis, steps)
            pl.semaphore_signal(
                barrier,
                inc=1,
                device_id={"tensor": y * SIDE + x},
                device_id_type=pl.DeviceIdType.MESH,
            )
    pl.semaphore_wait(barrier, 4)


class Copies:
    def __init__(self, place, send_sems, recv_sems):
        self.place, self.send, self.recv, self.used = place, send_sems, recv_sems, 0
        self.started = []

    def start(self, source, target, axis, steps):
        y, x = moved(self.place, axis, steps)
        n = self.used
        self.used += 1
        copy = pltpu.make_async_remote_copy(
            src_ref=source,
            dst_ref=target,
            send_sem=self.send.at[n],
            recv_sem=self.recv.at[n],
            device_id={"tensor": y * SIDE + x},
            device_id_type=pl.DeviceIdType.MESH,
        )
        copy.start()
        self.started.append(copy)
        return copy

    def finish(self):
        for copy in self.started:
            copy.wait_send()
        self.started = []


def gather(copies, bufs):
    place = copies.place
    jobs = []
    for buf in bufs:
        half = buf.shape[-1] // 2
        for h in range(2):
            jobs.append((buf, 1 - h, h, h * half, half))

    def block(job, r, s, part=None):
        buf, a, b, start, size = job
        y, x = moved(moved(place, a, r), b, s)
        if part is not None:
            size = size // 2
            start = start + part * size
        return buf.at[y, x, :, pl.ds(start, size)]

    def send(job, axis, steps, r, s, part=None):
        ref = block(job, r, s, part)
        return copies.start(ref, ref, axis, steps)

    first, spread, ahead = [], [], []
    for job in jobs:
        a, b = job[1], job[2]
        first.append([send(job, a, 1, 0, 0), send(job, a, -1, 0, 0)])
    for job in jobs:
        b = job[2]
        spread.append({0: [send(job, b, 1, 0, 0), send(job, b, -1, 0, 0)]})
    second = []
    for i, job in enumerate(jobs):
        a, b = job[1], job[2]
        first[i][0].wait_recv()
        one = send(job, a, 1, -1, 0, 0)
        spread[i][3] = [send(job, b, 1, -1, 0), send(job, b, -1, -1, 0)]
        first[i][1].wait_recv()
        two = send(job, a, -1, 1, 0, 1)
        spread[i][1] = [send(job, b, 1, 1, 0), send(job, b, -1, 1, 0)]
        second.append([one, two])
    for i, job in enumerate(jobs):
        b = job[2]
        spread[i][0][0].wait_recv()
        ahead.append([send(job, b, 1, 0, -1)])
    for i, job in enumerate(jobs):
        b = job[2]
        second[i][0].wait_recv()
        second[i][1].wait_recv()
        spread[i][2] = [send(job, b, 1, 2, 0), send(job, b, -1, 2, 0)]
    for i, job in enumerate(jobs):
        b = job[2]
        for r in DOWN:
            spread[i][r][1].wait_recv()
            ahead[i].append(send(job, b, -1, r, 1))
    for i, job in enumerate(jobs):
        b = job[2]
        spread[i][2][0].wait_recv()
        ahead[i].append(send(job, b, 1, 2, -1))
    for i, job in enumerate(jobs):
        spread[i][0][1].wait_recv()
        for r in DOWN:
            spread[i][r][0].wait_recv()
        spread[i][2][1].wait_recv()
        for copy in ahead[i]:
            copy.wait_recv()
    copies.finish()


def sum_blocks(copies, parts):
    place = copies.place
    jobs = []
    for part, land in parts:
        half = part.shape[-1] // 2
        for h in range(2):
            jobs.append((part, land, 15 * h, 1 - h, h, h * half, half))

    def block(job, r, s, quarter=None):
        part, _, _, a, b, start, size = job
        y, x = moved(moved(place, a, r), b, s)
        if quarter is not None:
            size = size // 2
            start = start + quarter * size
        return part.at[y, x, :, pl.ds(start, size)]

    def landing(job, n, quarter=None):
        ref = job[1].at[job[2] + n]
        if quarter is None:
            return ref
        size = job[6] // 2
        return ref.at[:, pl.ds(quarter * size, size)]

    def add(target, *others):
        total = target[...].astype(F32)
        for other in others:
            total = total + other[...].astype(F32)
        return total

    far, near = [], []
    for job in jobs:
        b = job[4]
        sent = {}
        for r in (2, 3, 1, 0):
            steps = 1 if r in UP else -1
            sent[r] = copies.start(block(job, r, 2), landing(job, r), b, steps)
        far.append(sent)
    order = (2, 3, 1, 0)
    for job in jobs:
        b = job[4]
        sent = {}
        for r in order:
            steps = -1 if r in UP else 1
            sent[r] = [
                copies.start(block(job, r, steps), landing(job, 4 + 2 * r + (0 if steps == 1 else 1)), b, steps)
            ]
        near.append(sent)
    for r in order:
        for i, job in enumerate(jobs):
            b = job[4]
            steps = 1 if r in UP else -1
            far[i][r].wait_recv()
            ref = block(job, r, steps)
            ref[...] = add(ref, landing(job, r)).astype(BF16)
            near[i][r].append(
                copies.start(ref, landing(job, 4 + 2 * r + (0 if steps == 1 else 1)), b, steps)
            )
    opposite, last = [], []
    for r in order[:3]:
        for i, job in enumerate(jobs):
            a = job[3]
            for copy in near[i][r]:
                copy.wait_recv()
            ref = block(job, r, 0)
            total = add(ref, landing(job, 4 + 2 * r), landing(job, 5 + 2 * r))
            if r == 2:
                ref[...] = total.astype(BF16)
                opposite.append(
                    [
                        copies.start(block(job, 2, 0, 0), landing(job, 12, 0), a, 1),
                        copies.start(block(job, 2, 0, 1), landing(job, 12, 1), a, -1),
                    ]
                )
                last.append({})
            else:
                quarter = 0 if r == 1 else 1
                opposite[i][quarter].wait_recv()
                size = job[6] // 2
                extra = landing(job, 12, quarter)[...].astype(F32)
                low, high = total[:, :size], total[:, size:]
                if quarter == 0:
                    low = low + extra
                else:
                    high = high + extra
                ref[:, pl.ds(0, size)] = low.astype(BF16)
                ref[:, pl.ds(size, size)] = high.astype(BF16)
                steps = 1 if r == 1 else -1
                last[i][r] = copies.start(ref, landing(job, 13 if r == 1 else 14), a, steps)
    results = []
    for i, job in enumerate(jobs):
        for copy in near[i][0]:
            copy.wait_recv()
        last[i][1].wait_recv()
        last[i][3].wait_recv()
        results.append(
            add(block(job, 0, 0), landing(job, 4), landing(job, 5), landing(job, 13), landing(job, 14))
        )
    copies.finish()
    return results


def sems(n):
    return [pltpu.SemaphoreType.DMA((n,)), pltpu.SemaphoreType.DMA((n,))]


VM = pl.BlockSpec(memory_space=pltpu.VMEM)


def gather_call(blocks, collective_id):
    count = len(blocks)

    def kernel(*refs):
        ins, outs, (send, recv) = refs[:count], refs[count : 2 * count], refs[2 * count :]
        place = at_grid()
        greet(place)
        for i, o in zip(ins, outs):
            o[place[0], place[1]] = i[...]
        gather(Copies(place, send, recv), outs)

    return pl.pallas_call(
        kernel,
        out_shape=[jax.ShapeDtypeStruct((SIDE, SIDE) + b.shape, b.dtype) for b in blocks],
        in_specs=[VM] * count,
        out_specs=[VM] * count,
        scratch_shapes=sems(GATHER_COPIES * count),
        compiler_params=pltpu.CompilerParams(
            collective_id=collective_id, has_side_effects=True, vmem_limit_bytes=48 << 20
        ),
    )(*blocks)


def sum_call(partials, collective_id):
    count = len(partials)

    def kernel(*refs):
        ins, outs = refs[:count], refs[count : 2 * count]
        lands, (send, recv) = refs[2 * count : 3 * count], refs[3 * count : 3 * count + 2]
        work = refs[3 * count + 2 :]
        place = at_grid()
        greet(place)
        for i, w in zip(ins, work):
            w[...] = i[...]
        results = sum_blocks(Copies(place, send, recv), list(zip(work, lands)))
        for n, out in enumerate(outs):
            half = out.shape[-1] // 2
            for h in range(2):
                out[:, h * half : (h + 1) * half] = results[2 * n + h]

    return pl.pallas_call(
        kernel,
        out_shape=[jax.ShapeDtypeStruct(p.shape[2:], F32) for p in partials],
        in_specs=[VM] * count,
        out_specs=[VM] * count,
        scratch_shapes=[
            pltpu.VMEM((30, p.shape[2], p.shape[3] // 2), BF16) for p in partials
        ]
        + sems(SUM_COPIES * count)
        + [pltpu.VMEM(p.shape, BF16) for p in partials],
        compiler_params=pltpu.CompilerParams(
            collective_id=collective_id, has_side_effects=True, vmem_limit_bytes=48 << 20
        ),
    )(*partials)


def swapped(value, axis):
    return lax.ppermute(value, axis, [(0, 1), (1, 0)])


def norm_parts(values):
    center = values - jnp.mean(values, -1, keepdims=True)
    scale = lax.rsqrt(jnp.mean(center * center, -1, keepdims=True) + EPSILON)
    return center * scale, scale


def norm_back(grad, unit, scale, gains):
    inner = grad * gains
    back = scale * (
        inner
        - jnp.mean(inner, -1, keepdims=True)
        - unit * jnp.mean(inner * unit, -1, keepdims=True)
    )
    return back, jnp.sum(grad * unit, 0), jnp.sum(grad, 0)


def gelu_exact(values):
    return jax.nn.gelu(values, approximate=False)


def folded(rows):
    half = rows.shape[-1] // 2
    return jnp.concatenate([rows[..., :half], rows[..., half:]], -2)


def unfolded(rows):
    count = rows.shape[-2] // 2
    return jnp.concatenate([rows[..., :count, :], rows[..., count:, :]], -1)


def gather_enc(rows, n):
    (full,) = gather_call([rows.astype(BF16)], n)
    return full.reshape(-1, rows.shape[-1])


def gather_dec(rows, n):
    (full,) = gather_call([folded(rows).astype(BF16)], n)
    return unfolded(full).reshape(-1, rows.shape[-1])


def gather_both(enc, dec, n):
    full, small = gather_call([enc.astype(BF16), folded(dec).astype(BF16)], n)
    return full.reshape(-1, enc.shape[-1]), unfolded(small).reshape(-1, dec.shape[-1])


def in_blocks(part):
    return part.astype(BF16).reshape(SIDE, SIDE, -1, part.shape[-1])


def sum_enc(part, n):
    return sum_call([in_blocks(part)], n)[0]


def sum_dec(part, n):
    return unfolded(sum_call([folded(in_blocks(part))], n)[0])


def sum_both(enc, dec, n):
    rows, small = sum_call([in_blocks(enc), folded(in_blocks(dec))], n)
    return rows, unfolded(small)


def dot(a, b):
    return jnp.dot(a, b, preferred_element_type=F32)


def dot_t(a, b):
    return lax.dot_general(a, b, (((1,), (1,)), ((), ())), preferred_element_type=F32)


def t_dot(a, b):
    return lax.dot_general(a, b, (((0,), (0,)), ((), ())), preferred_element_type=F32)


def scores_of(queries, key_rows, allowed):
    return jnp.where(allowed, dot_t(queries, key_rows) * HEAD ** (-0.5), MASKED)


def attend(queries, key_rows, value_rows, allowed):
    scores = scores_of(queries, key_rows, allowed)
    row_max = jnp.max(scores, -1, keepdims=True)
    exponent = jnp.exp(scores - row_max)
    row_sum = jnp.sum(exponent, -1, keepdims=True)
    probs_low = (exponent / row_sum).astype(BF16)
    return dot(probs_low, value_rows).astype(BF16), row_max + jnp.log(row_sum)


def attend_back(queries, key_rows, value_rows, log_total, allowed, attended_grad):
    scores = scores_of(queries, key_rows, allowed)
    probs = jnp.exp(scores - log_total)
    value_grad = t_dot(probs.astype(BF16), attended_grad)
    probs_grad = dot_t(attended_grad, value_rows)
    scores_grad = (probs * (probs_grad - jnp.sum(probs * probs_grad, -1, keepdims=True))).astype(
        BF16
    )
    query_grad = dot(scores_grad, key_rows) * HEAD ** (-0.5)
    key_grad = t_dot(scores_grad, queries) * HEAD ** (-0.5)
    return query_grad.astype(BF16), key_grad.astype(BF16), value_grad.astype(BF16)


def feedforward_back(full_back, full_in, up, down):
    hidden_raw, gelu_pull = jax.vjp(gelu_exact, dot(full_in, up))
    hidden = hidden_raw.astype(BF16)
    down_grad = t_dot(full_back, hidden)
    pre_grad = gelu_pull(dot(full_back, down))[0].astype(BF16)
    up_grad = t_dot(full_in, pre_grad)
    return pre_grad, up_grad, down_grad


def slot(weights, first, last):
    return weights[:, first * HEAD : last * HEAD]


def on_device(
    encoder_tokens,
    encoder_segments,
    decoder_tokens,
    decoder_segments,
    cotangent,
    attention_weight,
    feedforward_weight,
    norm_gain,
    norm_shift,
):
    section = lax.axis_index("section")
    on_encoder = section == 0
    mine = lambda a: lax.dynamic_index_in_dim(a, section, 0, keepdims=False)

    def layers(own):
        other = swapped(own, "section")
        return jnp.where(on_encoder, own, other), jnp.where(on_encoder, other, own)

    own_attention = jnp.concatenate([attention_weight[0, j] for j in range(6)], 1)
    we, wd = layers(own_attention)
    fe, fd = layers(feedforward_weight[0])
    ge, gd = layers(norm_gain[0])
    se, sd = layers(norm_shift[0])

    x = mine(encoder_tokens).astype(F32)
    y = mine(decoder_tokens).astype(F32)
    cot = mine(cotangent).astype(F32)
    e = mine(encoder_segments)
    c = mine(decoder_segments)
    position = jnp.arange(c.shape[0])
    allow_e = e[:, None] == e[None, :]
    allow_d = (c[:, None] == c[None, :]) & (position[:, None] >= position[None, :])
    allow_c = c[:, None] == e[None, :]

    unit0, scale0 = norm_parts(x)
    h0 = unit0 * ge[0] + se[0]
    full_h0, full_y = gather_both(h0, y, 1)
    qkv = dot(full_h0, slot(we, 0, 3)).astype(BF16)
    q, k, v = (slot(qkv, j, j + 1) for j in range(3))
    att_e, log_e = attend(q, k, v, allow_e)
    dqkv = dot(full_y, slot(wd, 0, 3)).astype(BF16)
    sq, sk, sv = (slot(dqkv, j, j + 1) for j in range(3))
    att_d, log_d = attend(sq, sk, sv, allow_d)
    part_e, part_d = sum_both(dot_t(att_e, slot(we, 3, 4)), dot_t(att_d, slot(wd, 3, 4)), 2)
    unit1, scale1 = norm_parts(h0 + part_e)
    h1 = unit1 * ge[1] + se[1]
    dunit0, dscale0 = norm_parts(y + part_d)
    d1 = dunit0 * gd[0] + sd[0]
    full_h1, full_d1 = gather_both(h1, d1, 3)
    hidden = gelu_exact(dot(full_h1, fe[0])).astype(BF16)
    cq = dot(full_d1, slot(wd, 4, 5)).astype(BF16)
    unit2, scale2 = norm_parts(h1 + sum_enc(dot_t(hidden, fe[1]), 4))
    full_m = gather_enc(unit2 * ge[2] + se[2], 5)
    kvc = dot(full_m, slot(we, 4, 6)).astype(BF16)
    kc, vc = slot(kvc, 0, 1), slot(kvc, 1, 2)

    att_c, log_c = attend(cq, kc, vc, allow_c)
    dunit1, dscale1 = norm_parts(d1 + sum_dec(dot_t(att_c, slot(wd, 5, 6)), 6))
    d2 = dunit1 * gd[1] + sd[1]
    full_d2 = gather_dec(d2, 7)
    dhidden = gelu_exact(dot(full_d2, fd[0])).astype(BF16)
    dunit2, dscale2 = norm_parts(d2 + sum_dec(dot_t(dhidden, fd[1]), 8))
    d3 = dunit2 * gd[2] + sd[2]
    dback2, dgain2, dshift2 = norm_back(cot, dunit2, dscale2, gd[2])
    full_db2 = gather_dec(dback2, 9)
    dpre, dup, ddown = feedforward_back(full_db2, full_d2, fd[0], fd[1])
    dback1, dgain1, dshift1 = norm_back(
        dback2 + sum_dec(dot_t(dpre, fd[0]), 10), dunit1, dscale1, gd[1]
    )
    full_db1 = gather_dec(dback1, 11)
    att_c_grad = dot(full_db1, slot(wd, 5, 6)).astype(BF16)
    d_w5 = t_dot(full_db1, att_c)
    cq_grad, kc_grad, vc_grad = attend_back(cq, kc, vc, log_c, allow_c, att_c_grad)
    kvc_grad = jnp.concatenate([kc_grad, vc_grad], 1)
    d_w4 = t_dot(full_d1, cq_grad)
    e_w45 = t_dot(full_m, kvc_grad)

    mem_grad, d1_grad = sum_both(
        dot_t(kvc_grad, slot(we, 4, 6)), dot_t(cq_grad, slot(wd, 4, 5)), 12
    )
    back2, gain2, shift2 = norm_back(mem_grad, unit2, scale2, ge[2])
    dback0, dgain0, dshift0 = norm_back(dback1 + d1_grad, dunit0, dscale0, gd[0])
    full_b2, full_db0 = gather_both(back2, dback0, 13)
    pre, up, down = feedforward_back(full_b2, full_h1, fe[0], fe[1])
    att_d_grad = dot(full_db0, slot(wd, 3, 4)).astype(BF16)
    d_w3 = t_dot(full_db0, att_d)
    dqkv_grad = jnp.concatenate(attend_back(sq, sk, sv, log_d, allow_d, att_d_grad), 1)
    d_w012 = t_dot(full_y, dqkv_grad)
    part_e, part_d = sum_both(dot_t(pre, fe[0]), dot_t(dqkv_grad, slot(wd, 0, 3)), 14)
    dec_grad = dback0 + part_d
    back1, gain1, shift1 = norm_back(back2 + part_e, unit1, scale1, ge[1])
    full_b1 = gather_enc(back1, 15)
    att_e_grad = dot(full_b1, slot(we, 3, 4)).astype(BF16)
    e_w3 = t_dot(full_b1, att_e)
    qkv_grad = jnp.concatenate(attend_back(q, k, v, log_e, allow_e, att_e_grad), 1)
    e_w012 = t_dot(full_h0, qkv_grad)
    enc_grad, gain0, shift0 = norm_back(
        back1 + sum_enc(dot_t(qkv_grad, slot(we, 0, 3)), 16), unit0, scale0, ge[0]
    )

    att_grads = jnp.stack(
        [jnp.concatenate([e_w012, e_w3, e_w45], 1), jnp.concatenate([d_w012, d_w3, d_w4, d_w5], 1)]
    ).astype(BF16)
    ffn_grads = jnp.stack([jnp.stack([up, down]), jnp.stack([dup, ddown])]).astype(BF16)
    small = jnp.stack(
        [
            jnp.stack([gain0, gain1, gain2, shift0, shift1, shift2]),
            jnp.stack([dgain0, dgain1, dgain2, dshift0, dshift1, dshift2]),
        ]
    )

    def own_layer(both):
        own = lax.dynamic_index_in_dim(both, section, 0, keepdims=False)
        other = lax.dynamic_index_in_dim(both, 1 - section, 0, keepdims=False)
        return own + swapped(other, "section")

    att_sum = lax.psum(own_layer(att_grads), "dp").astype(F32)
    ffn_sum = lax.psum(own_layer(ffn_grads), "dp").astype(F32)
    small_sum = lax.psum(own_layer(small), ("dp", "tensor"))

    half = x.shape[1] // 2

    def both_packs(rows, kind):
        halves = rows.reshape(rows.shape[0], 2, half)
        keep = lax.dynamic_index_in_dim(halves, section, 1, keepdims=False)
        give = lax.dynamic_index_in_dim(halves, 1 - section, 1, keepdims=False)
        got = swapped(give.astype(BF16), "section").astype(kind)
        keep = keep.astype(kind)
        return jnp.where(on_encoder, jnp.stack([keep, got]), jnp.stack([got, keep]))

    att_out = jnp.stack([slot(att_sum, j, j + 1) for j in range(6)])
    return (
        both_packs(d3, BF16),
        both_packs(enc_grad, F32),
        both_packs(dec_grad, F32),
        att_out[None],
        ffn_sum[None],
        small_sum[None, :3],
        small_sum[None, 3:],
    )


def solution(mesh):
    in_specs = (
        P("dp", "tensor", None),
        P("dp", None),
        P("dp", "tensor", None),
        P("dp", None),
        P("dp", "tensor", None),
        P("section", None, None, "tensor"),
        P("section", None, None, "tensor"),
        P("section", None, None),
        P("section", None, None),
    )
    out_specs = (
        P("dp", "tensor", "section"),
        P("dp", "tensor", "section"),
        P("dp", "tensor", "section"),
        P("section", None, None, "tensor"),
        P("section", None, None, "tensor"),
        P("section", None, None),
        P("section", None, None),
    )
    return jax.shard_map(
        on_device, mesh=mesh, in_specs=in_specs, out_specs=out_specs, check_vma=False
    )
```

```python
import jax
import jax.numpy as jnp
from jax import lax
from jax.experimental import pallas as pl
from jax.experimental.pallas import tpu as pltpu
from jax.sharding import PartitionSpec as P

HEAD = 64
EPSILON = 1e-05
MASKED = -1000000000.0

F32 = jnp.float32
BF16 = jnp.bfloat16
SIDE = 4
UP = (0, 2)
DOWN = (1, 3)
GATHER_COPIES = 32
SUM_COPIES = 32


def at_grid():
    index = lax.axis_index("tensor")
    return lax.div(index, SIDE), lax.rem(index, SIDE)


def moved(place, axis, steps):
    y, x = place
    if axis == 0:
        return lax.rem(y + steps % SIDE, SIDE), x
    return y, lax.rem(x + steps % SIDE, SIDE)


def greet(place):
    barrier = pltpu.get_barrier_semaphore()
    for axis in range(2):
        for steps in (1, -1):
            y, x = moved(place, axis, steps)
            pl.semaphore_signal(
                barrier,
                inc=1,
                device_id={"tensor": y * SIDE + x},
                device_id_type=pl.DeviceIdType.MESH,
            )
    pl.semaphore_wait(barrier, 4)


class Copies:
    def __init__(self, place, send_sems, recv_sems):
        self.place, self.send, self.recv, self.used = place, send_sems, recv_sems, 0
        self.started = []

    def start(self, source, target, axis, steps):
        y, x = moved(self.place, axis, steps)
        n = self.used
        self.used += 1
        copy = pltpu.make_async_remote_copy(
            src_ref=source,
            dst_ref=target,
            send_sem=self.send.at[n],
            recv_sem=self.recv.at[n],
            device_id={"tensor": y * SIDE + x},
            device_id_type=pl.DeviceIdType.MESH,
        )
        copy.start()
        self.started.append(copy)
        return copy

    def finish(self):
        for copy in self.started:
            copy.wait_send()
        self.started = []


def gather(copies, bufs):
    place = copies.place
    jobs = []
    for buf in bufs:
        half = buf.shape[-1] // 2
        for h in range(2):
            jobs.append((buf, 1 - h, h, h * half, half))

    def block(job, r, s, part=None):
        buf, a, b, start, size = job
        y, x = moved(moved(place, a, r), b, s)
        if part is not None:
            size = size // 2
            start = start + part * size
        return buf.at[y, x, :, pl.ds(start, size)]

    def send(job, axis, steps, r, s, part=None):
        ref = block(job, r, s, part)
        return copies.start(ref, ref, axis, steps)

    first, spread, ahead = [], [], []
    for job in jobs:
        a, b = job[1], job[2]
        first.append([send(job, a, 1, 0, 0), send(job, a, -1, 0, 0)])
    for job in jobs:
        b = job[2]
        spread.append({0: [send(job, b, 1, 0, 0), send(job, b, -1, 0, 0)]})
    second = []
    for i, job in enumerate(jobs):
        a, b = job[1], job[2]
        first[i][0].wait_recv()
        one = send(job, a, 1, -1, 0, 0)
        spread[i][3] = [send(job, b, 1, -1, 0), send(job, b, -1, -1, 0)]
        first[i][1].wait_recv()
        two = send(job, a, -1, 1, 0, 1)
        spread[i][1] = [send(job, b, 1, 1, 0), send(job, b, -1, 1, 0)]
        second.append([one, two])
    for i, job in enumerate(jobs):
        b = job[2]
        spread[i][0][0].wait_recv()
        ahead.append([send(job, b, 1, 0, -1)])
    for i, job in enumerate(jobs):
        b = job[2]
        second[i][0].wait_recv()
        second[i][1].wait_recv()
        spread[i][2] = [send(job, b, 1, 2, 0), send(job, b, -1, 2, 0)]
    for i, job in enumerate(jobs):
        b = job[2]
        for r in DOWN:
            spread[i][r][1].wait_recv()
            ahead[i].append(send(job, b, -1, r, 1))
    for i, job in enumerate(jobs):
        b = job[2]
        spread[i][2][0].wait_recv()
        ahead[i].append(send(job, b, 1, 2, -1))
    for i, job in enumerate(jobs):
        spread[i][0][1].wait_recv()
        for r in DOWN:
            spread[i][r][0].wait_recv()
        spread[i][2][1].wait_recv()
        for copy in ahead[i]:
            copy.wait_recv()
    copies.finish()


def sum_blocks(copies, parts):
    place = copies.place
    jobs = []
    for part, land in parts:
        half = part.shape[-1] // 2
        for h in range(2):
            jobs.append((part, land, 15 * h, 1 - h, h, h * half, half))

    def block(job, r, s, quarter=None):
        part, _, _, a, b, start, size = job
        y, x = moved(moved(place, a, r), b, s)
        if quarter is not None:
            size = size // 2
            start = start + quarter * size
        return part.at[y, x, :, pl.ds(start, size)]

    def landing(job, n, quarter=None):
        ref = job[1].at[job[2] + n]
        if quarter is None:
            return ref
        size = job[6] // 2
        return ref.at[:, pl.ds(quarter * size, size)]

    def add(target, *others):
        total = target[...].astype(F32)
        for other in others:
            total = total + other[...].astype(F32)
        return total

    far, near = [], []
    for job in jobs:
        b = job[4]
        sent = {}
        for r in (2, 3, 1, 0):
            steps = 1 if r in UP else -1
            sent[r] = copies.start(block(job, r, 2), landing(job, r), b, steps)
        far.append(sent)
    order = (2, 3, 1, 0)
    for job in jobs:
        b = job[4]
        sent = {}
        for r in order:
            steps = -1 if r in UP else 1
            sent[r] = [
                copies.start(block(job, r, steps), landing(job, 4 + 2 * r + (0 if steps == 1 else 1)), b, steps)
            ]
        near.append(sent)
    for r in order:
        for i, job in enumerate(jobs):
            b = job[4]
            steps = 1 if r in UP else -1
            far[i][r].wait_recv()
            ref = block(job, r, steps)
            ref[...] = add(ref, landing(job, r)).astype(BF16)
            near[i][r].append(
                copies.start(ref, landing(job, 4 + 2 * r + (0 if steps == 1 else 1)), b, steps)
            )
    opposite, last = [], []
    for r in order[:3]:
        for i, job in enumerate(jobs):
            a = job[3]
            for copy in near[i][r]:
                copy.wait_recv()
            ref = block(job, r, 0)
            total = add(ref, landing(job, 4 + 2 * r), landing(job, 5 + 2 * r))
            if r == 2:
                ref[...] = total.astype(BF16)
                opposite.append(
                    [
                        copies.start(block(job, 2, 0, 0), landing(job, 12, 0), a, 1),
                        copies.start(block(job, 2, 0, 1), landing(job, 12, 1), a, -1),
                    ]
                )
                last.append({})
            else:
                quarter = 0 if r == 1 else 1
                opposite[i][quarter].wait_recv()
                size = job[6] // 2
                extra = landing(job, 12, quarter)[...].astype(F32)
                low, high = total[:, :size], total[:, size:]
                if quarter == 0:
                    low = low + extra
                else:
                    high = high + extra
                ref[:, pl.ds(0, size)] = low.astype(BF16)
                ref[:, pl.ds(size, size)] = high.astype(BF16)
                steps = 1 if r == 1 else -1
                last[i][r] = copies.start(ref, landing(job, 13 if r == 1 else 14), a, steps)
    results = []
    for i, job in enumerate(jobs):
        for copy in near[i][0]:
            copy.wait_recv()
        last[i][1].wait_recv()
        last[i][3].wait_recv()
        results.append(
            add(block(job, 0, 0), landing(job, 4), landing(job, 5), landing(job, 13), landing(job, 14))
        )
    copies.finish()
    return results


def sems(n):
    return [pltpu.SemaphoreType.DMA((n,)), pltpu.SemaphoreType.DMA((n,))]


VM = pl.BlockSpec(memory_space=pltpu.VMEM)


def gather_call(blocks, collective_id):
    count = len(blocks)

    def kernel(*refs):
        ins, outs, (send, recv) = refs[:count], refs[count : 2 * count], refs[2 * count :]
        place = at_grid()
        greet(place)
        for i, o in zip(ins, outs):
            o[place[0], place[1]] = i[...]
        gather(Copies(place, send, recv), outs)

    return pl.pallas_call(
        kernel,
        out_shape=[jax.ShapeDtypeStruct((SIDE, SIDE) + b.shape, b.dtype) for b in blocks],
        in_specs=[VM] * count,
        out_specs=[VM] * count,
        scratch_shapes=sems(GATHER_COPIES * count),
        compiler_params=pltpu.CompilerParams(
            collective_id=collective_id, has_side_effects=True, vmem_limit_bytes=48 << 20
        ),
    )(*blocks)


def sum_call(partials, collective_id):
    count = len(partials)

    def kernel(*refs):
        ins, outs = refs[:count], refs[count : 2 * count]
        lands, (send, recv) = refs[2 * count : 3 * count], refs[3 * count : 3 * count + 2]
        work = refs[3 * count + 2 :]
        place = at_grid()
        greet(place)
        for i, w in zip(ins, work):
            w[...] = i[...]
        results = sum_blocks(Copies(place, send, recv), list(zip(work, lands)))
        for n, out in enumerate(outs):
            half = out.shape[-1] // 2
            for h in range(2):
                out[:, h * half : (h + 1) * half] = results[2 * n + h]

    return pl.pallas_call(
        kernel,
        out_shape=[jax.ShapeDtypeStruct(p.shape[2:], F32) for p in partials],
        in_specs=[VM] * count,
        out_specs=[VM] * count,
        scratch_shapes=[
            pltpu.VMEM((30, p.shape[2], p.shape[3] // 2), BF16) for p in partials
        ]
        + sems(SUM_COPIES * count)
        + [pltpu.VMEM(p.shape, BF16) for p in partials],
        compiler_params=pltpu.CompilerParams(
            collective_id=collective_id, has_side_effects=True, vmem_limit_bytes=48 << 20
        ),
    )(*partials)


def swapped(value, axis):
    return lax.ppermute(value, axis, [(0, 1), (1, 0)])


def norm_parts(values):
    center = values - jnp.mean(values, -1, keepdims=True)
    scale = lax.rsqrt(jnp.mean(center * center, -1, keepdims=True) + EPSILON)
    return center * scale, scale


def norm_back(grad, unit, scale, gains):
    inner = grad * gains
    back = scale * (
        inner
        - jnp.mean(inner, -1, keepdims=True)
        - unit * jnp.mean(inner * unit, -1, keepdims=True)
    )
    return back, jnp.sum(grad * unit, 0), jnp.sum(grad, 0)


def gelu_exact(values):
    return jax.nn.gelu(values, approximate=False)


MESH = pl.DeviceIdType.MESH


class Links:
    def __init__(self, send_sems, recv_sems):
        self.send, self.recv, self.used, self.started = send_sems, recv_sems, 0, []

    def start(self, source, target, device):
        n = self.used
        self.used += 1
        copy = pltpu.make_async_remote_copy(
            src_ref=source,
            dst_ref=target,
            send_sem=self.send.at[n],
            recv_sem=self.recv.at[n],
            device_id=device,
            device_id_type=MESH,
        )
        copy.start()
        self.started.append(copy)
        return copy

    def finish(self):
        for copy in self.started:
            copy.wait_send()
        self.started = []


TAIL_COPIES = 2 * 8 + 11 + 2


def tail_kernel(
    att, ffn, small, enc, out3, dec, att_out, ffn_out, small_out, enc_out, out3_out, dec_out, *scratch
):
    (work_a, work_f, core_a, core_f, side_a, side_f, pass_a, pass_f, over_a, over_f) = scratch[:10]
    (fin, core_s, z_s, y_s, x_s, give_e, give_d, land_e, land_d, send, recv) = scratch[10:]
    section, dp = lax.axis_index("section"), lax.axis_index("dp")
    zh, core = lax.div(dp, 2), lax.rem(dp, 2)
    y, x = at_grid()
    other = 1 - section
    sibling = {"dp": zh * 2 + 1 - core}
    across = [{"section": other, "dp": h * 2 + core} for h in range(2)]
    zh_plus = lax.rem(zh + section, 2)
    plus = {"section": other, "dp": zh_plus * 2 + core}
    minus = {"section": other, "dp": (1 - zh_plus) * 2 + core}
    far = {"dp": (1 - zh) * 2 + core}
    partner = {"section": other}
    columns = [{"tensor": lax.rem(y + d, SIDE) * SIDE + x} for d in (1, 2, 3)]
    rows = [{"tensor": y * SIDE + lax.rem(x + d, SIDE)} for d in (1, 2, 3)]
    barrier = pltpu.get_barrier_semaphore()
    for device in [sibling, *across, far, *columns, *rows]:
        pl.semaphore_signal(barrier, inc=1, device_id=device, device_id_type=MESH)
    pl.semaphore_wait(barrier, 10)
    links = Links(send, recv)

    jobs = [
        (att, work_a, core_a, side_a, pass_a, over_a, att_out),
        (ffn, work_f, core_f, side_f, pass_f, over_f, ffn_out),
    ]
    steps = [[], []]
    one = links.start(small.at[1 - core], core_s, sibling)
    for i, (grad, work, core_land, *_) in enumerate(jobs):
        half = grad.shape[1] // 2
        steps[i].append(
            links.start(grad.at[:, pl.ds((1 - core) * half, half)], core_land, sibling)
        )
    width = enc.shape[1] // 2
    there = pl.ds(pl.multiple_of(other * width, width), width)
    here = pl.ds(pl.multiple_of(section * width, width), width)
    give_e[...] = enc[:, there].astype(BF16)
    give_d[...] = jnp.concatenate([out3[:, there], dec[:, there]], 0).astype(BF16)
    swaps = [links.start(give_e, land_e, partner), links.start(give_d, land_d, partner)]
    one.wait_recv()
    fin[core] = small[core] + core_s[...]
    two = [links.start(fin.at[core], z_s.at[n], d) for n, d in enumerate([plus, minus, far])]
    for i, (grad, work, core_land, side, *_) in enumerate(jobs):
        half = grad.shape[1] // 2
        quarter = half // 2
        steps[i][0].wait_recv()
        work[...] = (
            grad[:, pl.ds(core * half, half)].astype(F32) + core_land[...].astype(F32)
        ).astype(BF16)
        steps[i].append(
            [
                links.start(work.at[other, pl.ds(h * quarter, quarter)], side.at[n], d)
                for n, (h, d) in enumerate(((zh_plus, plus), (1 - zh_plus, minus)))
            ]
        )
    for copy in two:
        copy.wait_recv()
    for copy in two:
        copy.wait_send()
    fin[core] = fin[core] + z_s[0] + z_s[1] + z_s[2]
    three = [links.start(fin.at[core], y_s.at[n], d) for n, d in enumerate(columns)]
    for i, (grad, work, core_land, side, passing, over, _) in enumerate(jobs):
        quarter = grad.shape[1] // 4
        for copy in steps[i][1]:
            copy.wait_recv()
        mine = work.at[section, pl.ds(zh * quarter, quarter)]
        mine[...] = (
            mine[...].astype(F32) + side[0].astype(F32) + side[1].astype(F32)
        ).astype(BF16)
        steps[i].append(
            [
                links.start(work.at[section, pl.ds(0, quarter)], passing.at[0], plus),
                links.start(work.at[section, pl.ds(quarter, quarter)], passing.at[1], minus),
            ]
        )
    for copy in three:
        copy.wait_recv()
    for copy in three:
        copy.wait_send()
    fin[core] = fin[core] + y_s[0] + y_s[1] + y_s[2]
    four = [links.start(fin.at[core], x_s.at[n], d) for n, d in enumerate(rows)]
    for i, (grad, work, core_land, side, passing, over, _) in enumerate(jobs):
        quarter = grad.shape[1] // 4
        ahead = []
        for n, device in enumerate((plus, minus)):
            steps[i][2][n].wait_recv()
            ahead.append(
                links.start(passing.at[n], over.at[pl.ds(n * quarter, quarter)], device)
            )
        steps[i].append(ahead)
    for copy in four:
        copy.wait_recv()
    for copy in four:
        copy.wait_send()
    fin[core] = fin[core] + x_s[0] + x_s[1] + x_s[2]
    five = links.start(fin.at[core], fin.at[core], sibling)
    for copy in swaps:
        copy.wait_recv()
    enc_out[section] = enc[:, here]
    enc_out[other] = land_e[...].astype(F32)
    got = land_d[...].astype(F32)
    count = out3.shape[0]
    out3_out[section] = out3[:, here]
    out3_out[other] = got[:count]
    dec_out[section] = dec[:, here]
    dec_out[other] = got[count:]
    last = []
    for i, (grad, work, core_land, side, passing, over, out) in enumerate(jobs):
        half = grad.shape[1] // 2
        for copy in steps[i][3]:
            copy.wait_recv()
        out[core] = (work[section].astype(F32) + over[...].astype(F32)).astype(BF16)
        last.append(links.start(out.at[core], out.at[core], sibling))
    five.wait_recv()
    small_out[...] = fin[section]
    for copy in last:
        copy.wait_recv()
    waited = {id(c) for c in two + three + four}
    for copy in links.started:
        if id(copy) not in waited:
            copy.wait_send()


def tail_call(att, ffn, small, enc, out3, dec, collective_id):
    grads = (att, ffn)
    shape = jax.ShapeDtypeStruct
    width = enc.shape[1] // 2

    def land(*lead):
        return [pltpu.VMEM((*lead(g), g.shape[2]), BF16) for lead in lead for g in grads]

    return pl.pallas_call(
        tail_kernel,
        out_shape=[shape((2, g.shape[1] // 2, g.shape[2]), BF16) for g in grads]
        + [
            shape(small.shape[1:], F32),
            shape((2, enc.shape[0], width), F32),
            shape((2, out3.shape[0], width), F32),
            shape((2, dec.shape[0], width), F32),
        ],
        in_specs=[VM] * 6,
        out_specs=[VM] * 6,
        scratch_shapes=land(
            lambda g: (2, g.shape[1] // 2),
            lambda g: (2, g.shape[1] // 2),
            lambda g: (2, g.shape[1] // 4),
            lambda g: (2, g.shape[1] // 4),
            lambda g: (g.shape[1] // 2,),
        )
        + [
            pltpu.VMEM(small.shape, F32),
            pltpu.VMEM(small.shape[1:], F32),
            pltpu.VMEM((3, *small.shape[1:]), F32),
            pltpu.VMEM((3, *small.shape[1:]), F32),
            pltpu.VMEM((3, *small.shape[1:]), F32),
            pltpu.VMEM((enc.shape[0], width), BF16),
            pltpu.VMEM((2 * dec.shape[0], width), BF16),
            pltpu.VMEM((enc.shape[0], width), BF16),
            pltpu.VMEM((2 * dec.shape[0], width), BF16),
        ]
        + sems(TAIL_COPIES),
        compiler_params=pltpu.CompilerParams(
            collective_id=collective_id, has_side_effects=True, vmem_limit_bytes=48 << 20
        ),
    )(att, ffn, small, enc, out3, dec)


INV_SQRT2 = 0.7071067811865476
INV_SQRT_2PI = 0.3989422804014327
FAR_FIRST = (10, 2, 8, 6, 14, 11, 9, 7, 13, 5, 15, 1, 3, 4, 12)


def gelu_parts(u):
    cdf = 0.5 * (1.0 + lax.erf(u * INV_SQRT2))
    return u * cdf, cdf + u * (INV_SQRT_2PI * jnp.exp(-0.5 * u * u))


def away(y, x, d):
    return lax.rem(y + d // SIDE, SIDE), lax.rem(x + d % SIDE, SIDE)


def greet_all(y, x):
    barrier = pltpu.get_barrier_semaphore()
    for d in range(1, SIDE * SIDE):
        ty, tx = away(y, x, d)
        pl.semaphore_signal(
            barrier, inc=1, device_id={"tensor": ty * SIDE + tx}, device_id_type=MESH
        )
    pl.semaphore_wait(barrier, SIDE * SIDE - 1)


def gather_small(links, y, x, buf, rows):
    count, half = rows.shape[0], rows.shape[1] // 2
    buf[y, x] = jnp.concatenate([rows[:, :half], rows[:, half:]], 0).astype(BF16)
    copies = []
    for d in FAR_FIRST:
        ty, tx = away(y, x, d)
        copies.append(links.start(buf.at[y, x], buf.at[y, x], {"tensor": ty * SIDE + tx}))
    for copy in copies:
        copy.wait_recv()
    return unfold_all(buf[...], count)


def unfold_all(blocks, count):
    half = blocks.shape[-1]
    split = blocks.astype(F32).reshape(SIDE * SIDE, 2, count, half)
    low = split[:, 0].reshape(SIDE * SIDE * count, half)
    high = split[:, 1].reshape(SIDE * SIDE * count, half)
    return jnp.concatenate([low, high], 1).astype(BF16)


def fold_all(part):
    count, half = part.shape[0] // (SIDE * SIDE), part.shape[1] // 2
    split = part.reshape(SIDE * SIDE, count, 2 * half)
    both = jnp.concatenate([split[:, :, :half], split[:, :, half:]], 1)
    return both.astype(BF16).reshape(SIDE, SIDE, 2 * count, half)


def sum_small(links, y, x, work, land, part):
    work[...] = fold_all(part)
    copies = []
    for n, d in enumerate(FAR_FIRST):
        ty, tx = away(y, x, d)
        copies.append(
            links.start(work.at[ty, tx], land.at[n], {"tensor": ty * SIDE + tx})
        )
    total = work[y, x].astype(F32)
    for n, copy in enumerate(copies):
        copy.wait_recv()
    total = total + jnp.sum(land[...].astype(F32), 0)
    count = total.shape[0] // 2
    return jnp.concatenate([total[:count], total[count:]], 1)


def decoder_kernel(
    cq, kvc, d1, cot, seg_d, seg_e, w5, ffn, gains, shifts, *rest
):
    (d3, dback1, full_d2, full_db2, full_db1, hid_out, pre_out, att_out) = rest[:8]
    (cq_grad, kvc_grad, grads, g_bufs, s_work, s_land, probs, send, recv) = rest[8:]
    y, x = at_grid()
    greet_all(y, x)
    links = Links(send, recv)
    kc, vc = kvc[:, :HEAD], kvc[:, HEAD:]
    allowed = seg_d[...] == seg_e[...]
    scores = jnp.where(allowed, dot_t(cq[...], kc) * HEAD ** (-0.5), MASKED)
    exponent = jnp.exp(scores - jnp.max(scores, -1, keepdims=True))
    probs[...] = exponent / jnp.sum(exponent, -1, keepdims=True)
    att = dot(probs[...].astype(BF16), vc).astype(BF16)
    att_out[...] = att
    part = sum_small(links, y, x, s_work.at[0], s_land.at[0], dot_t(att, w5[...]))
    unit1, scale1 = norm_parts(d1[...] + part)
    d2 = unit1 * gains[1:2, :] + shifts[1:2, :]
    full = gather_small(links, y, x, g_bufs.at[0], d2)
    full_d2[...] = full
    hidden, slope = gelu_parts(dot(full, ffn[0]))
    hidden = hidden.astype(BF16)
    hid_out[...] = hidden
    part = sum_small(links, y, x, s_work.at[1], s_land.at[1], dot_t(hidden, ffn[1]))
    unit2, scale2 = norm_parts(d2 + part)
    d3[...] = unit2 * gains[2:3, :] + shifts[2:3, :]
    back2, gain2, shift2 = norm_back(cot[...].astype(F32), unit2, scale2, gains[2:3, :])
    full = gather_small(links, y, x, g_bufs.at[1], back2)
    full_db2[...] = full
    pre = (dot(full, ffn[1]) * slope).astype(BF16)
    pre_out[...] = pre
    part = sum_small(links, y, x, s_work.at[2], s_land.at[2], dot_t(pre, ffn[0]))
    back1, gain1, shift1 = norm_back(back2 + part, unit1, scale1, gains[1:2, :])
    dback1[...] = back1
    full = gather_small(links, y, x, g_bufs.at[2], back1)
    full_db1[...] = full
    att_grad = dot(full, w5[...]).astype(BF16)
    p = probs[...]
    value_grad = t_dot(p.astype(BF16), att_grad)
    p_grad = dot_t(att_grad, vc)
    s_grad = (p * (p_grad - jnp.sum(p * p_grad, -1, keepdims=True))).astype(BF16)
    cq_grad[...] = (dot(s_grad, kc) * HEAD ** (-0.5)).astype(BF16)
    key_grad = t_dot(s_grad, cq[...]) * HEAD ** (-0.5)
    kvc_grad[...] = jnp.concatenate([key_grad, value_grad], 1).astype(BF16)
    grads[0:1, :] = gain1[None]
    grads[1:2, :] = gain2[None]
    grads[2:3, :] = shift1[None]
    grads[3:4, :] = shift2[None]
    grads[4:8, :] = jnp.zeros((4, grads.shape[1]), F32)
    links.finish()


def decoder_call(cq, kvc, d1, cot, seg_d, seg_e, w5, ffn, gains, shifts, collective_id):
    shape = jax.ShapeDtypeStruct
    rows, width = d1.shape
    full = SIDE * SIDE * rows
    hidden = ffn.shape[2]
    block = (SIDE, SIDE, 2 * rows, width // 2)
    return pl.pallas_call(
        decoder_kernel,
        out_shape=[
            shape((rows, width), F32),
            shape((rows, width), F32),
            shape((full, width), BF16),
            shape((full, width), BF16),
            shape((full, width), BF16),
            shape((full, hidden), BF16),
            shape((full, hidden), BF16),
            shape((full, HEAD), BF16),
            shape((full, HEAD), BF16),
            shape(kvc.shape, BF16),
            shape((8, width), F32),
        ],
        in_specs=[VM] * 10,
        out_specs=[VM] * 11,
        scratch_shapes=[
            pltpu.VMEM((3, *block), BF16),
            pltpu.VMEM((3, *block), BF16),
            pltpu.VMEM((3, SIDE * SIDE - 1, *block[2:]), BF16),
            pltpu.VMEM((full, kvc.shape[0]), F32),
        ]
        + sems(6 * (SIDE * SIDE - 1)),
        compiler_params=pltpu.CompilerParams(
            collective_id=collective_id, has_side_effects=True, vmem_limit_bytes=48 << 20
        ),
    )(cq, kvc, d1, cot, seg_d, seg_e, w5, ffn, gains, shifts)


def folded(rows):
    half = rows.shape[-1] // 2
    return jnp.concatenate([rows[..., :half], rows[..., half:]], -2)


def unfolded(rows):
    count = rows.shape[-2] // 2
    return jnp.concatenate([rows[..., :count, :], rows[..., count:, :]], -1)


def gather_enc(rows, n):
    (full,) = gather_call([rows.astype(BF16)], n)
    return full.reshape(-1, rows.shape[-1])


def gather_dec(rows, n):
    (full,) = gather_call([folded(rows).astype(BF16)], n)
    return unfolded(full).reshape(-1, rows.shape[-1])


def gather_both(enc, dec, n):
    full, small = gather_call([enc.astype(BF16), folded(dec).astype(BF16)], n)
    return full.reshape(-1, enc.shape[-1]), unfolded(small).reshape(-1, dec.shape[-1])


def in_blocks(part):
    return part.astype(BF16).reshape(SIDE, SIDE, -1, part.shape[-1])


def sum_enc(part, n):
    return sum_call([in_blocks(part)], n)[0]


def sum_dec(part, n):
    return unfolded(sum_call([folded(in_blocks(part))], n)[0])


def sum_both(enc, dec, n):
    rows, small = sum_call([in_blocks(enc), folded(in_blocks(dec))], n)
    return rows, unfolded(small)


def dot(a, b):
    return jnp.dot(a, b, preferred_element_type=F32)


def dot_t(a, b):
    return lax.dot_general(a, b, (((1,), (1,)), ((), ())), preferred_element_type=F32)


def t_dot(a, b):
    return lax.dot_general(a, b, (((0,), (0,)), ((), ())), preferred_element_type=F32)


def scores_of(queries, key_rows, allowed):
    return jnp.where(allowed, dot_t(queries, key_rows) * HEAD ** (-0.5), MASKED)


def attend(queries, key_rows, value_rows, allowed):
    scores = scores_of(queries, key_rows, allowed)
    row_max = jnp.max(scores, -1, keepdims=True)
    exponent = jnp.exp(scores - row_max)
    row_sum = jnp.sum(exponent, -1, keepdims=True)
    probs_low = (exponent / row_sum).astype(BF16)
    return dot(probs_low, value_rows).astype(BF16), row_max + jnp.log(row_sum)


def attend_back(queries, key_rows, value_rows, log_total, allowed, attended_grad):
    scores = scores_of(queries, key_rows, allowed)
    probs = jnp.exp(scores - log_total)
    value_grad = t_dot(probs.astype(BF16), attended_grad)
    probs_grad = dot_t(attended_grad, value_rows)
    scores_grad = (probs * (probs_grad - jnp.sum(probs * probs_grad, -1, keepdims=True))).astype(
        BF16
    )
    query_grad = dot(scores_grad, key_rows) * HEAD ** (-0.5)
    key_grad = t_dot(scores_grad, queries) * HEAD ** (-0.5)
    return query_grad.astype(BF16), key_grad.astype(BF16), value_grad.astype(BF16)


def feedforward_back(full_back, full_in, up, down):
    hidden_raw, gelu_pull = jax.vjp(gelu_exact, dot(full_in, up))
    hidden = hidden_raw.astype(BF16)
    down_grad = t_dot(full_back, hidden)
    pre_grad = gelu_pull(dot(full_back, down))[0].astype(BF16)
    up_grad = t_dot(full_in, pre_grad)
    return pre_grad, up_grad, down_grad


def slot(weights, first, last):
    return weights[:, first * HEAD : last * HEAD]


def on_device(
    encoder_tokens,
    encoder_segments,
    decoder_tokens,
    decoder_segments,
    cotangent,
    attention_weight,
    feedforward_weight,
    norm_gain,
    norm_shift,
):
    section = lax.axis_index("section")
    on_encoder = section == 0
    mine = lambda a: lax.dynamic_index_in_dim(a, section, 0, keepdims=False)

    def layers(own):
        other = swapped(own, "section")
        return jnp.where(on_encoder, own, other), jnp.where(on_encoder, other, own)

    own_attention = jnp.concatenate([attention_weight[0, j] for j in range(6)], 1)
    we, wd = layers(own_attention)
    fe, fd = layers(feedforward_weight[0])
    ge, gd = layers(norm_gain[0])
    se, sd = layers(norm_shift[0])

    x = mine(encoder_tokens).astype(F32)
    y = mine(decoder_tokens).astype(F32)
    cot = mine(cotangent).astype(F32)
    e = mine(encoder_segments)
    c = mine(decoder_segments)
    position = jnp.arange(c.shape[0])
    allow_e = e[:, None] == e[None, :]
    allow_d = (c[:, None] == c[None, :]) & (position[:, None] >= position[None, :])

    unit0, scale0 = norm_parts(x)
    h0 = unit0 * ge[0] + se[0]
    full_h0, full_y = gather_both(h0, y, 1)
    qkv = dot(full_h0, slot(we, 0, 3)).astype(BF16)
    q, k, v = (slot(qkv, j, j + 1) for j in range(3))
    att_e, log_e = attend(q, k, v, allow_e)
    dqkv = dot(full_y, slot(wd, 0, 3)).astype(BF16)
    sq, sk, sv = (slot(dqkv, j, j + 1) for j in range(3))
    att_d, log_d = attend(sq, sk, sv, allow_d)
    part_e, part_d = sum_both(dot_t(att_e, slot(we, 3, 4)), dot_t(att_d, slot(wd, 3, 4)), 2)
    unit1, scale1 = norm_parts(h0 + part_e)
    h1 = unit1 * ge[1] + se[1]
    dunit0, dscale0 = norm_parts(y + part_d)
    d1 = dunit0 * gd[0] + sd[0]
    full_h1, full_d1 = gather_both(h1, d1, 3)
    hidden = gelu_exact(dot(full_h1, fe[0])).astype(BF16)
    cq = dot(full_d1, slot(wd, 4, 5)).astype(BF16)
    unit2, scale2 = norm_parts(h1 + sum_enc(dot_t(hidden, fe[1]), 4))
    full_m = gather_enc(unit2 * ge[2] + se[2], 5)
    kvc = dot(full_m, slot(we, 4, 6)).astype(BF16)

    (d3, dback1, full_d2, full_db2, full_db1, dhidden, dpre, att_c, cq_grad, kvc_grad, dsmall) = (
        decoder_call(
            cq, kvc, d1, cot, c[:, None], e[None, :], slot(wd, 5, 6), fd, gd, sd, 6
        )
    )
    dup, ddown = t_dot(full_d2, dpre), t_dot(full_db2, dhidden)
    d_w5 = t_dot(full_db1, att_c)
    d_w4 = t_dot(full_d1, cq_grad)
    e_w45 = t_dot(full_m, kvc_grad)

    mem_grad, d1_grad = sum_both(
        dot_t(kvc_grad, slot(we, 4, 6)), dot_t(cq_grad, slot(wd, 4, 5)), 12
    )
    back2, gain2, shift2 = norm_back(mem_grad, unit2, scale2, ge[2])
    dback0, dgain0, dshift0 = norm_back(dback1 + d1_grad, dunit0, dscale0, gd[0])
    full_b2, full_db0 = gather_both(back2, dback0, 13)
    pre, up, down = feedforward_back(full_b2, full_h1, fe[0], fe[1])
    att_d_grad = dot(full_db0, slot(wd, 3, 4)).astype(BF16)
    d_w3 = t_dot(full_db0, att_d)
    dqkv_grad = jnp.concatenate(attend_back(sq, sk, sv, log_d, allow_d, att_d_grad), 1)
    d_w012 = t_dot(full_y, dqkv_grad)
    part_e, part_d = sum_both(dot_t(pre, fe[0]), dot_t(dqkv_grad, slot(wd, 0, 3)), 14)
    dec_grad = dback0 + part_d
    back1, gain1, shift1 = norm_back(back2 + part_e, unit1, scale1, ge[1])
    full_b1 = gather_enc(back1, 15)
    att_e_grad = dot(full_b1, slot(we, 3, 4)).astype(BF16)
    e_w3 = t_dot(full_b1, att_e)
    qkv_grad = jnp.concatenate(attend_back(q, k, v, log_e, allow_e, att_e_grad), 1)
    e_w012 = t_dot(full_h0, qkv_grad)
    enc_grad, gain0, shift0 = norm_back(
        back1 + sum_enc(dot_t(qkv_grad, slot(we, 0, 3)), 16), unit0, scale0, ge[0]
    )

    att_grads = jnp.stack(
        [jnp.concatenate([e_w012, e_w3, e_w45], 1), jnp.concatenate([d_w012, d_w3, d_w4, d_w5], 1)]
    ).astype(BF16)
    ffn_grads = jnp.stack([jnp.stack([up, down]), jnp.stack([dup, ddown])]).astype(BF16)
    none = jnp.zeros_like(gain0)
    small = jnp.stack(
        [
            jnp.stack([gain0, gain1, gain2, shift0, shift1, shift2, none, none]),
            jnp.stack([dgain0, dsmall[0], dsmall[1], dshift0, dsmall[2], dsmall[3], none, none]),
        ]
    )
    ffn_grads = ffn_grads.reshape(2, -1, ffn_grads.shape[-1])
    att_sum, ffn_sum, small_sum, enc_out, d3_out, dec_out = tail_call(
        att_grads, ffn_grads, small, enc_grad, d3, dec_grad, 7
    )
    att_sum = att_sum.reshape(att_grads.shape[1:]).astype(F32)
    att_out = jnp.stack([slot(att_sum, j, j + 1) for j in range(6)])
    return (
        d3_out.astype(BF16),
        enc_out,
        dec_out,
        att_out[None],
        ffn_sum.reshape(feedforward_weight.shape).astype(F32),
        small_sum[None, :3],
        small_sum[None, 3:6],
    )


def solution(mesh):
    in_specs = (
        P("dp", "tensor", None),
        P("dp", None),
        P("dp", "tensor", None),
        P("dp", None),
        P("dp", "tensor", None),
        P("section", None, None, "tensor"),
        P("section", None, None, "tensor"),
        P("section", None, None),
        P("section", None, None),
    )
    out_specs = (
        P("dp", "tensor", "section"),
        P("dp", "tensor", "section"),
        P("dp", "tensor", "section"),
        P("section", None, None, "tensor"),
        P("section", None, None, "tensor"),
        P("section", None, None),
        P("section", None, None),
    )
    return jax.shard_map(
        on_device, mesh=mesh, in_specs=in_specs, out_specs=out_specs, check_vma=False
    )
```

```python
import jax
import jax.numpy as jnp
from jax import lax
from jax.experimental import pallas as pl
from jax.experimental.pallas import tpu as pltpu
from jax.sharding import PartitionSpec as P

HEAD = 64
EPSILON = 1e-05
MASKED = -1000000000.0
SCALE = HEAD ** (-0.5)
F32 = jnp.float32
BF16 = jnp.bfloat16
MESH = pl.DeviceIdType.MESH
VM = pl.BlockSpec(memory_space=pltpu.VMEM)
SIDE = 4
DEVICES = SIDE * SIDE
UP = (0, 2)
DOWN = (1, 3)
RING_COPIES = 32
INV_SQRT2 = 0.7071067811865476
INV_SQRT_2PI = 0.3989422804014327
FAR_FIRST = (10, 2, 8, 6, 14, 11, 9, 7, 13, 5, 15, 1, 3, 4, 12)


def norm_parts(values):
    center = values - jnp.mean(values, -1, keepdims=True)
    scale = lax.rsqrt(jnp.mean(center * center, -1, keepdims=True) + EPSILON)
    return center * scale, scale


def norm_back(grad, unit, scale, gains):
    inner = grad * gains
    back = scale * (
        inner
        - jnp.mean(inner, -1, keepdims=True)
        - unit * jnp.mean(inner * unit, -1, keepdims=True)
    )
    return back, jnp.sum(grad * unit, 0, keepdims=True), jnp.sum(grad, 0, keepdims=True)


def gelu_parts(u):
    cdf = 0.5 * (1.0 + lax.erf(u * INV_SQRT2))
    return u * cdf, cdf + u * (INV_SQRT_2PI * jnp.exp(-0.5 * u * u))


def dot(a, b):
    return jnp.dot(a, b, preferred_element_type=F32)


def dot_t(a, b):
    return lax.dot_general(a, b, (((1,), (1,)), ((), ())), preferred_element_type=F32)


def t_dot(a, b):
    return lax.dot_general(a, b, (((0,), (0,)), ((), ())), preferred_element_type=F32)


def scores_of(queries, key_rows, allowed):
    return jnp.where(allowed, dot_t(queries, key_rows) * SCALE, MASKED)


def attend(queries, key_rows, value_rows, allowed):
    scores = scores_of(queries, key_rows, allowed)
    row_max = jnp.max(scores, -1, keepdims=True)
    exponent = jnp.exp(scores - row_max)
    row_sum = jnp.sum(exponent, -1, keepdims=True)
    probs_low = (exponent / row_sum).astype(BF16)
    return dot(probs_low, value_rows).astype(BF16), row_max + jnp.log(row_sum)


def attend_back(queries, key_rows, value_rows, log_total, allowed, attended_grad):
    probs = jnp.exp(scores_of(queries, key_rows, allowed) - log_total)
    value_grad = t_dot(probs.astype(BF16), attended_grad)
    probs_grad = dot_t(attended_grad, value_rows)
    scores_grad = (probs * (probs_grad - jnp.sum(probs * probs_grad, -1, keepdims=True))).astype(
        BF16
    )
    query_grad = dot(scores_grad, key_rows) * SCALE
    key_grad = t_dot(scores_grad, queries) * SCALE
    return query_grad.astype(BF16), key_grad.astype(BF16), value_grad.astype(BF16)


def at_grid():
    index = lax.axis_index("tensor")
    return lax.div(index, SIDE), lax.rem(index, SIDE)


def moved(place, dy, dx):
    return lax.rem(place[0] + dy % SIDE, SIDE), lax.rem(place[1] + dx % SIDE, SIDE)


def along(axis, steps):
    return (steps, 0) if axis == 0 else (0, steps)


def device_at(place):
    return {"tensor": place[0] * SIDE + place[1]}


def neighbours(place):
    return [device_at(moved(place, *along(axis, s))) for axis in range(2) for s in (1, -1)]


def greet(devices):
    barrier = pltpu.get_barrier_semaphore()
    for device in devices:
        pl.semaphore_signal(barrier, inc=1, device_id=device, device_id_type=MESH)
    pl.semaphore_wait(barrier, len(devices))


def sections():
    section, dp = lax.axis_index("section"), lax.axis_index("dp")
    zh, core = lax.div(dp, 2), lax.rem(dp, 2)
    return section, zh, core, {"section": 1 - section}, {"dp": zh * 2 + 1 - core}


class Links:
    def __init__(self, send_sems, recv_sems):
        self.send, self.recv, self.used, self.started = send_sems, recv_sems, 0, []

    def start(self, source, target, device):
        n = self.used
        self.used += 1
        copy = pltpu.make_async_remote_copy(
            src_ref=source,
            dst_ref=target,
            send_sem=self.send.at[n],
            recv_sem=self.recv.at[n],
            device_id=device,
            device_id_type=MESH,
        )
        copy.start()
        self.started.append(copy)
        return copy

    def finish(self):
        for copy in self.started:
            copy.wait_send()
        self.started = []


def sems(n):
    return [pltpu.SemaphoreType.DMA((n,)), pltpu.SemaphoreType.DMA((n,))]


def shape(dims, kind):
    return jax.ShapeDtypeStruct(tuple(dims), kind)


def params(collective_id):
    return pltpu.CompilerParams(
        collective_id=collective_id, has_side_effects=True, vmem_limit_bytes=56 << 20
    )


def fold(rows):
    half = rows.shape[1] // 2
    return jnp.concatenate([rows[:, :half], rows[:, half:]], 0)


def unfold(rows):
    count = rows.shape[0] // 2
    return jnp.concatenate([rows[:count], rows[count:]], 1)


def unfold_all(blocks):
    count, half = blocks.shape[2] // 2, blocks.shape[3]
    split = blocks.astype(F32).reshape(DEVICES, 2, count, half)
    low = split[:, 0].reshape(DEVICES * count, half)
    high = split[:, 1].reshape(DEVICES * count, half)
    return jnp.concatenate([low, high], 1).astype(BF16)


def fold_all(part):
    count, half = part.shape[0] // DEVICES, part.shape[1] // 2
    split = part.reshape(DEVICES, count, 2 * half)
    both = jnp.concatenate([split[:, :, :half], split[:, :, half:]], 1)
    return both.astype(BF16).reshape(SIDE, SIDE, 2 * count, half)


def gather(links, place, bufs, ready=None):
    jobs = []
    for buf in bufs:
        half = buf.shape[-1] // 2
        for h in range(2):
            jobs.append((buf, 1 - h, h, h * half, half))
    ready = ready or (lambda group: None)

    def send(job, axis, steps, r, s, part=None):
        buf, a, b, start, size = job
        y, x = moved(moved(place, *along(a, r)), *along(b, s))
        if part is not None:
            size = size // 2
            start = start + part * size
        ref = buf.at[y, x, :, pl.ds(start, size)]
        return links.start(ref, ref, device_at(moved(place, *along(axis, steps))))

    first, spread, second, ahead = [], [], [], []
    for job in jobs:
        first.append([send(job, job[1], 1, 0, 0), send(job, job[1], -1, 0, 0)])
    for job in jobs:
        spread.append({0: [send(job, job[2], 1, 0, 0), send(job, job[2], -1, 0, 0)]})
    ready([(0, 0)])
    for i, job in enumerate(jobs):
        a, b = job[1], job[2]
        first[i][0].wait_recv()
        one = send(job, a, 1, -1, 0, 0)
        spread[i][3] = [send(job, b, 1, -1, 0), send(job, b, -1, -1, 0)]
        first[i][1].wait_recv()
        two = send(job, a, -1, 1, 0, 1)
        spread[i][1] = [send(job, b, 1, 1, 0), send(job, b, -1, 1, 0)]
        second.append([one, two])
    for i, job in enumerate(jobs):
        spread[i][0][0].wait_recv()
        ahead.append([send(job, job[2], 1, 0, -1)])
    for i, job in enumerate(jobs):
        spread[i][0][1].wait_recv()
    ready([(0, 1), (0, 3), (1, 0), (3, 0)])
    for i, job in enumerate(jobs):
        second[i][0].wait_recv()
        second[i][1].wait_recv()
        spread[i][2] = [send(job, job[2], 1, 2, 0), send(job, job[2], -1, 2, 0)]
    for i, job in enumerate(jobs):
        for r in DOWN:
            spread[i][r][1].wait_recv()
            ahead[i].append(send(job, job[2], -1, r, 1))
    for i, job in enumerate(jobs):
        spread[i][2][0].wait_recv()
        ahead[i].append(send(job, job[2], 1, 2, -1))
    for i, job in enumerate(jobs):
        for r in DOWN:
            spread[i][r][0].wait_recv()
    ready([(1, 1), (1, 3), (3, 1), (3, 3)])
    for i, job in enumerate(jobs):
        ahead[i][0].wait_recv()
    ready([(0, 2), (2, 0)])
    for i, job in enumerate(jobs):
        spread[i][2][1].wait_recv()
        ahead[i][1].wait_recv()
        ahead[i][2].wait_recv()
    ready([(1, 2), (3, 2), (2, 1), (2, 3)])
    for i, job in enumerate(jobs):
        ahead[i][3].wait_recv()
    ready([(2, 2)])


PRODUCE = (
    [(2, 2), (2, 3), (2, 1), (3, 2), (1, 2), (2, 0), (0, 2)],
    [(3, 3), (3, 1), (1, 3), (1, 1), (3, 0), (1, 0), (0, 3), (0, 1), (0, 0)],
)


def sum_blocks(links, place, parts, produce=None):
    produce = produce or (lambda group: None)
    jobs = []
    for part, land in parts:
        half = part.shape[-1] // 2
        for h in range(2):
            jobs.append((part, land, 15 * h, 1 - h, h, h * half, half))

    def block(job, r, s, quarter=None):
        part, _, _, a, b, start, size = job
        y, x = moved(moved(place, *along(a, r)), *along(b, s))
        if quarter is not None:
            size = size // 2
            start = start + quarter * size
        return part.at[y, x, :, pl.ds(start, size)]

    def landing(job, n, quarter=None):
        ref = job[1].at[job[2] + n]
        if quarter is None:
            return ref
        size = job[6] // 2
        return ref.at[:, pl.ds(quarter * size, size)]

    def start(source, target, axis, steps):
        return links.start(source, target, device_at(moved(place, *along(axis, steps))))

    def add(target, *others):
        total = target[...].astype(F32)
        for other in others:
            total = total + other[...].astype(F32)
        return total

    def near_slot(job, r, steps):
        return landing(job, 4 + 2 * r + (0 if steps == 1 else 1))

    order = (2, 3, 1, 0)
    produce(PRODUCE[0])
    far = []
    for job in jobs:
        far.append(
            {r: start(block(job, r, 2), landing(job, r), job[4], 1 if r in UP else -1) for r in order}
        )
    produce(PRODUCE[1])
    near = []
    for job in jobs:
        sent = {}
        for r in order:
            steps = -1 if r in UP else 1
            sent[r] = [start(block(job, r, steps), near_slot(job, r, steps), job[4], steps)]
        near.append(sent)
    for r in order:
        for i, job in enumerate(jobs):
            steps = 1 if r in UP else -1
            far[i][r].wait_recv()
            ref = block(job, r, steps)
            ref[...] = add(ref, landing(job, r)).astype(BF16)
            near[i][r].append(start(ref, near_slot(job, r, steps), job[4], steps))
    opposite, last = [], []
    for r in order[:3]:
        for i, job in enumerate(jobs):
            for copy in near[i][r]:
                copy.wait_recv()
            ref = block(job, r, 0)
            total = add(ref, landing(job, 4 + 2 * r), landing(job, 5 + 2 * r))
            if r == 2:
                ref[...] = total.astype(BF16)
                opposite.append(
                    [
                        start(block(job, 2, 0, 0), landing(job, 12, 0), job[3], 1),
                        start(block(job, 2, 0, 1), landing(job, 12, 1), job[3], -1),
                    ]
                )
                last.append({})
            else:
                quarter = 0 if r == 1 else 1
                opposite[i][quarter].wait_recv()
                size = job[6] // 2
                extra = landing(job, 12, quarter)[...].astype(F32)
                low, high = total[:, :size], total[:, size:]
                if quarter == 0:
                    low = low + extra
                else:
                    high = high + extra
                ref[:, pl.ds(0, size)] = low.astype(BF16)
                ref[:, pl.ds(size, size)] = high.astype(BF16)
                last[i][r] = start(
                    ref, landing(job, 13 if r == 1 else 14), job[3], 1 if r == 1 else -1
                )
    results = []
    for i, job in enumerate(jobs):
        for copy in near[i][0]:
            copy.wait_recv()
        last[i][1].wait_recv()
        last[i][3].wait_recv()
        results.append(
            add(block(job, 0, 0), landing(job, 4), landing(job, 5), landing(job, 13), landing(job, 14))
        )
    return [jnp.concatenate(results[i : i + 2], 1) for i in range(0, len(results), 2)]


def gather_small(links, place, buf, rows):
    y, x = place
    buf[y, x] = fold(rows).astype(BF16)
    copies = []
    for d in FAR_FIRST:
        target = device_at(moved(place, d // SIDE, d % SIDE))
        copies.append(links.start(buf.at[y, x], buf.at[y, x], target))
    for copy in copies:
        copy.wait_recv()
    return unfold_all(buf[...])


def sum_small(links, place, work, land, part):
    work[...] = fold_all(part)
    copies = []
    for n, d in enumerate(FAR_FIRST):
        there = moved(place, d // SIDE, d % SIDE)
        copies.append(links.start(work.at[there[0], there[1]], land.at[n], device_at(there)))
    total = work[place[0], place[1]].astype(F32)
    for copy in copies:
        copy.wait_recv()
    return unfold(total + jnp.sum(land[...].astype(F32), 0))


def stacked(ref, place, group):
    blocks = []
    for dy, dx in group:
        y, x = moved(place, dy, dx)
        blocks.append(ref[y, x])
    return blocks[0] if len(blocks) == 1 else jnp.concatenate(blocks, 0)


def store_blocks(ref, place, group, rows):
    count = ref.shape[2]
    for n, (dy, dx) in enumerate(group):
        y, x = moved(place, dy, dx)
        ref[y, x] = rows[n * count : (n + 1) * count]


def wide(scale):
    return jnp.broadcast_to(scale, (scale.shape[0], 128))


def first_kernel(
    x, y, wt_in, gs_in, wt, gs, full_h0, h0, unit0, scale0, full_y, q, k, v, sq, sk, sv, *scratch
):
    xbuf, ybuf, send, recv = scratch
    place = at_grid()
    section, _, core, partner, sibling = sections()
    greet(neighbours(place) + [partner, sibling])
    links = Links(send, recv)
    half = wt_in.shape[0] // 2
    mine = pl.ds(core * half, half)
    gains_copy = links.start(gs_in, gs.at[section], partner)
    xbuf[place[0], place[1]] = x[...]
    ybuf[place[0], place[1]] = fold(y[...].astype(F32)).astype(BF16)
    passed = []

    def ready(group):
        if group == [(0, 0)]:
            passed.append(links.start(wt_in.at[mine], wt.at[section, mine], partner))
            gs[section] = gs_in[...]
            wt[section] = wt_in[...]
            gains_copy.wait_recv()
        if group == [(1, 1), (1, 3), (3, 1), (3, 3)]:
            passed[0].wait_recv()
            theirs = wt.at[1 - section, mine]
            passed.append(links.start(theirs, theirs, sibling))
        unit, scale = norm_parts(stacked(xbuf, place, group).astype(F32))
        rows = unit * gs[0, 0:1, :] + gs[0, 3:4, :]
        if group == [(0, 0)]:
            h0[...] = rows
            unit0[...] = unit
            scale0[...] = wide(scale)
        store_blocks(full_h0, place, group, rows.astype(BF16))

    gather(links, place, [xbuf, ybuf], ready)
    passed[1].wait_recv()
    count, width = x.shape
    for i in range(SIDE):
        rows = full_h0[i].reshape(SIDE * count, width)
        made = dot_t(rows, wt[0, 0 : 3 * HEAD, :]).astype(BF16)
        for j, ref in enumerate((q, k, v)):
            ref[i] = made[:, j * HEAD : (j + 1) * HEAD].reshape(SIDE, count, HEAD)
    rows = unfold_all(ybuf[...])
    full_y[...] = rows
    made = dot_t(rows, wt[1, 0 : 3 * HEAD, :]).astype(BF16)
    for j, ref in enumerate((sq, sk, sv)):
        ref[...] = made[:, j * HEAD : (j + 1) * HEAD]
    links.finish()


def first_call(x, y, wt, gs, collective_id):
    (rows, width), count = x.shape, y.shape[0]
    full = count * DEVICES
    return pl.pallas_call(
        first_kernel,
        out_shape=[
            shape((2, *wt.shape), BF16),
            shape((2, *gs.shape), F32),
            shape((SIDE, SIDE, rows, width), BF16),
            shape((rows, width), F32),
            shape((rows, width), F32),
            shape((rows, 128), F32),
            shape((full, width), BF16),
        ]
        + [shape((SIDE, SIDE, rows, HEAD), BF16)] * 3
        + [shape((full, HEAD), BF16)] * 3,
        in_specs=[VM] * 4,
        out_specs=[VM] * 13,
        scratch_shapes=[
            pltpu.VMEM((SIDE, SIDE, rows, width), BF16),
            pltpu.VMEM((SIDE, SIDE, 2 * count, width // 2), BF16),
        ]
        + sems(2 * RING_COPIES + 3),
        compiler_params=params(collective_id),
    )(x, y, wt, gs)


def forward_kernel(att_e, att_d, h0, y, wt, gs, ffn_in, *rest):
    (ffn, full_h1, full_m, full_d1, hidden, slope, kvc, cq, d1) = rest[:9]
    (unit1, scale1, unit2, scale2, dunit0, dscale0) = rest[9:15]
    (part, dpart, land_1, land_2, land_d, d1buf, send, recv) = rest[15:]
    place = at_grid()
    section, _, core, partner, sibling = sections()
    greet(neighbours(place) + [partner, sibling])
    links = Links(send, recv)
    passed = [links.start(ffn_in.at[core], ffn.at[section, core], partner)]

    def attended(group):
        rows = dot(stacked(att_e, place, group), wt[0, 3 * HEAD : 4 * HEAD, :])
        store_blocks(part, place, group, rows.astype(BF16))
        if group == PRODUCE[0]:
            dpart[...] = fold_all(dot(att_d[...], wt[1, 3 * HEAD : 4 * HEAD, :]))
        else:
            ffn[section] = ffn_in[...]

    sum_e, sum_d = sum_blocks(links, place, [(part, land_1), (dpart, land_d)], attended)
    passed[0].wait_recv()
    theirs = ffn.at[1 - section, core]
    passed.append(links.start(theirs, theirs, sibling))
    unit, scale = norm_parts(h0[...] + sum_e)
    unit1[...] = unit
    scale1[...] = wide(scale)
    h1 = unit * gs[0, 1:2, :] + gs[0, 4:5, :]
    full_h1[place[0], place[1]] = h1.astype(BF16)
    unit, scale = norm_parts(y[...].astype(F32) + unfold(sum_d))
    dunit0[...] = unit
    dscale0[...] = wide(scale)
    rows = unit * gs[1, 0:1, :] + gs[1, 3:4, :]
    d1[...] = rows
    d1buf[place[0], place[1]] = fold(rows).astype(BF16)

    def up(group):
        if group == [(0, 0)]:
            return
        if group == [(0, 1), (0, 3), (1, 0), (3, 0)]:
            passed[1].wait_recv()
            group = [(0, 0)] + group
        made, back = gelu_parts(dot(stacked(full_h1, place, group), ffn[0, 0]))
        store_blocks(hidden, place, group, made.astype(BF16))
        store_blocks(slope, place, group, back)

    gather(links, place, [full_h1, d1buf], up)
    links.finish()
    rows = unfold_all(d1buf[...])
    full_d1[...] = rows
    cq[...] = dot_t(rows, wt[1, 4 * HEAD : 5 * HEAD, :]).astype(BF16)

    def down(group):
        rows = dot_t(stacked(hidden, place, group), ffn[0, 1])
        store_blocks(part, place, group, rows.astype(BF16))

    (sum_e,) = sum_blocks(links, place, [(part, land_2)], down)
    unit, scale = norm_parts(h1 + sum_e)
    unit2[...] = unit
    scale2[...] = wide(scale)
    full_m[place[0], place[1]] = (unit * gs[0, 2:3, :] + gs[0, 5:6, :]).astype(BF16)

    def cross(group):
        rows = dot_t(stacked(full_m, place, group), wt[0, 4 * HEAD : 6 * HEAD, :])
        store_blocks(kvc, place, group, rows.astype(BF16))

    gather(links, place, [full_m], cross)
    links.finish()


def forward_call(att_e, att_d, h0, y, wt, gs, ffn, collective_id):
    (rows, width), count = h0.shape, y.shape[0]
    full, inner = count * DEVICES, ffn.shape[2]
    grid = (SIDE, SIDE)
    return pl.pallas_call(
        forward_kernel,
        out_shape=[
            shape((2, *ffn.shape), BF16),
            shape((*grid, rows, width), BF16),
            shape((*grid, rows, width), BF16),
            shape((full, width), BF16),
            shape((*grid, rows, inner), BF16),
            shape((*grid, rows, inner), F32),
            shape((*grid, rows, 2 * HEAD), BF16),
            shape((full, HEAD), BF16),
            shape((count, width), F32),
            shape((rows, width), F32),
            shape((rows, 128), F32),
            shape((rows, width), F32),
            shape((rows, 128), F32),
            shape((count, width), F32),
            shape((count, 128), F32),
        ],
        in_specs=[VM] * 7,
        out_specs=[VM] * 15,
        scratch_shapes=[
            pltpu.VMEM((*grid, rows, width), BF16),
            pltpu.VMEM((*grid, 2 * count, width // 2), BF16),
            pltpu.VMEM((30, rows, width // 2), BF16),
            pltpu.VMEM((30, rows, width // 2), BF16),
            pltpu.VMEM((30, 2 * count, width // 4), BF16),
            pltpu.VMEM((*grid, 2 * count, width // 2), BF16),
        ]
        + sems(6 * RING_COPIES + 2),
        compiler_params=params(collective_id),
    )(att_e, att_d, h0, y, wt, gs, ffn)


def decoder_kernel(cq, kvc, d1, cot, seg_d, seg_e, wt, ffn, gs, *rest):
    (d3, dback1, full_d2, full_db2, full_db1, hid_out, pre_out, att_out) = rest[:8]
    (cq_grad, kvc_grad, grads, g_bufs, s_work, s_land, probs, send, recv) = rest[8:]
    place = at_grid()
    greet([device_at(moved(place, d // SIDE, d % SIDE)) for d in range(1, DEVICES)])
    links = Links(send, recv)
    w5 = wt[1, 5 * HEAD : 6 * HEAD, :]
    kc, vc = kvc[:, :HEAD], kvc[:, HEAD:]
    scores = scores_of(cq[...], kc, seg_d[...] == seg_e[...])
    exponent = jnp.exp(scores - jnp.max(scores, -1, keepdims=True))
    probs[...] = exponent / jnp.sum(exponent, -1, keepdims=True)
    att = dot(probs[...].astype(BF16), vc).astype(BF16)
    att_out[...] = att
    part = sum_small(links, place, s_work.at[0], s_land.at[0], dot(att, w5))
    unit1, scale1 = norm_parts(d1[...] + part)
    d2 = unit1 * gs[1, 1:2, :] + gs[1, 4:5, :]
    full = gather_small(links, place, g_bufs.at[0], d2)
    full_d2[...] = full
    hidden, slope = gelu_parts(dot(full, ffn[1, 0]))
    hidden = hidden.astype(BF16)
    hid_out[...] = hidden
    part = sum_small(links, place, s_work.at[1], s_land.at[1], dot_t(hidden, ffn[1, 1]))
    unit2, scale2 = norm_parts(d2 + part)
    d3[...] = unit2 * gs[1, 2:3, :] + gs[1, 5:6, :]
    back2, gain2, shift2 = norm_back(cot[...].astype(F32), unit2, scale2, gs[1, 2:3, :])
    full = gather_small(links, place, g_bufs.at[1], back2)
    full_db2[...] = full
    pre = (dot(full, ffn[1, 1]) * slope).astype(BF16)
    pre_out[...] = pre
    part = sum_small(links, place, s_work.at[2], s_land.at[2], dot_t(pre, ffn[1, 0]))
    back1, gain1, shift1 = norm_back(back2 + part, unit1, scale1, gs[1, 1:2, :])
    dback1[...] = back1
    full = gather_small(links, place, g_bufs.at[2], back1)
    full_db1[...] = full
    att_grad = dot_t(full, w5).astype(BF16)
    p = probs[...]
    value_grad = t_dot(p.astype(BF16), att_grad)
    p_grad = dot_t(att_grad, vc)
    s_grad = (p * (p_grad - jnp.sum(p * p_grad, -1, keepdims=True))).astype(BF16)
    cq_grad[...] = (dot(s_grad, kc) * SCALE).astype(BF16)
    key_grad = t_dot(s_grad, cq[...]) * SCALE
    kvc_grad[...] = jnp.concatenate([key_grad, value_grad], 1).astype(BF16)
    grads[0:1, :] = gain1
    grads[1:2, :] = gain2
    grads[2:3, :] = shift1
    grads[3:4, :] = shift2
    grads[4:8, :] = jnp.zeros((4, grads.shape[1]), F32)
    links.finish()


def decoder_call(cq, kvc, d1, cot, seg_d, seg_e, wt, ffn, gs, collective_id):
    rows, width = d1.shape
    full, hidden = DEVICES * rows, ffn.shape[3]
    block = (SIDE, SIDE, 2 * rows, width // 2)
    return pl.pallas_call(
        decoder_kernel,
        out_shape=[
            shape((rows, width), F32),
            shape((rows, width), F32),
            shape((full, width), BF16),
            shape((full, width), BF16),
            shape((full, width), BF16),
            shape((full, hidden), BF16),
            shape((full, hidden), BF16),
            shape((full, HEAD), BF16),
            shape((full, HEAD), BF16),
            shape(kvc.shape, BF16),
            shape((8, width), F32),
        ],
        in_specs=[VM] * 9,
        out_specs=[VM] * 11,
        scratch_shapes=[
            pltpu.VMEM((3, *block), BF16),
            pltpu.VMEM((3, *block), BF16),
            pltpu.VMEM((3, DEVICES - 1, *block[2:]), BF16),
            pltpu.VMEM((full, kvc.shape[0]), F32),
        ]
        + sems(6 * (DEVICES - 1)),
        compiler_params=params(collective_id),
    )(cq, kvc, d1, cot, seg_d, seg_e, wt, ffn, gs)


def backward_kernel(*refs):
    (kvc_grad, cq_grad, dback1, wt, gs, ffn, unit1, scale1, unit2, scale2) = refs[:10]
    (dunit0, dscale0, slope, sq, sk, sv, log_d, seg_d, seg_dt) = refs[10:19]
    (full_b2, full_b1, full_db0, pre, dqkv_grad, att_grad, back1, dec_grad, grads) = refs[19:28]
    (part, dpart_1, dpart_2, land_1, land_2, dland_1, dland_2, dbuf, send, recv) = refs[28:]
    place = at_grid()
    greet(neighbours(place))
    links = Links(send, recv)

    def cross(group):
        rows = dot(stacked(kvc_grad, place, group), wt[0, 4 * HEAD : 6 * HEAD, :])
        store_blocks(part, place, group, rows.astype(BF16))

    dpart_1[...] = fold_all(dot(cq_grad[...], wt[1, 4 * HEAD : 5 * HEAD, :]))
    sum_e, sum_d = sum_blocks(links, place, [(part, land_1), (dpart_1, dland_1)], cross)
    back2, gain2, shift2 = norm_back(sum_e, unit2[...], scale2[:, 0:1], gs[0, 2:3, :])
    full_b2[place[0], place[1]] = back2.astype(BF16)
    dback0, dgain0, dshift0 = norm_back(
        dback1[...] + unfold(sum_d), dunit0[...], dscale0[:, 0:1], gs[1, 0:1, :]
    )
    dbuf[place[0], place[1]] = fold(dback0).astype(BF16)

    def down(group):
        rows = dot(stacked(full_b2, place, group), ffn[0, 1]) * stacked(slope, place, group)
        store_blocks(pre, place, group, rows.astype(BF16))

    gather(links, place, [full_b2, dbuf], down)
    links.finish()
    rows = unfold_all(dbuf[...])
    full_db0[...] = rows
    count = rows.shape[0]
    att_d_grad = dot_t(rows, wt[1, 3 * HEAD : 4 * HEAD, :]).astype(BF16)
    before = lax.broadcasted_iota(jnp.int32, (count, count), 1) <= lax.broadcasted_iota(
        jnp.int32, (count, count), 0
    )
    allowed = (seg_d[...] == seg_dt[...]) & before
    made = attend_back(sq[...], sk[...], sv[...], log_d[...], allowed, att_d_grad)
    made = jnp.concatenate([m.astype(F32) for m in made], 1).astype(BF16)
    dqkv_grad[...] = made
    dpart_2[...] = fold_all(dot(made, wt[1, 0 : 3 * HEAD, :]))

    def up(group):
        rows = dot_t(stacked(pre, place, group), ffn[0, 0])
        store_blocks(part, place, group, rows.astype(BF16))

    sum_e, sum_d = sum_blocks(links, place, [(part, land_2), (dpart_2, dland_2)], up)
    dec_grad[...] = dback0 + unfold(sum_d)
    rows, gain1, shift1 = norm_back(back2 + sum_e, unit1[...], scale1[:, 0:1], gs[0, 1:2, :])
    back1[...] = rows
    full_b1[place[0], place[1]] = rows.astype(BF16)

    def mixed(group):
        rows = dot_t(stacked(full_b1, place, group), wt[0, 3 * HEAD : 4 * HEAD, :])
        store_blocks(att_grad, place, group, rows.astype(BF16))

    gather(links, place, [full_b1], mixed)
    for i, row in enumerate((gain1, gain2, shift1, shift2, dgain0, dshift0)):
        grads[i : i + 1, :] = row
    grads[6:8, :] = jnp.zeros((2, grads.shape[1]), F32)
    links.finish()


def backward_call(args, collective_id):
    kvc_grad, cq_grad, dback1 = args[:3]
    rows, (count, width) = kvc_grad.shape[2], dback1.shape
    full, inner = count * DEVICES, args[5].shape[3]
    grid = (SIDE, SIDE)
    small = (*grid, 2 * count, width // 2)
    return pl.pallas_call(
        backward_kernel,
        out_shape=[
            shape((*grid, rows, width), BF16),
            shape((*grid, rows, width), BF16),
            shape((full, width), BF16),
            shape((*grid, rows, inner), BF16),
            shape((full, 3 * HEAD), BF16),
            shape((*grid, rows, HEAD), BF16),
            shape((rows, width), F32),
            shape((count, width), F32),
            shape((8, width), F32),
        ],
        in_specs=[VM] * 19,
        out_specs=[VM] * 9,
        scratch_shapes=[
            pltpu.VMEM((*grid, rows, width), BF16),
            pltpu.VMEM(small, BF16),
            pltpu.VMEM(small, BF16),
            pltpu.VMEM((30, rows, width // 2), BF16),
            pltpu.VMEM((30, rows, width // 2), BF16),
            pltpu.VMEM((30, 2 * count, width // 4), BF16),
            pltpu.VMEM((30, 2 * count, width // 4), BF16),
            pltpu.VMEM(small, BF16),
        ]
        + sems(7 * RING_COPIES),
        compiler_params=params(collective_id),
    )(*args)


def last_kernel(
    qkv_grad, wt, gs, back1, unit0, scale0, att, ffn, small, out3, dec, *rest
):
    (att_out, ffn_out, small_out, enc_out, out3_out, dec_out) = rest[:6]
    (part, land, work_a, work_f, core_a, core_f, side_a, side_f) = rest[6:14]
    (pass_a, pass_f, over_a, over_f, sums, fin, core_s, z_s, y_s, x_s) = rest[14:24]
    (enc, give_e, give_d, land_e, land_d, send, recv) = rest[24:]
    place = at_grid()
    section, zh, core, partner, sibling = sections()
    other = 1 - section
    zh_plus = lax.rem(zh + section, 2)
    plus = {"section": other, "dp": zh_plus * 2 + core}
    minus = {"section": other, "dp": (1 - zh_plus) * 2 + core}
    far = {"dp": (1 - zh) * 2 + core}
    columns = [device_at(moved(place, d, 0)) for d in (1, 2, 3)]
    rows = [device_at(moved(place, 0, d)) for d in (1, 2, 3)]
    greet([sibling, plus, minus, far, *columns, *rows])
    links = Links(send, recv)
    jobs = [
        (att, work_a, core_a, side_a, pass_a, over_a, att_out),
        (ffn, work_f, core_f, side_f, pass_f, over_f, ffn_out),
    ]
    step_core, step_side = [], []
    for grad, _, core_land, *_ in jobs:
        half = grad.shape[1] // 2
        step_core.append(
            links.start(grad.at[:, pl.ds((1 - core) * half, half)], core_land, sibling)
        )
    width = enc.shape[1] // 2
    there = pl.ds(pl.multiple_of(other * width, width), width)
    here = pl.ds(pl.multiple_of(section * width, width), width)
    give_d[...] = jnp.concatenate([out3[:, there], dec[:, there]], 0).astype(BF16)
    swap_d = links.start(give_d, land_d, partner)

    def heads(group):
        made = dot(stacked(qkv_grad, place, group), wt[0, 0 : 3 * HEAD, :])
        store_blocks(part, place, group, made.astype(BF16))
        if group == PRODUCE[0]:
            return
        for i, (grad, work, core_land, side, *_) in enumerate(jobs):
            half = grad.shape[1] // 2
            quarter = half // 2
            step_core[i].wait_recv()
            work[...] = (
                grad[:, pl.ds(core * half, half)].astype(F32) + core_land[...].astype(F32)
            ).astype(BF16)
            step_side.append(
                [
                    links.start(work.at[other, pl.ds(h * quarter, quarter)], side.at[n], d)
                    for n, (h, d) in enumerate(((zh_plus, plus), (1 - zh_plus, minus)))
                ]
            )

    (sum_e,) = sum_blocks(links, place, [(part, land)], heads)
    enc[...], gain0, shift0 = norm_back(
        back1[...] + sum_e, unit0[...], scale0[:, 0:1], gs[0, 0:1, :]
    )
    sums[...] = small[...]
    sums[0, 0:1, :] = gain0
    sums[0, 3:4, :] = shift0
    one = links.start(sums.at[1 - core], core_s, sibling)
    give_e[...] = enc[:, there].astype(BF16)
    swap_e = links.start(give_e, land_e, partner)
    step_pass = []
    for i, (grad, work, core_land, side, passing, over, _) in enumerate(jobs):
        quarter = grad.shape[1] // 4
        for copy in step_side[i]:
            copy.wait_recv()
        mine = work.at[section, pl.ds(zh * quarter, quarter)]
        mine[...] = (
            mine[...].astype(F32) + side[0].astype(F32) + side[1].astype(F32)
        ).astype(BF16)
        step_pass.append(
            [
                links.start(work.at[section, pl.ds(n * quarter, quarter)], passing.at[n], d)
                for n, d in enumerate((plus, minus))
            ]
        )

    def exchange(land_s, devices):
        copies = [links.start(fin.at[core], land_s.at[n], d) for n, d in enumerate(devices)]
        for copy in copies:
            copy.wait_recv()
        links.finish()
        fin[core] = fin[core] + land_s[0] + land_s[1] + land_s[2]

    one.wait_recv()
    fin[core] = sums[core] + core_s[...]
    exchange(y_s, columns)
    exchange(x_s, rows)
    step_over = []
    for i, (grad, work, core_land, side, passing, over, _) in enumerate(jobs):
        quarter = grad.shape[1] // 4
        ahead = []
        for n, device in enumerate((plus, minus)):
            step_pass[i][n].wait_recv()
            ahead.append(
                links.start(passing.at[n], over.at[pl.ds(n * quarter, quarter)], device)
            )
        step_over.append(ahead)
    exchange(z_s, [plus, minus, far])
    five = links.start(fin.at[core], fin.at[core], sibling)
    swap_e.wait_recv()
    swap_d.wait_recv()
    enc_out[section] = enc[:, here]
    enc_out[other] = land_e[...].astype(F32)
    got = land_d[...].astype(F32)
    count = out3.shape[0]
    out3_out[section] = out3[:, here]
    out3_out[other] = got[:count]
    dec_out[section] = dec[:, here]
    dec_out[other] = got[count:]
    last = []
    for i, (grad, work, core_land, side, passing, over, out) in enumerate(jobs):
        for copy in step_over[i]:
            copy.wait_recv()
        out[core] = (work[section].astype(F32) + over[...].astype(F32)).astype(BF16)
        last.append(links.start(out.at[core], out.at[core], sibling))
    five.wait_recv()
    small_out[...] = fin[section]
    for copy in last:
        copy.wait_recv()
    links.finish()


def last_call(args, collective_id):
    qkv_grad, back1, (att, ffn, small, out3, dec) = args[0], args[3], args[6:]
    rows, cols = back1.shape
    count, width = dec.shape[0], cols // 2
    grads = (att, ffn)

    def lands(lead):
        return [pltpu.VMEM((*lead(g), g.shape[2]), BF16) for g in grads]

    half = lambda g: (2, g.shape[1] // 2)
    quarter = lambda g: (2, g.shape[1] // 4)
    return pl.pallas_call(
        last_kernel,
        out_shape=[shape((*half(g), g.shape[2]), BF16) for g in grads]
        + [
            shape(small.shape[1:], F32),
            shape((2, rows, width), F32),
            shape((2, count, width), F32),
            shape((2, count, width), F32),
        ],
        in_specs=[VM] * 11,
        out_specs=[VM] * 6,
        scratch_shapes=[
            pltpu.VMEM((SIDE, SIDE, rows, cols), BF16),
            pltpu.VMEM((30, rows, width), BF16),
        ]
        + lands(half)
        + lands(half)
        + lands(quarter)
        + lands(quarter)
        + lands(lambda g: half(g)[1:])
        + [
            pltpu.VMEM(small.shape, F32),
            pltpu.VMEM(small.shape, F32),
            pltpu.VMEM(small.shape[1:], F32),
            pltpu.VMEM((3, *small.shape[1:]), F32),
            pltpu.VMEM((3, *small.shape[1:]), F32),
            pltpu.VMEM((3, *small.shape[1:]), F32),
            pltpu.VMEM((rows, cols), F32),
            pltpu.VMEM((rows, width), BF16),
            pltpu.VMEM((2 * count, width), BF16),
            pltpu.VMEM((rows, width), BF16),
            pltpu.VMEM((2 * count, width), BF16),
        ]
        + sems(RING_COPIES + 2 * 8 + 14),
        compiler_params=params(collective_id),
    )(*args)


def on_device(
    encoder_tokens,
    encoder_segments,
    decoder_tokens,
    decoder_segments,
    cotangent,
    attention_weight,
    feedforward_weight,
    norm_gain,
    norm_shift,
):
    section = lax.axis_index("section")
    mine = lambda a: lax.dynamic_index_in_dim(a, section, 0, keepdims=False)
    width, count = encoder_tokens.shape[2], decoder_tokens.shape[1]
    own_wt = jnp.swapaxes(attention_weight[0], 1, 2).reshape(6 * HEAD, width)
    own_gs = jnp.concatenate([norm_gain[0], norm_shift[0], jnp.zeros((2, width), F32)], 0)
    y = mine(decoder_tokens)
    e, c = mine(encoder_segments), mine(decoder_segments)
    position = jnp.arange(c.shape[0])
    allow_e = e[:, None] == e[None, :]
    allow_d = (c[:, None] == c[None, :]) & (position[:, None] >= position[None, :])
    flat = lambda a: a.reshape(-1, a.shape[-1])
    blocks = lambda a: a.reshape(SIDE, SIDE, -1, a.shape[-1])

    wt, gs, full_h0, h0, unit0, scale0, full_y, q, k, v, sq, sk, sv = first_call(
        mine(encoder_tokens), y, own_wt, own_gs, 1
    )
    q, k, v = flat(q), flat(k), flat(v)
    att_e, log_e = attend(q, k, v, allow_e)
    att_d, log_d = attend(sq, sk, sv, allow_d)
    (
        ffn, full_h1, full_m, full_d1, hidden, slope, kvc, cq, d1,
        unit1, scale1, unit2, scale2, dunit0, dscale0,
    ) = forward_call(blocks(att_e), att_d, h0, y, wt, gs, feedforward_weight[0], 2)
    (d3, dback1, full_d2, full_db2, full_db1, dhidden, dpre, att_c, cq_grad, kvc_grad, dsmall) = (
        decoder_call(
            cq, flat(kvc), d1, mine(cotangent), c[:, None], e[None, :], wt, ffn, gs, 3
        )
    )
    full_b2, full_b1, full_db0, pre, dqkv_grad, att_e_grad, back1, dec_grad, small_b = (
        backward_call(
            (
                blocks(kvc_grad), cq_grad, dback1, wt, gs, ffn, unit1, scale1, unit2, scale2,
                dunit0, dscale0, slope, sq, sk, sv, log_d, c[:, None], c[None, :],
            ),
            4,
        )
    )
    made = attend_back(q, k, v, log_e, allow_e, flat(att_e_grad))
    qkv_grad = jnp.concatenate(made, 1)

    att_grads = jnp.stack(
        [
            jnp.concatenate(
                [
                    t_dot(qkv_grad, flat(full_h0)),
                    t_dot(att_e, flat(full_b1)),
                    t_dot(kvc_grad, flat(full_m)),
                ],
                0,
            ),
            jnp.concatenate(
                [
                    t_dot(dqkv_grad, full_y),
                    t_dot(att_d, full_db0),
                    t_dot(cq_grad, full_d1),
                    t_dot(att_c, full_db1),
                ],
                0,
            ),
        ]
    ).astype(BF16)
    ffn_grads = jnp.stack(
        [
            jnp.concatenate(
                [t_dot(flat(full_h1), flat(pre)), t_dot(flat(full_b2), flat(hidden))], 0
            ),
            jnp.concatenate([t_dot(full_d2, dpre), t_dot(full_db2, dhidden)], 0),
        ]
    ).astype(BF16)
    none = jnp.zeros((1, width), F32)
    row = lambda a, i: a[i : i + 1]
    small = jnp.stack(
        [
            jnp.concatenate(
                [none, row(small_b, 0), row(small_b, 1), none, row(small_b, 2), row(small_b, 3)]
                + [none, none],
                0,
            ),
            jnp.concatenate(
                [row(small_b, 4), dsmall[0:2], row(small_b, 5), dsmall[2:4], none, none], 0
            ),
        ]
    )
    att_sum, ffn_sum, small_sum, enc_out, d3_out, dec_out = last_call(
        (
            blocks(qkv_grad), wt, gs, back1, unit0, scale0,
            att_grads, ffn_grads, small, d3, dec_grad,
        ),
        5,
    )
    att_sum = att_sum.reshape(6, HEAD, width).astype(F32)
    return (
        d3_out.astype(BF16),
        enc_out,
        dec_out,
        jnp.swapaxes(att_sum, 1, 2)[None],
        ffn_sum.reshape(feedforward_weight.shape).astype(F32),
        small_sum[None, :3],
        small_sum[None, 3:6],
    )


def solution(mesh):
    in_specs = (
        P("dp", "tensor", None),
        P("dp", None),
        P("dp", "tensor", None),
        P("dp", None),
        P("dp", "tensor", None),
        P("section", None, None, "tensor"),
        P("section", None, None, "tensor"),
        P("section", None, None),
        P("section", None, None),
    )
    out_specs = (
        P("dp", "tensor", "section"),
        P("dp", "tensor", "section"),
        P("dp", "tensor", "section"),
        P("section", None, None, "tensor"),
        P("section", None, None, "tensor"),
        P("section", None, None),
        P("section", None, None),
    )
    return jax.shard_map(
        on_device, mesh=mesh, in_specs=in_specs, out_specs=out_specs, check_vma=False
    )
```

```python
import jax
import jax.numpy as jnp
from jax import lax
from jax.experimental import pallas as pl
from jax.experimental.pallas import tpu as pltpu
from jax.sharding import PartitionSpec as P

HEAD = 64
EPSILON = 1e-05
MASKED = -1000000000.0
SCALE = HEAD ** (-0.5)
F32 = jnp.float32
BF16 = jnp.bfloat16
MESH = pl.DeviceIdType.MESH
VM = pl.BlockSpec(memory_space=pltpu.VMEM)
SIDE = 4
DEVICES = SIDE * SIDE
UP = (0, 2)
DOWN = (1, 3)
RING_COPIES = 32
CHUNKS = ((0, 48), (48, 32))
PAUSES = (1, 1, 1, 1, 1)
LAG = 0
RING = True
INV_SQRT2 = 0.7071067811865476
INV_SQRT_2PI = 0.3989422804014327
FAR_FIRST = (10, 2, 8, 6, 14, 11, 9, 7, 13, 5, 15, 1, 3, 4, 12)


def norm_parts(values):
    center = values - jnp.mean(values, -1, keepdims=True)
    scale = lax.rsqrt(jnp.mean(center * center, -1, keepdims=True) + EPSILON)
    return center * scale, scale


def norm_back(grad, unit, scale, gains):
    inner = grad * gains
    back = scale * (
        inner
        - jnp.mean(inner, -1, keepdims=True)
        - unit * jnp.mean(inner * unit, -1, keepdims=True)
    )
    return back, jnp.sum(grad * unit, 0, keepdims=True), jnp.sum(grad, 0, keepdims=True)


def gelu_parts(u):
    cdf = 0.5 * (1.0 + lax.erf(u * INV_SQRT2))
    return u * cdf, cdf + u * (INV_SQRT_2PI * jnp.exp(-0.5 * u * u))


def dot(a, b):
    return jnp.dot(a, b, preferred_element_type=F32)


def dot_t(a, b):
    return lax.dot_general(a, b, (((1,), (1,)), ((), ())), preferred_element_type=F32)


def t_dot(a, b):
    return lax.dot_general(a, b, (((0,), (0,)), ((), ())), preferred_element_type=F32)


def scores_of(queries, key_rows, allowed):
    return jnp.where(allowed, dot_t(queries, key_rows) * SCALE, MASKED)


def attend(queries, key_rows, value_rows, allowed):
    scores = scores_of(queries, key_rows, allowed)
    row_max = jnp.max(scores, -1, keepdims=True)
    exponent = jnp.exp(scores - row_max)
    row_sum = jnp.sum(exponent, -1, keepdims=True)
    probs_low = (exponent / row_sum).astype(BF16)
    return dot(probs_low, value_rows).astype(BF16), row_max + jnp.log(row_sum)


def attend_back(queries, key_rows, value_rows, log_total, allowed, attended_grad):
    probs = jnp.exp(scores_of(queries, key_rows, allowed) - log_total)
    value_grad = t_dot(probs.astype(BF16), attended_grad)
    probs_grad = dot_t(attended_grad, value_rows)
    scores_grad = (probs * (probs_grad - jnp.sum(probs * probs_grad, -1, keepdims=True))).astype(
        BF16
    )
    query_grad = dot(scores_grad, key_rows) * SCALE
    key_grad = t_dot(scores_grad, queries) * SCALE
    return query_grad.astype(BF16), key_grad.astype(BF16), value_grad.astype(BF16)


def at_grid():
    index = lax.axis_index("tensor")
    return lax.div(index, SIDE), lax.rem(index, SIDE)


def moved(place, dy, dx):
    return lax.rem(place[0] + dy % SIDE, SIDE), lax.rem(place[1] + dx % SIDE, SIDE)


def along(axis, steps):
    return (steps, 0) if axis == 0 else (0, steps)


def device_at(place):
    return {"tensor": place[0] * SIDE + place[1]}


def neighbours(place):
    return [device_at(moved(place, *along(axis, s))) for axis in range(2) for s in (1, 2, 3)]


def greet(devices):
    barrier = pltpu.get_barrier_semaphore()
    for device in devices:
        pl.semaphore_signal(barrier, inc=1, device_id=device, device_id_type=MESH)
    pl.semaphore_wait(barrier, len(devices))


def sections():
    section, dp = lax.axis_index("section"), lax.axis_index("dp")
    zh, core = lax.div(dp, 2), lax.rem(dp, 2)
    return section, zh, core, {"section": 1 - section}, {"dp": zh * 2 + 1 - core}


class Links:
    def __init__(self, send_sems, recv_sems, used=0):
        self.send, self.recv, self.used, self.started = send_sems, recv_sems, used, []

    def start(self, source, target, device):
        n = self.used
        self.used += 1
        copy = pltpu.make_async_remote_copy(
            src_ref=source,
            dst_ref=target,
            send_sem=self.send.at[n],
            recv_sem=self.recv.at[n],
            device_id=device,
            device_id_type=MESH,
        )
        copy.start()
        self.started.append(copy)
        return copy

    def finish(self):
        for copy in self.started:
            copy.wait_send()
        self.started = []


def sems(n):
    return [pltpu.SemaphoreType.DMA((n,)), pltpu.SemaphoreType.DMA((n,))]


def shape(dims, kind):
    return jax.ShapeDtypeStruct(tuple(dims), kind)


def params(collective_id):
    return pltpu.CompilerParams(
        collective_id=collective_id, has_side_effects=True, vmem_limit_bytes=56 << 20
    )


def fold(rows):
    half = rows.shape[1] // 2
    return jnp.concatenate([rows[:, :half], rows[:, half:]], 0)


def unfold(rows):
    count = rows.shape[0] // 2
    return jnp.concatenate([rows[:count], rows[count:]], 1)


def unfold_all(blocks):
    count, half = blocks.shape[2] // 2, blocks.shape[3]
    split = blocks.astype(F32).reshape(DEVICES, 2, count, half)
    low = split[:, 0].reshape(DEVICES * count, half)
    high = split[:, 1].reshape(DEVICES * count, half)
    return jnp.concatenate([low, high], 1).astype(BF16)


def fold_all(part):
    count, half = part.shape[0] // DEVICES, part.shape[1] // 2
    split = part.reshape(DEVICES, count, 2 * half)
    both = jnp.concatenate([split[:, :, :half], split[:, :, half:]], 1)
    return both.astype(BF16).reshape(SIDE, SIDE, 2 * count, half)


def gather(links, place, views, ready=None):
    jobs = []
    for buf, low, rows in views:
        half = buf.shape[-1] // 2
        for h in range(2):
            jobs.append((buf, 1 - h, h, h * half, half, pl.ds(low, rows)))
    ready = ready or (lambda group: None)

    def send(job, axis, steps, r, s):
        buf, a, b, start, size, rows = job
        y, x = moved(moved(place, *along(a, r)), *along(b, s))
        ref = buf.at[y, x, rows, pl.ds(start, size)]
        return links.start(ref, ref, device_at(moved(place, *along(axis, steps))))

    first, spread, ahead = [], [], []
    for job in jobs:
        first.append({-d % SIDE: send(job, job[1], d, 0, 0) for d in (2, 1, 3)})
    paths = ((1, 3), (3, 1)) if RING else ((2, 2), (1, 3), (3, 1))
    for job in jobs:
        spread.append({0: {s: send(job, job[2], d, 0, 0) for d, s in paths}})
    ready([(0, 0)])
    yield
    for r in (3, 1, 2):
        for i, job in enumerate(jobs):
            first[i][r].wait_recv()
            spread[i][r] = {s: send(job, job[2], d, r, 0) for d, s in paths}
    if RING:
        for i, job in enumerate(jobs):
            spread[i][0][3].wait_recv()
            ahead.append({0: send(job, job[2], 1, 0, 3)})
            spread[i][0][1].wait_recv()
    else:
        for i, job in enumerate(jobs):
            spread[i][0][3].wait_recv()
            spread[i][0][1].wait_recv()
            ahead.append({r: spread[i][r][2] for r in range(SIDE)})
    ready([(0, 1), (0, 3), (1, 0), (3, 0)])
    yield
    if RING:
        for r in DOWN:
            for i, job in enumerate(jobs):
                spread[i][r][1].wait_recv()
                ahead[i][r] = send(job, job[2], -1, r, 1)
        for i, job in enumerate(jobs):
            spread[i][2][3].wait_recv()
            ahead[i][2] = send(job, job[2], 1, 2, 3)
        for r in DOWN:
            for i, job in enumerate(jobs):
                spread[i][r][3].wait_recv()
    else:
        for r in DOWN:
            for i, job in enumerate(jobs):
                spread[i][r][1].wait_recv()
                spread[i][r][3].wait_recv()
    ready([(1, 1), (1, 3), (3, 1), (3, 3)])
    for i, job in enumerate(jobs):
        ahead[i][0].wait_recv()
    ready([(0, 2), (2, 0)])
    yield
    for i, job in enumerate(jobs):
        if not RING:
            spread[i][2][3].wait_recv()
        spread[i][2][1].wait_recv()
        ahead[i][1].wait_recv()
        ahead[i][3].wait_recv()
    ready([(1, 2), (3, 2), (2, 1), (2, 3)])
    for i, job in enumerate(jobs):
        ahead[i][2].wait_recv()
    ready([(2, 2)])


PRODUCE = (
    [(2, 2), (2, 3), (2, 1), (3, 2), (1, 2), (2, 0), (0, 2)],
    [(3, 3), (3, 1), (1, 3), (1, 1), (3, 0), (1, 0), (0, 3), (0, 1), (0, 0)],
)


def sum_blocks(links, place, views, produce=None):
    produce = produce or (lambda group: None)
    jobs = []
    for part, land, low, rows in views:
        half = part.shape[-1] // 2
        for h in range(2):
            jobs.append((part, land, 15 * h, 1 - h, h, h * half, half, pl.ds(low, rows)))

    def block(job, r, s):
        part, _, _, a, b, start, size, rows = job
        y, x = moved(moved(place, *along(a, r)), *along(b, s))
        return part.at[y, x, rows, pl.ds(start, size)]

    def landing(job, n):
        return job[1].at[job[2] + n, job[7]]

    def start(source, target, axis, steps):
        return links.start(source, target, device_at(moved(place, *along(axis, steps))))

    def add(target, *others):
        total = target[...].astype(F32)
        for other in others:
            total = total + other[...].astype(F32)
        return total

    def near_slot(job, r, steps):
        return landing(job, 4 + 2 * r + (0 if steps == 1 else 1))

    order = (2, 3, 1, 0)
    produce(PRODUCE[0])
    near = [{r: [] for r in order} for _ in jobs]
    if RING:
        far = []
        for job in jobs:
            far.append(
                {
                    r: start(block(job, r, 2), landing(job, r), job[4], 1 if r in UP else -1)
                    for r in order
                }
            )
        produce(PRODUCE[1])
        for i, job in enumerate(jobs):
            for r in order:
                steps = -1 if r in UP else 1
                near[i][r].append(
                    start(block(job, r, steps), near_slot(job, r, steps), job[4], steps)
                )
        yield
        for r in order:
            for i, job in enumerate(jobs):
                steps = 1 if r in UP else -1
                far[i][r].wait_recv()
                ref = block(job, r, steps)
                ref[...] = add(ref, landing(job, r)).astype(BF16)
                near[i][r].append(start(ref, near_slot(job, r, steps), job[4], steps))
    else:
        for s in (2, 1, 3):
            for r in order:
                for i, job in enumerate(jobs):
                    slot = landing(job, 4 * (s - 1) + r)
                    near[i][r].append(start(block(job, r, s), slot, job[4], s))
            if s == 2:
                produce(PRODUCE[1])
    yield
    last = [{} for _ in jobs]
    results = []
    for r in order:
        if r == 0:
            yield
        for i, job in enumerate(jobs):
            for copy in near[i][r]:
                copy.wait_recv()
            ref = block(job, r, 0)
            if RING:
                total = add(ref, landing(job, 4 + 2 * r), landing(job, 5 + 2 * r))
            else:
                total = add(ref, landing(job, r), landing(job, 4 + r), landing(job, 8 + r))
            if r == 0:
                results.append(total)
            else:
                ref[...] = total.astype(BF16)
                last[i][r] = start(ref, landing(job, 11 + r), job[3], r)
    for i, job in enumerate(jobs):
        for r in order[:3]:
            last[i][r].wait_recv()
            results[i] = results[i] + landing(job, 11 + r)[...].astype(F32)
    return [jnp.concatenate(results[i : i + 2], 1) for i in range(0, len(results), 2)]


def run(chains, lag=0):
    turn, active = 0, list(enumerate(chains))
    while active:
        for n, chain in list(active):
            if turn >= n * lag:
                try:
                    next(chain)
                except StopIteration:
                    active.remove((n, chain))
        turn += 1


def pack_places():
    section, zh, core, partner, sibling = sections()
    zh_plus = lax.rem(zh + section, 2)
    plus = {"section": 1 - section, "dp": zh_plus * 2 + core}
    minus = {"section": 1 - section, "dp": (1 - zh_plus) * 2 + core}
    return section, zh, core, sibling, zh_plus, plus, minus


PACK_COPIES = 8


def pack_scratch(rows, cols):
    half, quarter = rows // 2, rows // 4
    return [
        pltpu.VMEM((2, half, cols), BF16),
        pltpu.VMEM((2, half, cols), BF16),
        pltpu.VMEM((2, quarter, cols), BF16),
        pltpu.VMEM((2, quarter, cols), BF16),
        pltpu.VMEM((half, cols), BF16),
    ]


def pause(n):
    for _ in range(n):
        yield


def pack_sum(links, grad, out, scratch):
    work, core_land, side, passing, over = scratch
    section, zh, core, sibling, zh_plus, plus, minus = pack_places()
    other = 1 - section
    half = grad.shape[1] // 2
    quarter = half // 2
    first = links.start(grad.at[:, pl.ds((1 - core) * half, half)], core_land, sibling)
    yield from pause(PAUSES[0])
    first.wait_recv()
    work[...] = (
        grad[:, pl.ds(core * half, half)].astype(F32) + core_land[...].astype(F32)
    ).astype(BF16)
    second = [
        links.start(work.at[other, pl.ds(h * quarter, quarter)], side.at[n], d)
        for n, (h, d) in enumerate(((zh_plus, plus), (1 - zh_plus, minus)))
    ]
    yield from pause(PAUSES[1])
    for copy in second:
        copy.wait_recv()
    mine = work.at[section, pl.ds(zh * quarter, quarter)]
    mine[...] = (mine[...].astype(F32) + side[0].astype(F32) + side[1].astype(F32)).astype(BF16)
    third = [
        links.start(work.at[section, pl.ds(n * quarter, quarter)], passing.at[n], d)
        for n, d in enumerate((plus, minus))
    ]
    yield from pause(PAUSES[2])
    fourth = []
    for n, device in enumerate((plus, minus)):
        third[n].wait_recv()
        fourth.append(links.start(passing.at[n], over.at[pl.ds(n * quarter, quarter)], device))
    yield from pause(PAUSES[3])
    for copy in fourth:
        copy.wait_recv()
    out[core] = (work[section].astype(F32) + over[...].astype(F32)).astype(BF16)
    last = links.start(out.at[core], out.at[core], sibling)
    yield from pause(PAUSES[4])
    last.wait_recv()
    links.finish()


def gather_small(links, place, buf, rows):
    y, x = place
    buf[y, x] = fold(rows).astype(BF16)
    copies = []
    for d in FAR_FIRST:
        target = device_at(moved(place, d // SIDE, d % SIDE))
        copies.append(links.start(buf.at[y, x], buf.at[y, x], target))
    for copy in copies:
        copy.wait_recv()
    return unfold_all(buf[...])


def sum_small(links, place, work, land, part):
    work[...] = fold_all(part)
    copies = []
    for n, d in enumerate(FAR_FIRST):
        there = moved(place, d // SIDE, d % SIDE)
        copies.append(links.start(work.at[there[0], there[1]], land.at[n], device_at(there)))
    total = work[place[0], place[1]].astype(F32)
    for copy in copies:
        copy.wait_recv()
    return unfold(total + jnp.sum(land[...].astype(F32), 0))


def stacked(ref, place, group, low=0, rows=None):
    rows = ref.shape[2] if rows is None else rows
    blocks = []
    for dy, dx in group:
        y, x = moved(place, dy, dx)
        blocks.append(ref[y, x, low : low + rows])
    return blocks[0] if len(blocks) == 1 else jnp.concatenate(blocks, 0)


def store_blocks(ref, place, group, values, low=0):
    rows = values.shape[0] // len(group)
    for n, (dy, dx) in enumerate(group):
        y, x = moved(place, dy, dx)
        ref[y, x, low : low + rows] = values[n * rows : (n + 1) * rows]


def wide(scale):
    return jnp.broadcast_to(scale, (scale.shape[0], 128))


def first_kernel(
    x, y, wt_in, gs_in, wt, gs, full_h0, h0, unit0, scale0, full_y, q, k, v, sq, sk, sv, *scratch
):
    xbuf, ybuf, send, recv = scratch
    place = at_grid()
    section, _, core, partner, sibling = sections()
    greet(neighbours(place) + [partner, sibling])
    links = Links(send, recv)
    half = wt_in.shape[0] // 2
    mine = pl.ds(core * half, half)
    gains_copy = links.start(gs_in, gs.at[section], partner)
    xbuf[place[0], place[1]] = x[...]
    ybuf[place[0], place[1]] = fold(y[...].astype(F32)).astype(BF16)
    passed = []

    def ready(group):
        if group == [(0, 0)]:
            passed.append(links.start(wt_in.at[mine], wt.at[section, mine], partner))
            gs[section] = gs_in[...]
            wt[section] = wt_in[...]
            gains_copy.wait_recv()
        if group == [(1, 1), (1, 3), (3, 1), (3, 3)]:
            passed[0].wait_recv()
            theirs = wt.at[1 - section, mine]
            passed.append(links.start(theirs, theirs, sibling))
        unit, scale = norm_parts(stacked(xbuf, place, group).astype(F32))
        rows = unit * gs[0, 0:1, :] + gs[0, 3:4, :]
        if group == [(0, 0)]:
            h0[...] = rows
            unit0[...] = unit
            scale0[...] = wide(scale)
        store_blocks(full_h0, place, group, rows.astype(BF16))

    views = [(xbuf, 0, x.shape[0]), (ybuf, 0, ybuf.shape[2])]
    run([gather(links, place, views, ready)])
    passed[1].wait_recv()
    count, width = x.shape
    for i in range(SIDE):
        rows = full_h0[i].reshape(SIDE * count, width)
        made = dot_t(rows, wt[0, 0 : 3 * HEAD, :]).astype(BF16)
        for j, ref in enumerate((q, k, v)):
            ref[i] = made[:, j * HEAD : (j + 1) * HEAD].reshape(SIDE, count, HEAD)
    rows = unfold_all(ybuf[...])
    full_y[...] = rows
    made = dot_t(rows, wt[1, 0 : 3 * HEAD, :]).astype(BF16)
    for j, ref in enumerate((sq, sk, sv)):
        ref[...] = made[:, j * HEAD : (j + 1) * HEAD]
    links.finish()


def first_call(x, y, wt, gs, collective_id):
    (rows, width), count = x.shape, y.shape[0]
    full = count * DEVICES
    return pl.pallas_call(
        first_kernel,
        out_shape=[
            shape((2, *wt.shape), BF16),
            shape((2, *gs.shape), F32),
            shape((SIDE, SIDE, rows, width), BF16),
            shape((rows, width), F32),
            shape((rows, width), F32),
            shape((rows, 128), F32),
            shape((full, width), BF16),
        ]
        + [shape((SIDE, SIDE, rows, HEAD), BF16)] * 3
        + [shape((full, HEAD), BF16)] * 3,
        in_specs=[VM] * 4,
        out_specs=[VM] * 13,
        scratch_shapes=[
            pltpu.VMEM((SIDE, SIDE, rows, width), BF16),
            pltpu.VMEM((SIDE, SIDE, 2 * count, width // 2), BF16),
        ]
        + sems(2 * RING_COPIES + 3),
        compiler_params=params(collective_id),
    )(x, y, wt, gs)


def forward_kernel(att_e, att_d, h0, y, wt, gs, ffn_in, *rest):
    (ffn, full_h1, full_m, full_d1, hidden, slope, kvc, cq, d1) = rest[:9]
    (unit1, scale1, unit2, scale2, dunit0, dscale0) = rest[9:15]
    (part, dpart, land_1, land_2, land_d, d1buf, send, recv) = rest[15:]
    place = at_grid()
    section, _, core, partner, sibling = sections()
    greet(neighbours(place) + [partner, sibling])
    shared = Links(send, recv)
    passed = [shared.start(ffn_in.at[core], ffn.at[section, core], partner)]

    def chain(links, low, rows, with_dec):
        here = pl.ds(low, rows)

        def attended(group):
            made = dot(stacked(att_e, place, group, low, rows), wt[0, 3 * HEAD : 4 * HEAD, :])
            store_blocks(part, place, group, made.astype(BF16), low)
            if with_dec and group == PRODUCE[0]:
                dpart[...] = fold_all(dot(att_d[...], wt[1, 3 * HEAD : 4 * HEAD, :]))
            if low == 0 and group == PRODUCE[1]:
                ffn[section] = ffn_in[...]

        views = [(part, land_1, low, rows)]
        if with_dec:
            views.append((dpart, land_d, 0, dpart.shape[2]))
        sums = yield from sum_blocks(links, place, views, attended)
        unit, scale = norm_parts(h0[here] + sums[0])
        unit1[here] = unit
        scale1[here] = wide(scale)
        h1 = unit * gs[0, 1:2, :] + gs[0, 4:5, :]
        full_h1[place[0], place[1], here] = h1.astype(BF16)
        views = [(full_h1, low, rows)]
        if with_dec:
            unit, scale = norm_parts(y[...].astype(F32) + unfold(sums[1]))
            dunit0[...] = unit
            dscale0[...] = wide(scale)
            made = unit * gs[1, 0:1, :] + gs[1, 3:4, :]
            d1[...] = made
            d1buf[place[0], place[1]] = fold(made).astype(BF16)
            views.append((d1buf, 0, d1buf.shape[2]))
        if low == 0:
            passed[0].wait_recv()
            theirs = ffn.at[1 - section, core]
            passed.append(shared.start(theirs, theirs, sibling))

        def up(group):
            if group == [(0, 0)]:
                return
            if group == [(0, 1), (0, 3), (1, 0), (3, 0)]:
                if low == 0:
                    passed[1].wait_recv()
                group = [(0, 0)] + group
            made, back = gelu_parts(dot(stacked(full_h1, place, group, low, rows), ffn[0, 0]))
            store_blocks(hidden, place, group, made.astype(BF16), low)
            store_blocks(slope, place, group, back, low)

        yield from gather(links, place, views, up)
        links.finish()
        if with_dec:
            made = unfold_all(d1buf[...])
            full_d1[...] = made
            cq[...] = dot_t(made, wt[1, 4 * HEAD : 5 * HEAD, :]).astype(BF16)

        def down(group):
            made = dot_t(stacked(hidden, place, group, low, rows), ffn[0, 1])
            store_blocks(part, place, group, made.astype(BF16), low)

        sums = yield from sum_blocks(links, place, [(part, land_2, low, rows)], down)
        unit, scale = norm_parts(h1 + sums[0])
        unit2[here] = unit
        scale2[here] = wide(scale)
        full_m[place[0], place[1], here] = (unit * gs[0, 2:3, :] + gs[0, 5:6, :]).astype(BF16)

        def cross(group):
            made = dot_t(stacked(full_m, place, group, low, rows), wt[0, 4 * HEAD : 6 * HEAD, :])
            store_blocks(kvc, place, group, made.astype(BF16), low)

        yield from gather(links, place, [(full_m, low, rows)], cross)
        links.finish()

    chains = []
    for n, (low, rows) in enumerate(CHUNKS):
        links = Links(send, recv, 2 + 6 * RING_COPIES * n)
        chains.append(chain(links, low, rows, n == len(CHUNKS) - 1))
    run(chains, LAG)
    shared.finish()


def forward_call(att_e, att_d, h0, y, wt, gs, ffn, collective_id):
    (rows, width), count = h0.shape, y.shape[0]
    full, inner = count * DEVICES, ffn.shape[2]
    grid = (SIDE, SIDE)
    return pl.pallas_call(
        forward_kernel,
        out_shape=[
            shape((2, *ffn.shape), BF16),
            shape((*grid, rows, width), BF16),
            shape((*grid, rows, width), BF16),
            shape((full, width), BF16),
            shape((*grid, rows, inner), BF16),
            shape((*grid, rows, inner), F32),
            shape((*grid, rows, 2 * HEAD), BF16),
            shape((full, HEAD), BF16),
            shape((count, width), F32),
            shape((rows, width), F32),
            shape((rows, 128), F32),
            shape((rows, width), F32),
            shape((rows, 128), F32),
            shape((count, width), F32),
            shape((count, 128), F32),
        ],
        in_specs=[VM] * 7,
        out_specs=[VM] * 15,
        scratch_shapes=[
            pltpu.VMEM((*grid, rows, width), BF16),
            pltpu.VMEM((*grid, 2 * count, width // 2), BF16),
            pltpu.VMEM((30, rows, width // 2), BF16),
            pltpu.VMEM((30, rows, width // 2), BF16),
            pltpu.VMEM((30, 2 * count, width // 4), BF16),
            pltpu.VMEM((*grid, 2 * count, width // 2), BF16),
        ]
        + sems(6 * RING_COPIES * len(CHUNKS) + 2),
        compiler_params=params(collective_id),
    )(att_e, att_d, h0, y, wt, gs, ffn)


def decoder_kernel(cq, kvc, d1, cot, seg_d, seg_e, wt, ffn, gs, *rest):
    (d3, dback1, full_d2, full_db2, full_db1, hid_out, pre_out, att_out) = rest[:8]
    (cq_grad, kvc_grad, grads, g_bufs, s_work, s_land, probs, send, recv) = rest[8:]
    place = at_grid()
    greet([device_at(moved(place, d // SIDE, d % SIDE)) for d in range(1, DEVICES)])
    links = Links(send, recv)
    w5 = wt[1, 5 * HEAD : 6 * HEAD, :]
    kc, vc = kvc[:, :HEAD], kvc[:, HEAD:]
    scores = scores_of(cq[...], kc, seg_d[...] == seg_e[...])
    exponent = jnp.exp(scores - jnp.max(scores, -1, keepdims=True))
    probs[...] = exponent / jnp.sum(exponent, -1, keepdims=True)
    att = dot(probs[...].astype(BF16), vc).astype(BF16)
    att_out[...] = att
    part = sum_small(links, place, s_work.at[0], s_land.at[0], dot(att, w5))
    unit1, scale1 = norm_parts(d1[...] + part)
    d2 = unit1 * gs[1, 1:2, :] + gs[1, 4:5, :]
    full = gather_small(links, place, g_bufs.at[0], d2)
    full_d2[...] = full
    hidden, slope = gelu_parts(dot(full, ffn[1, 0]))
    hidden = hidden.astype(BF16)
    hid_out[...] = hidden
    part = sum_small(links, place, s_work.at[1], s_land.at[1], dot_t(hidden, ffn[1, 1]))
    unit2, scale2 = norm_parts(d2 + part)
    d3[...] = unit2 * gs[1, 2:3, :] + gs[1, 5:6, :]
    back2, gain2, shift2 = norm_back(cot[...].astype(F32), unit2, scale2, gs[1, 2:3, :])
    full = gather_small(links, place, g_bufs.at[1], back2)
    full_db2[...] = full
    pre = (dot(full, ffn[1, 1]) * slope).astype(BF16)
    pre_out[...] = pre
    part = sum_small(links, place, s_work.at[2], s_land.at[2], dot_t(pre, ffn[1, 0]))
    back1, gain1, shift1 = norm_back(back2 + part, unit1, scale1, gs[1, 1:2, :])
    dback1[...] = back1
    full = gather_small(links, place, g_bufs.at[2], back1)
    full_db1[...] = full
    att_grad = dot_t(full, w5).astype(BF16)
    p = probs[...]
    value_grad = t_dot(p.astype(BF16), att_grad)
    p_grad = dot_t(att_grad, vc)
    s_grad = (p * (p_grad - jnp.sum(p * p_grad, -1, keepdims=True))).astype(BF16)
    cq_grad[...] = (dot(s_grad, kc) * SCALE).astype(BF16)
    key_grad = t_dot(s_grad, cq[...]) * SCALE
    kvc_grad[...] = jnp.concatenate([key_grad, value_grad], 1).astype(BF16)
    grads[0:1, :] = gain1
    grads[1:2, :] = gain2
    grads[2:3, :] = shift1
    grads[3:4, :] = shift2
    grads[4:8, :] = jnp.zeros((4, grads.shape[1]), F32)
    links.finish()


def decoder_call(cq, kvc, d1, cot, seg_d, seg_e, wt, ffn, gs, collective_id):
    rows, width = d1.shape
    full, hidden = DEVICES * rows, ffn.shape[3]
    block = (SIDE, SIDE, 2 * rows, width // 2)
    return pl.pallas_call(
        decoder_kernel,
        out_shape=[
            shape((rows, width), F32),
            shape((rows, width), F32),
            shape((full, width), BF16),
            shape((full, width), BF16),
            shape((full, width), BF16),
            shape((full, hidden), BF16),
            shape((full, hidden), BF16),
            shape((full, HEAD), BF16),
            shape((full, HEAD), BF16),
            shape(kvc.shape, BF16),
            shape((8, width), F32),
        ],
        in_specs=[VM] * 9,
        out_specs=[VM] * 11,
        scratch_shapes=[
            pltpu.VMEM((3, *block), BF16),
            pltpu.VMEM((3, *block), BF16),
            pltpu.VMEM((3, DEVICES - 1, *block[2:]), BF16),
            pltpu.VMEM((full, kvc.shape[0]), F32),
        ]
        + sems(6 * (DEVICES - 1)),
        compiler_params=params(collective_id),
    )(cq, kvc, d1, cot, seg_d, seg_e, wt, ffn, gs)


def backward_kernel(*refs):
    (kvc_grad, cq_grad, dback1, wt, gs, ffn, unit1, scale1, unit2, scale2) = refs[:10]
    (dunit0, dscale0, slope, sq, sk, sv, log_d, seg_d, seg_dt) = refs[10:19]
    (full_h1, hidden, dec_ffn) = refs[19:22]
    (full_b1, full_db0, dqkv_grad, att_grad, back1, dec_grad, grads, ffn_sum) = refs[22:30]
    (full_b2, pre, part, dpart_1, dpart_2, land_1, land_2, dland_1, dland_2, dbuf) = refs[30:40]
    (ffn_grad, *pack_refs, send, recv) = refs[40:]
    place = at_grid()
    _, _, _, sibling, _, plus, minus = pack_places()
    greet(neighbours(place) + [sibling, plus, minus])

    def chain(links, low, rows, with_dec):
        here = pl.ds(low, rows)

        def cross(group):
            made = dot(stacked(kvc_grad, place, group, low, rows), wt[0, 4 * HEAD : 6 * HEAD, :])
            store_blocks(part, place, group, made.astype(BF16), low)
            if with_dec and group == PRODUCE[0]:
                dpart_1[...] = fold_all(dot(cq_grad[...], wt[1, 4 * HEAD : 5 * HEAD, :]))

        views = [(part, land_1, low, rows)]
        if with_dec:
            views.append((dpart_1, dland_1, 0, dpart_1.shape[2]))
        sums = yield from sum_blocks(links, place, views, cross)
        back2, gain2, shift2 = norm_back(sums[0], unit2[here], scale2[here, 0:1], gs[0, 2:3, :])
        full_b2[place[0], place[1], here] = back2.astype(BF16)
        views = [(full_b2, low, rows)]
        if with_dec:
            dback0, dgain0, dshift0 = norm_back(
                dback1[...] + unfold(sums[1]), dunit0[...], dscale0[:, 0:1], gs[1, 0:1, :]
            )
            dbuf[place[0], place[1]] = fold(dback0).astype(BF16)
            views.append((dbuf, 0, dbuf.shape[2]))

        def down(group):
            made = dot(stacked(full_b2, place, group, low, rows), ffn[0, 1])
            made = made * stacked(slope, place, group, low, rows)
            store_blocks(pre, place, group, made.astype(BF16), low)

        yield from gather(links, place, views, down)
        links.finish()
        ready_rows.append(rows)
        views = [(part, land_2, low, rows)]
        if with_dec:
            made = unfold_all(dbuf[...])
            full_db0[...] = made
            count = made.shape[0]
            att_d_grad = dot_t(made, wt[1, 3 * HEAD : 4 * HEAD, :]).astype(BF16)
            before = lax.broadcasted_iota(jnp.int32, (count, count), 1) <= lax.broadcasted_iota(
                jnp.int32, (count, count), 0
            )
            allowed = (seg_d[...] == seg_dt[...]) & before
            made = attend_back(sq[...], sk[...], sv[...], log_d[...], allowed, att_d_grad)
            made = jnp.concatenate([m.astype(F32) for m in made], 1).astype(BF16)
            dqkv_grad[...] = made
            dpart_2[...] = fold_all(dot(made, wt[1, 0 : 3 * HEAD, :]))
            views.append((dpart_2, dland_2, 0, dpart_2.shape[2]))

        def up(group):
            made = dot_t(stacked(pre, place, group, low, rows), ffn[0, 0])
            store_blocks(part, place, group, made.astype(BF16), low)

        sums = yield from sum_blocks(links, place, views, up)
        made, gain1, shift1 = norm_back(
            back2 + sums[0], unit1[here], scale1[here, 0:1], gs[0, 1:2, :]
        )
        back1[here] = made
        full_b1[place[0], place[1], here] = made.astype(BF16)
        totals.append((gain1, gain2, shift1, shift2))
        if with_dec:
            dec_grad[...] = dback0 + unfold(sums[1])
            grads[4:5, :] = dgain0
            grads[5:6, :] = dshift0

        def mixed(group):
            made = dot_t(stacked(full_b1, place, group, low, rows), wt[0, 3 * HEAD : 4 * HEAD, :])
            store_blocks(att_grad, place, group, made.astype(BF16), low)

        yield from gather(links, place, [(full_b1, low, rows)], mixed)
        links.finish()

    def ffn_chain(links):
        while len(ready_rows) < len(CHUNKS):
            yield
        whole = lambda ref: ref[...].reshape(DEVICES * ref.shape[2], ref.shape[3])
        count = full_h1.shape[3]
        ffn_grad[0, :count] = t_dot(whole(pre), whole(full_h1)).T.astype(BF16)
        ffn_grad[1] = dec_ffn[...]
        yield
        ffn_grad[0, count:] = t_dot(whole(hidden), whole(full_b2)).T.astype(BF16)
        yield from pack_sum(links, ffn_grad, ffn_sum, pack_refs)

    totals, chains, ready_rows = [], [], []
    for n, (low, rows) in enumerate(CHUNKS):
        links = Links(send, recv, PACK_COPIES + 7 * RING_COPIES * n)
        chains.append(chain(links, low, rows, n == len(CHUNKS) - 1))
    chains.append(ffn_chain(Links(send, recv)))
    run(chains, LAG)
    for i in range(4):
        grads[i : i + 1, :] = sum(total[i] for total in totals)
    grads[6:8, :] = jnp.zeros((2, grads.shape[1]), F32)


def backward_call(args, collective_id):
    kvc_grad, cq_grad, dback1 = args[:3]
    rows, (count, width) = kvc_grad.shape[2], dback1.shape
    full, inner = count * DEVICES, args[5].shape[3]
    grid = (SIDE, SIDE)
    small = (*grid, 2 * count, width // 2)
    return pl.pallas_call(
        backward_kernel,
        out_shape=[
            shape((*grid, rows, width), BF16),
            shape((full, width), BF16),
            shape((full, 3 * HEAD), BF16),
            shape((*grid, rows, HEAD), BF16),
            shape((rows, width), F32),
            shape((count, width), F32),
            shape((8, width), F32),
            shape((2, width, inner), BF16),
        ],
        in_specs=[VM] * 22,
        out_specs=[VM] * 8,
        scratch_shapes=[
            pltpu.VMEM((*grid, rows, width), BF16),
            pltpu.VMEM((*grid, rows, inner), BF16),
            pltpu.VMEM((*grid, rows, width), BF16),
            pltpu.VMEM(small, BF16),
            pltpu.VMEM(small, BF16),
            pltpu.VMEM((30, rows, width // 2), BF16),
            pltpu.VMEM((30, rows, width // 2), BF16),
            pltpu.VMEM((30, 2 * count, width // 4), BF16),
            pltpu.VMEM((30, 2 * count, width // 4), BF16),
            pltpu.VMEM(small, BF16),
            pltpu.VMEM((2, 2 * width, inner), BF16),
        ]
        + pack_scratch(2 * width, inner)
        + sems(PACK_COPIES + 7 * RING_COPIES * len(CHUNKS)),
        compiler_params=params(collective_id),
    )(*args)


def last_kernel(qkv_grad, wt, gs, back1, unit0, scale0, att, small, out3, dec, *rest):
    (att_out, small_out, enc_out, out3_out, dec_out, part, land, *pack_refs) = rest[:12]
    (fin, core_s, y_s, x_s, z_s, late, late_t, late_p) = rest[12:20]
    (enc, give_e, give_d, land_e, land_d, send, recv) = rest[20:]
    place = at_grid()
    section, zh, core, sibling, _, plus, minus = pack_places()
    other = 1 - section
    partner = {"section": other}
    far = {"dp": (1 - zh) * 2 + core}
    columns = [device_at(moved(place, d, 0)) for d in (1, 2, 3)]
    rows = [device_at(moved(place, 0, d)) for d in (1, 2, 3)]
    tensor = [device_at(moved(place, d // SIDE, d % SIDE)) for d in FAR_FIRST]
    packs = []
    for d in range(1, 8):
        mine = section * 4 + zh * 2 + core
        there = lax.rem(mine + d, 8)
        packs.append({"section": lax.div(there, 4), "dp": lax.rem(there, 4)})
    greet(tensor + packs)
    width = enc.shape[1] // 2
    there = pl.ds(pl.multiple_of(other * width, width), width)
    here = pl.ds(pl.multiple_of(section * width, width), width)

    def early(links):
        give_d[...] = jnp.concatenate([out3[:, there], dec[:, there]], 0).astype(BF16)
        swap = links.start(give_d, land_d, partner)
        one = links.start(small.at[1 - core], core_s, sibling)
        yield
        one.wait_recv()
        fin[core] = small[core] + core_s[...]
        for land_s, devices in ((y_s, columns), (x_s, rows), (z_s, [plus, minus, far])):
            copies = [links.start(fin.at[core], land_s.at[n], d) for n, d in enumerate(devices)]
            yield
            for copy in copies:
                copy.wait_recv()
            links.finish()
            fin[core] = fin[core] + land_s[0] + land_s[1] + land_s[2]
        five = links.start(fin.at[core], fin.at[core], sibling)
        yield
        five.wait_recv()
        swap.wait_recv()
        links.finish()

    def heads(group):
        made = dot(stacked(qkv_grad, place, group), wt[0, 0 : 3 * HEAD, :])
        store_blocks(part, place, group, made.astype(BF16))

    def rest_of(links):
        (sum_e,) = yield from sum_blocks(links, place, [(part, land, 0, enc.shape[0])], heads)
        made, gain0, shift0 = norm_back(
            back1[...] + sum_e, unit0[...], scale0[:, 0:1], gs[0, 0:1, :]
        )
        enc[...] = made
        quarter = width // 2
        both = [row[:, i * quarter : (i + 1) * quarter] for row in (gain0, shift0) for i in range(4)]
        late[...] = jnp.concatenate(both, 0)
        copies = [links.start(late, late_t.at[n], d) for n, d in enumerate(tensor)]
        give_e[...] = enc[:, there].astype(BF16)
        swap = links.start(give_e, land_e, partner)
        yield
        for copy in copies:
            copy.wait_recv()
        links.finish()
        late[...] = late[...] + jnp.sum(late_t[...], 0)
        copies = [links.start(late, late_p.at[n], d) for n, d in enumerate(packs)]
        enc_out[section] = enc[:, here]
        yield
        for copy in copies:
            copy.wait_recv()
        swap.wait_recv()
        links.finish()

    chains = [
        rest_of(Links(send, recv, 2 * PACK_COPIES + 16)),
        pack_sum(Links(send, recv), att, att_out, pack_refs),
        early(Links(send, recv, PACK_COPIES)),
    ]
    run(chains)
    enc_out[other] = land_e[...].astype(F32)
    got = land_d[...].astype(F32)
    count = out3.shape[0]
    out3_out[section] = out3[:, here]
    out3_out[other] = got[:count]
    dec_out[section] = dec[:, here]
    dec_out[other] = got[count:]
    small_out[...] = fin[section]
    total = late[...] + jnp.sum(late_p[...], 0)
    quarter = width // 2
    for i in range(8):
        row = 0 if i < 4 else 3
        cols = slice((i % 4) * quarter, (i % 4 + 1) * quarter)
        added = jnp.where(section == 0, total[i : i + 1], 0.0)
        small_out[row : row + 1, cols] = small_out[row : row + 1, cols] + added


def last_call(args, collective_id):
    back1, (att, small, out3, dec) = args[3], args[6:]
    rows, cols = back1.shape
    count, width = dec.shape[0], cols // 2
    small_rows = small.shape[1:]
    return pl.pallas_call(
        last_kernel,
        out_shape=[
            shape((2, att.shape[1] // 2, att.shape[2]), BF16),
            shape(small_rows, F32),
            shape((2, rows, width), F32),
            shape((2, count, width), F32),
            shape((2, count, width), F32),
        ],
        in_specs=[VM] * 10,
        out_specs=[VM] * 5,
        scratch_shapes=[
            pltpu.VMEM((SIDE, SIDE, rows, cols), BF16),
            pltpu.VMEM((30, rows, width), BF16),
        ]
        + pack_scratch(*att.shape[1:])
        + [
            pltpu.VMEM(small.shape, F32),
            pltpu.VMEM(small_rows, F32),
            pltpu.VMEM((3, *small_rows), F32),
            pltpu.VMEM((3, *small_rows), F32),
            pltpu.VMEM((3, *small_rows), F32),
            pltpu.VMEM((8, width // 2), F32),
            pltpu.VMEM((DEVICES - 1, 8, width // 2), F32),
            pltpu.VMEM((7, 8, width // 2), F32),
            pltpu.VMEM((rows, cols), F32),
            pltpu.VMEM((rows, width), BF16),
            pltpu.VMEM((2 * count, width), BF16),
            pltpu.VMEM((rows, width), BF16),
            pltpu.VMEM((2 * count, width), BF16),
        ]
        + sems(2 * PACK_COPIES + 16 + RING_COPIES + DEVICES + 7),
        compiler_params=params(collective_id),
    )(*args)


def on_device(
    encoder_tokens,
    encoder_segments,
    decoder_tokens,
    decoder_segments,
    cotangent,
    attention_weight,
    feedforward_weight,
    norm_gain,
    norm_shift,
):
    section = lax.axis_index("section")
    mine = lambda a: lax.dynamic_index_in_dim(a, section, 0, keepdims=False)
    width, count = encoder_tokens.shape[2], decoder_tokens.shape[1]
    own_wt = jnp.swapaxes(attention_weight[0], 1, 2).reshape(6 * HEAD, width)
    own_gs = jnp.concatenate([norm_gain[0], norm_shift[0], jnp.zeros((2, width), F32)], 0)
    y = mine(decoder_tokens)
    e, c = mine(encoder_segments), mine(decoder_segments)
    position = jnp.arange(c.shape[0])
    allow_e = e[:, None] == e[None, :]
    allow_d = (c[:, None] == c[None, :]) & (position[:, None] >= position[None, :])
    flat = lambda a: a.reshape(-1, a.shape[-1])
    blocks = lambda a: a.reshape(SIDE, SIDE, -1, a.shape[-1])

    wt, gs, full_h0, h0, unit0, scale0, full_y, q, k, v, sq, sk, sv = first_call(
        mine(encoder_tokens), y, own_wt, own_gs, 1
    )
    q, k, v = flat(q), flat(k), flat(v)
    att_e, log_e = attend(q, k, v, allow_e)
    att_d, log_d = attend(sq, sk, sv, allow_d)
    (
        ffn, full_h1, full_m, full_d1, hidden, slope, kvc, cq, d1,
        unit1, scale1, unit2, scale2, dunit0, dscale0,
    ) = forward_call(blocks(att_e), att_d, h0, y, wt, gs, feedforward_weight[0], 2)
    (d3, dback1, full_d2, full_db2, full_db1, dhidden, dpre, att_c, cq_grad, kvc_grad, dsmall) = (
        decoder_call(
            cq, flat(kvc), d1, mine(cotangent), c[:, None], e[None, :], wt, ffn, gs, 3
        )
    )
    dec_ffn = jnp.concatenate([t_dot(full_d2, dpre), t_dot(full_db2, dhidden)], 0).astype(BF16)
    full_b1, full_db0, dqkv_grad, att_e_grad, back1, dec_grad, small_b, ffn_sum = backward_call(
        (
            blocks(kvc_grad), cq_grad, dback1, wt, gs, ffn, unit1, scale1, unit2, scale2,
            dunit0, dscale0, slope, sq, sk, sv, log_d, c[:, None], c[None, :],
            full_h1, hidden, dec_ffn,
        ),
        4,
    )
    made = attend_back(q, k, v, log_e, allow_e, flat(att_e_grad))
    qkv_grad = jnp.concatenate(made, 1)

    att_grads = jnp.stack(
        [
            jnp.concatenate(
                [
                    t_dot(qkv_grad, flat(full_h0)),
                    t_dot(att_e, flat(full_b1)),
                    t_dot(kvc_grad, flat(full_m)),
                ],
                0,
            ),
            jnp.concatenate(
                [
                    t_dot(dqkv_grad, full_y),
                    t_dot(att_d, full_db0),
                    t_dot(cq_grad, full_d1),
                    t_dot(att_c, full_db1),
                ],
                0,
            ),
        ]
    ).astype(BF16)
    none = jnp.zeros((1, width), F32)
    row = lambda a, i: a[i : i + 1]
    small = jnp.stack(
        [
            jnp.concatenate(
                [none, row(small_b, 0), row(small_b, 1), none, row(small_b, 2), row(small_b, 3)]
                + [none, none],
                0,
            ),
            jnp.concatenate(
                [row(small_b, 4), dsmall[0:2], row(small_b, 5), dsmall[2:4], none, none], 0
            ),
        ]
    )
    att_sum, small_sum, enc_out, d3_out, dec_out = last_call(
        (
            blocks(qkv_grad), wt, gs, back1, unit0, scale0,
            att_grads, small, d3, dec_grad,
        ),
        5,
    )
    att_sum = att_sum.reshape(6, HEAD, width).astype(F32)
    return (
        d3_out.astype(BF16),
        enc_out,
        dec_out,
        jnp.swapaxes(att_sum, 1, 2)[None],
        ffn_sum.reshape(feedforward_weight.shape).astype(F32),
        small_sum[None, :3],
        small_sum[None, 3:6],
    )


def solution(mesh):
    in_specs = (
        P("dp", "tensor", None),
        P("dp", None),
        P("dp", "tensor", None),
        P("dp", None),
        P("dp", "tensor", None),
        P("section", None, None, "tensor"),
        P("section", None, None, "tensor"),
        P("section", None, None),
        P("section", None, None),
    )
    out_specs = (
        P("dp", "tensor", "section"),
        P("dp", "tensor", "section"),
        P("dp", "tensor", "section"),
        P("section", None, None, "tensor"),
        P("section", None, None, "tensor"),
        P("section", None, None),
        P("section", None, None),
    )
    return jax.shard_map(
        on_device, mesh=mesh, in_specs=in_specs, out_specs=out_specs, check_vma=False
    )
```

```python
import jax
import jax.numpy as jnp
from jax import lax
from jax.experimental import pallas as pl
from jax.experimental.pallas import tpu as pltpu
from jax.sharding import PartitionSpec as P

HEAD = 64
EPSILON = 1e-05
MASKED = -1000000000.0
SCALE = HEAD ** (-0.5)
F32 = jnp.float32
BF16 = jnp.bfloat16
MESH = pl.DeviceIdType.MESH
VM = pl.BlockSpec(memory_space=pltpu.VMEM)
SIDE = 4
DEVICES = SIDE * SIDE
UP = (0, 2)
DOWN = (1, 3)
RING_COPIES = 32
CHUNKS = ((0, 48), (48, 32))
PAUSES = (1, 1, 1, 1, 1)
LAG = 0
RING = True
INV_SQRT2 = 0.7071067811865476
INV_SQRT_2PI = 0.3989422804014327
FAR_FIRST = (10, 2, 8, 6, 14, 11, 9, 7, 13, 5, 15, 1, 3, 4, 12)


def norm_parts(values):
    center = values - jnp.mean(values, -1, keepdims=True)
    scale = lax.rsqrt(jnp.mean(center * center, -1, keepdims=True) + EPSILON)
    return center * scale, scale


def norm_back(grad, unit, scale, gains):
    inner = grad * gains
    back = scale * (
        inner
        - jnp.mean(inner, -1, keepdims=True)
        - unit * jnp.mean(inner * unit, -1, keepdims=True)
    )
    return back, jnp.sum(grad * unit, 0, keepdims=True), jnp.sum(grad, 0, keepdims=True)


def gelu_parts(u):
    cdf = 0.5 * (1.0 + lax.erf(u * INV_SQRT2))
    return u * cdf, cdf + u * (INV_SQRT_2PI * jnp.exp(-0.5 * u * u))


def dot(a, b):
    return jnp.dot(a, b, preferred_element_type=F32)


def dot_t(a, b):
    return lax.dot_general(a, b, (((1,), (1,)), ((), ())), preferred_element_type=F32)


def t_dot(a, b):
    return lax.dot_general(a, b, (((0,), (0,)), ((), ())), preferred_element_type=F32)


def scores_of(queries, key_rows, allowed):
    return jnp.where(allowed, dot_t(queries, key_rows) * SCALE, MASKED)


def attend(queries, key_rows, value_rows, allowed):
    scores = scores_of(queries, key_rows, allowed)
    row_max = jnp.max(scores, -1, keepdims=True)
    exponent = jnp.exp(scores - row_max)
    row_sum = jnp.sum(exponent, -1, keepdims=True)
    probs_low = (exponent / row_sum).astype(BF16)
    return dot(probs_low, value_rows).astype(BF16), row_max + jnp.log(row_sum)


def attend_back(queries, key_rows, value_rows, log_total, allowed, attended_grad):
    probs = jnp.exp(scores_of(queries, key_rows, allowed) - log_total)
    value_grad = t_dot(attended_grad, probs.astype(BF16))
    probs_grad = dot_t(attended_grad, value_rows)
    scores_grad = (probs * (probs_grad - jnp.sum(probs * probs_grad, -1, keepdims=True))).astype(
        BF16
    )
    return dot(scores_grad, key_rows) * SCALE, t_dot(queries, scores_grad) * SCALE, value_grad


def at_grid():
    index = lax.axis_index("tensor")
    return lax.div(index, SIDE), lax.rem(index, SIDE)


def moved(place, dy, dx):
    return lax.rem(place[0] + dy % SIDE, SIDE), lax.rem(place[1] + dx % SIDE, SIDE)


def along(axis, steps):
    return (steps, 0) if axis == 0 else (0, steps)


def device_at(place):
    return {"tensor": place[0] * SIDE + place[1]}


def neighbours(place):
    return [device_at(moved(place, *along(axis, s))) for axis in range(2) for s in (1, 2, 3)]


def greet(devices):
    barrier = pltpu.get_barrier_semaphore()
    for device in devices:
        pl.semaphore_signal(barrier, inc=1, device_id=device, device_id_type=MESH)
    pl.semaphore_wait(barrier, len(devices))


def sections():
    section, dp = lax.axis_index("section"), lax.axis_index("dp")
    zh, core = lax.div(dp, 2), lax.rem(dp, 2)
    return section, zh, core, {"section": 1 - section}, {"dp": zh * 2 + 1 - core}


class Links:
    def __init__(self, send_sems, recv_sems, used=0):
        self.send, self.recv, self.used, self.started = send_sems, recv_sems, used, []

    def start(self, source, target, device):
        n = self.used
        self.used += 1
        copy = pltpu.make_async_remote_copy(
            src_ref=source,
            dst_ref=target,
            send_sem=self.send.at[n],
            recv_sem=self.recv.at[n],
            device_id=device,
            device_id_type=MESH,
        )
        copy.start()
        self.started.append(copy)
        return copy

    def finish(self):
        for copy in self.started:
            copy.wait_send()
        self.started = []


def sems(n):
    return [pltpu.SemaphoreType.DMA((n,)), pltpu.SemaphoreType.DMA((n,))]


def shape(dims, kind):
    return jax.ShapeDtypeStruct(tuple(dims), kind)


def params(collective_id):
    return pltpu.CompilerParams(
        collective_id=collective_id, has_side_effects=True, vmem_limit_bytes=56 << 20
    )


def fold(rows):
    half = rows.shape[1] // 2
    return jnp.concatenate([rows[:, :half], rows[:, half:]], 0)


def unfold(rows):
    count = rows.shape[0] // 2
    return jnp.concatenate([rows[:count], rows[count:]], 1)


def unfold_all(blocks):
    count, half = blocks.shape[2] // 2, blocks.shape[3]
    split = blocks.astype(F32).reshape(DEVICES, 2, count, half)
    low = split[:, 0].reshape(DEVICES * count, half)
    high = split[:, 1].reshape(DEVICES * count, half)
    return jnp.concatenate([low, high], 1).astype(BF16)


def fold_all(part):
    count, half = part.shape[0] // DEVICES, part.shape[1] // 2
    split = part.reshape(DEVICES, count, 2 * half)
    both = jnp.concatenate([split[:, :, :half], split[:, :, half:]], 1)
    return both.astype(BF16).reshape(SIDE, SIDE, 2 * count, half)


def own_row(ref):
    return jnp.where(lax.axis_index("section") == 0, ref[0:1, :], ref[1:2, :]).astype(F32)


def column(row):
    return jnp.broadcast_to(row, (128, row.shape[1])).T


def gather(links, place, views, ready=None):
    jobs = []
    for buf, low, rows in views:
        half = buf.shape[-1] // 2
        for h in range(2):
            jobs.append((buf, 1 - h, h, h * half, half, pl.ds(low, rows)))
    ready = ready or (lambda group: None)

    def send(job, axis, steps, r, s):
        buf, a, b, start, size, rows = job
        y, x = moved(moved(place, *along(a, r)), *along(b, s))
        ref = buf.at[y, x, rows, pl.ds(start, size)]
        return links.start(ref, ref, device_at(moved(place, *along(axis, steps))))

    first, spread, ahead = [], [], []
    for job in jobs:
        first.append({-d % SIDE: send(job, job[1], d, 0, 0) for d in (2, 1, 3)})
    paths = ((1, 3), (3, 1)) if RING else ((2, 2), (1, 3), (3, 1))
    for job in jobs:
        spread.append({0: {s: send(job, job[2], d, 0, 0) for d, s in paths}})
    ready([(0, 0)])
    yield
    for r in (3, 1, 2):
        for i, job in enumerate(jobs):
            first[i][r].wait_recv()
            spread[i][r] = {s: send(job, job[2], d, r, 0) for d, s in paths}
    if RING:
        for i, job in enumerate(jobs):
            spread[i][0][3].wait_recv()
            ahead.append({0: send(job, job[2], 1, 0, 3)})
            spread[i][0][1].wait_recv()
    else:
        for i, job in enumerate(jobs):
            spread[i][0][3].wait_recv()
            spread[i][0][1].wait_recv()
            ahead.append({r: spread[i][r][2] for r in range(SIDE)})
    ready([(0, 1), (0, 3), (1, 0), (3, 0)])
    yield
    if RING:
        for r in DOWN:
            for i, job in enumerate(jobs):
                spread[i][r][1].wait_recv()
                ahead[i][r] = send(job, job[2], -1, r, 1)
        for i, job in enumerate(jobs):
            spread[i][2][3].wait_recv()
            ahead[i][2] = send(job, job[2], 1, 2, 3)
        for r in DOWN:
            for i, job in enumerate(jobs):
                spread[i][r][3].wait_recv()
    else:
        for r in DOWN:
            for i, job in enumerate(jobs):
                spread[i][r][1].wait_recv()
                spread[i][r][3].wait_recv()
    ready([(1, 1), (1, 3), (3, 1), (3, 3)])
    for i, job in enumerate(jobs):
        ahead[i][0].wait_recv()
    ready([(0, 2), (2, 0)])
    yield
    for i, job in enumerate(jobs):
        if not RING:
            spread[i][2][3].wait_recv()
        spread[i][2][1].wait_recv()
        ahead[i][1].wait_recv()
        ahead[i][3].wait_recv()
    ready([(1, 2), (3, 2), (2, 1), (2, 3)])
    for i, job in enumerate(jobs):
        ahead[i][2].wait_recv()
    ready([(2, 2)])


PRODUCE = (
    [(2, 2), (2, 3), (2, 1), (3, 2), (1, 2), (2, 0), (0, 2)],
    [(3, 3), (3, 1), (1, 3), (1, 1), (3, 0), (1, 0), (0, 3), (0, 1), (0, 0)],
)


def sum_blocks(links, place, views, produce=None):
    produce = produce or (lambda group: None)
    jobs = []
    for part, land, low, rows in views:
        half = part.shape[-1] // 2
        for h in range(2):
            jobs.append((part, land, 15 * h, 1 - h, h, h * half, half, pl.ds(low, rows)))

    def block(job, r, s):
        part, _, _, a, b, start, size, rows = job
        y, x = moved(moved(place, *along(a, r)), *along(b, s))
        return part.at[y, x, rows, pl.ds(start, size)]

    def landing(job, n):
        return job[1].at[job[2] + n, job[7]]

    def start(source, target, axis, steps):
        return links.start(source, target, device_at(moved(place, *along(axis, steps))))

    def add(target, *others):
        total = target[...].astype(F32)
        for other in others:
            total = total + other[...].astype(F32)
        return total

    def near_slot(job, r, steps):
        return landing(job, 4 + 2 * r + (0 if steps == 1 else 1))

    order = (2, 3, 1, 0)
    produce(PRODUCE[0])
    near = [{r: [] for r in order} for _ in jobs]
    if RING:
        far = []
        for job in jobs:
            far.append(
                {
                    r: start(block(job, r, 2), landing(job, r), job[4], 1 if r in UP else -1)
                    for r in order
                }
            )
        produce(PRODUCE[1])
        for i, job in enumerate(jobs):
            for r in order:
                steps = -1 if r in UP else 1
                near[i][r].append(
                    start(block(job, r, steps), near_slot(job, r, steps), job[4], steps)
                )
        yield
        for r in order:
            for i, job in enumerate(jobs):
                steps = 1 if r in UP else -1
                far[i][r].wait_recv()
                ref = block(job, r, steps)
                ref[...] = add(ref, landing(job, r)).astype(BF16)
                near[i][r].append(start(ref, near_slot(job, r, steps), job[4], steps))
    else:
        for s in (2, 1, 3):
            for r in order:
                for i, job in enumerate(jobs):
                    slot = landing(job, 4 * (s - 1) + r)
                    near[i][r].append(start(block(job, r, s), slot, job[4], s))
            if s == 2:
                produce(PRODUCE[1])
    yield
    last = [{} for _ in jobs]
    results = []
    for r in order:
        if r == 0:
            yield
        for i, job in enumerate(jobs):
            for copy in near[i][r]:
                copy.wait_recv()
            ref = block(job, r, 0)
            if RING:
                total = add(ref, landing(job, 4 + 2 * r), landing(job, 5 + 2 * r))
            else:
                total = add(ref, landing(job, r), landing(job, 4 + r), landing(job, 8 + r))
            if r == 0:
                results.append(total)
            else:
                ref[...] = total.astype(BF16)
                last[i][r] = start(ref, landing(job, 11 + r), job[3], r)
    for i, job in enumerate(jobs):
        for r in order[:3]:
            last[i][r].wait_recv()
            results[i] = results[i] + landing(job, 11 + r)[...].astype(F32)
    return [jnp.concatenate(results[i : i + 2], 1) for i in range(0, len(results), 2)]


def run(chains, lag=0):
    turn, active = 0, list(enumerate(chains))
    while active:
        for n, chain in list(active):
            if turn >= n * lag:
                try:
                    next(chain)
                except StopIteration:
                    active.remove((n, chain))
        turn += 1


def pack_places():
    section, zh, core, partner, sibling = sections()
    zh_plus = lax.rem(zh + section, 2)
    plus = {"section": 1 - section, "dp": zh_plus * 2 + core}
    minus = {"section": 1 - section, "dp": (1 - zh_plus) * 2 + core}
    return section, zh, core, sibling, zh_plus, plus, minus


PACK_COPIES = 8


def pack_scratch(rows, cols):
    half, quarter = rows // 2, rows // 4
    return [
        pltpu.VMEM((2, half, cols), BF16),
        pltpu.VMEM((2, half, cols), BF16),
        pltpu.VMEM((2, quarter, cols), BF16),
        pltpu.VMEM((2, quarter, cols), BF16),
        pltpu.VMEM((half, cols), BF16),
    ]


def pause(n):
    for _ in range(n):
        yield


def pack_sum(links, grad, out, scratch):
    work, core_land, side, passing, over = scratch
    section, zh, core, sibling, zh_plus, plus, minus = pack_places()
    other = 1 - section
    half = grad.shape[1] // 2
    quarter = half // 2
    first = links.start(grad.at[:, pl.ds((1 - core) * half, half)], core_land, sibling)
    yield from pause(PAUSES[0])
    first.wait_recv()
    work[...] = (
        grad[:, pl.ds(core * half, half)].astype(F32) + core_land[...].astype(F32)
    ).astype(BF16)
    second = [
        links.start(work.at[other, pl.ds(h * quarter, quarter)], side.at[n], d)
        for n, (h, d) in enumerate(((zh_plus, plus), (1 - zh_plus, minus)))
    ]
    yield from pause(PAUSES[1])
    for copy in second:
        copy.wait_recv()
    mine = work.at[section, pl.ds(zh * quarter, quarter)]
    mine[...] = (mine[...].astype(F32) + side[0].astype(F32) + side[1].astype(F32)).astype(BF16)
    third = [
        links.start(work.at[section, pl.ds(n * quarter, quarter)], passing.at[n], d)
        for n, d in enumerate((plus, minus))
    ]
    yield from pause(PAUSES[2])
    fourth = []
    for n, device in enumerate((plus, minus)):
        third[n].wait_recv()
        fourth.append(links.start(passing.at[n], over.at[pl.ds(n * quarter, quarter)], device))
    yield from pause(PAUSES[3])
    for copy in fourth:
        copy.wait_recv()
    out[core] = (work[section].astype(F32) + over[...].astype(F32)).astype(BF16)
    last = links.start(out.at[core], out.at[core], sibling)
    yield from pause(PAUSES[4])
    last.wait_recv()
    links.finish()


def gather_small(links, place, buf, rows):
    y, x = place
    buf[y, x] = fold(rows).astype(BF16)
    copies = []
    for d in FAR_FIRST:
        target = device_at(moved(place, d // SIDE, d % SIDE))
        copies.append(links.start(buf.at[y, x], buf.at[y, x], target))
    for copy in copies:
        copy.wait_recv()
    return unfold_all(buf[...])


def sum_small(links, place, work, land, part):
    work[...] = fold_all(part)
    copies = []
    for n, d in enumerate(FAR_FIRST):
        there = moved(place, d // SIDE, d % SIDE)
        copies.append(links.start(work.at[there[0], there[1]], land.at[n], device_at(there)))
    total = work[place[0], place[1]].astype(F32)
    for copy in copies:
        copy.wait_recv()
    return unfold(total + jnp.sum(land[...].astype(F32), 0))


def stacked(ref, place, group, low=0, rows=None):
    rows = ref.shape[2] if rows is None else rows
    blocks = []
    for dy, dx in group:
        y, x = moved(place, dy, dx)
        blocks.append(ref[y, x, low : low + rows])
    return blocks[0] if len(blocks) == 1 else jnp.concatenate(blocks, 0)


def store_blocks(ref, place, group, values, low=0):
    rows = values.shape[0] // len(group)
    for n, (dy, dx) in enumerate(group):
        y, x = moved(place, dy, dx)
        ref[y, x, low : low + rows] = values[n * rows : (n + 1) * rows]


def whole(ref):
    return ref[...].reshape(DEVICES * ref.shape[2], ref.shape[3])


def wide(scale):
    return jnp.broadcast_to(scale, (scale.shape[0], 128))


def first_kernel(
    tokens, dec_tokens, seg_d, wt_in, gain_in, shift_in, wt, gs, full_h0, h0, unit0, scale0, *rest
):
    (full_y, q, k, v, sq, sk, sv, att_d, log_d, xbuf, ybuf, gs_in, send, recv) = rest
    place = at_grid()
    section, _, core, partner, sibling = sections()
    greet(neighbours(place) + [partner, sibling])
    links = Links(send, recv)
    half = wt_in.shape[0] // 2
    mine = pl.ds(core * half, half)
    x, y = tokens.at[section], dec_tokens.at[section]
    gs_in[0:3, :] = gain_in[...]
    gs_in[3:6, :] = shift_in[...]
    gs_in[6:8, :] = jnp.zeros((2, x.shape[1]), F32)
    gains_copy = links.start(gs_in, gs.at[section], partner)
    xbuf[place[0], place[1]] = x[...]
    ybuf[place[0], place[1]] = fold(y[...].astype(F32)).astype(BF16)
    passed = []

    def ready(group):
        if group == [(0, 0)]:
            passed.append(links.start(wt_in.at[mine], wt.at[section, mine], partner))
            gs[section] = gs_in[...]
            wt[section] = wt_in[...]
            gains_copy.wait_recv()
        if group == [(1, 1), (1, 3), (3, 1), (3, 3)]:
            passed[0].wait_recv()
            theirs = wt.at[1 - section, mine]
            passed.append(links.start(theirs, theirs, sibling))
        unit, scale = norm_parts(stacked(xbuf, place, group).astype(F32))
        rows = unit * gs[0, 0:1, :] + gs[0, 3:4, :]
        if group == [(0, 0)]:
            h0[...] = rows
            unit0[...] = unit
            scale0[...] = wide(scale)
        store_blocks(full_h0, place, group, rows.astype(BF16))

    views = [(xbuf, 0, x.shape[0]), (ybuf, 0, ybuf.shape[2])]
    run([gather(links, place, views, ready)])
    passed[1].wait_recv()
    count, width = x.shape
    for i in range(SIDE):
        rows = full_h0[i].reshape(SIDE * count, width)
        made = dot_t(rows, wt[0, 0 : 3 * HEAD, :]).astype(BF16)
        for j, ref in enumerate((q, k, v)):
            ref[i] = made[:, j * HEAD : (j + 1) * HEAD].reshape(SIDE, count, HEAD)
    rows = unfold_all(ybuf[...])
    full_y[...] = rows
    made = dot_t(rows, wt[1, 0 : 3 * HEAD, :]).astype(BF16)
    for j, ref in enumerate((sq, sk, sv)):
        ref[...] = made[:, j * HEAD : (j + 1) * HEAD]
    row = own_row(seg_d)
    att, log_total = attend(sq[...], sk[...], sv[...], before(row))
    att_d[...] = att
    log_d[...] = wide(log_total)
    links.finish()


def before(row):
    count = row.shape[1]
    place = [lax.broadcasted_iota(jnp.int32, (count, count), i) for i in range(2)]
    return (column(row)[:, 0:1] == row) & (place[1] <= place[0])


def first_call(tokens, dec_tokens, seg_d, wt, gain, shift, collective_id):
    (_, rows, width), count = tokens.shape, dec_tokens.shape[1]
    full = count * DEVICES
    return pl.pallas_call(
        first_kernel,
        out_shape=[
            shape((2, *wt.shape), BF16),
            shape((2, 8, width), F32),
            shape((SIDE, SIDE, rows, width), BF16),
            shape((rows, width), F32),
            shape((rows, width), F32),
            shape((rows, 128), F32),
            shape((full, width), BF16),
        ]
        + [shape((SIDE, SIDE, rows, HEAD), BF16)] * 3
        + [shape((full, HEAD), BF16)] * 4
        + [shape((full, 128), F32)],
        in_specs=[VM] * 6,
        out_specs=[VM] * 15,
        scratch_shapes=[
            pltpu.VMEM((SIDE, SIDE, rows, width), BF16),
            pltpu.VMEM((SIDE, SIDE, 2 * count, width // 2), BF16),
            pltpu.VMEM((8, width), F32),
        ]
        + sems(2 * RING_COPIES + 3),
        compiler_params=params(collective_id),
    )(tokens, dec_tokens, seg_d, wt, gain, shift)


def forward_kernel(q, k, v, seg_e, att_d, h0, dec_tokens, wt, gs, ffn_in, *rest):
    (ffn, full_h1, full_m, full_d1, hidden, slope, kvc, cq, d1) = rest[:9]
    (unit1, scale1, unit2, scale2, dunit0, dscale0, att_e, log_e, seg_col) = rest[9:18]
    (part, dpart, land_1, land_2, land_d, d1buf, send, recv) = rest[18:]
    place = at_grid()
    section, _, core, partner, sibling = sections()
    greet(neighbours(place) + [partner, sibling])
    y = dec_tokens.at[section]
    row = own_row(seg_e)
    seg_col[...] = column(row).reshape(seg_col.shape)
    shared = Links(send, recv)
    passed = [shared.start(ffn_in.at[core], ffn.at[section, core], partner)]

    def chain(links, low, rows, with_dec):
        here = pl.ds(low, rows)

        def attended(group):
            allowed = stacked(seg_col, place, group, low, rows)[:, 0:1] == row
            queries = stacked(q, place, group, low, rows)
            att, log_total = attend(queries, whole(k), whole(v), allowed)
            store_blocks(att_e, place, group, att, low)
            store_blocks(log_e, place, group, wide(log_total), low)
            made = dot(att, wt[0, 3 * HEAD : 4 * HEAD, :])
            store_blocks(part, place, group, made.astype(BF16), low)
            if with_dec and group == PRODUCE[0]:
                dpart[...] = fold_all(dot(att_d[...], wt[1, 3 * HEAD : 4 * HEAD, :]))
            if low == 0 and group == PRODUCE[1]:
                ffn[section] = ffn_in[...]

        views = [(part, land_1, low, rows)]
        if with_dec:
            views.append((dpart, land_d, 0, dpart.shape[2]))
        sums = yield from sum_blocks(links, place, views, attended)
        unit, scale = norm_parts(h0[here] + sums[0])
        unit1[here] = unit
        scale1[here] = wide(scale)
        h1 = unit * gs[0, 1:2, :] + gs[0, 4:5, :]
        full_h1[place[0], place[1], here] = h1.astype(BF16)
        views = [(full_h1, low, rows)]
        if with_dec:
            unit, scale = norm_parts(y[...].astype(F32) + unfold(sums[1]))
            dunit0[...] = unit
            dscale0[...] = wide(scale)
            made = unit * gs[1, 0:1, :] + gs[1, 3:4, :]
            d1[...] = made
            d1buf[place[0], place[1]] = fold(made).astype(BF16)
            views.append((d1buf, 0, d1buf.shape[2]))
        if low == 0:
            passed[0].wait_recv()
            theirs = ffn.at[1 - section, core]
            passed.append(shared.start(theirs, theirs, sibling))

        def up(group):
            if group == [(0, 0)]:
                return
            if group == [(0, 1), (0, 3), (1, 0), (3, 0)]:
                if low == 0:
                    passed[1].wait_recv()
                group = [(0, 0)] + group
            made, back = gelu_parts(dot(stacked(full_h1, place, group, low, rows), ffn[0, 0]))
            store_blocks(hidden, place, group, made.astype(BF16), low)
            store_blocks(slope, place, group, back, low)

        yield from gather(links, place, views, up)
        links.finish()
        if with_dec:
            made = unfold_all(d1buf[...])
            full_d1[...] = made
            cq[...] = dot_t(made, wt[1, 4 * HEAD : 5 * HEAD, :]).astype(BF16)

        def down(group):
            made = dot_t(stacked(hidden, place, group, low, rows), ffn[0, 1])
            store_blocks(part, place, group, made.astype(BF16), low)

        sums = yield from sum_blocks(links, place, [(part, land_2, low, rows)], down)
        unit, scale = norm_parts(h1 + sums[0])
        unit2[here] = unit
        scale2[here] = wide(scale)
        full_m[place[0], place[1], here] = (unit * gs[0, 2:3, :] + gs[0, 5:6, :]).astype(BF16)

        def cross(group):
            made = dot_t(stacked(full_m, place, group, low, rows), wt[0, 4 * HEAD : 6 * HEAD, :])
            store_blocks(kvc, place, group, made.astype(BF16), low)

        yield from gather(links, place, [(full_m, low, rows)], cross)
        links.finish()

    chains = []
    for n, (low, rows) in enumerate(CHUNKS):
        links = Links(send, recv, 2 + 6 * RING_COPIES * n)
        chains.append(chain(links, low, rows, n == len(CHUNKS) - 1))
    run(chains, LAG)
    shared.finish()


def forward_call(q, k, v, seg_e, att_d, h0, dec_tokens, wt, gs, ffn, collective_id):
    (rows, width), count = h0.shape, dec_tokens.shape[1]
    full, inner = count * DEVICES, ffn.shape[2]
    grid = (SIDE, SIDE)
    return pl.pallas_call(
        forward_kernel,
        out_shape=[
            shape((2, *ffn.shape), BF16),
            shape((*grid, rows, width), BF16),
            shape((*grid, rows, width), BF16),
            shape((full, width), BF16),
            shape((*grid, rows, inner), BF16),
            shape((*grid, rows, inner), F32),
            shape((*grid, rows, 2 * HEAD), BF16),
            shape((full, HEAD), BF16),
            shape((count, width), F32),
            shape((rows, width), F32),
            shape((rows, 128), F32),
            shape((rows, width), F32),
            shape((rows, 128), F32),
            shape((count, width), F32),
            shape((count, 128), F32),
            shape((*grid, rows, HEAD), BF16),
            shape((*grid, rows, 128), F32),
            shape((*grid, rows, 128), F32),
        ],
        in_specs=[VM] * 10,
        out_specs=[VM] * 18,
        scratch_shapes=[
            pltpu.VMEM((*grid, rows, width), BF16),
            pltpu.VMEM((*grid, 2 * count, width // 2), BF16),
            pltpu.VMEM((30, rows, width // 2), BF16),
            pltpu.VMEM((30, rows, width // 2), BF16),
            pltpu.VMEM((30, 2 * count, width // 4), BF16),
            pltpu.VMEM((*grid, 2 * count, width // 2), BF16),
        ]
        + sems(6 * RING_COPIES * len(CHUNKS) + 2),
        compiler_params=params(collective_id),
    )(q, k, v, seg_e, att_d, h0, dec_tokens, wt, gs, ffn)


def decoder_kernel(cq, kvc, d1, cot, seg_d, seg_e, wt, ffn, gs, *rest):
    (d3, dback1, full_d2, full_db2, full_db1, hid_out, pre_out, att_out) = rest[:8]
    (cq_grad, kvc_grad, grads, g_bufs, s_work, s_land, probs, send, recv) = rest[8:]
    place = at_grid()
    greet([device_at(moved(place, d // SIDE, d % SIDE)) for d in range(1, DEVICES)])
    links = Links(send, recv)
    w5 = wt[1, 5 * HEAD : 6 * HEAD, :]
    both = whole(kvc)
    kc, vc = both[:, :HEAD], both[:, HEAD:]
    allowed = column(own_row(seg_d))[:, 0:1] == own_row(seg_e)
    scores = scores_of(cq[...], kc, allowed)
    exponent = jnp.exp(scores - jnp.max(scores, -1, keepdims=True))
    probs[...] = exponent / jnp.sum(exponent, -1, keepdims=True)
    att = dot(probs[...].astype(BF16), vc).astype(BF16)
    att_out[...] = att
    part = sum_small(links, place, s_work.at[0], s_land.at[0], dot(att, w5))
    unit1, scale1 = norm_parts(d1[...] + part)
    d2 = unit1 * gs[1, 1:2, :] + gs[1, 4:5, :]
    full = gather_small(links, place, g_bufs.at[0], d2)
    full_d2[...] = full
    hidden, slope = gelu_parts(dot(full, ffn[1, 0]))
    hidden = hidden.astype(BF16)
    hid_out[...] = hidden
    part = sum_small(links, place, s_work.at[1], s_land.at[1], dot_t(hidden, ffn[1, 1]))
    unit2, scale2 = norm_parts(d2 + part)
    d3[...] = unit2 * gs[1, 2:3, :] + gs[1, 5:6, :]
    back2, gain2, shift2 = norm_back(cot[lax.axis_index("section")].astype(F32), unit2, scale2, gs[1, 2:3, :])
    full = gather_small(links, place, g_bufs.at[1], back2)
    full_db2[...] = full
    pre = (dot(full, ffn[1, 1]) * slope).astype(BF16)
    pre_out[...] = pre
    part = sum_small(links, place, s_work.at[2], s_land.at[2], dot_t(pre, ffn[1, 0]))
    back1, gain1, shift1 = norm_back(back2 + part, unit1, scale1, gs[1, 1:2, :])
    dback1[...] = back1
    full = gather_small(links, place, g_bufs.at[2], back1)
    full_db1[...] = full
    att_grad = dot_t(full, w5).astype(BF16)
    p = probs[...]
    value_grad = t_dot(att_grad, p.astype(BF16))
    p_grad = dot_t(att_grad, vc)
    s_grad = (p * (p_grad - jnp.sum(p * p_grad, -1, keepdims=True))).astype(BF16)
    cq_grad[...] = (dot(s_grad, kc) * SCALE).astype(BF16)
    key_grad = t_dot(cq[...], s_grad) * SCALE
    both = jnp.concatenate([key_grad, value_grad], 0).T.astype(BF16)
    kvc_grad[...] = both.reshape(kvc_grad.shape)
    grads[0:1, :] = gain1
    grads[1:2, :] = gain2
    grads[2:3, :] = shift1
    grads[3:4, :] = shift2
    grads[4:8, :] = jnp.zeros((4, grads.shape[1]), F32)
    links.finish()


def decoder_call(cq, kvc, d1, cot, seg_d, seg_e, wt, ffn, gs, collective_id):
    rows, width = d1.shape
    full, hidden = DEVICES * rows, ffn.shape[3]
    block = (SIDE, SIDE, 2 * rows, width // 2)
    return pl.pallas_call(
        decoder_kernel,
        out_shape=[
            shape((rows, width), F32),
            shape((rows, width), F32),
            shape((full, width), BF16),
            shape((full, width), BF16),
            shape((full, width), BF16),
            shape((full, hidden), BF16),
            shape((full, hidden), BF16),
            shape((full, HEAD), BF16),
            shape((full, HEAD), BF16),
            shape(kvc.shape, BF16),
            shape((8, width), F32),
        ],
        in_specs=[VM] * 9,
        out_specs=[VM] * 11,
        scratch_shapes=[
            pltpu.VMEM((3, *block), BF16),
            pltpu.VMEM((3, *block), BF16),
            pltpu.VMEM((3, DEVICES - 1, *block[2:]), BF16),
            pltpu.VMEM((full, DEVICES * kvc.shape[2]), F32),
        ]
        + sems(6 * (DEVICES - 1)),
        compiler_params=params(collective_id),
    )(cq, kvc, d1, cot, seg_d, seg_e, wt, ffn, gs)


def backward_kernel(*refs):
    (kvc_grad, cq_grad, dback1, wt, gs, ffn, unit1, scale1, unit2, scale2) = refs[:10]
    (dunit0, dscale0, slope, sq, sk, sv, log_d, seg_d, full_h1, hidden) = refs[10:20]
    (full_m, full_d1, full_y, full_d2, full_db1, full_db2, dpre, dhidden) = refs[20:28]
    (att_c, att_d) = refs[28:30]
    (full_b1, att_grad, back1, dec_grad, grads, ffn_sum, wt_grad) = refs[30:37]
    (full_b2, pre, part, dpart_1, dpart_2, land_1, land_2, dland_1, dland_2, dbuf) = refs[37:47]
    (ffn_grad, *pack_refs, send, recv) = refs[47:]
    place = at_grid()
    _, _, _, sibling, _, plus, minus = pack_places()
    greet(neighbours(place) + [sibling, plus, minus])

    def chain(links, low, rows, with_dec):
        here = pl.ds(low, rows)

        def cross(group):
            made = dot(stacked(kvc_grad, place, group, low, rows), wt[0, 4 * HEAD : 6 * HEAD, :])
            store_blocks(part, place, group, made.astype(BF16), low)
            if with_dec and group == PRODUCE[0]:
                dpart_1[...] = fold_all(dot(cq_grad[...], wt[1, 4 * HEAD : 5 * HEAD, :]))

        views = [(part, land_1, low, rows)]
        if with_dec:
            views.append((dpart_1, dland_1, 0, dpart_1.shape[2]))
        sums = yield from sum_blocks(links, place, views, cross)
        back2, gain2, shift2 = norm_back(sums[0], unit2[here], scale2[here, 0:1], gs[0, 2:3, :])
        full_b2[place[0], place[1], here] = back2.astype(BF16)
        views = [(full_b2, low, rows)]
        if with_dec:
            dback0, dgain0, dshift0 = norm_back(
                dback1[...] + unfold(sums[1]), dunit0[...], dscale0[:, 0:1], gs[1, 0:1, :]
            )
            dbuf[place[0], place[1]] = fold(dback0).astype(BF16)
            views.append((dbuf, 0, dbuf.shape[2]))

        def down(group):
            made = dot(stacked(full_b2, place, group, low, rows), ffn[0, 1])
            made = made * stacked(slope, place, group, low, rows)
            store_blocks(pre, place, group, made.astype(BF16), low)

        yield from gather(links, place, views, down)
        links.finish()
        ready_rows.append(rows)
        views = [(part, land_2, low, rows)]
        if with_dec:
            full_db0 = unfold_all(dbuf[...])
            att_d_grad = dot_t(full_db0, wt[1, 3 * HEAD : 4 * HEAD, :]).astype(BF16)
            made = attend_back(
                sq[...], sk[...], sv[...], log_d[:, 0:1], before(own_row(seg_d)), att_d_grad
            )
            made = jnp.concatenate([made[0], made[1].T, made[2].T], 1).astype(BF16)
            late.extend([made, full_db0])
            dpart_2[...] = fold_all(dot(made, wt[1, 0 : 3 * HEAD, :]))
            views.append((dpart_2, dland_2, 0, dpart_2.shape[2]))

        def up(group):
            made = dot_t(stacked(pre, place, group, low, rows), ffn[0, 0])
            store_blocks(part, place, group, made.astype(BF16), low)

        sums = yield from sum_blocks(links, place, views, up)
        made, gain1, shift1 = norm_back(
            back2 + sums[0], unit1[here], scale1[here, 0:1], gs[0, 1:2, :]
        )
        back1[here] = made
        full_b1[place[0], place[1], here] = made.astype(BF16)
        totals.append((gain1, gain2, shift1, shift2))
        if with_dec:
            dec_grad[...] = dback0 + unfold(sums[1])
            grads[4:5, :] = dgain0
            grads[5:6, :] = dshift0

        def mixed(group):
            made = dot_t(stacked(full_b1, place, group, low, rows), wt[0, 3 * HEAD : 4 * HEAD, :])
            store_blocks(att_grad, place, group, made.astype(BF16), low)

        yield from gather(links, place, [(full_b1, low, rows)], mixed)
        links.finish()

    def weight_chain(links):
        def put(layer, first, rows):
            wt_grad[layer, first * HEAD : first * HEAD + rows.shape[0], :] = rows.astype(BF16)

        count = full_h1.shape[3]
        yield
        put(0, 4, t_dot(whole(kvc_grad), whole(full_m)))
        ffn_grad[1, :count] = t_dot(dpre[...], full_d2[...]).T.astype(BF16)
        yield
        ffn_grad[1, count:] = t_dot(dhidden[...], full_db2[...]).T.astype(BF16)
        put(1, 4, t_dot(cq_grad[...], full_d1[...]))
        put(1, 5, t_dot(att_c[...], full_db1[...]))
        while len(ready_rows) < len(CHUNKS):
            yield
        ffn_grad[0, :count] = t_dot(whole(pre), whole(full_h1)).T.astype(BF16)
        yield
        ffn_grad[0, count:] = t_dot(whole(hidden), whole(full_b2)).T.astype(BF16)
        yield from pack_sum(links, ffn_grad, ffn_sum, pack_refs)
        put(1, 0, t_dot(late[0], full_y[...]))
        put(1, 3, t_dot(att_d[...], late[1]))
        unused = slice(0, 4 * HEAD)
        wt_grad[0, unused, :] = jnp.zeros((4 * HEAD, count), BF16)

    late = []
    totals, chains, ready_rows = [], [], []
    for n, (low, rows) in enumerate(CHUNKS):
        links = Links(send, recv, PACK_COPIES + 7 * RING_COPIES * n)
        chains.append(chain(links, low, rows, n == len(CHUNKS) - 1))
    chains.append(weight_chain(Links(send, recv)))
    run(chains, LAG)
    for i in range(4):
        grads[i : i + 1, :] = sum(total[i] for total in totals)
    grads[6:8, :] = jnp.zeros((2, grads.shape[1]), F32)


def backward_call(args, collective_id):
    kvc_grad, _, dback1 = args[:3]
    rows, (count, width) = kvc_grad.shape[2], dback1.shape
    inner = args[5].shape[3]
    grid = (SIDE, SIDE)
    small = (*grid, 2 * count, width // 2)
    return pl.pallas_call(
        backward_kernel,
        out_shape=[
            shape((*grid, rows, width), BF16),
            shape((*grid, rows, HEAD), BF16),
            shape((rows, width), F32),
            shape((count, width), F32),
            shape((8, width), F32),
            shape((2, width, inner), BF16),
            shape((2, 6 * HEAD, width), BF16),
        ],
        in_specs=[VM] * 30,
        out_specs=[VM] * 7,
        scratch_shapes=[
            pltpu.VMEM((*grid, rows, width), BF16),
            pltpu.VMEM((*grid, rows, inner), BF16),
            pltpu.VMEM((*grid, rows, width), BF16),
            pltpu.VMEM(small, BF16),
            pltpu.VMEM(small, BF16),
            pltpu.VMEM((30, rows, width // 2), BF16),
            pltpu.VMEM((30, rows, width // 2), BF16),
            pltpu.VMEM((30, 2 * count, width // 4), BF16),
            pltpu.VMEM((30, 2 * count, width // 4), BF16),
            pltpu.VMEM(small, BF16),
            pltpu.VMEM((2, 2 * width, inner), BF16),
        ]
        + pack_scratch(2 * width, inner)
        + sems(PACK_COPIES + 7 * RING_COPIES * len(CHUNKS)),
        compiler_params=params(collective_id),
    )(*args)


def last_kernel(q, k, v, seg_e, seg_col, log_e, att_e, att_grad, full_b1, full_h0, *refs):
    (wt, gs, back1, unit0, scale0, wt_grad, small_b, small_d, out3, dec, *rest) = refs
    (att_out, small_out, enc_out, out3_out, dec_out, part, land, *pack_refs) = rest[:12]
    (fin, core_s, y_s, x_s, z_s, late, late_t, late_p) = rest[12:20]
    (enc, give_e, give_d, land_e, land_d, qkv_grad, att, small, send, recv) = rest[20:]
    place = at_grid()
    section, zh, core, sibling, _, plus, minus = pack_places()
    other = 1 - section
    partner = {"section": other}
    far = {"dp": (1 - zh) * 2 + core}
    columns = [device_at(moved(place, d, 0)) for d in (1, 2, 3)]
    rows = [device_at(moved(place, 0, d)) for d in (1, 2, 3)]
    tensor = [device_at(moved(place, d // SIDE, d % SIDE)) for d in FAR_FIRST]
    packs = []
    for d in range(1, 8):
        mine = section * 4 + zh * 2 + core
        there = lax.rem(mine + d, 8)
        packs.append({"section": lax.div(there, 4), "dp": lax.rem(there, 4)})
    greet(tensor + packs)
    width = enc.shape[1] // 2
    there = pl.ds(pl.multiple_of(other * width, width), width)
    here = pl.ds(pl.multiple_of(section * width, width), width)

    att[...] = wt_grad[...]
    small[...] = jnp.zeros(small.shape, F32)
    for layer, to, source, frm in (
        (0, 1, small_b, 0), (0, 2, small_b, 1), (0, 4, small_b, 2), (0, 5, small_b, 3),
        (1, 0, small_b, 4), (1, 3, small_b, 5),
        (1, 1, small_d, 0), (1, 2, small_d, 1), (1, 4, small_d, 2), (1, 5, small_d, 3),
    ):
        small[layer, to : to + 1, :] = source[frm : frm + 1, :]

    def early(links):
        give_d[...] = jnp.concatenate([out3[:, there], dec[:, there]], 0).astype(BF16)
        swap = links.start(give_d, land_d, partner)
        one = links.start(small.at[1 - core], core_s, sibling)
        yield
        one.wait_recv()
        fin[core] = small[core] + core_s[...]
        for land_s, devices in ((y_s, columns), (x_s, rows), (z_s, [plus, minus, far])):
            copies = [links.start(fin.at[core], land_s.at[n], d) for n, d in enumerate(devices)]
            yield
            for copy in copies:
                copy.wait_recv()
            links.finish()
            fin[core] = fin[core] + land_s[0] + land_s[1] + land_s[2]
        five = links.start(fin.at[core], fin.at[core], sibling)
        yield
        five.wait_recv()
        swap.wait_recv()
        links.finish()

    def heads(group):
        made = dot(stacked(qkv_grad, place, group), wt[0, 0 : 3 * HEAD, :])
        store_blocks(part, place, group, made.astype(BF16))
        if group == PRODUCE[1]:
            made = t_dot(whole(qkv_grad), whole(full_h0))
            att[0, 0 : 3 * HEAD, :] = made.astype(BF16)
            att[0, 3 * HEAD : 4 * HEAD, :] = t_dot(whole(att_e), whole(full_b1)).astype(BF16)

    def attention_back():
        row, count = own_row(seg_e), q.shape[2]
        key_rows, value_rows = whole(k), whole(v)
        totals = [0.0, 0.0]
        for i in range(SIDE):
            some = lambda ref: ref[i].reshape(SIDE * count, ref.shape[3])
            made = attend_back(
                some(q), key_rows, value_rows, some(log_e)[:, 0:1],
                some(seg_col)[:, 0:1] == row, some(att_grad),
            )
            qkv_grad[i, :, :, 0:HEAD] = made[0].astype(BF16).reshape(SIDE, count, HEAD)
            totals = [total + part for total, part in zip(totals, made[1:])]
        both = jnp.concatenate(totals, 0).T.astype(BF16)
        qkv_grad[:, :, :, HEAD : 3 * HEAD] = both.reshape(SIDE, SIDE, count, 2 * HEAD)

    def rest_of(links):
        attention_back()
        (sum_e,) = yield from sum_blocks(links, place, [(part, land, 0, enc.shape[0])], heads)
        made, gain0, shift0 = norm_back(
            back1[...] + sum_e, unit0[...], scale0[:, 0:1], gs[0, 0:1, :]
        )
        enc[...] = made
        quarter = width // 2
        both = [row[:, i * quarter : (i + 1) * quarter] for row in (gain0, shift0) for i in range(4)]
        late[...] = jnp.concatenate(both, 0)
        copies = [links.start(late, late_t.at[n], d) for n, d in enumerate(tensor)]
        give_e[...] = enc[:, there].astype(BF16)
        swap = links.start(give_e, land_e, partner)
        yield
        for copy in copies:
            copy.wait_recv()
        links.finish()
        late[...] = late[...] + jnp.sum(late_t[...], 0)
        copies = [links.start(late, late_p.at[n], d) for n, d in enumerate(packs)]
        enc_out[section] = enc[:, here]
        yield
        for copy in copies:
            copy.wait_recv()
        swap.wait_recv()
        links.finish()

    chains = [
        early(Links(send, recv, PACK_COPIES)),
        rest_of(Links(send, recv, 2 * PACK_COPIES + 16)),
        pack_sum(Links(send, recv), att, att_out, pack_refs),
    ]
    run(chains)
    enc_out[other] = land_e[...].astype(F32)
    got = land_d[...].astype(F32)
    count = out3.shape[0]
    out3_out[section] = out3[:, here]
    out3_out[other] = got[:count]
    dec_out[section] = dec[:, here]
    dec_out[other] = got[count:]
    small_out[...] = fin[section]
    total = late[...] + jnp.sum(late_p[...], 0)
    quarter = width // 2
    for i in range(8):
        row = 0 if i < 4 else 3
        cols = slice((i % 4) * quarter, (i % 4 + 1) * quarter)
        added = jnp.where(section == 0, total[i : i + 1], 0.0)
        small_out[row : row + 1, cols] = small_out[row : row + 1, cols] + added


def last_call(args, collective_id):
    back1, att, dec = args[12], args[15], args[19]
    rows, cols = back1.shape
    count, width = dec.shape[0], cols // 2
    small_rows = (8, cols)
    return pl.pallas_call(
        last_kernel,
        out_shape=[
            shape((2, att.shape[1] // 2, att.shape[2]), BF16),
            shape(small_rows, F32),
            shape((2, rows, width), F32),
            shape((2, count, width), F32),
            shape((2, count, width), F32),
        ],
        in_specs=[VM] * 20,
        out_specs=[VM] * 5,
        scratch_shapes=[
            pltpu.VMEM((SIDE, SIDE, rows, cols), BF16),
            pltpu.VMEM((30, rows, width), BF16),
        ]
        + pack_scratch(*att.shape[1:])
        + [
            pltpu.VMEM((2, *small_rows), F32),
            pltpu.VMEM(small_rows, F32),
            pltpu.VMEM((3, *small_rows), F32),
            pltpu.VMEM((3, *small_rows), F32),
            pltpu.VMEM((3, *small_rows), F32),
            pltpu.VMEM((8, width // 2), F32),
            pltpu.VMEM((DEVICES - 1, 8, width // 2), F32),
            pltpu.VMEM((7, 8, width // 2), F32),
            pltpu.VMEM((rows, cols), F32),
            pltpu.VMEM((rows, width), BF16),
            pltpu.VMEM((2 * count, width), BF16),
            pltpu.VMEM((rows, width), BF16),
            pltpu.VMEM((2 * count, width), BF16),
            pltpu.VMEM((SIDE, SIDE, rows, 3 * HEAD), BF16),
            pltpu.VMEM(att.shape, BF16),
            pltpu.VMEM((2, *small_rows), F32),
        ]
        + sems(2 * PACK_COPIES + 16 + RING_COPIES + DEVICES + 7),
        compiler_params=params(collective_id),
    )(*args)


def on_device(
    encoder_tokens,
    encoder_segments,
    decoder_tokens,
    decoder_segments,
    cotangent,
    attention_weight,
    feedforward_weight,
    norm_gain,
    norm_shift,
):
    width = encoder_tokens.shape[2]
    own_wt = jnp.swapaxes(attention_weight[0], 1, 2).reshape(6 * HEAD, width)
    (
        wt, gs, full_h0, h0, unit0, scale0, full_y, q, k, v, sq, sk, sv, att_d, log_d,
    ) = first_call(
        encoder_tokens, decoder_tokens, decoder_segments, own_wt, norm_gain[0], norm_shift[0], 1
    )
    (
        ffn, full_h1, full_m, full_d1, hidden, slope, kvc, cq, d1,
        unit1, scale1, unit2, scale2, dunit0, dscale0, att_e, log_e, seg_col,
    ) = forward_call(
        q, k, v, encoder_segments, att_d, h0, decoder_tokens, wt, gs, feedforward_weight[0], 2
    )
    (d3, dback1, full_d2, full_db2, full_db1, dhidden, dpre, att_c, cq_grad, kvc_grad, small_d) = (
        decoder_call(
            cq, kvc, d1, cotangent, decoder_segments, encoder_segments, wt, ffn, gs, 3
        )
    )
    full_b1, att_grad, back1, dec_grad, small_b, ffn_sum, wt_grad = backward_call(
        (
            kvc_grad, cq_grad, dback1, wt, gs, ffn, unit1, scale1, unit2, scale2,
            dunit0, dscale0, slope, sq, sk, sv, log_d, decoder_segments, full_h1, hidden,
            full_m, full_d1, full_y, full_d2, full_db1, full_db2, dpre, dhidden, att_c, att_d,
        ),
        4,
    )
    att_sum, small_sum, enc_out, d3_out, dec_out = last_call(
        (
            q, k, v, encoder_segments, seg_col, log_e, att_e, att_grad, full_b1, full_h0,
            wt, gs, back1, unit0, scale0, wt_grad, small_b, small_d, d3, dec_grad,
        ),
        5,
    )
    att_sum = att_sum.reshape(6, HEAD, width).astype(F32)
    return (
        d3_out.astype(BF16),
        enc_out,
        dec_out,
        jnp.swapaxes(att_sum, 1, 2)[None],
        ffn_sum.reshape(feedforward_weight.shape).astype(F32),
        small_sum[None, :3],
        small_sum[None, 3:6],
    )


def solution(mesh):
    in_specs = (
        P("dp", "tensor", None),
        P("dp", None),
        P("dp", "tensor", None),
        P("dp", None),
        P("dp", "tensor", None),
        P("section", None, None, "tensor"),
        P("section", None, None, "tensor"),
        P("section", None, None),
        P("section", None, None),
    )
    out_specs = (
        P("dp", "tensor", "section"),
        P("dp", "tensor", "section"),
        P("dp", "tensor", "section"),
        P("section", None, None, "tensor"),
        P("section", None, None, "tensor"),
        P("section", None, None),
        P("section", None, None),
    )
    return jax.shard_map(
        on_device, mesh=mesh, in_specs=in_specs, out_specs=out_specs, check_vma=False
    )
```

```python
import functools

import jax
import jax.numpy as jnp
from jax import lax
from jax.experimental import pallas as pl
from jax.experimental.pallas import tpu as pltpu
from jax.sharding import PartitionSpec as P

HEAD = 64
EPSILON = 1e-05
MASKED = -1000000000.0
SCALE = HEAD ** (-0.5)
F32 = jnp.float32
BF16 = jnp.bfloat16
MESH = pl.DeviceIdType.MESH
VM = pl.BlockSpec(memory_space=pltpu.VMEM)
SIDE = 4
DEVICES = SIDE * SIDE
UP = (0, 2)
DOWN = (1, 3)
RING_COPIES = 30
CHUNKS = ((0, 48), (48, 32))
PAUSES = (1, 1, 1, 1, 1)
LAG = 0
VMEM_BYTES = 60 << 20
RING = True
INV_SQRT2 = 0.7071067811865476
INV_SQRT_2PI = 0.3989422804014327
FAR_FIRST = (10, 2, 8, 6, 14, 11, 9, 7, 13, 5, 15, 1, 3, 4, 12)


def norm_parts(values):
    center = values - jnp.mean(values, -1, keepdims=True)
    scale = lax.rsqrt(jnp.mean(center * center, -1, keepdims=True) + EPSILON)
    return center * scale, scale


def norm_back(grad, unit, scale, gains):
    inner = grad * gains
    back = scale * (
        inner
        - jnp.mean(inner, -1, keepdims=True)
        - unit * jnp.mean(inner * unit, -1, keepdims=True)
    )
    return back, jnp.sum(grad * unit, 0, keepdims=True), jnp.sum(grad, 0, keepdims=True)


def gelu_parts(u):
    cdf = 0.5 * (1.0 + lax.erf(u * INV_SQRT2))
    return u * cdf, cdf + u * (INV_SQRT_2PI * jnp.exp(-0.5 * u * u))


def dot(a, b):
    return jnp.dot(a, b, preferred_element_type=F32)


def dot_t(a, b):
    return lax.dot_general(a, b, (((1,), (1,)), ((), ())), preferred_element_type=F32)


def t_dot(a, b):
    return lax.dot_general(a, b, (((0,), (0,)), ((), ())), preferred_element_type=F32)


def scores_of(queries, key_rows, allowed):
    return jnp.where(allowed, dot_t(queries, key_rows) * SCALE, MASKED)


def attend(queries, key_rows, value_rows, allowed):
    scores = scores_of(queries, key_rows, allowed)
    row_max = jnp.max(scores, -1, keepdims=True)
    exponent = jnp.exp(scores - row_max)
    row_sum = jnp.sum(exponent, -1, keepdims=True)
    probs_low = (exponent / row_sum).astype(BF16)
    return dot(probs_low, value_rows).astype(BF16), row_max + jnp.log(row_sum)


def attend_back(queries, key_rows, value_rows, log_total, allowed, attended_grad):
    probs = jnp.exp(scores_of(queries, key_rows, allowed) - log_total)
    value_grad = t_dot(attended_grad, probs.astype(BF16))
    probs_grad = dot_t(attended_grad, value_rows)
    scores_grad = (probs * (probs_grad - jnp.sum(probs * probs_grad, -1, keepdims=True))).astype(
        BF16
    )
    return dot(scores_grad, key_rows) * SCALE, t_dot(queries, scores_grad) * SCALE, value_grad


def at_grid():
    index = lax.axis_index("tensor")
    return lax.div(index, SIDE), lax.rem(index, SIDE)


def moved(place, dy, dx):
    return lax.rem(place[0] + dy % SIDE, SIDE), lax.rem(place[1] + dx % SIDE, SIDE)


def along(axis, steps):
    return (steps, 0) if axis == 0 else (0, steps)


def device_at(place):
    return {"tensor": place[0] * SIDE + place[1]}


def tensor_peers(place):
    return [device_at(moved(place, d // SIDE, d % SIDE)) for d in FAR_FIRST]


def pack_peers():
    mine = lax.axis_index("section") * 4 + lax.axis_index("dp")
    others = [lax.rem(mine + d, 8) for d in range(1, 8)]
    return [{"section": lax.div(n, 4), "dp": lax.rem(n, 4)} for n in others]


def greet(devices):
    barrier = pltpu.get_barrier_semaphore()
    for device in devices:
        pl.semaphore_signal(barrier, inc=1, device_id=device, device_id_type=MESH)
    pl.semaphore_wait(barrier, len(devices))


def sections():
    section, dp = lax.axis_index("section"), lax.axis_index("dp")
    zh, core = lax.div(dp, 2), lax.rem(dp, 2)
    return section, zh, core, {"section": 1 - section}, {"dp": zh * 2 + 1 - core}


class Links:
    def __init__(self, send_sems, recv_sems, used=0):
        self.send, self.recv, self.used, self.started = send_sems, recv_sems, used, []

    def start(self, source, target, device):
        n = self.used
        self.used += 1
        copy = pltpu.make_async_remote_copy(
            src_ref=source,
            dst_ref=target,
            send_sem=self.send.at[n],
            recv_sem=self.recv.at[n],
            device_id=device,
            device_id_type=MESH,
        )
        copy.start()
        self.started.append(copy)
        return copy

    def finish(self):
        for copy in self.started:
            copy.wait_send()
        self.started = []


def sems(n):
    return [pltpu.SemaphoreType.DMA((n,)), pltpu.SemaphoreType.DMA((n,))]


def shape(dims, kind):
    return jax.ShapeDtypeStruct(tuple(dims), kind)


def fold(rows):
    half = rows.shape[1] // 2
    return jnp.concatenate([rows[:, :half], rows[:, half:]], 0)


def unfold(rows):
    count = rows.shape[0] // 2
    return jnp.concatenate([rows[:count], rows[count:]], 1)


def unfold_all(blocks):
    count, half = blocks.shape[2] // 2, blocks.shape[3]
    split = blocks.astype(F32).reshape(DEVICES, 2, count, half)
    low = split[:, 0].reshape(DEVICES * count, half)
    high = split[:, 1].reshape(DEVICES * count, half)
    return jnp.concatenate([low, high], 1).astype(BF16)


def fold_all(part):
    count, half = part.shape[0] // DEVICES, part.shape[1] // 2
    split = part.reshape(DEVICES, count, 2 * half)
    both = jnp.concatenate([split[:, :, :half], split[:, :, half:]], 1)
    return both.astype(BF16).reshape(SIDE, SIDE, 2 * count, half)


def own_row(ref):
    return jnp.where(lax.axis_index("section") == 0, ref[0:1, :], ref[1:2, :]).astype(F32)


def column(row):
    return jnp.broadcast_to(row, (128, row.shape[1])).T


def gather(links, place, views, ready=None):
    jobs = []
    for buf, low, rows in views:
        half = buf.shape[-1] // 2
        for h in range(2):
            jobs.append((buf, 1 - h, h, h * half, half, pl.ds(low, rows)))
    ready = ready or (lambda group: None)

    def send(job, axis, steps, r, s):
        buf, a, b, start, size, rows = job
        y, x = moved(moved(place, *along(a, r)), *along(b, s))
        ref = buf.at[y, x, rows, pl.ds(start, size)]
        return links.start(ref, ref, device_at(moved(place, *along(axis, steps))))

    first, spread, ahead = [], [], []
    for job in jobs:
        first.append({-d % SIDE: send(job, job[1], d, 0, 0) for d in (2, 1, 3)})
    paths = ((1, 3), (3, 1)) if RING else ((2, 2), (1, 3), (3, 1))
    for job in jobs:
        spread.append({0: {s: send(job, job[2], d, 0, 0) for d, s in paths}})
    ready([(0, 0)])
    yield
    for r in (3, 1, 2):
        for i, job in enumerate(jobs):
            first[i][r].wait_recv()
            spread[i][r] = {s: send(job, job[2], d, r, 0) for d, s in paths}
    if RING:
        for i, job in enumerate(jobs):
            spread[i][0][3].wait_recv()
            ahead.append({0: send(job, job[2], 1, 0, 3)})
            spread[i][0][1].wait_recv()
    else:
        for i, job in enumerate(jobs):
            spread[i][0][3].wait_recv()
            spread[i][0][1].wait_recv()
            ahead.append({r: spread[i][r][2] for r in range(SIDE)})
    ready([(0, 1), (0, 3), (1, 0), (3, 0)])
    yield
    if RING:
        for r in DOWN:
            for i, job in enumerate(jobs):
                spread[i][r][1].wait_recv()
                ahead[i][r] = send(job, job[2], -1, r, 1)
        for i, job in enumerate(jobs):
            spread[i][2][3].wait_recv()
            ahead[i][2] = send(job, job[2], 1, 2, 3)
        for r in DOWN:
            for i, job in enumerate(jobs):
                spread[i][r][3].wait_recv()
    else:
        for r in DOWN:
            for i, job in enumerate(jobs):
                spread[i][r][1].wait_recv()
                spread[i][r][3].wait_recv()
    ready([(1, 1), (1, 3), (3, 1), (3, 3)])
    for i, job in enumerate(jobs):
        ahead[i][0].wait_recv()
    ready([(0, 2), (2, 0)])
    yield
    for i, job in enumerate(jobs):
        if not RING:
            spread[i][2][3].wait_recv()
        spread[i][2][1].wait_recv()
        ahead[i][1].wait_recv()
        ahead[i][3].wait_recv()
    ready([(1, 2), (3, 2), (2, 1), (2, 3)])
    for i, job in enumerate(jobs):
        ahead[i][2].wait_recv()
    ready([(2, 2)])


PRODUCE = (
    [(2, 2), (2, 3), (2, 1), (3, 2), (1, 2), (2, 0), (0, 2)],
    [(3, 3), (3, 1), (1, 3), (1, 1), (3, 0), (1, 0), (0, 3), (0, 1), (0, 0)],
)


def sum_blocks(links, place, views, produce=None):
    produce = produce or (lambda group: None)
    jobs = []
    for part, land, low, rows in views:
        half = part.shape[-1] // 2
        for h in range(2):
            jobs.append((part, land, 15 * h, 1 - h, h, h * half, half, pl.ds(low, rows)))

    def block(job, r, s):
        part, _, _, a, b, start, size, rows = job
        y, x = moved(moved(place, *along(a, r)), *along(b, s))
        return part.at[y, x, rows, pl.ds(start, size)]

    def landing(job, n):
        return job[1].at[job[2] + n, job[7]]

    def start(source, target, axis, steps):
        return links.start(source, target, device_at(moved(place, *along(axis, steps))))

    def add(target, *others):
        total = target[...].astype(F32)
        for other in others:
            total = total + other[...].astype(F32)
        return total

    def near_slot(job, r, steps):
        return landing(job, 4 + 2 * r + (0 if steps == 1 else 1))

    order = (2, 3, 1, 0)
    produce(PRODUCE[0])
    near = [{r: [] for r in order} for _ in jobs]
    if RING:
        far = []
        for job in jobs:
            far.append(
                {
                    r: start(block(job, r, 2), landing(job, r), job[4], 1 if r in UP else -1)
                    for r in order
                }
            )
        produce(PRODUCE[1])
        for i, job in enumerate(jobs):
            for r in order:
                steps = -1 if r in UP else 1
                near[i][r].append(
                    start(block(job, r, steps), near_slot(job, r, steps), job[4], steps)
                )
        yield
        for r in order:
            for i, job in enumerate(jobs):
                steps = 1 if r in UP else -1
                far[i][r].wait_recv()
                ref = block(job, r, steps)
                ref[...] = add(ref, landing(job, r)).astype(BF16)
                near[i][r].append(start(ref, near_slot(job, r, steps), job[4], steps))
    else:
        for s in (2, 1, 3):
            for r in order:
                for i, job in enumerate(jobs):
                    slot = landing(job, 4 * (s - 1) + r)
                    near[i][r].append(start(block(job, r, s), slot, job[4], s))
            if s == 2:
                produce(PRODUCE[1])
    yield
    last = [{} for _ in jobs]
    results = []
    for r in order:
        if r == 0:
            yield
        for i, job in enumerate(jobs):
            for copy in near[i][r]:
                copy.wait_recv()
            ref = block(job, r, 0)
            if RING:
                total = add(ref, landing(job, 4 + 2 * r), landing(job, 5 + 2 * r))
            else:
                total = add(ref, landing(job, r), landing(job, 4 + r), landing(job, 8 + r))
            if r == 0:
                results.append(total)
            else:
                ref[...] = total.astype(BF16)
                last[i][r] = start(ref, landing(job, 11 + r), job[3], r)
    for i, job in enumerate(jobs):
        for r in order[:3]:
            last[i][r].wait_recv()
            results[i] = results[i] + landing(job, 11 + r)[...].astype(F32)
    return [jnp.concatenate(results[i : i + 2], 1) for i in range(0, len(results), 2)]


def run(chains, lag=0):
    turn, active = 0, list(enumerate(chains))
    while active:
        for n, chain in list(active):
            if turn >= n * lag:
                try:
                    next(chain)
                except StopIteration:
                    active.remove((n, chain))
        turn += 1


def pack_places():
    section, zh, core, partner, sibling = sections()
    zh_plus = lax.rem(zh + section, 2)
    plus = {"section": 1 - section, "dp": zh_plus * 2 + core}
    minus = {"section": 1 - section, "dp": (1 - zh_plus) * 2 + core}
    return section, zh, core, sibling, zh_plus, plus, minus


PACK_COPIES = 8


def pack_scratch(rows, cols):
    half, quarter = rows // 2, rows // 4
    return [
        pltpu.VMEM((2, half, cols), BF16),
        pltpu.VMEM((2, half, cols), BF16),
        pltpu.VMEM((2, quarter, cols), BF16),
        pltpu.VMEM((2, quarter, cols), BF16),
        pltpu.VMEM((half, cols), BF16),
    ]


def pause(n):
    for _ in range(n):
        yield


def pack_sum(links, grad, out, scratch):
    work, core_land, side, passing, over = scratch
    section, zh, core, sibling, zh_plus, plus, minus = pack_places()
    other = 1 - section
    half = grad.shape[1] // 2
    quarter = half // 2
    first = links.start(grad.at[:, pl.ds((1 - core) * half, half)], core_land, sibling)
    yield from pause(PAUSES[0])
    first.wait_recv()
    work[...] = (
        grad[:, pl.ds(core * half, half)].astype(F32) + core_land[...].astype(F32)
    ).astype(BF16)
    second = [
        links.start(work.at[other, pl.ds(h * quarter, quarter)], side.at[n], d)
        for n, (h, d) in enumerate(((zh_plus, plus), (1 - zh_plus, minus)))
    ]
    yield from pause(PAUSES[1])
    for copy in second:
        copy.wait_recv()
    mine = work.at[section, pl.ds(zh * quarter, quarter)]
    mine[...] = (mine[...].astype(F32) + side[0].astype(F32) + side[1].astype(F32)).astype(BF16)
    third = [
        links.start(work.at[section, pl.ds(n * quarter, quarter)], passing.at[n], d)
        for n, d in enumerate((plus, minus))
    ]
    yield from pause(PAUSES[2])
    fourth = []
    for n, device in enumerate((plus, minus)):
        third[n].wait_recv()
        fourth.append(links.start(passing.at[n], over.at[pl.ds(n * quarter, quarter)], device))
    yield from pause(PAUSES[3])
    for copy in fourth:
        copy.wait_recv()
    out[core] = (work[section].astype(F32) + over[...].astype(F32)).astype(BF16)
    last = links.start(out.at[core], out.at[core], sibling)
    yield from pause(PAUSES[4])
    last.wait_recv()
    links.finish()


def gather_small(links, place, buf, rows):
    y, x = place
    buf[y, x] = fold(rows).astype(BF16)
    copies = []
    for d in FAR_FIRST:
        target = device_at(moved(place, d // SIDE, d % SIDE))
        copies.append(links.start(buf.at[y, x], buf.at[y, x], target))
    for copy in copies:
        copy.wait_recv()
    return unfold_all(buf[...])


def sum_small(links, place, work, land, part):
    work[...] = fold_all(part)
    copies = []
    for n, d in enumerate(FAR_FIRST):
        there = moved(place, d // SIDE, d % SIDE)
        copies.append(links.start(work.at[there[0], there[1]], land.at[n], device_at(there)))
    total = work[place[0], place[1]].astype(F32)
    for copy in copies:
        copy.wait_recv()
    return unfold(total + jnp.sum(land[...].astype(F32), 0))


def stacked(ref, place, group, low=0, rows=None):
    rows = ref.shape[2] if rows is None else rows
    blocks = []
    for dy, dx in group:
        y, x = moved(place, dy, dx)
        blocks.append(ref[y, x, low : low + rows])
    return blocks[0] if len(blocks) == 1 else jnp.concatenate(blocks, 0)


def store_blocks(ref, place, group, values, low=0):
    rows = values.shape[0] // len(group)
    for n, (dy, dx) in enumerate(group):
        y, x = moved(place, dy, dx)
        ref[y, x, low : low + rows] = values[n * rows : (n + 1) * rows]


def whole(ref):
    return ref[...].reshape(DEVICES * ref.shape[2], ref.shape[3])


def wide(scale):
    return jnp.broadcast_to(scale, (scale.shape[0], 128))


def first_part(
    tokens, dec_tokens, seg_d, wt_in, gain_in, shift_in, wt, gs, full_h0, h0, unit0, scale0, *rest
):
    (full_y, q, k, v, sq, sk, sv, att_d, log_d, xbuf, ybuf, gs_in, send, recv) = rest
    place = at_grid()
    section, _, core, partner, sibling = sections()
    links = Links(send, recv)
    half = wt_in.shape[0] // 2
    mine = pl.ds(core * half, half)
    x, y = tokens.at[section], dec_tokens.at[section]
    for i in range(3):
        gs_in[i : i + 1, :] = gain_in[i]
        gs_in[3 + i : 4 + i, :] = shift_in[i]
    gs_in[6:8, :] = jnp.zeros((2, x.shape[1]), F32)
    gains_copy = links.start(gs_in, gs.at[section], partner)
    xbuf[place[0], place[1]] = x[...]
    ybuf[place[0], place[1]] = fold(y[...].astype(F32)).astype(BF16)
    passed = []

    def ready(group):
        if group == [(0, 0)]:
            passed.append(links.start(wt_in.at[mine], wt.at[section, mine], partner))
            gs[section] = gs_in[...]
            wt[section] = wt_in[...]
            gains_copy.wait_recv()
        if group == [(1, 1), (1, 3), (3, 1), (3, 3)]:
            passed[0].wait_recv()
            theirs = wt.at[1 - section, mine]
            passed.append(links.start(theirs, theirs, sibling))
        unit, scale = norm_parts(stacked(xbuf, place, group).astype(F32))
        rows = unit * gs[0, 0:1, :] + gs[0, 3:4, :]
        if group == [(0, 0)]:
            h0[...] = rows
            unit0[...] = unit
            scale0[...] = wide(scale)
        store_blocks(full_h0, place, group, rows.astype(BF16))

    views = [(xbuf, 0, x.shape[0]), (ybuf, 0, ybuf.shape[2])]
    run([gather(links, place, views, ready)])
    passed[1].wait_recv()
    count, width = x.shape
    for i in range(SIDE):
        rows = full_h0[i].reshape(SIDE * count, width)
        made = dot_t(rows, wt[0, 0 : 3 * HEAD, :]).astype(BF16)
        for j, ref in enumerate((q, k, v)):
            ref[i] = made[:, j * HEAD : (j + 1) * HEAD].reshape(SIDE, count, HEAD)
    rows = unfold_all(ybuf[...])
    full_y[...] = rows
    made = dot_t(rows, wt[1, 0 : 3 * HEAD, :]).astype(BF16)
    for j, ref in enumerate((sq, sk, sv)):
        ref[...] = made[:, j * HEAD : (j + 1) * HEAD]
    row = own_row(seg_d)
    att, log_total = attend(sq[...], sk[...], sv[...], before(row))
    att_d[...] = att
    log_d[...] = wide(log_total)
    links.finish()


def before(row):
    count = row.shape[1]
    place = [lax.broadcasted_iota(jnp.int32, (count, count), i) for i in range(2)]
    return (column(row)[:, 0:1] == row) & (place[1] <= place[0])


def forward_part(q, k, v, seg_e, att_d, h0, dec_tokens, wt, gs, ffn_in, *rest):
    (ffn, full_h1, full_m, full_d1, hidden, slope, kvc, cq, d1) = rest[:9]
    (unit1, scale1, unit2, scale2, dunit0, dscale0, att_e, log_e, seg_col) = rest[9:18]
    (part, dpart, land_1, land_2, land_d, d1buf, send, recv) = rest[18:]
    place = at_grid()
    section, _, core, partner, sibling = sections()
    y = dec_tokens.at[section]
    row = own_row(seg_e)
    seg_col[...] = column(row).reshape(seg_col.shape)
    shared = Links(send, recv)
    passed = [shared.start(ffn_in.at[core], ffn.at[section, core], partner)]

    def chain(links, low, rows, with_dec):
        here = pl.ds(low, rows)

        def attended(group):
            allowed = stacked(seg_col, place, group, low, rows)[:, 0:1] == row
            queries = stacked(q, place, group, low, rows)
            att, log_total = attend(queries, whole(k), whole(v), allowed)
            store_blocks(att_e, place, group, att, low)
            store_blocks(log_e, place, group, wide(log_total), low)
            made = dot(att, wt[0, 3 * HEAD : 4 * HEAD, :])
            store_blocks(part, place, group, made.astype(BF16), low)
            if with_dec and group == PRODUCE[0]:
                dpart[...] = fold_all(dot(att_d[...], wt[1, 3 * HEAD : 4 * HEAD, :]))
            if low == 0 and group == PRODUCE[1]:
                ffn[section] = ffn_in[...]

        views = [(part, land_1, low, rows)]
        if with_dec:
            views.append((dpart, land_d, 0, dpart.shape[2]))
        sums = yield from sum_blocks(links, place, views, attended)
        unit, scale = norm_parts(h0[here] + sums[0])
        unit1[here] = unit
        scale1[here] = wide(scale)
        h1 = unit * gs[0, 1:2, :] + gs[0, 4:5, :]
        full_h1[place[0], place[1], here] = h1.astype(BF16)
        views = [(full_h1, low, rows)]
        if with_dec:
            unit, scale = norm_parts(y[...].astype(F32) + unfold(sums[1]))
            dunit0[...] = unit
            dscale0[...] = wide(scale)
            made = unit * gs[1, 0:1, :] + gs[1, 3:4, :]
            d1[...] = made
            d1buf[place[0], place[1]] = fold(made).astype(BF16)
            views.append((d1buf, 0, d1buf.shape[2]))
        if low == 0:
            passed[0].wait_recv()
            theirs = ffn.at[1 - section, core]
            passed.append(shared.start(theirs, theirs, sibling))

        def up(group):
            if group == [(0, 0)]:
                return
            if group == [(0, 1), (0, 3), (1, 0), (3, 0)]:
                if low == 0:
                    passed[1].wait_recv()
                group = [(0, 0)] + group
            made, back = gelu_parts(dot(stacked(full_h1, place, group, low, rows), ffn[0, 0]))
            store_blocks(hidden, place, group, made.astype(BF16), low)
            store_blocks(slope, place, group, back, low)

        yield from gather(links, place, views, up)
        links.finish()
        if with_dec:
            made = unfold_all(d1buf[...])
            full_d1[...] = made
            cq[...] = dot_t(made, wt[1, 4 * HEAD : 5 * HEAD, :]).astype(BF16)

        def down(group):
            made = dot_t(stacked(hidden, place, group, low, rows), ffn[0, 1])
            store_blocks(part, place, group, made.astype(BF16), low)

        sums = yield from sum_blocks(links, place, [(part, land_2, low, rows)], down)
        unit, scale = norm_parts(h1 + sums[0])
        unit2[here] = unit
        scale2[here] = wide(scale)
        full_m[place[0], place[1], here] = (unit * gs[0, 2:3, :] + gs[0, 5:6, :]).astype(BF16)

        def cross(group):
            made = dot_t(stacked(full_m, place, group, low, rows), wt[0, 4 * HEAD : 6 * HEAD, :])
            store_blocks(kvc, place, group, made.astype(BF16), low)

        yield from gather(links, place, [(full_m, low, rows)], cross)
        links.finish()

    chains = []
    for n, (low, rows) in enumerate(CHUNKS):
        links = Links(send, recv, 2 + 6 * RING_COPIES * n)
        chains.append(chain(links, low, rows, n == len(CHUNKS) - 1))
    run(chains, LAG)
    shared.finish()


def decoder_part(cq, kvc, d1, cot, seg_d, seg_e, wt, ffn, gs, *rest):
    (d3, dback1, full_d2, full_db2, full_db1, hid_out, pre_out, att_out) = rest[:8]
    (cq_grad, kvc_grad, grads, g_bufs, s_work, s_land, probs, send, recv) = rest[8:]
    place = at_grid()
    links = Links(send, recv)
    w5 = wt[1, 5 * HEAD : 6 * HEAD, :]
    both = whole(kvc)
    kc, vc = both[:, :HEAD], both[:, HEAD:]
    allowed = column(own_row(seg_d))[:, 0:1] == own_row(seg_e)
    scores = scores_of(cq[...], kc, allowed)
    exponent = jnp.exp(scores - jnp.max(scores, -1, keepdims=True))
    probs[...] = exponent / jnp.sum(exponent, -1, keepdims=True)
    att = dot(probs[...].astype(BF16), vc).astype(BF16)
    att_out[...] = att
    part = sum_small(links, place, s_work.at[0], s_land.at[0], dot(att, w5))
    unit1, scale1 = norm_parts(d1[...] + part)
    d2 = unit1 * gs[1, 1:2, :] + gs[1, 4:5, :]
    full = gather_small(links, place, g_bufs.at[0], d2)
    full_d2[...] = full
    hidden, slope = gelu_parts(dot(full, ffn[1, 0]))
    hidden = hidden.astype(BF16)
    hid_out[...] = hidden
    part = sum_small(links, place, s_work.at[1], s_land.at[1], dot_t(hidden, ffn[1, 1]))
    unit2, scale2 = norm_parts(d2 + part)
    d3[...] = unit2 * gs[1, 2:3, :] + gs[1, 5:6, :]
    back2, gain2, shift2 = norm_back(cot[lax.axis_index("section")].astype(F32), unit2, scale2, gs[1, 2:3, :])
    full = gather_small(links, place, g_bufs.at[1], back2)
    full_db2[...] = full
    pre = (dot(full, ffn[1, 1]) * slope).astype(BF16)
    pre_out[...] = pre
    part = sum_small(links, place, s_work.at[2], s_land.at[2], dot_t(pre, ffn[1, 0]))
    back1, gain1, shift1 = norm_back(back2 + part, unit1, scale1, gs[1, 1:2, :])
    dback1[...] = back1
    full = gather_small(links, place, g_bufs.at[2], back1)
    full_db1[...] = full
    att_grad = dot_t(full, w5).astype(BF16)
    p = probs[...]
    value_grad = t_dot(att_grad, p.astype(BF16))
    p_grad = dot_t(att_grad, vc)
    s_grad = (p * (p_grad - jnp.sum(p * p_grad, -1, keepdims=True))).astype(BF16)
    cq_grad[...] = (dot(s_grad, kc) * SCALE).astype(BF16)
    key_grad = t_dot(cq[...], s_grad) * SCALE
    both = jnp.concatenate([key_grad, value_grad], 0).T.astype(BF16)
    kvc_grad[...] = both.reshape(kvc_grad.shape)
    grads[0:1, :] = gain1
    grads[1:2, :] = gain2
    grads[2:3, :] = shift1
    grads[3:4, :] = shift2
    grads[4:8, :] = jnp.zeros((4, grads.shape[1]), F32)
    links.finish()


def backward_part(*refs):
    (kvc_grad, cq_grad, dback1, wt, gs, ffn, unit1, scale1, unit2, scale2) = refs[:10]
    (dunit0, dscale0, slope, sq, sk, sv, log_d, seg_d, full_h1, hidden) = refs[10:20]
    (full_m, full_d1, full_y, full_d2, full_db1, full_db2, dpre, dhidden) = refs[20:28]
    (att_c, att_d) = refs[28:30]
    (full_b1, att_grad, back1, dec_grad, grads, ffn_sum, wt_grad) = refs[30:37]
    (full_b2, pre, part, dpart_1, dpart_2, land_1, land_2, dland_1, dland_2, dbuf) = refs[37:47]
    (ffn_grad, *pack_refs, send, recv) = refs[47:]
    place = at_grid()

    def chain(links, low, rows, with_dec):
        here = pl.ds(low, rows)

        def cross(group):
            made = dot(stacked(kvc_grad, place, group, low, rows), wt[0, 4 * HEAD : 6 * HEAD, :])
            store_blocks(part, place, group, made.astype(BF16), low)
            if with_dec and group == PRODUCE[0]:
                dpart_1[...] = fold_all(dot(cq_grad[...], wt[1, 4 * HEAD : 5 * HEAD, :]))

        views = [(part, land_1, low, rows)]
        if with_dec:
            views.append((dpart_1, dland_1, 0, dpart_1.shape[2]))
        sums = yield from sum_blocks(links, place, views, cross)
        back2, gain2, shift2 = norm_back(sums[0], unit2[here], scale2[here, 0:1], gs[0, 2:3, :])
        full_b2[place[0], place[1], here] = back2.astype(BF16)
        views = [(full_b2, low, rows)]
        if with_dec:
            dback0, dgain0, dshift0 = norm_back(
                dback1[...] + unfold(sums[1]), dunit0[...], dscale0[:, 0:1], gs[1, 0:1, :]
            )
            dbuf[place[0], place[1]] = fold(dback0).astype(BF16)
            views.append((dbuf, 0, dbuf.shape[2]))

        def down(group):
            made = dot(stacked(full_b2, place, group, low, rows), ffn[0, 1])
            made = made * stacked(slope, place, group, low, rows)
            store_blocks(pre, place, group, made.astype(BF16), low)

        yield from gather(links, place, views, down)
        links.finish()
        ready_rows.append(rows)
        views = [(part, land_2, low, rows)]
        if with_dec:
            full_db0 = unfold_all(dbuf[...])
            att_d_grad = dot_t(full_db0, wt[1, 3 * HEAD : 4 * HEAD, :]).astype(BF16)
            made = attend_back(
                sq[...], sk[...], sv[...], log_d[:, 0:1], before(own_row(seg_d)), att_d_grad
            )
            made = jnp.concatenate([made[0], made[1].T, made[2].T], 1).astype(BF16)
            late.extend([made, full_db0])
            dpart_2[...] = fold_all(dot(made, wt[1, 0 : 3 * HEAD, :]))
            views.append((dpart_2, dland_2, 0, dpart_2.shape[2]))

        def up(group):
            made = dot_t(stacked(pre, place, group, low, rows), ffn[0, 0])
            store_blocks(part, place, group, made.astype(BF16), low)

        sums = yield from sum_blocks(links, place, views, up)
        made, gain1, shift1 = norm_back(
            back2 + sums[0], unit1[here], scale1[here, 0:1], gs[0, 1:2, :]
        )
        back1[here] = made
        full_b1[place[0], place[1], here] = made.astype(BF16)
        totals.append((gain1, gain2, shift1, shift2))
        if with_dec:
            dec_grad[...] = dback0 + unfold(sums[1])
            grads[4:5, :] = dgain0
            grads[5:6, :] = dshift0

        def mixed(group):
            made = dot_t(stacked(full_b1, place, group, low, rows), wt[0, 3 * HEAD : 4 * HEAD, :])
            store_blocks(att_grad, place, group, made.astype(BF16), low)

        yield from gather(links, place, [(full_b1, low, rows)], mixed)
        links.finish()

    def weight_chain(links):
        def put(layer, first, rows):
            wt_grad[layer, first * HEAD : first * HEAD + rows.shape[0], :] = rows.astype(BF16)

        count = full_h1.shape[3]
        yield
        put(0, 4, t_dot(whole(kvc_grad), whole(full_m)))
        ffn_grad[1, :count] = t_dot(dpre[...], full_d2[...]).T.astype(BF16)
        yield
        ffn_grad[1, count:] = t_dot(dhidden[...], full_db2[...]).T.astype(BF16)
        put(1, 4, t_dot(cq_grad[...], full_d1[...]))
        put(1, 5, t_dot(att_c[...], full_db1[...]))
        while len(ready_rows) < len(CHUNKS):
            yield
        ffn_grad[0, :count] = t_dot(whole(pre), whole(full_h1)).T.astype(BF16)
        yield
        ffn_grad[0, count:] = t_dot(whole(hidden), whole(full_b2)).T.astype(BF16)
        yield from pack_sum(links, ffn_grad, ffn_sum, pack_refs)
        put(1, 0, t_dot(late[0], full_y[...]))
        put(1, 3, t_dot(att_d[...], late[1]))
        unused = slice(0, 4 * HEAD)
        wt_grad[0, unused, :] = jnp.zeros((4 * HEAD, count), BF16)

    late = []
    totals, chains, ready_rows = [], [], []
    for n, (low, rows) in enumerate(CHUNKS):
        links = Links(send, recv, PACK_COPIES + 7 * RING_COPIES * n)
        chains.append(chain(links, low, rows, n == len(CHUNKS) - 1))
    chains.append(weight_chain(Links(send, recv)))
    run(chains, LAG)
    for i in range(4):
        grads[i : i + 1, :] = sum(total[i] for total in totals)
    grads[6:8, :] = jnp.zeros((2, grads.shape[1]), F32)


def last_part(q, k, v, seg_e, seg_col, log_e, att_e, att_grad, full_b1, full_h0, *refs):
    (wt, gs, back1, unit0, scale0, wt_grad, small_b, small_d, out3, dec, *rest) = refs
    (att_out, small_out, enc_out, out3_out, dec_out, part, land, *pack_refs) = rest[:12]
    (fin, core_s, y_s, x_s, z_s, late, late_t, late_p) = rest[12:20]
    (enc, give_e, give_d, land_e, land_d, qkv_grad, att, small, send, recv) = rest[20:]
    place = at_grid()
    section, zh, core, sibling, _, plus, minus = pack_places()
    other = 1 - section
    partner = {"section": other}
    far = {"dp": (1 - zh) * 2 + core}
    columns = [device_at(moved(place, d, 0)) for d in (1, 2, 3)]
    rows = [device_at(moved(place, 0, d)) for d in (1, 2, 3)]
    tensor, packs = tensor_peers(place), pack_peers()
    width = enc.shape[1] // 2
    there = pl.ds(pl.multiple_of(other * width, width), width)
    here = pl.ds(pl.multiple_of(section * width, width), width)

    att[...] = wt_grad[...]
    small[...] = jnp.zeros(small.shape, F32)
    for layer, to, source, frm in (
        (0, 1, small_b, 0), (0, 2, small_b, 1), (0, 4, small_b, 2), (0, 5, small_b, 3),
        (1, 0, small_b, 4), (1, 3, small_b, 5),
        (1, 1, small_d, 0), (1, 2, small_d, 1), (1, 4, small_d, 2), (1, 5, small_d, 3),
    ):
        small[layer, to : to + 1, :] = source[frm : frm + 1, :]

    def early(links):
        give_d[...] = jnp.concatenate([out3[:, there], dec[:, there]], 0).astype(BF16)
        swap = links.start(give_d, land_d, partner)
        one = links.start(small.at[1 - core], core_s, sibling)
        yield
        one.wait_recv()
        fin[core] = small[core] + core_s[...]
        for land_s, devices in ((y_s, columns), (x_s, rows), (z_s, [plus, minus, far])):
            copies = [links.start(fin.at[core], land_s.at[n], d) for n, d in enumerate(devices)]
            yield
            for copy in copies:
                copy.wait_recv()
            links.finish()
            fin[core] = fin[core] + land_s[0] + land_s[1] + land_s[2]
        five = links.start(fin.at[core], fin.at[core], sibling)
        yield
        five.wait_recv()
        swap.wait_recv()
        links.finish()

    def heads(group):
        made = dot(stacked(qkv_grad, place, group), wt[0, 0 : 3 * HEAD, :])
        store_blocks(part, place, group, made.astype(BF16))
        if group == PRODUCE[1]:
            made = t_dot(whole(qkv_grad), whole(full_h0))
            att[0, 0 : 3 * HEAD, :] = made.astype(BF16)
            att[0, 3 * HEAD : 4 * HEAD, :] = t_dot(whole(att_e), whole(full_b1)).astype(BF16)

    def attention_back():
        row, count = own_row(seg_e), q.shape[2]
        key_rows, value_rows = whole(k), whole(v)
        totals = [0.0, 0.0]
        for i in range(SIDE):
            some = lambda ref: ref[i].reshape(SIDE * count, ref.shape[3])
            made = attend_back(
                some(q), key_rows, value_rows, some(log_e)[:, 0:1],
                some(seg_col)[:, 0:1] == row, some(att_grad),
            )
            qkv_grad[i, :, :, 0:HEAD] = made[0].astype(BF16).reshape(SIDE, count, HEAD)
            totals = [total + part for total, part in zip(totals, made[1:])]
        both = jnp.concatenate(totals, 0).T.astype(BF16)
        qkv_grad[:, :, :, HEAD : 3 * HEAD] = both.reshape(SIDE, SIDE, count, 2 * HEAD)

    def rest_of(links):
        attention_back()
        (sum_e,) = yield from sum_blocks(links, place, [(part, land, 0, enc.shape[0])], heads)
        made, gain0, shift0 = norm_back(
            back1[...] + sum_e, unit0[...], scale0[:, 0:1], gs[0, 0:1, :]
        )
        enc[...] = made
        quarter = width // 2
        both = [row[:, i * quarter : (i + 1) * quarter] for row in (gain0, shift0) for i in range(4)]
        late[...] = jnp.concatenate(both, 0)
        copies = [links.start(late, late_t.at[n], d) for n, d in enumerate(tensor)]
        give_e[...] = enc[:, there].astype(BF16)
        swap = links.start(give_e, land_e, partner)
        yield
        for copy in copies:
            copy.wait_recv()
        links.finish()
        late[...] = late[...] + jnp.sum(late_t[...], 0)
        copies = [links.start(late, late_p.at[n], d) for n, d in enumerate(packs)]
        enc_out[section] = enc[:, here]
        yield
        for copy in copies:
            copy.wait_recv()
        swap.wait_recv()
        links.finish()

    chains = [
        early(Links(send, recv, PACK_COPIES)),
        rest_of(Links(send, recv, 2 * PACK_COPIES + 16)),
        pack_sum(Links(send, recv), att, att_out, pack_refs),
    ]
    run(chains)
    enc_out[other] = land_e[...].astype(F32)
    got = land_d[...].astype(F32)
    count = out3.shape[0]
    out3_out[section] = out3[:, here]
    out3_out[other] = got[:count]
    dec_out[section] = dec[:, here]
    dec_out[other] = got[count:]
    small_out[...] = fin[section]
    total = late[...] + jnp.sum(late_p[...], 0)
    quarter = width // 2
    for i in range(8):
        row = 0 if i < 4 else 3
        cols = slice((i % 4) * quarter, (i % 4 + 1) * quarter)
        added = jnp.where(section == 0, total[i : i + 1], 0.0)
        small_out[row : row + 1, cols] = small_out[row : row + 1, cols] + added


def layers_kernel(names, *refs):
    r = dict(zip(names, refs))
    place = at_grid()
    greet(tensor_peers(place) + pack_peers())

    def some(*chosen):
        return [r[name] for name in chosen]

    first_part(
        *some("tokens", "dec_tokens", "seg_d", "wt_in", "gain_in", "shift_in", "wt", "gs", "full_h0", "h0", "unit0", "scale0"),
        *some("full_y", "q", "k", "v", "sq", "sk", "sv", "att_d", "log_d", "part", "dbuf_0", "gs_in", "send_1", "recv_1"),
    )
    forward_part(
        *some("q", "k", "v", "seg_e", "att_d", "h0", "dec_tokens", "wt", "gs", "ffn_in"),
        *some("ffn", "full_h1", "full_m", "full_d1", "hidden", "slope", "kvc", "cq", "d1"),
        *some("unit1", "scale1", "unit2", "scale2", "dunit0", "dscale0", "att_e", "log_e", "seg_col"),
        *some("part", "dpart_0", "land_1", "land_2", "dland_0", "dbuf_1", "send_2", "recv_2"),
    )
    decoder_part(
        *some("cq", "kvc", "d1", "cot", "seg_d", "seg_e", "wt", "ffn", "gs"),
        *some("d3", "dback1", "full_d2", "full_db2", "full_db1", "dhidden", "dpre", "att_c"),
        *some("cq_grad", "kvc_grad", "small_d", "g_bufs", "s_work", "s_land", "probs", "send_3", "recv_3"),
    )
    backward_part(
        *some("kvc_grad", "cq_grad", "dback1", "wt", "gs", "ffn", "unit1", "scale1", "unit2", "scale2"),
        *some("dunit0", "dscale0", "slope", "sq", "sk", "sv", "log_d", "seg_d", "full_h1", "hidden"),
        *some("full_m", "full_d1", "full_y", "full_d2", "full_db1", "full_db2", "dpre", "dhidden", "att_c", "att_d"),
        *some("full_b1", "att_grad", "back1", "dec_grad", "small_b", "ffn_sum", "wt_grad"),
        *some("full_b2", "pre", "part", "dpart_1", "dpart_2", "land_1", "land_2", "dland_1", "dland_2", "dbuf_2"),
        *some("ffn_grad", "fpack_0", "fpack_1", "fpack_2", "fpack_3", "fpack_4", "send_4", "recv_4"),
    )
    last_part(
        *some("q", "k", "v", "seg_e", "seg_col", "log_e", "att_e", "att_grad", "full_b1", "full_h0"),
        *some("wt", "gs", "back1", "unit0", "scale0", "wt_grad", "small_b", "small_d", "d3", "dec_grad"),
        *some("att_out", "small_out", "enc_out", "out3_out", "dec_out"),
        *some("part", "land_1", "apack_0", "apack_1", "apack_2", "apack_3", "apack_4"),
        *some("fin", "core_s", "y_s", "x_s", "z_s", "late", "late_t", "late_p"),
        *some("enc", "give_e", "give_d", "land_e", "land_d", "qkv_grad", "att", "small", "send_5", "recv_5"),
    )


def layers_call(args, collective_id):
    tokens, dec_tokens, ffn = args["tokens"], args["dec_tokens"], args["ffn_in"]
    (_, rows, width), count, inner = tokens.shape, dec_tokens.shape[1], ffn.shape[2]
    half, full, grid = width // 2, count * DEVICES, (SIDE, SIDE)
    low, wide_rows, head = (*grid, rows, width), (*grid, rows, 128), (*grid, rows, HEAD)
    small_block = (*grid, 2 * count, half)
    outs = {
        "att_out": ((2, 3 * HEAD, width), BF16),
        "small_out": ((8, width), F32),
        "enc_out": ((2, rows, half), F32),
        "out3_out": ((2, count, half), F32),
        "dec_out": ((2, count, half), F32),
        "ffn_sum": ((2, width, inner), BF16),
    }
    kept = {
        "wt": ((2, 6 * HEAD, width), BF16),
        "gs": ((2, 8, width), F32),
        "ffn": ((2, 2, width, inner), BF16),
    }
    for name in ("full_h0", "full_h1", "full_m", "full_b1", "full_b2", "part",):
        kept[name] = (low, BF16)
    for name in ("h0", "unit0", "unit1", "unit2", "back1", "enc",):
        kept[name] = ((rows, width), F32)
    for name in ("scale0", "scale1", "scale2",):
        kept[name] = ((rows, 128), F32)
    for name in ("full_y", "full_d1", "full_d2", "full_db1", "full_db2",):
        kept[name] = ((full, width), BF16)
    for name in ("q", "k", "v", "att_e", "att_grad",):
        kept[name] = (head, BF16)
    for name in ("sq", "sk", "sv", "att_d", "cq", "att_c", "cq_grad",):
        kept[name] = ((full, HEAD), BF16)
    for name in ("d1", "dunit0", "d3", "dback1", "dec_grad", "small_b", "small_d", "gs_in",):
        kept[name] = ((8, width), F32)
    for name in ("dbuf_0", "dbuf_1", "dbuf_2", "dpart_0", "dpart_1", "dpart_2",):
        kept[name] = (small_block, BF16)
    for name in ("land_1", "land_2",):
        kept[name] = ((30, rows, half), BF16)
    for name in ("dland_0", "dland_1", "dland_2",):
        kept[name] = ((30, 2 * count, half // 2), BF16)
    for name in ("hidden", "pre",):
        kept[name] = ((*grid, rows, inner), BF16)
    for name in ("kvc", "kvc_grad",):
        kept[name] = ((*grid, rows, 2 * HEAD), BF16)
    for name in ("dhidden", "dpre",):
        kept[name] = ((full, inner), BF16)
    for name in ("wt_grad", "att",):
        kept[name] = ((2, 6 * HEAD, width), BF16)
    for name in ("y_s", "x_s", "z_s",):
        kept[name] = ((3, 8, width), F32)
    for name in ("fin", "small",):
        kept[name] = ((2, 8, width), F32)
    for name in ("give_e", "land_e",):
        kept[name] = ((rows, half), BF16)
    for name in ("give_d", "land_d",):
        kept[name] = ((2 * count, half), BF16)
    kept |= {
        "slope": ((*grid, rows, inner), F32),
        "log_e": (wide_rows, F32),
        "seg_col": (wide_rows, F32),
        "log_d": ((full, 128), F32),
        "dscale0": ((count, 128), F32),
        "g_bufs": ((3, *small_block), BF16),
        "s_work": ((3, *small_block), BF16),
        "s_land": ((3, DEVICES - 1, 2 * count, half), BF16),
        "probs": ((full, DEVICES * rows), F32),
        "ffn_grad": ((2, 2 * width, inner), BF16),
        "core_s": ((8, width), F32),
        "late": ((8, width // 4), F32),
        "late_t": ((DEVICES - 1, 8, width // 4), F32),
        "late_p": ((7, 8, width // 4), F32),
        "qkv_grad": ((*grid, rows, 3 * HEAD), BF16),
    }
    scratch = {name: pltpu.VMEM(dims, kind) for name, (dims, kind) in kept.items()}
    for i, buf in enumerate(pack_scratch(2 * width, inner)):
        scratch[f"fpack_{i}"] = buf
    for i, buf in enumerate(pack_scratch(6 * HEAD, width)):
        scratch[f"apack_{i}"] = buf
    ring = RING_COPIES
    for i, copies in enumerate(
        (
            2 * ring + 3,
            2 + 6 * ring * len(CHUNKS),
            6 * (DEVICES - 1),
            PACK_COPIES + 7 * ring * len(CHUNKS),
            2 * PACK_COPIES + 16 + ring + DEVICES + 7,
        )
    ):
        scratch[f"send_{i + 1}"], scratch[f"recv_{i + 1}"] = sems(copies)
    return pl.pallas_call(
        functools.partial(layers_kernel, [*args, *outs, *scratch]),
        out_shape=[shape(*spec) for spec in outs.values()],
        in_specs=[VM] * len(args),
        out_specs=[VM] * len(outs),
        scratch_shapes=list(scratch.values()),
        compiler_params=pltpu.CompilerParams(
            collective_id=collective_id, has_side_effects=True, vmem_limit_bytes=VMEM_BYTES
        ),
    )(*args.values())


def results_kernel(att, ffn, small, enc, out3, dec, *outs):
    (att_out, ffn_out, gain_out, shift_out, enc_out, out3_out, dec_out) = outs
    att_out[...] = att[...].astype(F32)
    ffn_out[...] = ffn[...].astype(F32)
    for i in range(3):
        gain_out[i] = small[i : i + 1, :]
        shift_out[i] = small[3 + i : 4 + i, :]
    enc_out[...] = enc[...]
    out3_out[...] = out3[...].astype(BF16)
    dec_out[...] = dec[...]


def results_call(att, ffn, small, enc, out3, dec):
    width = small.shape[1]
    return pl.pallas_call(
        results_kernel,
        out_shape=[
            shape(att.shape, F32),
            shape(ffn.shape, F32),
            shape((3, 1, width), F32),
            shape((3, 1, width), F32),
            shape(enc.shape, F32),
            shape(out3.shape, BF16),
            shape(dec.shape, F32),
        ],
        in_specs=[VM] * 6,
        out_specs=[VM] * 7,
        compiler_params=pltpu.CompilerParams(vmem_limit_bytes=32 << 20),
    )(att, ffn, small, enc, out3, dec)


def on_device(
    encoder_tokens,
    encoder_segments,
    decoder_tokens,
    decoder_segments,
    cotangent,
    attention_weight,
    feedforward_weight,
    norm_gain,
    norm_shift,
):
    width = encoder_tokens.shape[2]
    own_wt = jnp.swapaxes(attention_weight[0], 1, 2).reshape(6 * HEAD, width)
    args = {
        "tokens": encoder_tokens,
        "dec_tokens": decoder_tokens,
        "cot": cotangent,
        "seg_e": encoder_segments,
        "seg_d": decoder_segments,
        "wt_in": own_wt,
        "gain_in": jnp.swapaxes(norm_gain, 0, 1),
        "shift_in": jnp.swapaxes(norm_shift, 0, 1),
        "ffn_in": feedforward_weight[0],
    }
    att_sum, small_sum, enc_out, d3_out, dec_out, ffn_sum = layers_call(args, 1)
    att_out, ffn_out, gain_out, shift_out, enc_out, d3_out, dec_out = results_call(
        att_sum, ffn_sum, small_sum, enc_out, d3_out, dec_out
    )
    return (
        d3_out,
        enc_out,
        dec_out,
        jnp.swapaxes(att_out.reshape(6, HEAD, width), 1, 2)[None],
        ffn_out.reshape(feedforward_weight.shape),
        jnp.swapaxes(gain_out, 0, 1),
        jnp.swapaxes(shift_out, 0, 1),
    )


def solution(mesh):
    in_specs = (
        P("dp", "tensor", None),
        P("dp", None),
        P("dp", "tensor", None),
        P("dp", None),
        P("dp", "tensor", None),
        P("section", None, None, "tensor"),
        P("section", None, None, "tensor"),
        P("section", None, None),
        P("section", None, None),
    )
    out_specs = (
        P("dp", "tensor", "section"),
        P("dp", "tensor", "section"),
        P("dp", "tensor", "section"),
        P("section", None, None, "tensor"),
        P("section", None, None, "tensor"),
        P("section", None, None),
        P("section", None, None),
    )
    return jax.shard_map(
        on_device, mesh=mesh, in_specs=in_specs, out_specs=out_specs, check_vma=False
    )
```

```python
import functools
import types

import jax
import jax.numpy as jnp
from jax import lax
from jax.experimental import pallas as pl
from jax.experimental.pallas import tpu as pltpu
from jax.sharding import PartitionSpec as P

HEAD = 64
EPSILON = 1e-05
MASKED = -1000000000.0
SCALE = HEAD ** (-0.5)
F32 = jnp.float32
BF16 = jnp.bfloat16
MESH = pl.DeviceIdType.MESH
VM = pl.BlockSpec(memory_space=pltpu.VMEM)
SIDE = 4
DEVICES = SIDE * SIDE
UP = (0, 2)
DOWN = (1, 3)
RING_COPIES = 30
CHUNKS = ((0, 48), (48, 32))
PAUSES = (1, 1, 1, 1, 1)
LAG = 0
VMEM_BYTES = 60 << 20
RING = True
INV_SQRT2 = 0.7071067811865476
INV_SQRT_2PI = 0.3989422804014327
FAR_FIRST = (10, 2, 8, 6, 14, 11, 9, 7, 13, 5, 15, 1, 3, 4, 12)


def norm_parts(values):
    center = values - jnp.mean(values, -1, keepdims=True)
    scale = lax.rsqrt(jnp.mean(center * center, -1, keepdims=True) + EPSILON)
    return center * scale, scale


def norm_back(grad, unit, scale, gains):
    inner = grad * gains
    back = scale * (
        inner
        - jnp.mean(inner, -1, keepdims=True)
        - unit * jnp.mean(inner * unit, -1, keepdims=True)
    )
    return back, jnp.sum(grad * unit, 0, keepdims=True), jnp.sum(grad, 0, keepdims=True)


def gelu_parts(u):
    cdf = 0.5 * (1.0 + lax.erf(u * INV_SQRT2))
    return u * cdf, cdf + u * (INV_SQRT_2PI * jnp.exp(-0.5 * u * u))


def dot(a, b):
    return jnp.dot(a, b, preferred_element_type=F32)


def dot_t(a, b):
    return lax.dot_general(a, b, (((1,), (1,)), ((), ())), preferred_element_type=F32)


def t_dot(a, b):
    return lax.dot_general(a, b, (((0,), (0,)), ((), ())), preferred_element_type=F32)


def scores_of(queries, key_rows, allowed):
    return jnp.where(allowed, dot_t(queries, key_rows) * SCALE, MASKED)


def attend(queries, key_rows, value_rows, allowed):
    scores = scores_of(queries, key_rows, allowed)
    row_max = jnp.max(scores, -1, keepdims=True)
    exponent = jnp.exp(scores - row_max)
    row_sum = jnp.sum(exponent, -1, keepdims=True)
    probs_low = (exponent / row_sum).astype(BF16)
    return dot(probs_low, value_rows).astype(BF16), row_max + jnp.log(row_sum)


def attend_back(queries, key_rows, value_rows, log_total, allowed, attended_grad):
    probs = jnp.exp(scores_of(queries, key_rows, allowed) - log_total)
    value_grad = t_dot(attended_grad, probs.astype(BF16))
    probs_grad = dot_t(attended_grad, value_rows)
    scores_grad = (probs * (probs_grad - jnp.sum(probs * probs_grad, -1, keepdims=True))).astype(
        BF16
    )
    return dot(scores_grad, key_rows) * SCALE, t_dot(queries, scores_grad) * SCALE, value_grad


def at_grid():
    index = lax.axis_index("tensor")
    return lax.div(index, SIDE), lax.rem(index, SIDE)


def moved(place, dy, dx):
    return lax.rem(place[0] + dy % SIDE, SIDE), lax.rem(place[1] + dx % SIDE, SIDE)


def along(axis, steps):
    return (steps, 0) if axis == 0 else (0, steps)


def device_at(place):
    return {"tensor": place[0] * SIDE + place[1]}


def tensor_peers(place):
    return [device_at(moved(place, d // SIDE, d % SIDE)) for d in FAR_FIRST]


def pack_peers():
    mine = lax.axis_index("section") * 4 + lax.axis_index("dp")
    others = [lax.rem(mine + d, 8) for d in range(1, 8)]
    return [{"section": lax.div(n, 4), "dp": lax.rem(n, 4)} for n in others]


def greet(devices):
    barrier = pltpu.get_barrier_semaphore()
    for device in devices:
        pl.semaphore_signal(barrier, inc=1, device_id=device, device_id_type=MESH)
    pl.semaphore_wait(barrier, len(devices))


def sections():
    section, dp = lax.axis_index("section"), lax.axis_index("dp")
    zh, core = lax.div(dp, 2), lax.rem(dp, 2)
    return section, zh, core, {"section": 1 - section}, {"dp": zh * 2 + 1 - core}


class Links:
    def __init__(self, send_sems, recv_sems, used=0):
        self.send, self.recv, self.used, self.started = send_sems, recv_sems, used, []

    def start(self, source, target, device):
        n = self.used
        self.used += 1
        copy = pltpu.make_async_remote_copy(
            src_ref=source,
            dst_ref=target,
            send_sem=self.send.at[n],
            recv_sem=self.recv.at[n],
            device_id=device,
            device_id_type=MESH,
        )
        copy.start()
        self.started.append(copy)
        return copy

    def finish(self):
        for copy in self.started:
            copy.wait_send()
        self.started = []


def sems(n):
    return [pltpu.SemaphoreType.DMA((n,)), pltpu.SemaphoreType.DMA((n,))]


def shape(dims, kind):
    return jax.ShapeDtypeStruct(tuple(dims), kind)


def fold(rows):
    half = rows.shape[1] // 2
    return jnp.concatenate([rows[:, :half], rows[:, half:]], 0)


def unfold(rows):
    count = rows.shape[0] // 2
    return jnp.concatenate([rows[:count], rows[count:]], 1)


def unfold_all(blocks):
    count, half = blocks.shape[2] // 2, blocks.shape[3]
    split = blocks.astype(F32).reshape(DEVICES, 2, count, half)
    low = split[:, 0].reshape(DEVICES * count, half)
    high = split[:, 1].reshape(DEVICES * count, half)
    return jnp.concatenate([low, high], 1).astype(BF16)


def fold_all(part):
    count, half = part.shape[0] // DEVICES, part.shape[1] // 2
    split = part.reshape(DEVICES, count, 2 * half)
    both = jnp.concatenate([split[:, :, :half], split[:, :, half:]], 1)
    return both.astype(BF16).reshape(SIDE, SIDE, 2 * count, half)


def own_row(ref):
    return jnp.where(lax.axis_index("section") == 0, ref[0:1, :], ref[1:2, :]).astype(F32)


def column(row):
    return jnp.broadcast_to(row, (128, row.shape[1])).T


def gather(links, place, views, ready=None):
    jobs = []
    for buf, low, rows in views:
        half = buf.shape[-1] // 2
        for h in range(2):
            jobs.append((buf, 1 - h, h, h * half, half, pl.ds(low, rows)))
    ready = ready or (lambda group: None)

    def send(job, axis, steps, r, s):
        buf, a, b, start, size, rows = job
        y, x = moved(moved(place, *along(a, r)), *along(b, s))
        ref = buf.at[y, x, rows, pl.ds(start, size)]
        return links.start(ref, ref, device_at(moved(place, *along(axis, steps))))

    first, spread, ahead = [], [], []
    for job in jobs:
        first.append({-d % SIDE: send(job, job[1], d, 0, 0) for d in (2, 1, 3)})
    paths = ((1, 3), (3, 1)) if RING else ((2, 2), (1, 3), (3, 1))
    for job in jobs:
        spread.append({0: {s: send(job, job[2], d, 0, 0) for d, s in paths}})
    ready([(0, 0)])
    yield
    for r in (3, 1, 2):
        for i, job in enumerate(jobs):
            first[i][r].wait_recv()
            spread[i][r] = {s: send(job, job[2], d, r, 0) for d, s in paths}
    if RING:
        for i, job in enumerate(jobs):
            spread[i][0][3].wait_recv()
            ahead.append({0: send(job, job[2], 1, 0, 3)})
            spread[i][0][1].wait_recv()
    else:
        for i, job in enumerate(jobs):
            spread[i][0][3].wait_recv()
            spread[i][0][1].wait_recv()
            ahead.append({r: spread[i][r][2] for r in range(SIDE)})
    ready([(0, 1), (0, 3), (1, 0), (3, 0)])
    yield
    if RING:
        for r in DOWN:
            for i, job in enumerate(jobs):
                spread[i][r][1].wait_recv()
                ahead[i][r] = send(job, job[2], -1, r, 1)
        for i, job in enumerate(jobs):
            spread[i][2][3].wait_recv()
            ahead[i][2] = send(job, job[2], 1, 2, 3)
        for r in DOWN:
            for i, job in enumerate(jobs):
                spread[i][r][3].wait_recv()
    else:
        for r in DOWN:
            for i, job in enumerate(jobs):
                spread[i][r][1].wait_recv()
                spread[i][r][3].wait_recv()
    ready([(1, 1), (1, 3), (3, 1), (3, 3)])
    for i, job in enumerate(jobs):
        ahead[i][0].wait_recv()
    ready([(0, 2), (2, 0)])
    yield
    for i, job in enumerate(jobs):
        if not RING:
            spread[i][2][3].wait_recv()
        spread[i][2][1].wait_recv()
        ahead[i][1].wait_recv()
        ahead[i][3].wait_recv()
    ready([(1, 2), (3, 2), (2, 1), (2, 3)])
    for i, job in enumerate(jobs):
        ahead[i][2].wait_recv()
    ready([(2, 2)])


AT_ONCE = ([(0, 1), (0, 3), (1, 0), (3, 0)], [(0, 2), (2, 0)], [(2, 2)])
PRODUCE = (
    [(2, 2), (2, 3), (2, 1), (3, 2), (1, 2), (2, 0), (0, 2)],
    [(3, 3), (3, 1), (1, 3), (1, 1), (3, 0), (1, 0), (0, 3), (0, 1), (0, 0)],
)


def sum_blocks(links, place, views, produce=None):
    produce = produce or (lambda group: None)
    jobs = []
    for part, land, low, rows in views:
        half = part.shape[-1] // 2
        for h in range(2):
            jobs.append((part, land, 15 * h, 1 - h, h, h * half, half, pl.ds(low, rows)))

    def block(job, r, s):
        part, _, _, a, b, start, size, rows = job
        y, x = moved(moved(place, *along(a, r)), *along(b, s))
        return part.at[y, x, rows, pl.ds(start, size)]

    def landing(job, n):
        return job[1].at[job[2] + n, job[7]]

    def start(source, target, axis, steps):
        return links.start(source, target, device_at(moved(place, *along(axis, steps))))

    def add(target, *others):
        total = target[...].astype(F32)
        for other in others:
            total = total + other[...].astype(F32)
        return total

    def near_slot(job, r, steps):
        return landing(job, 4 + 2 * r + (0 if steps == 1 else 1))

    order = (2, 3, 1, 0)
    produce(PRODUCE[0])
    near = [{r: [] for r in order} for _ in jobs]
    if RING:
        far = []
        for job in jobs:
            far.append(
                {
                    r: start(block(job, r, 2), landing(job, r), job[4], 1 if r in UP else -1)
                    for r in order
                }
            )
        produce(PRODUCE[1])
        for i, job in enumerate(jobs):
            for r in order:
                steps = -1 if r in UP else 1
                near[i][r].append(
                    start(block(job, r, steps), near_slot(job, r, steps), job[4], steps)
                )
        yield
        for r in order:
            for i, job in enumerate(jobs):
                steps = 1 if r in UP else -1
                far[i][r].wait_recv()
                ref = block(job, r, steps)
                ref[...] = add(ref, landing(job, r)).astype(BF16)
                near[i][r].append(start(ref, near_slot(job, r, steps), job[4], steps))
    else:
        for s in (2, 1, 3):
            for r in order:
                for i, job in enumerate(jobs):
                    slot = landing(job, 4 * (s - 1) + r)
                    near[i][r].append(start(block(job, r, s), slot, job[4], s))
            if s == 2:
                produce(PRODUCE[1])
    yield
    last = [{} for _ in jobs]
    results = []
    for r in order:
        if r == 0:
            yield
        for i, job in enumerate(jobs):
            for copy in near[i][r]:
                copy.wait_recv()
            ref = block(job, r, 0)
            if RING:
                total = add(ref, landing(job, 4 + 2 * r), landing(job, 5 + 2 * r))
            else:
                total = add(ref, landing(job, r), landing(job, 4 + r), landing(job, 8 + r))
            if r == 0:
                results.append(total)
            else:
                ref[...] = total.astype(BF16)
                last[i][r] = start(ref, landing(job, 11 + r), job[3], r)
    for i, job in enumerate(jobs):
        for r in order[:3]:
            last[i][r].wait_recv()
            results[i] = results[i] + landing(job, 11 + r)[...].astype(F32)
    return [jnp.concatenate(results[i : i + 2], 1) for i in range(0, len(results), 2)]


def run(chains, lag=0):
    turn, active = 0, list(enumerate(chains))
    while active:
        for n, chain in list(active):
            if turn >= n * lag:
                try:
                    next(chain)
                except StopIteration:
                    active.remove((n, chain))
        turn += 1


def pack_places():
    section, zh, core, partner, sibling = sections()
    zh_plus = lax.rem(zh + section, 2)
    plus = {"section": 1 - section, "dp": zh_plus * 2 + core}
    minus = {"section": 1 - section, "dp": (1 - zh_plus) * 2 + core}
    return section, zh, core, sibling, zh_plus, plus, minus


PACK_COPIES = 8


def pack_scratch(rows, cols):
    half, quarter = rows // 2, rows // 4
    return [
        pltpu.VMEM((2, half, cols), BF16),
        pltpu.VMEM((2, half, cols), BF16),
        pltpu.VMEM((2, quarter, cols), BF16),
        pltpu.VMEM((2, quarter, cols), BF16),
        pltpu.VMEM((half, cols), BF16),
    ]


def pause(n):
    for _ in range(n):
        yield


def pack_sum(links, grad, out, scratch):
    work, core_land, side, passing, over = scratch
    section, zh, core, sibling, zh_plus, plus, minus = pack_places()
    other = 1 - section
    half = grad.shape[1] // 2
    quarter = half // 2
    first = links.start(grad.at[:, pl.ds((1 - core) * half, half)], core_land, sibling)
    yield from pause(PAUSES[0])
    first.wait_recv()
    work[...] = (
        grad[:, pl.ds(core * half, half)].astype(F32) + core_land[...].astype(F32)
    ).astype(BF16)
    second = [
        links.start(work.at[other, pl.ds(h * quarter, quarter)], side.at[n], d)
        for n, (h, d) in enumerate(((zh_plus, plus), (1 - zh_plus, minus)))
    ]
    yield from pause(PAUSES[1])
    for copy in second:
        copy.wait_recv()
    mine = work.at[section, pl.ds(zh * quarter, quarter)]
    mine[...] = (mine[...].astype(F32) + side[0].astype(F32) + side[1].astype(F32)).astype(BF16)
    third = [
        links.start(work.at[section, pl.ds(n * quarter, quarter)], passing.at[n], d)
        for n, d in enumerate((plus, minus))
    ]
    yield from pause(PAUSES[2])
    fourth = []
    for n, device in enumerate((plus, minus)):
        third[n].wait_recv()
        fourth.append(links.start(passing.at[n], over.at[pl.ds(n * quarter, quarter)], device))
    yield from pause(PAUSES[3])
    for copy in fourth:
        copy.wait_recv()
    out[core] = (work[section].astype(F32) + over[...].astype(F32)).astype(BF16)
    last = links.start(out.at[core], out.at[core], sibling)
    yield from pause(PAUSES[4])
    last.wait_recv()
    links.finish()


def gather_small(links, place, buf, rows):
    y, x = place
    buf[y, x] = fold(rows).astype(BF16)
    copies = []
    for d in FAR_FIRST:
        target = device_at(moved(place, d // SIDE, d % SIDE))
        copies.append(links.start(buf.at[y, x], buf.at[y, x], target))
    for copy in copies:
        copy.wait_recv()
    return unfold_all(buf[...])


def sum_small(links, place, work, land, part):
    work[...] = fold_all(part)
    copies = []
    for n, d in enumerate(FAR_FIRST):
        there = moved(place, d // SIDE, d % SIDE)
        copies.append(links.start(work.at[there[0], there[1]], land.at[n], device_at(there)))
    total = work[place[0], place[1]].astype(F32)
    for copy in copies:
        copy.wait_recv()
    return unfold(total + jnp.sum(land[...].astype(F32), 0))


def stacked(ref, place, group, low=0, rows=None):
    rows = ref.shape[2] if rows is None else rows
    blocks = []
    for dy, dx in group:
        y, x = moved(place, dy, dx)
        blocks.append(ref[y, x, low : low + rows])
    return blocks[0] if len(blocks) == 1 else jnp.concatenate(blocks, 0)


def store_blocks(ref, place, group, values, low=0):
    rows = values.shape[0] // len(group)
    for n, (dy, dx) in enumerate(group):
        y, x = moved(place, dy, dx)
        ref[y, x, low : low + rows] = values[n * rows : (n + 1) * rows]


def whole(ref):
    return ref[...].reshape(DEVICES * ref.shape[2], ref.shape[3])


def wide(scale):
    return jnp.broadcast_to(scale, (scale.shape[0], 128))


def first_part(
    tokens, dec_tokens, seg_d, wt_in, gain_in, shift_in, wt, gs, full_h0, h0, unit0, scale0, *rest
):
    (full_y, q, k, v, sq, sk, sv, att_d, log_d, xbuf, ybuf, gs_in, send, recv) = rest
    place = at_grid()
    section, _, core, partner, sibling = sections()
    links = Links(send, recv)
    half = wt_in.shape[0] // 2
    mine = pl.ds(core * half, half)
    x, y = tokens.at[section], dec_tokens.at[section]
    for i in range(3):
        gs_in[i : i + 1, :] = gain_in[i]
        gs_in[3 + i : 4 + i, :] = shift_in[i]
    gs_in[6:8, :] = jnp.zeros((2, x.shape[1]), F32)
    gains_copy = links.start(gs_in, gs.at[section], partner)
    xbuf[place[0], place[1]] = x[...]
    ybuf[place[0], place[1]] = fold(y[...].astype(F32)).astype(BF16)
    passed = []

    def ready(group):
        if group == [(0, 0)]:
            passed.append(links.start(wt_in.at[mine], wt.at[section, mine], partner))
            gs[section] = gs_in[...]
            wt[section] = wt_in[...]
            gains_copy.wait_recv()
        if group == [(1, 1), (1, 3), (3, 1), (3, 3)]:
            passed[0].wait_recv()
            theirs = wt.at[1 - section, mine]
            passed.append(links.start(theirs, theirs, sibling))
        unit, scale = norm_parts(stacked(xbuf, place, group).astype(F32))
        rows = unit * gs[0, 0:1, :] + gs[0, 3:4, :]
        if group == [(0, 0)]:
            h0[...] = rows
            unit0[...] = unit
            scale0[...] = wide(scale)
        store_blocks(full_h0, place, group, rows.astype(BF16))

    views = [(xbuf, 0, x.shape[0]), (ybuf, 0, ybuf.shape[2])]
    run([gather(links, place, views, ready)])
    passed[1].wait_recv()
    count, width = x.shape
    for i in range(SIDE):
        rows = full_h0[i].reshape(SIDE * count, width)
        made = dot_t(rows, wt[0, 0 : 3 * HEAD, :]).astype(BF16)
        for j, ref in enumerate((q, k, v)):
            ref[i] = made[:, j * HEAD : (j + 1) * HEAD].reshape(SIDE, count, HEAD)
    rows = unfold_all(ybuf[...])
    full_y[...] = rows
    made = dot_t(rows, wt[1, 0 : 3 * HEAD, :]).astype(BF16)
    for j, ref in enumerate((sq, sk, sv)):
        ref[...] = made[:, j * HEAD : (j + 1) * HEAD]
    row = own_row(seg_d)
    att, log_total = attend(sq[...], sk[...], sv[...], before(row))
    att_d[...] = att
    log_d[...] = wide(log_total)
    links.finish()


def before(row):
    count = row.shape[1]
    place = [lax.broadcasted_iota(jnp.int32, (count, count), i) for i in range(2)]
    return (column(row)[:, 0:1] == row) & (place[1] <= place[0])


def forward_part(q, k, v, seg_e, att_d, h0, dec_tokens, wt, gs, ffn_in, *rest):
    (ffn, full_h1, full_m, full_d1, hidden, slope, kvc, cq, d1) = rest[:9]
    (unit1, scale1, unit2, scale2, dunit0, dscale0, att_e, log_e, seg_col) = rest[9:18]
    (part, dpart, land_1, land_2, land_d, d1buf, send, recv) = rest[18:]
    place = at_grid()
    section, _, core, partner, sibling = sections()
    y = dec_tokens.at[section]
    row = own_row(seg_e)
    seg_col[...] = column(row).reshape(seg_col.shape)
    shared = Links(send, recv)
    passed = [shared.start(ffn_in.at[core], ffn.at[section, core], partner)]

    def chain(links, low, rows, with_dec):
        here = pl.ds(low, rows)

        def attended(group):
            allowed = stacked(seg_col, place, group, low, rows)[:, 0:1] == row
            queries = stacked(q, place, group, low, rows)
            att, log_total = attend(queries, whole(k), whole(v), allowed)
            store_blocks(att_e, place, group, att, low)
            store_blocks(log_e, place, group, wide(log_total), low)
            made = dot(att, wt[0, 3 * HEAD : 4 * HEAD, :])
            store_blocks(part, place, group, made.astype(BF16), low)
            if with_dec and group == PRODUCE[0]:
                dpart[...] = fold_all(dot(att_d[...], wt[1, 3 * HEAD : 4 * HEAD, :]))
            if low == 0 and group == PRODUCE[1]:
                ffn[section] = ffn_in[...]

        views = [(part, land_1, low, rows)]
        if with_dec:
            views.append((dpart, land_d, 0, dpart.shape[2]))
        sums = yield from sum_blocks(links, place, views, attended)
        unit, scale = norm_parts(h0[here] + sums[0])
        unit1[here] = unit
        scale1[here] = wide(scale)
        h1 = unit * gs[0, 1:2, :] + gs[0, 4:5, :]
        full_h1[place[0], place[1], here] = h1.astype(BF16)
        views = [(full_h1, low, rows)]
        if with_dec:
            unit, scale = norm_parts(y[...].astype(F32) + unfold(sums[1]))
            dunit0[...] = unit
            dscale0[...] = wide(scale)
            made = unit * gs[1, 0:1, :] + gs[1, 3:4, :]
            d1[...] = made
            d1buf[place[0], place[1]] = fold(made).astype(BF16)
            views.append((d1buf, 0, d1buf.shape[2]))
        if low == 0:
            passed[0].wait_recv()
            theirs = ffn.at[1 - section, core]
            passed.append(shared.start(theirs, theirs, sibling))

        def up(group):
            if group == [(0, 0)]:
                return
            if group == [(0, 1), (0, 3), (1, 0), (3, 0)]:
                if low == 0:
                    passed[1].wait_recv()
                group = [(0, 0)] + group
            made, back = gelu_parts(dot(stacked(full_h1, place, group, low, rows), ffn[0, 0]))
            store_blocks(hidden, place, group, made.astype(BF16), low)
            store_blocks(slope, place, group, back, low)

        yield from gather(links, place, views, up)
        links.finish()
        if with_dec:
            made = unfold_all(d1buf[...])
            full_d1[...] = made
            cq[...] = dot_t(made, wt[1, 4 * HEAD : 5 * HEAD, :]).astype(BF16)

        def down(group):
            made = dot_t(stacked(hidden, place, group, low, rows), ffn[0, 1])
            store_blocks(part, place, group, made.astype(BF16), low)

        sums = yield from sum_blocks(links, place, [(part, land_2, low, rows)], down)
        unit, scale = norm_parts(h1 + sums[0])
        unit2[here] = unit
        scale2[here] = wide(scale)
        full_m[place[0], place[1], here] = (unit * gs[0, 2:3, :] + gs[0, 5:6, :]).astype(BF16)

        def cross(group):
            made = dot_t(stacked(full_m, place, group, low, rows), wt[0, 4 * HEAD : 6 * HEAD, :])
            store_blocks(kvc, place, group, made.astype(BF16), low)

        yield from gather(links, place, [(full_m, low, rows)], cross)
        links.finish()

    chains = []
    for n, (low, rows) in enumerate(CHUNKS):
        links = Links(send, recv, 2 + 6 * RING_COPIES * n)
        chains.append(chain(links, low, rows, n == len(CHUNKS) - 1))
    run(chains, LAG)
    shared.finish()


def decoder_part(cq, kvc, d1, cot, seg_d, seg_e, wt, ffn, gs, *rest):
    (d3, dback1, full_d2, full_db2, full_db1, hid_out, pre_out, att_out) = rest[:8]
    (cq_grad, kvc_grad, grads, g_bufs, s_work, s_land, probs, send, recv) = rest[8:]
    place = at_grid()
    links = Links(send, recv)
    w5 = wt[1, 5 * HEAD : 6 * HEAD, :]
    both = whole(kvc)
    kc, vc = both[:, :HEAD], both[:, HEAD:]
    allowed = column(own_row(seg_d))[:, 0:1] == own_row(seg_e)
    scores = scores_of(cq[...], kc, allowed)
    exponent = jnp.exp(scores - jnp.max(scores, -1, keepdims=True))
    probs[...] = exponent / jnp.sum(exponent, -1, keepdims=True)
    att = dot(probs[...].astype(BF16), vc).astype(BF16)
    att_out[...] = att
    part = sum_small(links, place, s_work.at[0], s_land.at[0], dot(att, w5))
    unit1, scale1 = norm_parts(d1[...] + part)
    d2 = unit1 * gs[1, 1:2, :] + gs[1, 4:5, :]
    full = gather_small(links, place, g_bufs.at[0], d2)
    full_d2[...] = full
    hidden, slope = gelu_parts(dot(full, ffn[1, 0]))
    hidden = hidden.astype(BF16)
    hid_out[...] = hidden
    part = sum_small(links, place, s_work.at[1], s_land.at[1], dot_t(hidden, ffn[1, 1]))
    unit2, scale2 = norm_parts(d2 + part)
    d3[...] = unit2 * gs[1, 2:3, :] + gs[1, 5:6, :]
    back2, gain2, shift2 = norm_back(cot[lax.axis_index("section")].astype(F32), unit2, scale2, gs[1, 2:3, :])
    full = gather_small(links, place, g_bufs.at[1], back2)
    full_db2[...] = full
    pre = (dot(full, ffn[1, 1]) * slope).astype(BF16)
    pre_out[...] = pre
    part = sum_small(links, place, s_work.at[2], s_land.at[2], dot_t(pre, ffn[1, 0]))
    back1, gain1, shift1 = norm_back(back2 + part, unit1, scale1, gs[1, 1:2, :])
    dback1[...] = back1
    full = gather_small(links, place, g_bufs.at[2], back1)
    full_db1[...] = full
    att_grad = dot_t(full, w5).astype(BF16)
    p = probs[...]
    value_grad = t_dot(att_grad, p.astype(BF16))
    p_grad = dot_t(att_grad, vc)
    s_grad = (p * (p_grad - jnp.sum(p * p_grad, -1, keepdims=True))).astype(BF16)
    cq_grad[...] = (dot(s_grad, kc) * SCALE).astype(BF16)
    key_grad = t_dot(cq[...], s_grad) * SCALE
    both = jnp.concatenate([key_grad, value_grad], 0).T.astype(BF16)
    kvc_grad[...] = both.reshape(kvc_grad.shape)
    grads[0:1, :] = gain1
    grads[1:2, :] = gain2
    grads[2:3, :] = shift1
    grads[3:4, :] = shift2
    grads[4:8, :] = jnp.zeros((4, grads.shape[1]), F32)
    links.finish()


def backward_part(*refs):
    (kvc_grad, cq_grad, dback1, wt, gs, ffn, unit1, scale1, unit2, scale2) = refs[:10]
    (dunit0, dscale0, slope, sq, sk, sv, log_d, seg_d, full_h1, hidden) = refs[10:20]
    (full_m, full_d1, full_y, full_d2, full_db1, full_db2, dpre, dhidden) = refs[20:28]
    (att_c, att_d, q, k, v, seg_e, seg_col, log_e) = refs[28:36]
    (full_b1, qkv_grad, kv_sum, back1, dec_grad, grads, ffn_sum, wt_grad) = refs[36:44]
    (full_b2, pre, part, dpart_1, dpart_2, land_1, land_2, dland_1, dland_2, dbuf) = refs[44:54]
    (ffn_grad, *pack_refs, send, recv) = refs[54:]
    kv_sum[...] = jnp.zeros(kv_sum.shape, F32)
    row = own_row(seg_e)
    place = at_grid()

    def chain(links, low, rows, with_dec):
        here = pl.ds(low, rows)

        def cross(group):
            made = dot(stacked(kvc_grad, place, group, low, rows), wt[0, 4 * HEAD : 6 * HEAD, :])
            store_blocks(part, place, group, made.astype(BF16), low)
            if with_dec and group == PRODUCE[0]:
                dpart_1[...] = fold_all(dot(cq_grad[...], wt[1, 4 * HEAD : 5 * HEAD, :]))

        views = [(part, land_1, low, rows)]
        if with_dec:
            views.append((dpart_1, dland_1, 0, dpart_1.shape[2]))
        sums = yield from sum_blocks(links, place, views, cross)
        back2, gain2, shift2 = norm_back(sums[0], unit2[here], scale2[here, 0:1], gs[0, 2:3, :])
        full_b2[place[0], place[1], here] = back2.astype(BF16)
        views = [(full_b2, low, rows)]
        if with_dec:
            dback0, dgain0, dshift0 = norm_back(
                dback1[...] + unfold(sums[1]), dunit0[...], dscale0[:, 0:1], gs[1, 0:1, :]
            )
            dbuf[place[0], place[1]] = fold(dback0).astype(BF16)
            views.append((dbuf, 0, dbuf.shape[2]))

        def down(group):
            made = dot(stacked(full_b2, place, group, low, rows), ffn[0, 1])
            made = made * stacked(slope, place, group, low, rows)
            store_blocks(pre, place, group, made.astype(BF16), low)

        yield from gather(links, place, views, down)
        links.finish()
        ready_rows.append(rows)
        views = [(part, land_2, low, rows)]
        if with_dec:
            full_db0 = unfold_all(dbuf[...])
            att_d_grad = dot_t(full_db0, wt[1, 3 * HEAD : 4 * HEAD, :]).astype(BF16)
            made = attend_back(
                sq[...], sk[...], sv[...], log_d[:, 0:1], before(own_row(seg_d)), att_d_grad
            )
            made = jnp.concatenate([made[0], made[1].T, made[2].T], 1).astype(BF16)
            late.extend([made, full_db0])
            dpart_2[...] = fold_all(dot(made, wt[1, 0 : 3 * HEAD, :]))
            views.append((dpart_2, dland_2, 0, dpart_2.shape[2]))

        def up(group):
            made = dot_t(stacked(pre, place, group, low, rows), ffn[0, 0])
            store_blocks(part, place, group, made.astype(BF16), low)

        sums = yield from sum_blocks(links, place, views, up)
        made, gain1, shift1 = norm_back(
            back2 + sums[0], unit1[here], scale1[here, 0:1], gs[0, 1:2, :]
        )
        back1[here] = made
        full_b1[place[0], place[1], here] = made.astype(BF16)
        totals.append((gain1, gain2, shift1, shift2))
        if with_dec:
            dec_grad[...] = dback0 + unfold(sums[1])
            grads[4:5, :] = dgain0
            grads[5:6, :] = dshift0

        pending = []

        def mixed(group):
            pending.extend(group)
            if group not in AT_ONCE:
                return
            some = lambda ref: stacked(ref, place, pending, low, rows)
            att_grad = dot_t(some(full_b1), wt[0, 3 * HEAD : 4 * HEAD, :]).astype(BF16)
            made = attend_back(
                some(q), whole(k), whole(v), some(log_e)[:, 0:1], some(seg_col)[:, 0:1] == row, att_grad
            )
            for n, (dy, dx) in enumerate(pending):
                at_y, at_x = moved(place, dy, dx)
                block = made[0][n * rows : (n + 1) * rows].astype(BF16)
                qkv_grad[at_y, at_x, here, 0:HEAD] = block
            kv_sum[...] += jnp.concatenate(made[1:], 0)
            pending.clear()

        yield from gather(links, place, [(full_b1, low, rows)], mixed)
        links.finish()

    def weight_chain(links):
        def put(layer, first, rows):
            wt_grad[layer, first * HEAD : first * HEAD + rows.shape[0], :] = rows.astype(BF16)

        count = full_h1.shape[3]
        yield
        put(0, 4, t_dot(whole(kvc_grad), whole(full_m)))
        ffn_grad[1, :count] = t_dot(dpre[...], full_d2[...]).T.astype(BF16)
        yield
        ffn_grad[1, count:] = t_dot(dhidden[...], full_db2[...]).T.astype(BF16)
        put(1, 4, t_dot(cq_grad[...], full_d1[...]))
        put(1, 5, t_dot(att_c[...], full_db1[...]))
        while len(ready_rows) < len(CHUNKS):
            yield
        ffn_grad[0, :count] = t_dot(whole(pre), whole(full_h1)).T.astype(BF16)
        yield
        ffn_grad[0, count:] = t_dot(whole(hidden), whole(full_b2)).T.astype(BF16)
        yield from pack_sum(links, ffn_grad, ffn_sum, pack_refs)
        put(1, 0, t_dot(late[0], full_y[...]))
        put(1, 3, t_dot(att_d[...], late[1]))
        unused = slice(0, 4 * HEAD)
        wt_grad[0, unused, :] = jnp.zeros((4 * HEAD, count), BF16)

    late = []
    totals, chains, ready_rows = [], [], []
    for n, (low, rows) in enumerate(CHUNKS):
        links = Links(send, recv, PACK_COPIES + 7 * RING_COPIES * n)
        chains.append(chain(links, low, rows, n == len(CHUNKS) - 1))
    chains.append(weight_chain(Links(send, recv)))
    run(chains, LAG)
    for i in range(4):
        grads[i : i + 1, :] = sum(total[i] for total in totals)
    grads[6:8, :] = jnp.zeros((2, grads.shape[1]), F32)


def last_part(kv_sum, qkv_grad, att_e, full_b1, full_h0, *refs):
    (wt, gs, back1, unit0, scale0, wt_grad, small_b, small_d, out3, dec, *rest) = refs
    (att_out, small_out, enc_out, out3_out, dec_out, part, land, *pack_refs) = rest[:12]
    (fin, core_s, y_s, x_s, z_s, late, late_t, late_p) = rest[12:20]
    (enc, give_e, give_d, land_e, land_d, att, small, send, recv) = rest[20:]
    place = at_grid()
    section, zh, core, sibling, _, plus, minus = pack_places()
    other = 1 - section
    partner = {"section": other}
    far = {"dp": (1 - zh) * 2 + core}
    columns = [device_at(moved(place, d, 0)) for d in (1, 2, 3)]
    rows = [device_at(moved(place, 0, d)) for d in (1, 2, 3)]
    tensor, packs = tensor_peers(place), pack_peers()
    width = enc.shape[1] // 2
    there = pl.ds(pl.multiple_of(other * width, width), width)
    here = pl.ds(pl.multiple_of(section * width, width), width)

    att[...] = wt_grad[...]
    small[...] = jnp.zeros(small.shape, F32)
    for layer, to, source, frm in (
        (0, 1, small_b, 0), (0, 2, small_b, 1), (0, 4, small_b, 2), (0, 5, small_b, 3),
        (1, 0, small_b, 4), (1, 3, small_b, 5),
        (1, 1, small_d, 0), (1, 2, small_d, 1), (1, 4, small_d, 2), (1, 5, small_d, 3),
    ):
        small[layer, to : to + 1, :] = source[frm : frm + 1, :]

    def early(links):
        give_d[...] = jnp.concatenate([out3[:, there], dec[:, there]], 0).astype(BF16)
        swap = links.start(give_d, land_d, partner)
        one = links.start(small.at[1 - core], core_s, sibling)
        yield
        one.wait_recv()
        fin[core] = small[core] + core_s[...]
        for land_s, devices in ((y_s, columns), (x_s, rows), (z_s, [plus, minus, far])):
            copies = [links.start(fin.at[core], land_s.at[n], d) for n, d in enumerate(devices)]
            yield
            for copy in copies:
                copy.wait_recv()
            links.finish()
            fin[core] = fin[core] + land_s[0] + land_s[1] + land_s[2]
        five = links.start(fin.at[core], fin.at[core], sibling)
        yield
        five.wait_recv()
        swap.wait_recv()
        links.finish()

    def heads(group):
        made = dot(stacked(qkv_grad, place, group), wt[0, 0 : 3 * HEAD, :])
        store_blocks(part, place, group, made.astype(BF16))

    def weights(links):
        made = t_dot(whole(qkv_grad), whole(full_h0))
        att[0, 0 : 3 * HEAD, :] = made.astype(BF16)
        att[0, 3 * HEAD : 4 * HEAD, :] = t_dot(whole(att_e), whole(full_b1)).astype(BF16)
        yield from pack_sum(links, att, att_out, pack_refs)

    both = kv_sum[...].T.astype(BF16)
    rows_each = qkv_grad.shape[2]
    qkv_grad[:, :, :, HEAD : 3 * HEAD] = both.reshape(SIDE, SIDE, rows_each, 2 * HEAD)

    def rest_of(links):
        (sum_e,) = yield from sum_blocks(links, place, [(part, land, 0, enc.shape[0])], heads)
        made, gain0, shift0 = norm_back(
            back1[...] + sum_e, unit0[...], scale0[:, 0:1], gs[0, 0:1, :]
        )
        enc[...] = made
        quarter = width // 2
        both = [row[:, i * quarter : (i + 1) * quarter] for row in (gain0, shift0) for i in range(4)]
        late[...] = jnp.concatenate(both, 0)
        copies = [links.start(late, late_t.at[n], d) for n, d in enumerate(tensor)]
        give_e[...] = enc[:, there].astype(BF16)
        swap = links.start(give_e, land_e, partner)
        yield
        for copy in copies:
            copy.wait_recv()
        links.finish()
        late[...] = late[...] + jnp.sum(late_t[...], 0)
        copies = [links.start(late, late_p.at[n], d) for n, d in enumerate(packs)]
        enc_out[section] = enc[:, here]
        yield
        for copy in copies:
            copy.wait_recv()
        swap.wait_recv()
        links.finish()

    chains = [
        early(Links(send, recv, PACK_COPIES)),
        rest_of(Links(send, recv, 2 * PACK_COPIES + 16)),
        weights(Links(send, recv)),
    ]
    run(chains)
    enc_out[other] = land_e[...].astype(F32)
    got = land_d[...].astype(F32)
    count = out3.shape[0]
    out3_out[section] = out3[:, here]
    out3_out[other] = got[:count]
    dec_out[section] = dec[:, here]
    dec_out[other] = got[count:]
    small_out[...] = fin[section]
    total = late[...] + jnp.sum(late_p[...], 0)
    quarter = width // 2
    for i in range(8):
        row = 0 if i < 4 else 3
        cols = slice((i % 4) * quarter, (i % 4 + 1) * quarter)
        added = jnp.where(section == 0, total[i : i + 1], 0.0)
        small_out[row : row + 1, cols] = small_out[row : row + 1, cols] + added


def layers_kernel(names, *refs):
    r = types.SimpleNamespace(**dict(zip(names, refs)))
    more = refs[len(names) :]
    ffn_pack, att_pack, copies = more[:5], more[5:10], more[10:]
    place = at_grid()
    greet(tensor_peers(place) + pack_peers())

    first_part(
        r.tokens, r.dec_tokens, r.seg_d, r.wt_in, r.gain_in, r.shift_in, r.wt, r.gs, r.full_h0, r.h0, r.unit0, r.scale0,
        r.full_y, r.q, r.k, r.v, r.sq, r.sk, r.sv, r.att_d, r.log_d, r.part, r.dbuf_0, r.gs_in, *copies[0:2],
    )
    forward_part(
        r.q, r.k, r.v, r.seg_e, r.att_d, r.h0, r.dec_tokens, r.wt, r.gs, r.ffn_in,
        r.ffn, r.full_h1, r.full_m, r.full_d1, r.hidden, r.slope, r.kvc, r.cq, r.d1,
        r.unit1, r.scale1, r.unit2, r.scale2, r.dunit0, r.dscale0, r.att_e, r.log_e, r.seg_col,
        r.part, r.dpart_0, r.land_1, r.land_2, r.dland_0, r.dbuf_1, *copies[2:4],
    )
    decoder_part(
        r.cq, r.kvc, r.d1, r.cot, r.seg_d, r.seg_e, r.wt, r.ffn, r.gs,
        r.d3, r.dback1, r.full_d2, r.full_db2, r.full_db1, r.dhidden, r.dpre, r.att_c,
        r.cq_grad, r.kvc_grad, r.small_d, r.g_bufs, r.s_work, r.s_land, r.probs, *copies[4:6],
    )
    backward_part(
        r.kvc_grad, r.cq_grad, r.dback1, r.wt, r.gs, r.ffn, r.unit1, r.scale1, r.unit2, r.scale2,
        r.dunit0, r.dscale0, r.slope, r.sq, r.sk, r.sv, r.log_d, r.seg_d, r.full_h1, r.hidden,
        r.full_m, r.full_d1, r.full_y, r.full_d2, r.full_db1, r.full_db2, r.dpre, r.dhidden, r.att_c, r.att_d,
        r.q, r.k, r.v, r.seg_e, r.seg_col, r.log_e, r.full_b1, r.qkv_grad, r.kv_sum, r.back1, r.dec_grad, r.small_b, r.ffn_sum, r.wt_grad,
        r.full_b2, r.pre, r.part, r.dpart_1, r.dpart_2, r.land_1, r.land_2, r.dland_1, r.dland_2, r.dbuf_2,
        r.ffn_grad, *ffn_pack, *copies[6:8],
    )
    last_part(
        r.kv_sum, r.qkv_grad, r.att_e, r.full_b1, r.full_h0,
        r.wt, r.gs, r.back1, r.unit0, r.scale0, r.wt_grad, r.small_b, r.small_d, r.d3, r.dec_grad,
        r.att_out, r.small_out, r.enc_out, r.out3_out, r.dec_out,
        r.part, r.land_1, *att_pack,
        r.fin, r.core_s, r.y_s, r.x_s, r.z_s, r.late, r.late_t, r.late_p,
        r.enc, r.give_e, r.give_d, r.land_e, r.land_d, r.att, r.small, *copies[8:10],
    )


def layers_call(args, collective_id):
    tokens, dec_tokens, ffn = args["tokens"], args["dec_tokens"], args["ffn_in"]
    (_, rows, width), count, inner = tokens.shape, dec_tokens.shape[1], ffn.shape[2]
    half, full, grid = width // 2, count * DEVICES, (SIDE, SIDE)
    low, wide_rows, head = (*grid, rows, width), (*grid, rows, 128), (*grid, rows, HEAD)
    small_block = (*grid, 2 * count, half)
    outs = dict(
        att_out=((2, 3 * HEAD, width), BF16),
        small_out=((8, width), F32),
        enc_out=((2, rows, half), F32),
        out3_out=((2, count, half), F32),
        dec_out=((2, count, half), F32),
        ffn_sum=((2, width, inner), BF16),
    )
    kept = dict(
        wt=((2, 6 * HEAD, width), BF16),
        gs=((2, 8, width), F32),
        ffn=((2, 2, width, inner), BF16),
    )
    kept |= dict(full_h0=(low, BF16), full_h1=(low, BF16), full_m=(low, BF16), full_b1=(low, BF16), full_b2=(low, BF16), part=(low, BF16))
    kept |= dict(h0=((rows, width), F32), unit0=((rows, width), F32), unit1=((rows, width), F32), unit2=((rows, width), F32), back1=((rows, width), F32), enc=((rows, width), F32))
    kept |= dict(scale0=((rows, 128), F32), scale1=((rows, 128), F32), scale2=((rows, 128), F32))
    kept |= dict(full_y=((full, width), BF16), full_d1=((full, width), BF16), full_d2=((full, width), BF16), full_db1=((full, width), BF16), full_db2=((full, width), BF16))
    kept |= dict(q=(head, BF16), k=(head, BF16), v=(head, BF16), att_e=(head, BF16))
    kept |= dict(sq=((full, HEAD), BF16), sk=((full, HEAD), BF16), sv=((full, HEAD), BF16), att_d=((full, HEAD), BF16), cq=((full, HEAD), BF16), att_c=((full, HEAD), BF16), cq_grad=((full, HEAD), BF16))
    kept |= dict(d1=((8, width), F32), dunit0=((8, width), F32), d3=((8, width), F32), dback1=((8, width), F32), dec_grad=((8, width), F32), small_b=((8, width), F32), small_d=((8, width), F32), gs_in=((8, width), F32))
    kept |= dict(dbuf_0=(small_block, BF16), dbuf_1=(small_block, BF16), dbuf_2=(small_block, BF16), dpart_0=(small_block, BF16), dpart_1=(small_block, BF16), dpart_2=(small_block, BF16))
    kept |= dict(land_1=((30, rows, half), BF16), land_2=((30, rows, half), BF16))
    kept |= dict(dland_0=((30, 2 * count, half // 2), BF16), dland_1=((30, 2 * count, half // 2), BF16), dland_2=((30, 2 * count, half // 2), BF16))
    kept |= dict(hidden=((*grid, rows, inner), BF16), pre=((*grid, rows, inner), BF16))
    kept |= dict(kvc=((*grid, rows, 2 * HEAD), BF16), kvc_grad=((*grid, rows, 2 * HEAD), BF16))
    kept |= dict(dhidden=((full, inner), BF16), dpre=((full, inner), BF16))
    kept |= dict(wt_grad=((2, 6 * HEAD, width), BF16), att=((2, 6 * HEAD, width), BF16))
    kept |= dict(y_s=((3, 8, width), F32), x_s=((3, 8, width), F32), z_s=((3, 8, width), F32))
    kept |= dict(fin=((2, 8, width), F32), small=((2, 8, width), F32))
    kept |= dict(give_e=((rows, half), BF16), land_e=((rows, half), BF16))
    kept |= dict(give_d=((2 * count, half), BF16), land_d=((2 * count, half), BF16))
    kept |= dict(
        slope=((*grid, rows, inner), F32),
        log_e=(wide_rows, F32),
        seg_col=(wide_rows, F32),
        log_d=((full, 128), F32),
        dscale0=((count, 128), F32),
        g_bufs=((3, *small_block), BF16),
        s_work=((3, *small_block), BF16),
        s_land=((3, DEVICES - 1, 2 * count, half), BF16),
        probs=((full, DEVICES * rows), F32),
        ffn_grad=((2, 2 * width, inner), BF16),
        core_s=((8, width), F32),
        late=((8, width // 4), F32),
        late_t=((DEVICES - 1, 8, width // 4), F32),
        late_p=((7, 8, width // 4), F32),
        qkv_grad=((*grid, rows, 3 * HEAD), BF16),
        kv_sum=((2 * HEAD, DEVICES * rows), F32),
    )
    scratch = {name: pltpu.VMEM(dims, kind) for name, (dims, kind) in kept.items()}
    ffn_pack, att_pack = pack_scratch(2 * width, inner), pack_scratch(6 * HEAD, width)
    ring = RING_COPIES
    copies = [
        sems(n)
        for n in (
            2 * ring + 3,
            2 + 6 * ring * len(CHUNKS),
            6 * (DEVICES - 1),
            PACK_COPIES + 7 * ring * len(CHUNKS),
            2 * PACK_COPIES + 16 + ring + DEVICES + 7,
        )
    ]
    more = [*ffn_pack, *att_pack, *(sem for pair in copies for sem in pair)]
    return pl.pallas_call(
        functools.partial(layers_kernel, [*args, *outs, *scratch]),
        out_shape=[shape(*spec) for spec in outs.values()],
        in_specs=[VM] * len(args),
        out_specs=[VM] * len(outs),
        scratch_shapes=[*scratch.values(), *more],
        compiler_params=pltpu.CompilerParams(
            collective_id=collective_id, has_side_effects=True, vmem_limit_bytes=VMEM_BYTES
        ),
    )(*args.values())


def results_kernel(att, ffn, small, enc, out3, dec, *outs):
    (att_out, ffn_out, gain_out, shift_out, enc_out, out3_out, dec_out) = outs
    att_out[...] = att[...].astype(F32)
    ffn_out[...] = ffn[...].astype(F32)
    for i in range(3):
        gain_out[i] = small[i : i + 1, :]
        shift_out[i] = small[3 + i : 4 + i, :]
    enc_out[...] = enc[...]
    out3_out[...] = out3[...].astype(BF16)
    dec_out[...] = dec[...]


def results_call(att, ffn, small, enc, out3, dec):
    width = small.shape[1]
    return pl.pallas_call(
        results_kernel,
        out_shape=[
            shape(att.shape, F32),
            shape(ffn.shape, F32),
            shape((3, 1, width), F32),
            shape((3, 1, width), F32),
            shape(enc.shape, F32),
            shape(out3.shape, BF16),
            shape(dec.shape, F32),
        ],
        in_specs=[VM] * 6,
        out_specs=[VM] * 7,
        compiler_params=pltpu.CompilerParams(vmem_limit_bytes=VMEM_BYTES),
    )(att, ffn, small, enc, out3, dec)


def on_device(
    encoder_tokens,
    encoder_segments,
    decoder_tokens,
    decoder_segments,
    cotangent,
    attention_weight,
    feedforward_weight,
    norm_gain,
    norm_shift,
):
    width = encoder_tokens.shape[2]
    own_wt = jnp.swapaxes(attention_weight[0], 1, 2).reshape(6 * HEAD, width)
    args = dict(
        tokens=encoder_tokens,
        dec_tokens=decoder_tokens,
        cot=cotangent,
        seg_e=encoder_segments,
        seg_d=decoder_segments,
        wt_in=own_wt,
        gain_in=jnp.swapaxes(norm_gain, 0, 1),
        shift_in=jnp.swapaxes(norm_shift, 0, 1),
        ffn_in=feedforward_weight[0],
    )
    att_sum, small_sum, enc_out, d3_out, dec_out, ffn_sum = layers_call(args, 1)
    att_out, ffn_out, gain_out, shift_out, enc_out, d3_out, dec_out = results_call(
        att_sum, ffn_sum, small_sum, enc_out, d3_out, dec_out
    )
    return (
        d3_out,
        enc_out,
        dec_out,
        jnp.swapaxes(att_out.reshape(6, HEAD, width), 1, 2)[None],
        ffn_out.reshape(feedforward_weight.shape),
        jnp.swapaxes(gain_out, 0, 1),
        jnp.swapaxes(shift_out, 0, 1),
    )


def solution(mesh):
    in_specs = (
        P("dp", "tensor", None),
        P("dp", None),
        P("dp", "tensor", None),
        P("dp", None),
        P("dp", "tensor", None),
        P("section", None, None, "tensor"),
        P("section", None, None, "tensor"),
        P("section", None, None),
        P("section", None, None),
    )
    out_specs = (
        P("dp", "tensor", "section"),
        P("dp", "tensor", "section"),
        P("dp", "tensor", "section"),
        P("section", None, None, "tensor"),
        P("section", None, None, "tensor"),
        P("section", None, None),
        P("section", None, None),
    )
    return jax.shard_map(
        on_device, mesh=mesh, in_specs=in_specs, out_specs=out_specs, check_vma=False
    )
```

```python
import functools
import types

import jax
import jax.numpy as jnp
from jax import lax
from jax.experimental import pallas as pl
from jax.experimental.pallas import tpu as pltpu
from jax.sharding import PartitionSpec as P

HEAD = 64
EPSILON = 1e-05
MASKED = -1000000000.0
SCALE = HEAD ** (-0.5)
F32 = jnp.float32
BF16 = jnp.bfloat16
MESH = pl.DeviceIdType.MESH
VM = pl.BlockSpec(memory_space=pltpu.VMEM)
SIDE = 4
DEVICES = SIDE * SIDE
UP = (0, 2)
DOWN = (1, 3)
RING_COPIES = 30
CHUNKS = ((0, 48), (48, 32))
PAUSES = (1, 2, 2, 2, 1)
LAG = 0
VMEM_BYTES = 60 << 20
AT_FFN, AT_FIRST, AT_FFN_PACK, AT_ATT_PACK, AT_EARLY, AT_LATE, AT_SMALL = 0, 2, 5, 13, 21, 33, 55
AT_SUM, AT_GATHER, ALL_COPIES = (85, 145), (115, 205), 265
RING = True
INV_SQRT2 = 0.7071067811865476
INV_SQRT_2PI = 0.3989422804014327
FAR_FIRST = (10, 2, 8, 6, 14, 11, 9, 7, 13, 5, 15, 1, 3, 4, 12)


def norm_parts(values):
    center = values - jnp.mean(values, -1, keepdims=True)
    scale = lax.rsqrt(jnp.mean(center * center, -1, keepdims=True) + EPSILON)
    return center * scale, scale


def norm_back(grad, unit, scale, gains):
    inner = grad * gains
    back = scale * (
        inner
        - jnp.mean(inner, -1, keepdims=True)
        - unit * jnp.mean(inner * unit, -1, keepdims=True)
    )
    return back, jnp.sum(grad * unit, 0, keepdims=True), jnp.sum(grad, 0, keepdims=True)


def gelu_parts(u):
    cdf = 0.5 * (1.0 + lax.erf(u * INV_SQRT2))
    return u * cdf, cdf + u * (INV_SQRT_2PI * jnp.exp(-0.5 * u * u))


def dot(a, b):
    return jnp.dot(a, b, preferred_element_type=F32)


def dot_t(a, b):
    return lax.dot_general(a, b, (((1,), (1,)), ((), ())), preferred_element_type=F32)


def t_dot(a, b):
    return lax.dot_general(a, b, (((0,), (0,)), ((), ())), preferred_element_type=F32)


def scores_of(queries, key_rows, allowed):
    return jnp.where(allowed, dot_t(queries, key_rows) * SCALE, MASKED)


def attend(queries, key_rows, value_rows, allowed):
    scores = scores_of(queries, key_rows, allowed)
    row_max = jnp.max(scores, -1, keepdims=True)
    exponent = jnp.exp(scores - row_max)
    row_sum = jnp.sum(exponent, -1, keepdims=True)
    probs_low = (exponent / row_sum).astype(BF16)
    return dot(probs_low, value_rows).astype(BF16), row_max + jnp.log(row_sum)


def attend_back(queries, key_rows, value_rows, log_total, allowed, attended_grad):
    probs = jnp.exp(scores_of(queries, key_rows, allowed) - log_total)
    value_grad = t_dot(attended_grad, probs.astype(BF16))
    probs_grad = dot_t(attended_grad, value_rows)
    scores_grad = (probs * (probs_grad - jnp.sum(probs * probs_grad, -1, keepdims=True))).astype(
        BF16
    )
    return dot(scores_grad, key_rows) * SCALE, t_dot(queries, scores_grad) * SCALE, value_grad


def at_grid():
    index = lax.axis_index("tensor")
    return lax.div(index, SIDE), lax.rem(index, SIDE)


def moved(place, dy, dx):
    return lax.rem(place[0] + dy % SIDE, SIDE), lax.rem(place[1] + dx % SIDE, SIDE)


def along(axis, steps):
    return (steps, 0) if axis == 0 else (0, steps)


def device_at(place):
    return {"tensor": place[0] * SIDE + place[1]}


def tensor_peers(place):
    return [device_at(moved(place, d // SIDE, d % SIDE)) for d in FAR_FIRST]


def pack_peers():
    mine = lax.axis_index("section") * 4 + lax.axis_index("dp")
    others = [lax.rem(mine + d, 8) for d in range(1, 8)]
    return [{"section": lax.div(n, 4), "dp": lax.rem(n, 4)} for n in others]


def greet(devices):
    barrier = pltpu.get_barrier_semaphore()
    for device in devices:
        pl.semaphore_signal(barrier, inc=1, device_id=device, device_id_type=MESH)
    pl.semaphore_wait(barrier, len(devices))


def sections():
    section, dp = lax.axis_index("section"), lax.axis_index("dp")
    zh, core = lax.div(dp, 2), lax.rem(dp, 2)
    return section, zh, core, {"section": 1 - section}, {"dp": zh * 2 + 1 - core}


class Links:
    def __init__(self, send_sems, recv_sems, used=0):
        self.send, self.recv, self.used, self.started = send_sems, recv_sems, used, []

    def start(self, source, target, device):
        n = self.used
        self.used += 1
        copy = pltpu.make_async_remote_copy(
            src_ref=source,
            dst_ref=target,
            send_sem=self.send.at[n],
            recv_sem=self.recv.at[n],
            device_id=device,
            device_id_type=MESH,
        )
        copy.start()
        self.started.append(copy)
        return copy

    def finish(self, used=None):
        for copy in self.started:
            copy.wait_send()
        self.started = []
        self.used = self.used if used is None else used


def sems(n):
    return [pltpu.SemaphoreType.DMA((n,)), pltpu.SemaphoreType.DMA((n,))]


def shape(dims, kind):
    return jax.ShapeDtypeStruct(tuple(dims), kind)


def fold(rows):
    half = rows.shape[1] // 2
    return jnp.concatenate([rows[:, :half], rows[:, half:]], 0)


def unfold(rows):
    count = rows.shape[0] // 2
    return jnp.concatenate([rows[:count], rows[count:]], 1)


def unfold_all(blocks):
    count, half = blocks.shape[2] // 2, blocks.shape[3]
    split = blocks.astype(F32).reshape(DEVICES, 2, count, half)
    low = split[:, 0].reshape(DEVICES * count, half)
    high = split[:, 1].reshape(DEVICES * count, half)
    return jnp.concatenate([low, high], 1).astype(BF16)


def fold_all(part):
    count, half = part.shape[0] // DEVICES, part.shape[1] // 2
    split = part.reshape(DEVICES, count, 2 * half)
    both = jnp.concatenate([split[:, :, :half], split[:, :, half:]], 1)
    return both.astype(BF16).reshape(SIDE, SIDE, 2 * count, half)


def own_row(ref):
    return jnp.where(lax.axis_index("section") == 0, ref[0:1, :], ref[1:2, :]).astype(F32)


def column(row):
    return jnp.broadcast_to(row, (128, row.shape[1])).T


def gather(links, place, views, ready=None):
    jobs = []
    for buf, low, rows in views:
        half = buf.shape[-1] // 2
        for h in range(2):
            jobs.append((buf, 1 - h, h, h * half, half, pl.ds(low, rows)))
    ready = ready or (lambda group: None)

    def send(job, axis, steps, r, s):
        buf, a, b, start, size, rows = job
        y, x = moved(moved(place, *along(a, r)), *along(b, s))
        ref = buf.at[y, x, rows, pl.ds(start, size)]
        return links.start(ref, ref, device_at(moved(place, *along(axis, steps))))

    first, spread, ahead = [], [], []
    for job in jobs:
        first.append({-d % SIDE: send(job, job[1], d, 0, 0) for d in (2, 1, 3)})
    paths = ((1, 3), (3, 1)) if RING else ((2, 2), (1, 3), (3, 1))
    for job in jobs:
        spread.append({0: {s: send(job, job[2], d, 0, 0) for d, s in paths}})
    ready([(0, 0)])
    yield
    for r in (3, 1, 2):
        for i, job in enumerate(jobs):
            first[i][r].wait_recv()
            spread[i][r] = {s: send(job, job[2], d, r, 0) for d, s in paths}
    if RING:
        for i, job in enumerate(jobs):
            spread[i][0][3].wait_recv()
            ahead.append({0: send(job, job[2], 1, 0, 3)})
            spread[i][0][1].wait_recv()
    else:
        for i, job in enumerate(jobs):
            spread[i][0][3].wait_recv()
            spread[i][0][1].wait_recv()
            ahead.append({r: spread[i][r][2] for r in range(SIDE)})
    ready([(0, 1), (0, 3), (1, 0), (3, 0)])
    yield
    if RING:
        for r in DOWN:
            for i, job in enumerate(jobs):
                spread[i][r][1].wait_recv()
                ahead[i][r] = send(job, job[2], -1, r, 1)
        for i, job in enumerate(jobs):
            spread[i][2][3].wait_recv()
            ahead[i][2] = send(job, job[2], 1, 2, 3)
        for r in DOWN:
            for i, job in enumerate(jobs):
                spread[i][r][3].wait_recv()
    else:
        for r in DOWN:
            for i, job in enumerate(jobs):
                spread[i][r][1].wait_recv()
                spread[i][r][3].wait_recv()
    ready([(1, 1), (1, 3), (3, 1), (3, 3)])
    for i, job in enumerate(jobs):
        ahead[i][0].wait_recv()
    ready([(0, 2), (2, 0)])
    yield
    for i, job in enumerate(jobs):
        if not RING:
            spread[i][2][3].wait_recv()
        spread[i][2][1].wait_recv()
        ahead[i][1].wait_recv()
        ahead[i][3].wait_recv()
    ready([(1, 2), (3, 2), (2, 1), (2, 3)])
    for i, job in enumerate(jobs):
        ahead[i][2].wait_recv()
    ready([(2, 2)])


AT_ONCE = ([(0, 1), (0, 3), (1, 0), (3, 0)], [(0, 2), (2, 0)], [(2, 2)])
PRODUCE = (
    [(2, 2), (2, 3), (2, 1), (3, 2), (1, 2), (2, 0), (0, 2)],
    [(3, 3), (3, 1), (1, 3), (1, 1), (3, 0), (1, 0), (0, 3), (0, 1), (0, 0)],
)


def sum_blocks(links, place, views, produce=None):
    produce = produce or (lambda group: None)
    jobs = []
    for part, land, low, rows in views:
        half = part.shape[-1] // 2
        for h in range(2):
            jobs.append((part, land, 15 * h, 1 - h, h, h * half, half, pl.ds(low, rows)))

    def block(job, r, s):
        part, _, _, a, b, start, size, rows = job
        y, x = moved(moved(place, *along(a, r)), *along(b, s))
        return part.at[y, x, rows, pl.ds(start, size)]

    def landing(job, n):
        return job[1].at[job[2] + n, job[7]]

    def start(source, target, axis, steps):
        return links.start(source, target, device_at(moved(place, *along(axis, steps))))

    def add(target, *others):
        total = target[...].astype(F32)
        for other in others:
            total = total + other[...].astype(F32)
        return total

    def near_slot(job, r, steps):
        return landing(job, 4 + 2 * r + (0 if steps == 1 else 1))

    order = (2, 3, 1, 0)
    produce(PRODUCE[0])
    near = [{r: [] for r in order} for _ in jobs]
    if RING:
        far = []
        for job in jobs:
            far.append(
                {
                    r: start(block(job, r, 2), landing(job, r), job[4], 1 if r in UP else -1)
                    for r in order
                }
            )
        produce(PRODUCE[1])
        for i, job in enumerate(jobs):
            for r in order:
                steps = -1 if r in UP else 1
                near[i][r].append(
                    start(block(job, r, steps), near_slot(job, r, steps), job[4], steps)
                )
        yield
        for r in order:
            for i, job in enumerate(jobs):
                steps = 1 if r in UP else -1
                far[i][r].wait_recv()
                ref = block(job, r, steps)
                ref[...] = add(ref, landing(job, r)).astype(BF16)
                near[i][r].append(start(ref, near_slot(job, r, steps), job[4], steps))
    else:
        for s in (2, 1, 3):
            for r in order:
                for i, job in enumerate(jobs):
                    slot = landing(job, 4 * (s - 1) + r)
                    near[i][r].append(start(block(job, r, s), slot, job[4], s))
            if s == 2:
                produce(PRODUCE[1])
    yield
    last = [{} for _ in jobs]
    results = []
    for r in order:
        if r == 0:
            yield
        for i, job in enumerate(jobs):
            for copy in near[i][r]:
                copy.wait_recv()
            ref = block(job, r, 0)
            if RING:
                total = add(ref, landing(job, 4 + 2 * r), landing(job, 5 + 2 * r))
            else:
                total = add(ref, landing(job, r), landing(job, 4 + r), landing(job, 8 + r))
            if r == 0:
                results.append(total)
            else:
                ref[...] = total.astype(BF16)
                last[i][r] = start(ref, landing(job, 11 + r), job[3], r)
    for i, job in enumerate(jobs):
        for r in order[:3]:
            last[i][r].wait_recv()
            results[i] = results[i] + landing(job, 11 + r)[...].astype(F32)
    return [jnp.concatenate(results[i : i + 2], 1) for i in range(0, len(results), 2)]


def run(chains, lag=0, background=None):
    turn, active = 0, list(enumerate(chains))
    while active:
        for n, chain in list(active):
            if turn >= n * lag:
                try:
                    next(chain)
                except StopIteration:
                    active.remove((n, chain))
        if background is not None:
            next(background, None)
        turn += 1


def pack_places():
    section, zh, core, partner, sibling = sections()
    zh_plus = lax.rem(zh + section, 2)
    plus = {"section": 1 - section, "dp": zh_plus * 2 + core}
    minus = {"section": 1 - section, "dp": (1 - zh_plus) * 2 + core}
    return section, zh, core, sibling, zh_plus, plus, minus


PACK_COPIES = 8


def pack_scratch(rows, cols):
    half, quarter = rows // 2, rows // 4
    return [
        pltpu.VMEM((2, half, cols), BF16),
        pltpu.VMEM((2, half, cols), BF16),
        pltpu.VMEM((2, quarter, cols), BF16),
        pltpu.VMEM((2, quarter, cols), BF16),
        pltpu.VMEM((half, cols), BF16),
    ]


def pause(n):
    for _ in range(n):
        yield


def pack_sum(links, grad, out, scratch):
    work, core_land, side, passing, over = scratch
    section, zh, core, sibling, zh_plus, plus, minus = pack_places()
    other = 1 - section
    half = grad.shape[1] // 2
    quarter = half // 2
    first = links.start(grad.at[:, pl.ds((1 - core) * half, half)], core_land, sibling)
    yield from pause(PAUSES[0])
    first.wait_recv()
    work[...] = (
        grad[:, pl.ds(core * half, half)].astype(F32) + core_land[...].astype(F32)
    ).astype(BF16)
    second = [
        links.start(work.at[other, pl.ds(h * quarter, quarter)], side.at[n], d)
        for n, (h, d) in enumerate(((zh_plus, plus), (1 - zh_plus, minus)))
    ]
    yield from pause(PAUSES[1])
    for copy in second:
        copy.wait_recv()
    mine = work.at[section, pl.ds(zh * quarter, quarter)]
    mine[...] = (mine[...].astype(F32) + side[0].astype(F32) + side[1].astype(F32)).astype(BF16)
    third = [
        links.start(work.at[section, pl.ds(n * quarter, quarter)], passing.at[n], d)
        for n, d in enumerate((plus, minus))
    ]
    yield from pause(PAUSES[2])
    fourth = []
    for n, device in enumerate((plus, minus)):
        third[n].wait_recv()
        fourth.append(links.start(passing.at[n], over.at[pl.ds(n * quarter, quarter)], device))
    yield from pause(PAUSES[3])
    for copy in fourth:
        copy.wait_recv()
    out[core] = (work[section].astype(F32) + over[...].astype(F32)).astype(BF16)
    last = links.start(out.at[core], out.at[core], sibling)
    yield from pause(PAUSES[4])
    last.wait_recv()
    links.finish()


def gather_small(links, place, buf, rows):
    y, x = place
    buf[y, x] = fold(rows).astype(BF16)
    links.finish(AT_SMALL + DEVICES - 1)
    copies = []
    for d in FAR_FIRST:
        target = device_at(moved(place, d // SIDE, d % SIDE))
        copies.append(links.start(buf.at[y, x], buf.at[y, x], target))
    for copy in copies:
        copy.wait_recv()
    return unfold_all(buf[...])


def sum_small(links, place, work, land, part):
    work[...] = fold_all(part)
    links.finish(AT_SMALL + 0)
    copies = []
    for n, d in enumerate(FAR_FIRST):
        there = moved(place, d // SIDE, d % SIDE)
        copies.append(links.start(work.at[there[0], there[1]], land.at[n], device_at(there)))
    total = work[place[0], place[1]].astype(F32)
    for copy in copies:
        copy.wait_recv()
    return unfold(total + jnp.sum(land[...].astype(F32), 0))


def stacked(ref, place, group, low=0, rows=None):
    rows = ref.shape[2] if rows is None else rows
    blocks = []
    for dy, dx in group:
        y, x = moved(place, dy, dx)
        blocks.append(ref[y, x, low : low + rows])
    return blocks[0] if len(blocks) == 1 else jnp.concatenate(blocks, 0)


def store_blocks(ref, place, group, values, low=0):
    rows = values.shape[0] // len(group)
    for n, (dy, dx) in enumerate(group):
        y, x = moved(place, dy, dx)
        ref[y, x, low : low + rows] = values[n * rows : (n + 1) * rows]


def whole(ref):
    return ref[...].reshape(DEVICES * ref.shape[2], ref.shape[3])


def wide(scale):
    return jnp.broadcast_to(scale, (scale.shape[0], 128))


def first_part(
    tokens, dec_tokens, seg_d, wt_in, gain_in, shift_in, wt, gs, full_h0, h0, unit0, scale0, *rest
):
    (full_y, q, k, v, sq, sk, sv, att_d, log_d, xbuf, ybuf, gs_in, send, recv) = rest
    place = at_grid()
    section, _, core, partner, sibling = sections()
    links, extra = Links(send, recv, AT_GATHER[1]), Links(send, recv, AT_FIRST)
    half = wt_in.shape[0] // 2
    mine = pl.ds(core * half, half)
    x, y = tokens.at[section], dec_tokens.at[section]
    for i in range(3):
        gs_in[i : i + 1, :] = gain_in[i]
        gs_in[3 + i : 4 + i, :] = shift_in[i]
    gs_in[6:8, :] = jnp.zeros((2, x.shape[1]), F32)
    gains_copy = extra.start(gs_in, gs.at[section], partner)
    xbuf[place[0], place[1]] = x[...]
    ybuf[place[0], place[1]] = fold(y[...].astype(F32)).astype(BF16)
    passed = []

    def ready(group):
        if group == [(0, 0)]:
            passed.append(extra.start(wt_in.at[mine], wt.at[section, mine], partner))
            gs[section] = gs_in[...]
            wt[section] = wt_in[...]
            gains_copy.wait_recv()
        if group == [(1, 1), (1, 3), (3, 1), (3, 3)]:
            passed[0].wait_recv()
            theirs = wt.at[1 - section, mine]
            passed.append(extra.start(theirs, theirs, sibling))
        unit, scale = norm_parts(stacked(xbuf, place, group).astype(F32))
        rows = unit * gs[0, 0:1, :] + gs[0, 3:4, :]
        if group == [(0, 0)]:
            h0[...] = rows
            unit0[...] = unit
            scale0[...] = wide(scale)
        store_blocks(full_h0, place, group, rows.astype(BF16))

    views = [(xbuf, 0, x.shape[0]), (ybuf, 0, ybuf.shape[2])]
    run([gather(links, place, views, ready)])
    passed[1].wait_recv()
    count, width = x.shape
    for i in range(SIDE):
        rows = full_h0[i].reshape(SIDE * count, width)
        made = dot_t(rows, wt[0, 0 : 3 * HEAD, :]).astype(BF16)
        for j, ref in enumerate((q, k, v)):
            ref[i] = made[:, j * HEAD : (j + 1) * HEAD].reshape(SIDE, count, HEAD)
    rows = unfold_all(ybuf[...])
    full_y[...] = rows
    made = dot_t(rows, wt[1, 0 : 3 * HEAD, :]).astype(BF16)
    for j, ref in enumerate((sq, sk, sv)):
        ref[...] = made[:, j * HEAD : (j + 1) * HEAD]
    row = own_row(seg_d)
    att, log_total = attend(sq[...], sk[...], sv[...], before(row))
    att_d[...] = att
    log_d[...] = wide(log_total)
    links.finish()
    extra.finish()


def before(row):
    count = row.shape[1]
    place = [lax.broadcasted_iota(jnp.int32, (count, count), i) for i in range(2)]
    return (column(row)[:, 0:1] == row) & (place[1] <= place[0])


def forward_part(q, k, v, seg_e, att_d, h0, dec_tokens, wt, gs, ffn_in, *rest):
    (ffn, full_h1, full_m, full_d1, hidden, slope, kvc, cq, d1) = rest[:9]
    (unit1, scale1, unit2, scale2, dunit0, dscale0, att_e, log_e, seg_col) = rest[9:18]
    (part, dpart, land_1, land_2, land_d, d1buf, send, recv) = rest[18:]
    place = at_grid()
    section, _, core, partner, sibling = sections()
    y = dec_tokens.at[section]
    row = own_row(seg_e)
    seg_col[...] = column(row).reshape(seg_col.shape)
    shared = Links(send, recv, AT_FFN)
    passed = [shared.start(ffn_in.at[core], ffn.at[section, core], partner)]

    def chain(links, low, rows, with_dec):
        here = pl.ds(low, rows)
        at_sum, at_gather = AT_SUM[with_dec], AT_GATHER[with_dec]
        links.used = at_sum

        def attended(group):
            allowed = stacked(seg_col, place, group, low, rows)[:, 0:1] == row
            queries = stacked(q, place, group, low, rows)
            att, log_total = attend(queries, whole(k), whole(v), allowed)
            store_blocks(att_e, place, group, att, low)
            store_blocks(log_e, place, group, wide(log_total), low)
            made = dot(att, wt[0, 3 * HEAD : 4 * HEAD, :])
            store_blocks(part, place, group, made.astype(BF16), low)
            if with_dec and group == PRODUCE[0]:
                dpart[...] = fold_all(dot(att_d[...], wt[1, 3 * HEAD : 4 * HEAD, :]))
            if low == 0 and group == PRODUCE[1]:
                ffn[section] = ffn_in[...]

        views = [(part, land_1, low, rows)]
        if with_dec:
            views.append((dpart, land_d, 0, dpart.shape[2]))
        sums = yield from sum_blocks(links, place, views, attended)
        unit, scale = norm_parts(h0[here] + sums[0])
        unit1[here] = unit
        scale1[here] = wide(scale)
        h1 = unit * gs[0, 1:2, :] + gs[0, 4:5, :]
        full_h1[place[0], place[1], here] = h1.astype(BF16)
        views = [(full_h1, low, rows)]
        if with_dec:
            unit, scale = norm_parts(y[...].astype(F32) + unfold(sums[1]))
            dunit0[...] = unit
            dscale0[...] = wide(scale)
            made = unit * gs[1, 0:1, :] + gs[1, 3:4, :]
            d1[...] = made
            d1buf[place[0], place[1]] = fold(made).astype(BF16)
            views.append((d1buf, 0, d1buf.shape[2]))
        if low == 0:
            passed[0].wait_recv()
            theirs = ffn.at[1 - section, core]
            passed.append(shared.start(theirs, theirs, sibling))

        def up(group):
            if group == [(0, 0)]:
                return
            if group == [(0, 1), (0, 3), (1, 0), (3, 0)]:
                if low == 0:
                    passed[1].wait_recv()
                group = [(0, 0)] + group
            made, back = gelu_parts(dot(stacked(full_h1, place, group, low, rows), ffn[0, 0]))
            store_blocks(hidden, place, group, made.astype(BF16), low)
            store_blocks(slope, place, group, back, low)

        links.used = at_gather
        yield from gather(links, place, views, up)
        links.finish(at_sum)
        if with_dec:
            made = unfold_all(d1buf[...])
            full_d1[...] = made
            cq[...] = dot_t(made, wt[1, 4 * HEAD : 5 * HEAD, :]).astype(BF16)

        def down(group):
            made = dot_t(stacked(hidden, place, group, low, rows), ffn[0, 1])
            store_blocks(part, place, group, made.astype(BF16), low)

        sums = yield from sum_blocks(links, place, [(part, land_2, low, rows)], down)
        unit, scale = norm_parts(h1 + sums[0])
        unit2[here] = unit
        scale2[here] = wide(scale)
        full_m[place[0], place[1], here] = (unit * gs[0, 2:3, :] + gs[0, 5:6, :]).astype(BF16)

        def cross(group):
            made = dot_t(stacked(full_m, place, group, low, rows), wt[0, 4 * HEAD : 6 * HEAD, :])
            store_blocks(kvc, place, group, made.astype(BF16), low)

        links.used = at_gather
        yield from gather(links, place, [(full_m, low, rows)], cross)
        links.finish()

    chains = []
    for n, (low, rows) in enumerate(CHUNKS):
        links = Links(send, recv)
        chains.append(chain(links, low, rows, n == len(CHUNKS) - 1))
    run(chains, LAG)
    shared.finish()


def decoder_part(cq, kvc, d1, cot, seg_d, seg_e, wt, ffn, gs, *rest):
    (d3, dback1, full_d2, full_db2, full_db1, hid_out, pre_out, att_out) = rest[:8]
    (cq_grad, kvc_grad, grads, g_bufs, s_work, s_land, probs, send, recv) = rest[8:]
    place = at_grid()
    links = Links(send, recv, AT_SMALL)
    w5 = wt[1, 5 * HEAD : 6 * HEAD, :]
    both = whole(kvc)
    kc, vc = both[:, :HEAD], both[:, HEAD:]
    allowed = column(own_row(seg_d))[:, 0:1] == own_row(seg_e)
    scores = scores_of(cq[...], kc, allowed)
    exponent = jnp.exp(scores - jnp.max(scores, -1, keepdims=True))
    probs[...] = exponent / jnp.sum(exponent, -1, keepdims=True)
    att = dot(probs[...].astype(BF16), vc).astype(BF16)
    att_out[...] = att
    part = sum_small(links, place, s_work.at[0], s_land.at[0], dot(att, w5))
    unit1, scale1 = norm_parts(d1[...] + part)
    d2 = unit1 * gs[1, 1:2, :] + gs[1, 4:5, :]
    full = gather_small(links, place, g_bufs.at[0], d2)
    full_d2[...] = full
    hidden, slope = gelu_parts(dot(full, ffn[1, 0]))
    hidden = hidden.astype(BF16)
    hid_out[...] = hidden
    part = sum_small(links, place, s_work.at[1], s_land.at[1], dot_t(hidden, ffn[1, 1]))
    unit2, scale2 = norm_parts(d2 + part)
    d3[...] = unit2 * gs[1, 2:3, :] + gs[1, 5:6, :]
    back2, gain2, shift2 = norm_back(cot[lax.axis_index("section")].astype(F32), unit2, scale2, gs[1, 2:3, :])
    full = gather_small(links, place, g_bufs.at[1], back2)
    full_db2[...] = full
    pre = (dot(full, ffn[1, 1]) * slope).astype(BF16)
    pre_out[...] = pre
    part = sum_small(links, place, s_work.at[2], s_land.at[2], dot_t(pre, ffn[1, 0]))
    back1, gain1, shift1 = norm_back(back2 + part, unit1, scale1, gs[1, 1:2, :])
    dback1[...] = back1
    full = gather_small(links, place, g_bufs.at[2], back1)
    full_db1[...] = full
    att_grad = dot_t(full, w5).astype(BF16)
    p = probs[...]
    value_grad = t_dot(att_grad, p.astype(BF16))
    p_grad = dot_t(att_grad, vc)
    s_grad = (p * (p_grad - jnp.sum(p * p_grad, -1, keepdims=True))).astype(BF16)
    cq_grad[...] = (dot(s_grad, kc) * SCALE).astype(BF16)
    key_grad = t_dot(cq[...], s_grad) * SCALE
    both = jnp.concatenate([key_grad, value_grad], 0).T.astype(BF16)
    kvc_grad[...] = both.reshape(kvc_grad.shape)
    grads[0:1, :] = gain1
    grads[1:2, :] = gain2
    grads[2:3, :] = shift1
    grads[3:4, :] = shift2
    grads[4:8, :] = jnp.zeros((4, grads.shape[1]), F32)
    links.finish()


def backward_part(*refs):
    (kvc_grad, cq_grad, dback1, wt, gs, ffn, unit1, scale1, unit2, scale2) = refs[:10]
    (dunit0, dscale0, slope, sq, sk, sv, log_d, seg_d, full_h1, hidden) = refs[10:20]
    (full_m, full_d1, full_y, full_d2, full_db1, full_db2, dpre, dhidden) = refs[20:28]
    (att_c, att_d, q, k, v, seg_e, seg_col, log_e) = refs[28:36]
    (full_b1, qkv_grad, kv_sum, back1, dec_grad, grads, ffn_sum, wt_grad) = refs[36:44]
    (full_b2, pre, part, dpart_1, dpart_2, land_1, land_2, dland_1, dland_2, dbuf) = refs[44:54]
    (ffn_grad, *pack_refs, send, recv) = refs[54:]
    kv_sum[...] = jnp.zeros(kv_sum.shape, F32)
    row = own_row(seg_e)
    place = at_grid()

    def chain(links, low, rows, with_dec):
        here = pl.ds(low, rows)
        at_sum, at_gather = AT_SUM[with_dec], AT_GATHER[with_dec]
        links.used = at_sum

        def cross(group):
            made = dot(stacked(kvc_grad, place, group, low, rows), wt[0, 4 * HEAD : 6 * HEAD, :])
            store_blocks(part, place, group, made.astype(BF16), low)
            if with_dec and group == PRODUCE[0]:
                dpart_1[...] = fold_all(dot(cq_grad[...], wt[1, 4 * HEAD : 5 * HEAD, :]))

        views = [(part, land_1, low, rows)]
        if with_dec:
            views.append((dpart_1, dland_1, 0, dpart_1.shape[2]))
        sums = yield from sum_blocks(links, place, views, cross)
        back2, gain2, shift2 = norm_back(sums[0], unit2[here], scale2[here, 0:1], gs[0, 2:3, :])
        full_b2[place[0], place[1], here] = back2.astype(BF16)
        views = [(full_b2, low, rows)]
        if with_dec:
            dback0, dgain0, dshift0 = norm_back(
                dback1[...] + unfold(sums[1]), dunit0[...], dscale0[:, 0:1], gs[1, 0:1, :]
            )
            dbuf[place[0], place[1]] = fold(dback0).astype(BF16)
            views.append((dbuf, 0, dbuf.shape[2]))

        def down(group):
            made = dot(stacked(full_b2, place, group, low, rows), ffn[0, 1])
            made = made * stacked(slope, place, group, low, rows)
            store_blocks(pre, place, group, made.astype(BF16), low)

        links.used = at_gather
        yield from gather(links, place, views, down)
        links.finish(at_sum)
        ready_rows.append(rows)
        views = [(part, land_2, low, rows)]
        if with_dec:
            full_db0 = unfold_all(dbuf[...])
            att_d_grad = dot_t(full_db0, wt[1, 3 * HEAD : 4 * HEAD, :]).astype(BF16)
            made = attend_back(
                sq[...], sk[...], sv[...], log_d[:, 0:1], before(own_row(seg_d)), att_d_grad
            )
            made = jnp.concatenate([made[0], made[1].T, made[2].T], 1).astype(BF16)
            late.extend([made, full_db0])
            dpart_2[...] = fold_all(dot(made, wt[1, 0 : 3 * HEAD, :]))
            views.append((dpart_2, dland_2, 0, dpart_2.shape[2]))

        def up(group):
            made = dot_t(stacked(pre, place, group, low, rows), ffn[0, 0])
            store_blocks(part, place, group, made.astype(BF16), low)

        sums = yield from sum_blocks(links, place, views, up)
        made, gain1, shift1 = norm_back(
            back2 + sums[0], unit1[here], scale1[here, 0:1], gs[0, 1:2, :]
        )
        back1[here] = made
        full_b1[place[0], place[1], here] = made.astype(BF16)
        totals.append((gain1, gain2, shift1, shift2))
        if with_dec:
            dec_grad[...] = dback0 + unfold(sums[1])
            grads[4:5, :] = dgain0
            grads[5:6, :] = dshift0

        pending = []

        def mixed(group):
            pending.extend(group)
            if group not in AT_ONCE:
                return
            some = lambda ref: stacked(ref, place, pending, low, rows)
            att_grad = dot_t(some(full_b1), wt[0, 3 * HEAD : 4 * HEAD, :]).astype(BF16)
            made = attend_back(
                some(q), whole(k), whole(v), some(log_e)[:, 0:1], some(seg_col)[:, 0:1] == row, att_grad
            )
            for n, (dy, dx) in enumerate(pending):
                at_y, at_x = moved(place, dy, dx)
                block = made[0][n * rows : (n + 1) * rows].astype(BF16)
                qkv_grad[at_y, at_x, here, 0:HEAD] = block
            kv_sum[...] += jnp.concatenate(made[1:], 0)
            pending.clear()

        links.used = at_gather
        yield from gather(links, place, [(full_b1, low, rows)], mixed)
        links.finish()

    def weight_chain(links):
        def put(layer, first, rows):
            wt_grad[layer, first * HEAD : first * HEAD + rows.shape[0], :] = rows.astype(BF16)

        count = full_h1.shape[3]
        yield
        put(0, 4, t_dot(whole(kvc_grad), whole(full_m)))
        ffn_grad[1, :count] = t_dot(dpre[...], full_d2[...]).T.astype(BF16)
        yield
        ffn_grad[1, count:] = t_dot(dhidden[...], full_db2[...]).T.astype(BF16)
        put(1, 4, t_dot(cq_grad[...], full_d1[...]))
        put(1, 5, t_dot(att_c[...], full_db1[...]))
        while len(ready_rows) < len(CHUNKS):
            yield
        ffn_grad[0, :count] = t_dot(whole(pre), whole(full_h1)).T.astype(BF16)
        yield
        ffn_grad[0, count:] = t_dot(whole(hidden), whole(full_b2)).T.astype(BF16)
        adding = pack_sum(links, ffn_grad, ffn_sum, pack_refs)
        next(adding)
        put(1, 0, t_dot(late[0], full_y[...]))
        put(1, 3, t_dot(att_d[...], late[1]))
        yield
        yield from adding

    late = []
    totals, chains, ready_rows = [], [], []
    for n, (low, rows) in enumerate(CHUNKS):
        links = Links(send, recv)
        chains.append(chain(links, low, rows, n == len(CHUNKS) - 1))
    background = weight_chain(Links(send, recv, AT_FFN_PACK))
    run(chains, LAG, background)
    for i in range(4):
        grads[i : i + 1, :] = sum(total[i] for total in totals)
    grads[6:8, :] = jnp.zeros((2, grads.shape[1]), F32)
    return background


def last_part(background, kv_sum, qkv_grad, att_e, full_b1, full_h0, *refs):
    (wt, gs, back1, unit0, scale0, wt_grad, small_b, small_d, out3, dec, *rest) = refs
    (att_out, small_out, enc_out, out3_out, dec_out, part, land, *pack_refs) = rest[:12]
    (fin, core_s, y_s, x_s, z_s, late, late_t, late_p) = rest[12:20]
    (enc, give_e, give_d, land_e, land_d, att, small, send, recv) = rest[20:]
    place = at_grid()
    section, zh, core, sibling, _, plus, minus = pack_places()
    other = 1 - section
    partner = {"section": other}
    far = {"dp": (1 - zh) * 2 + core}
    columns = [device_at(moved(place, d, 0)) for d in (1, 2, 3)]
    rows = [device_at(moved(place, 0, d)) for d in (1, 2, 3)]
    tensor, packs = tensor_peers(place), pack_peers()
    width = enc.shape[1] // 2
    there = pl.ds(pl.multiple_of(other * width, width), width)
    here = pl.ds(pl.multiple_of(section * width, width), width)

    small[...] = jnp.zeros(small.shape, F32)
    for layer, to, source, frm in (
        (0, 1, small_b, 0), (0, 2, small_b, 1), (0, 4, small_b, 2), (0, 5, small_b, 3),
        (1, 0, small_b, 4), (1, 3, small_b, 5),
        (1, 1, small_d, 0), (1, 2, small_d, 1), (1, 4, small_d, 2), (1, 5, small_d, 3),
    ):
        small[layer, to : to + 1, :] = source[frm : frm + 1, :]

    def early(links):
        give_d[...] = jnp.concatenate([out3[:, there], dec[:, there]], 0).astype(BF16)
        swap = links.start(give_d, land_d, partner)
        one = links.start(small.at[1 - core], core_s, sibling)
        yield
        one.wait_recv()
        fin[core] = small[core] + core_s[...]
        for land_s, devices in ((y_s, columns), (x_s, rows), (z_s, [plus, minus, far])):
            copies = [links.start(fin.at[core], land_s.at[n], d) for n, d in enumerate(devices)]
            yield
            for copy in copies:
                copy.wait_recv()
            links.finish()
            fin[core] = fin[core] + land_s[0] + land_s[1] + land_s[2]
        five = links.start(fin.at[core], fin.at[core], sibling)
        yield
        five.wait_recv()
        swap.wait_recv()
        links.finish()

    def heads(group):
        made = dot(stacked(qkv_grad, place, group), wt[0, 0 : 3 * HEAD, :])
        store_blocks(part, place, group, made.astype(BF16))

    def weights(links):
        att[1] = wt_grad[1]
        att[0, 4 * HEAD : 6 * HEAD, :] = wt_grad[0, 4 * HEAD : 6 * HEAD, :]
        made = t_dot(whole(qkv_grad), whole(full_h0))
        att[0, 0 : 3 * HEAD, :] = made.astype(BF16)
        att[0, 3 * HEAD : 4 * HEAD, :] = t_dot(whole(att_e), whole(full_b1)).astype(BF16)
        yield from pack_sum(links, att, att_out, pack_refs)

    both = kv_sum[...].T.astype(BF16)
    rows_each = qkv_grad.shape[2]
    qkv_grad[:, :, :, HEAD : 3 * HEAD] = both.reshape(SIDE, SIDE, rows_each, 2 * HEAD)

    def rest_of(links):
        (sum_e,) = yield from sum_blocks(links, place, [(part, land, 0, enc.shape[0])], heads)
        made, gain0, shift0 = norm_back(
            back1[...] + sum_e, unit0[...], scale0[:, 0:1], gs[0, 0:1, :]
        )
        enc[...] = made
        quarter = width // 2
        both = [row[:, i * quarter : (i + 1) * quarter] for row in (gain0, shift0) for i in range(4)]
        late[...] = jnp.concatenate(both, 0)
        links.used = AT_LATE
        copies = [links.start(late, late_t.at[n], d) for n, d in enumerate(tensor)]
        give_e[...] = enc[:, there].astype(BF16)
        swap = links.start(give_e, land_e, partner)
        yield
        for copy in copies:
            copy.wait_recv()
        links.finish()
        late[...] = late[...] + jnp.sum(late_t[...], 0)
        copies = [links.start(late, late_p.at[n], d) for n, d in enumerate(packs)]
        enc_out[section] = enc[:, here]
        yield
        for copy in copies:
            copy.wait_recv()
        swap.wait_recv()
        links.finish()

    chains = [
        early(Links(send, recv, AT_EARLY)),
        rest_of(Links(send, recv, AT_SUM[0])),
        weights(Links(send, recv, AT_ATT_PACK)),
        background,
    ]
    run(chains)
    enc_out[other] = land_e[...].astype(F32)
    got = land_d[...].astype(F32)
    count = out3.shape[0]
    out3_out[section] = out3[:, here]
    out3_out[other] = got[:count]
    dec_out[section] = dec[:, here]
    dec_out[other] = got[count:]
    small_out[...] = fin[section]
    total = late[...] + jnp.sum(late_p[...], 0)
    quarter = width // 2
    for i in range(8):
        row = 0 if i < 4 else 3
        cols = slice((i % 4) * quarter, (i % 4 + 1) * quarter)
        added = jnp.where(section == 0, total[i : i + 1], 0.0)
        small_out[row : row + 1, cols] = small_out[row : row + 1, cols] + added


def layers_kernel(names, *refs):
    r = types.SimpleNamespace(**dict(zip(names, refs)))
    more = refs[len(names) :]
    ffn_pack, att_pack, copies = more[:5], more[5:10], more[10:]
    place = at_grid()
    greet(tensor_peers(place) + pack_peers())

    first_part(
        r.tokens, r.dec_tokens, r.seg_d, r.wt_in, r.gain_in, r.shift_in, r.wt, r.gs, r.full_h0, r.h0, r.unit0, r.scale0,
        r.full_y, r.q, r.k, r.v, r.sq, r.sk, r.sv, r.att_d, r.log_d, r.part, r.dbuf_0, r.gs_in, *copies,
    )
    forward_part(
        r.q, r.k, r.v, r.seg_e, r.att_d, r.h0, r.dec_tokens, r.wt, r.gs, r.ffn_in,
        r.ffn, r.full_h1, r.full_m, r.full_d1, r.hidden, r.slope, r.kvc, r.cq, r.d1,
        r.unit1, r.scale1, r.unit2, r.scale2, r.dunit0, r.dscale0, r.att_e, r.log_e, r.seg_col,
        r.part, r.dpart_0, r.land_1, r.land_2, r.dland_0, r.dbuf_1, *copies,
    )
    decoder_part(
        r.cq, r.kvc, r.d1, r.cot, r.seg_d, r.seg_e, r.wt, r.ffn, r.gs,
        r.d3, r.dback1, r.full_d2, r.full_db2, r.full_db1, r.dhidden, r.dpre, r.att_c,
        r.cq_grad, r.kvc_grad, r.small_d, r.g_bufs, r.s_work, r.s_land, r.probs, *copies,
    )
    background = backward_part(
        r.kvc_grad, r.cq_grad, r.dback1, r.wt, r.gs, r.ffn, r.unit1, r.scale1, r.unit2, r.scale2,
        r.dunit0, r.dscale0, r.slope, r.sq, r.sk, r.sv, r.log_d, r.seg_d, r.full_h1, r.hidden,
        r.full_m, r.full_d1, r.full_y, r.full_d2, r.full_db1, r.full_db2, r.dpre, r.dhidden, r.att_c, r.att_d,
        r.q, r.k, r.v, r.seg_e, r.seg_col, r.log_e, r.full_b1, r.qkv_grad, r.kv_sum, r.back1, r.dec_grad, r.small_b, r.ffn_sum, r.wt_grad,
        r.full_b2, r.pre, r.part, r.dpart_1, r.dpart_2, r.land_1, r.land_2, r.dland_1, r.dland_2, r.dbuf_2,
        r.ffn_grad, *ffn_pack, *copies,
    )
    last_part(
        background, r.kv_sum, r.qkv_grad, r.att_e, r.full_b1, r.full_h0,
        r.wt, r.gs, r.back1, r.unit0, r.scale0, r.wt_grad, r.small_b, r.small_d, r.d3, r.dec_grad,
        r.att_out, r.small_out, r.enc_out, r.out3_out, r.dec_out,
        r.part, r.land_1, *att_pack,
        r.fin, r.core_s, r.y_s, r.x_s, r.z_s, r.late, r.late_t, r.late_p,
        r.enc, r.give_e, r.give_d, r.land_e, r.land_d, r.att, r.small, *copies,
    )


def layers_call(args, collective_id):
    tokens, dec_tokens, ffn = args["tokens"], args["dec_tokens"], args["ffn_in"]
    (_, rows, width), count, inner = tokens.shape, dec_tokens.shape[1], ffn.shape[2]
    half, full, grid = width // 2, count * DEVICES, (SIDE, SIDE)
    low, wide_rows, head = (*grid, rows, width), (*grid, rows, 128), (*grid, rows, HEAD)
    small_block = (*grid, 2 * count, half)
    outs = dict(
        att_out=((2, 3 * HEAD, width), BF16),
        small_out=((8, width), F32),
        enc_out=((2, rows, half), F32),
        out3_out=((2, count, half), F32),
        dec_out=((2, count, half), F32),
        ffn_sum=((2, width, inner), BF16),
    )
    kept = dict(
        wt=((2, 6 * HEAD, width), BF16),
        gs=((2, 8, width), F32),
        ffn=((2, 2, width, inner), BF16),
    )
    kept |= dict(full_h0=(low, BF16), full_h1=(low, BF16), full_m=(low, BF16), full_b1=(low, BF16), full_b2=(low, BF16), part=(low, BF16))
    kept |= dict(h0=((rows, width), F32), unit0=((rows, width), F32), unit1=((rows, width), F32), unit2=((rows, width), F32), back1=((rows, width), F32), enc=((rows, width), F32))
    kept |= dict(scale0=((rows, 128), F32), scale1=((rows, 128), F32), scale2=((rows, 128), F32))
    kept |= dict(full_y=((full, width), BF16), full_d1=((full, width), BF16), full_d2=((full, width), BF16), full_db1=((full, width), BF16), full_db2=((full, width), BF16))
    kept |= dict(q=(head, BF16), k=(head, BF16), v=(head, BF16), att_e=(head, BF16))
    kept |= dict(sq=((full, HEAD), BF16), sk=((full, HEAD), BF16), sv=((full, HEAD), BF16), att_d=((full, HEAD), BF16), cq=((full, HEAD), BF16), att_c=((full, HEAD), BF16), cq_grad=((full, HEAD), BF16))
    kept |= dict(d1=((8, width), F32), dunit0=((8, width), F32), d3=((8, width), F32), dback1=((8, width), F32), dec_grad=((8, width), F32), small_b=((8, width), F32), small_d=((8, width), F32), gs_in=((8, width), F32))
    kept |= dict(dbuf_0=(small_block, BF16), dbuf_1=(small_block, BF16), dbuf_2=(small_block, BF16), dpart_0=(small_block, BF16), dpart_1=(small_block, BF16), dpart_2=(small_block, BF16))
    kept |= dict(land_1=((30, rows, half), BF16), land_2=((30, rows, half), BF16))
    kept |= dict(dland_0=((30, 2 * count, half // 2), BF16), dland_1=((30, 2 * count, half // 2), BF16), dland_2=((30, 2 * count, half // 2), BF16))
    kept |= dict(hidden=((*grid, rows, inner), BF16), pre=((*grid, rows, inner), BF16))
    kept |= dict(kvc=((*grid, rows, 2 * HEAD), BF16), kvc_grad=((*grid, rows, 2 * HEAD), BF16))
    kept |= dict(dhidden=((full, inner), BF16), dpre=((full, inner), BF16))
    kept |= dict(wt_grad=((2, 6 * HEAD, width), BF16), att=((2, 6 * HEAD, width), BF16))
    kept |= dict(y_s=((3, 8, width), F32), x_s=((3, 8, width), F32), z_s=((3, 8, width), F32))
    kept |= dict(fin=((2, 8, width), F32), small=((2, 8, width), F32))
    kept |= dict(give_e=((rows, half), BF16), land_e=((rows, half), BF16))
    kept |= dict(give_d=((2 * count, half), BF16), land_d=((2 * count, half), BF16))
    kept |= dict(
        slope=((*grid, rows, inner), F32),
        log_e=(wide_rows, F32),
        seg_col=(wide_rows, F32),
        log_d=((full, 128), F32),
        dscale0=((count, 128), F32),
        g_bufs=((3, *small_block), BF16),
        s_work=((3, *small_block), BF16),
        s_land=((3, DEVICES - 1, 2 * count, half), BF16),
        probs=((full, DEVICES * rows), F32),
        ffn_grad=((2, 2 * width, inner), BF16),
        core_s=((8, width), F32),
        late=((8, width // 4), F32),
        late_t=((DEVICES - 1, 8, width // 4), F32),
        late_p=((7, 8, width // 4), F32),
        qkv_grad=((*grid, rows, 3 * HEAD), BF16),
        kv_sum=((2 * HEAD, DEVICES * rows), F32),
    )
    scratch = {name: pltpu.VMEM(dims, kind) for name, (dims, kind) in kept.items()}
    ffn_pack, att_pack = pack_scratch(2 * width, inner), pack_scratch(6 * HEAD, width)
    more = [*ffn_pack, *att_pack, *sems(ALL_COPIES)]
    return pl.pallas_call(
        functools.partial(layers_kernel, [*args, *outs, *scratch]),
        out_shape=[shape(*spec) for spec in outs.values()],
        in_specs=[VM] * len(args),
        out_specs=[VM] * len(outs),
        scratch_shapes=[*scratch.values(), *more],
        compiler_params=pltpu.CompilerParams(
            collective_id=collective_id, has_side_effects=True, vmem_limit_bytes=VMEM_BYTES
        ),
    )(*args.values())


def results_kernel(att, ffn, small, enc, out3, dec, *outs):
    (att_out, ffn_out, gain_out, shift_out, enc_out, out3_out, dec_out) = outs
    att_out[...] = att[...].astype(F32)
    ffn_out[...] = ffn[...].astype(F32)
    for i in range(3):
        gain_out[i] = small[i : i + 1, :]
        shift_out[i] = small[3 + i : 4 + i, :]
    enc_out[...] = enc[...]
    out3_out[...] = out3[...].astype(BF16)
    dec_out[...] = dec[...]


def results_call(att, ffn, small, enc, out3, dec):
    width = small.shape[1]
    return pl.pallas_call(
        results_kernel,
        out_shape=[
            shape(att.shape, F32),
            shape(ffn.shape, F32),
            shape((3, 1, width), F32),
            shape((3, 1, width), F32),
            shape(enc.shape, F32),
            shape(out3.shape, BF16),
            shape(dec.shape, F32),
        ],
        in_specs=[VM] * 6,
        out_specs=[VM] * 7,
        compiler_params=pltpu.CompilerParams(vmem_limit_bytes=VMEM_BYTES),
    )(att, ffn, small, enc, out3, dec)


def on_device(
    encoder_tokens,
    encoder_segments,
    decoder_tokens,
    decoder_segments,
    cotangent,
    attention_weight,
    feedforward_weight,
    norm_gain,
    norm_shift,
):
    width = encoder_tokens.shape[2]
    own_wt = jnp.swapaxes(attention_weight[0], 1, 2).reshape(6 * HEAD, width)
    args = dict(
        tokens=encoder_tokens,
        dec_tokens=decoder_tokens,
        cot=cotangent,
        seg_e=encoder_segments,
        seg_d=decoder_segments,
        wt_in=own_wt,
        gain_in=jnp.swapaxes(norm_gain, 0, 1),
        shift_in=jnp.swapaxes(norm_shift, 0, 1),
        ffn_in=feedforward_weight[0],
    )
    att_sum, small_sum, enc_out, d3_out, dec_out, ffn_sum = layers_call(args, 1)
    att_out, ffn_out, gain_out, shift_out, enc_out, d3_out, dec_out = results_call(
        att_sum, ffn_sum, small_sum, enc_out, d3_out, dec_out
    )
    return (
        d3_out,
        enc_out,
        dec_out,
        jnp.swapaxes(att_out.reshape(6, HEAD, width), 1, 2)[None],
        ffn_out.reshape(feedforward_weight.shape),
        jnp.swapaxes(gain_out, 0, 1),
        jnp.swapaxes(shift_out, 0, 1),
    )


def solution(mesh):
    in_specs = (
        P("dp", "tensor", None),
        P("dp", None),
        P("dp", "tensor", None),
        P("dp", None),
        P("dp", "tensor", None),
        P("section", None, None, "tensor"),
        P("section", None, None, "tensor"),
        P("section", None, None),
        P("section", None, None),
    )
    out_specs = (
        P("dp", "tensor", "section"),
        P("dp", "tensor", "section"),
        P("dp", "tensor", "section"),
        P("section", None, None, "tensor"),
        P("section", None, None, "tensor"),
        P("section", None, None),
        P("section", None, None),
    )
    return jax.shard_map(
        on_device, mesh=mesh, in_specs=in_specs, out_specs=out_specs, check_vma=False
    )
```

```python
import functools
import types

import jax
import jax.numpy as jnp
from jax import lax
from jax.experimental import pallas as pl
from jax.experimental.pallas import tpu as pltpu
from jax.sharding import PartitionSpec as P

HEAD = 64
EPSILON = 1e-05
MASKED = -1000000000.0
SCALE = HEAD ** (-0.5)
F32 = jnp.float32
BF16 = jnp.bfloat16
MESH = pl.DeviceIdType.MESH
VM = pl.BlockSpec(memory_space=pltpu.VMEM)
SIDE = 4
DEVICES = SIDE * SIDE
UP = (0, 2)
DOWN = (1, 3)
RING_COPIES = 30
CHUNKS = ((0, 48), (48, 32))
LAST_CHUNKS = ((0, 32), (32, 48))
PAUSES = (1, 1, 2, 1)
LAG = 0
VMEM_BYTES = 60 << 20
AT_FFN, AT_FIRST, AT_FFN_PACK, AT_ATT_PACK, AT_EARLY, AT_LATE, AT_SMALL = 0, 2, 5, 13, 21, 33, 55
AT_45_PACK = 266
AT_SUM, AT_GATHER, ALL_COPIES = (85, 146), (116, 206), 271
RING = True
INV_SQRT2 = 0.7071067811865476
INV_SQRT_2PI = 0.3989422804014327
FAR_FIRST = (10, 2, 8, 6, 14, 11, 9, 7, 13, 5, 15, 1, 3, 4, 12)


def norm_parts(values):
    center = values - jnp.mean(values, -1, keepdims=True)
    scale = lax.rsqrt(jnp.mean(center * center, -1, keepdims=True) + EPSILON)
    return center * scale, scale


def norm_back(grad, unit, scale, gains):
    inner = grad * gains
    back = scale * (
        inner
        - jnp.mean(inner, -1, keepdims=True)
        - unit * jnp.mean(inner * unit, -1, keepdims=True)
    )
    return back, jnp.sum(grad * unit, 0, keepdims=True), jnp.sum(grad, 0, keepdims=True)


def gelu_parts(u):
    cdf = 0.5 * (1.0 + lax.erf(u * INV_SQRT2))
    return u * cdf, cdf + u * (INV_SQRT_2PI * jnp.exp(-0.5 * u * u))


def dot(a, b):
    return jnp.dot(a, b, preferred_element_type=F32)


def dot_t(a, b):
    return lax.dot_general(a, b, (((1,), (1,)), ((), ())), preferred_element_type=F32)


def t_dot(a, b):
    return lax.dot_general(a, b, (((0,), (0,)), ((), ())), preferred_element_type=F32)


def scores_of(queries, key_rows, allowed):
    return jnp.where(allowed, dot_t(queries, key_rows) * SCALE, MASKED)


def attend(queries, key_rows, value_rows, allowed):
    scores = scores_of(queries, key_rows, allowed)
    row_max = jnp.max(scores, -1, keepdims=True)
    exponent = jnp.exp(scores - row_max)
    row_sum = jnp.sum(exponent, -1, keepdims=True)
    probs_low = (exponent / row_sum).astype(BF16)
    return dot(probs_low, value_rows).astype(BF16), row_max + jnp.log(row_sum)


def attend_back(queries, key_rows, value_rows, log_total, allowed, attended_grad):
    probs = jnp.exp(scores_of(queries, key_rows, allowed) - log_total)
    value_grad = t_dot(attended_grad, probs.astype(BF16))
    probs_grad = dot_t(attended_grad, value_rows)
    scores_grad = (probs * (probs_grad - jnp.sum(probs * probs_grad, -1, keepdims=True))).astype(
        BF16
    )
    return dot(scores_grad, key_rows) * SCALE, t_dot(queries, scores_grad) * SCALE, value_grad


def at_grid():
    index = lax.axis_index("tensor")
    return lax.div(index, SIDE), lax.rem(index, SIDE)


def moved(place, dy, dx):
    return lax.rem(place[0] + dy % SIDE, SIDE), lax.rem(place[1] + dx % SIDE, SIDE)


def along(axis, steps):
    return (steps, 0) if axis == 0 else (0, steps)


def device_at(place):
    return {"tensor": place[0] * SIDE + place[1]}


def tensor_peers(place):
    return [device_at(moved(place, d // SIDE, d % SIDE)) for d in FAR_FIRST]


def pack_peers():
    mine = lax.axis_index("section") * 4 + lax.axis_index("dp")
    others = [lax.rem(mine + d, 8) for d in range(1, 8)]
    return [{"section": lax.div(n, 4), "dp": lax.rem(n, 4)} for n in others]


def greet(devices):
    barrier = pltpu.get_barrier_semaphore()
    for device in devices:
        pl.semaphore_signal(barrier, inc=1, device_id=device, device_id_type=MESH)
    pl.semaphore_wait(barrier, len(devices))


def sections():
    section, dp = lax.axis_index("section"), lax.axis_index("dp")
    zh, core = lax.div(dp, 2), lax.rem(dp, 2)
    return section, zh, core, {"section": 1 - section}, {"dp": zh * 2 + 1 - core}


class Links:
    def __init__(self, send_sems, recv_sems, used=0):
        self.send, self.recv, self.used, self.started = send_sems, recv_sems, used, []

    def start(self, source, target, device):
        n = self.used
        self.used += 1
        copy = pltpu.make_async_remote_copy(
            src_ref=source,
            dst_ref=target,
            send_sem=self.send.at[n],
            recv_sem=self.recv.at[n],
            device_id=device,
            device_id_type=MESH,
        )
        copy.start()
        self.started.append(copy)
        return copy

    def finish(self, used=None):
        for copy in self.started:
            copy.wait_send()
        self.started = []
        self.used = self.used if used is None else used


def sems(n):
    return [pltpu.SemaphoreType.DMA((n,)), pltpu.SemaphoreType.DMA((n,))]


def shape(dims, kind):
    return jax.ShapeDtypeStruct(tuple(dims), kind)


def fold(rows):
    half = rows.shape[1] // 2
    return jnp.concatenate([rows[:, :half], rows[:, half:]], 0)


def unfold(rows):
    count = rows.shape[0] // 2
    return jnp.concatenate([rows[:count], rows[count:]], 1)


def unfold_all(blocks):
    count, half = blocks.shape[2] // 2, blocks.shape[3]
    split = blocks.astype(F32).reshape(DEVICES, 2, count, half)
    low = split[:, 0].reshape(DEVICES * count, half)
    high = split[:, 1].reshape(DEVICES * count, half)
    return jnp.concatenate([low, high], 1).astype(BF16)


def fold_all(part):
    count, half = part.shape[0] // DEVICES, part.shape[1] // 2
    split = part.reshape(DEVICES, count, 2 * half)
    both = jnp.concatenate([split[:, :, :half], split[:, :, half:]], 1)
    return both.astype(BF16).reshape(SIDE, SIDE, 2 * count, half)


def own_row(ref):
    return jnp.where(lax.axis_index("section") == 0, ref[0:1, :], ref[1:2, :]).astype(F32)


def column(row):
    return jnp.broadcast_to(row, (128, row.shape[1])).T


def gather(links, place, views, ready=None):
    jobs = []
    for buf, low, rows in views:
        half = buf.shape[-1] // 2
        for h in range(2):
            jobs.append((buf, 1 - h, h, h * half, half, pl.ds(low, rows)))
    ready = ready or (lambda group: None)

    def send(job, axis, steps, r, s):
        buf, a, b, start, size, rows = job
        y, x = moved(moved(place, *along(a, r)), *along(b, s))
        ref = buf.at[y, x, rows, pl.ds(start, size)]
        return links.start(ref, ref, device_at(moved(place, *along(axis, steps))))

    first, spread, ahead = [], [], []
    for job in jobs:
        first.append({-d % SIDE: send(job, job[1], d, 0, 0) for d in (1, 3, 2)})
    paths = ((1, 3), (3, 1)) if RING else ((2, 2), (1, 3), (3, 1))
    for job in jobs:
        spread.append({0: {s: send(job, job[2], d, 0, 0) for d, s in paths}})
    ready([(0, 0)])
    yield
    for r in (3, 1, 2):
        for i, job in enumerate(jobs):
            first[i][r].wait_recv()
            spread[i][r] = {s: send(job, job[2], d, r, 0) for d, s in paths}
    if RING:
        for i, job in enumerate(jobs):
            spread[i][0][3].wait_recv()
            ahead.append({0: send(job, job[2], 1, 0, 3)})
            spread[i][0][1].wait_recv()
    else:
        for i, job in enumerate(jobs):
            spread[i][0][3].wait_recv()
            spread[i][0][1].wait_recv()
            ahead.append({r: spread[i][r][2] for r in range(SIDE)})
    ready([(0, 1), (0, 3), (1, 0), (3, 0)])
    yield
    if RING:
        for r in DOWN:
            for i, job in enumerate(jobs):
                spread[i][r][1].wait_recv()
                ahead[i][r] = send(job, job[2], -1, r, 1)
        for i, job in enumerate(jobs):
            spread[i][2][3].wait_recv()
            ahead[i][2] = send(job, job[2], 1, 2, 3)
        for r in DOWN:
            for i, job in enumerate(jobs):
                spread[i][r][3].wait_recv()
    else:
        for r in DOWN:
            for i, job in enumerate(jobs):
                spread[i][r][1].wait_recv()
                spread[i][r][3].wait_recv()
    ready([(1, 1), (1, 3), (3, 1), (3, 3)])
    for i, job in enumerate(jobs):
        ahead[i][0].wait_recv()
    ready([(0, 2), (2, 0)])
    yield
    for i, job in enumerate(jobs):
        if not RING:
            spread[i][2][3].wait_recv()
        spread[i][2][1].wait_recv()
        ahead[i][1].wait_recv()
        ahead[i][3].wait_recv()
    ready([(1, 2), (3, 2), (2, 1), (2, 3)])
    for i, job in enumerate(jobs):
        ahead[i][2].wait_recv()
    ready([(2, 2)])


AT_ONCE = ([(0, 1), (0, 3), (1, 0), (3, 0)], [(0, 2), (2, 0)], [(2, 2)])
PRODUCE = (
    [(2, 2), (2, 3), (2, 1), (3, 2), (1, 2), (2, 0), (0, 2)],
    [(3, 3), (3, 1), (1, 3), (1, 1), (3, 0), (1, 0), (0, 3), (0, 1), (0, 0)],
)


def sum_blocks(links, place, views, produce=None):
    produce = produce or (lambda group: None)
    jobs = []
    for part, land, low, rows in views:
        half = part.shape[-1] // 2
        for h in range(2):
            jobs.append((part, land, 15 * h, 1 - h, h, h * half, half, pl.ds(low, rows)))

    def block(job, r, s):
        part, _, _, a, b, start, size, rows = job
        y, x = moved(moved(place, *along(a, r)), *along(b, s))
        return part.at[y, x, rows, pl.ds(start, size)]

    def landing(job, n):
        return job[1].at[job[2] + n, job[7]]

    def start(source, target, axis, steps):
        return links.start(source, target, device_at(moved(place, *along(axis, steps))))

    def add(target, *others):
        total = target[...].astype(F32)
        for other in others:
            total = total + other[...].astype(F32)
        return total

    def near_slot(job, r, steps):
        return landing(job, 4 + 2 * r + (0 if steps == 1 else 1))

    order = (2, 3, 1, 0)
    produce(PRODUCE[0])
    near = [{r: [] for r in order} for _ in jobs]
    if RING:
        far = []
        for job in jobs:
            far.append(
                {
                    r: start(block(job, r, 2), landing(job, r), job[4], 1 if r in UP else -1)
                    for r in order
                }
            )
        produce(PRODUCE[1])
        for i, job in enumerate(jobs):
            for r in order:
                steps = -1 if r in UP else 1
                near[i][r].append(
                    start(block(job, r, steps), near_slot(job, r, steps), job[4], steps)
                )
        yield
        for r in order:
            for i, job in enumerate(jobs):
                steps = 1 if r in UP else -1
                far[i][r].wait_recv()
                ref = block(job, r, steps)
                ref[...] = add(ref, landing(job, r)).astype(BF16)
                near[i][r].append(start(ref, near_slot(job, r, steps), job[4], steps))
    else:
        for s in (2, 1, 3):
            for r in order:
                for i, job in enumerate(jobs):
                    slot = landing(job, 4 * (s - 1) + r)
                    near[i][r].append(start(block(job, r, s), slot, job[4], s))
            if s == 2:
                produce(PRODUCE[1])
    yield
    last = [{} for _ in jobs]
    results = []
    for r in order:
        if r == 0:
            yield
        for i, job in enumerate(jobs):
            for copy in near[i][r]:
                copy.wait_recv()
            ref = block(job, r, 0)
            if RING:
                total = add(ref, landing(job, 4 + 2 * r), landing(job, 5 + 2 * r))
            else:
                total = add(ref, landing(job, r), landing(job, 4 + r), landing(job, 8 + r))
            if r == 0:
                results.append(total)
            else:
                ref[...] = total.astype(BF16)
                last[i][r] = start(ref, landing(job, 11 + r), job[3], r)
    for i, job in enumerate(jobs):
        for r in order[:3]:
            last[i][r].wait_recv()
            results[i] = results[i] + landing(job, 11 + r)[...].astype(F32)
    return [jnp.concatenate(results[i : i + 2], 1) for i in range(0, len(results), 2)]


def run(chains, lag=0, background=None):
    turn, active = 0, list(enumerate(chains))
    while active:
        for n, chain in list(active):
            if turn >= n * lag:
                try:
                    next(chain)
                except StopIteration:
                    active.remove((n, chain))
        if background is not None:
            next(background, None)
        turn += 1


def pack_places():
    section, zh, core, partner, sibling = sections()
    zh_plus = lax.rem(zh + section, 2)
    plus = {"section": 1 - section, "dp": zh_plus * 2 + core}
    minus = {"section": 1 - section, "dp": (1 - zh_plus) * 2 + core}
    return section, zh, core, sibling, zh_plus, plus, minus


PACK_COPIES = 8


def pack_scratch(rows, cols):
    half, quarter = rows // 2, rows // 4
    return [
        pltpu.VMEM((2, half, cols), BF16),
        pltpu.VMEM((2, half, cols), BF16),
        pltpu.VMEM((2, quarter, cols), BF16),
        pltpu.VMEM((half, cols), BF16),
    ]


def pause(n):
    for _ in range(n):
        yield


def pack_sum(links, grad, out, scratch):
    work, core_land, side, over = scratch
    section, zh, core, sibling, zh_plus, plus, minus = pack_places()
    other = 1 - section
    half = grad.shape[1] // 2
    quarter = half // 2
    first = links.start(grad.at[:, pl.ds((1 - core) * half, half)], core_land, sibling)
    yield from pause(PAUSES[0])
    first.wait_recv()
    work[...] = (
        grad[:, pl.ds(core * half, half)].astype(F32) + core_land[...].astype(F32)
    ).astype(BF16)
    second = [
        links.start(work.at[other, pl.ds(h * quarter, quarter)], side.at[n], d)
        for n, (h, d) in enumerate(((zh_plus, plus), (1 - zh_plus, minus)))
    ]
    yield from pause(PAUSES[1])
    for copy in second:
        copy.wait_recv()
    mine = work.at[section, pl.ds(zh * quarter, quarter)]
    mine[...] = (mine[...].astype(F32) + side[0].astype(F32) + side[1].astype(F32)).astype(BF16)
    third = links.start(work.at[section], over, {"dp": (1 - zh) * 2 + core})
    yield from pause(PAUSES[2])
    third.wait_recv()
    out[core] = (work[section].astype(F32) + over[...].astype(F32)).astype(BF16)
    last = links.start(out.at[core], out.at[core], sibling)
    yield from pause(PAUSES[3])
    last.wait_recv()
    links.finish()


def gather_small(links, place, buf, rows):
    y, x = place
    buf[y, x] = fold(rows).astype(BF16)
    links.finish(AT_SMALL + DEVICES - 1)
    copies = []
    for d in FAR_FIRST:
        target = device_at(moved(place, d // SIDE, d % SIDE))
        copies.append(links.start(buf.at[y, x], buf.at[y, x], target))
    for copy in copies:
        copy.wait_recv()
    return unfold_all(buf[...])


def sum_small(links, place, work, land, part, meanwhile=None):
    work[...] = fold_all(part)
    links.finish(AT_SMALL + 0)
    copies = []
    for n, d in enumerate(FAR_FIRST):
        there = moved(place, d // SIDE, d % SIDE)
        copies.append(links.start(work.at[there[0], there[1]], land.at[n], device_at(there)))
    if meanwhile is not None:
        meanwhile()
    total = work[place[0], place[1]].astype(F32)
    for copy in copies:
        copy.wait_recv()
    return unfold(total + jnp.sum(land[...].astype(F32), 0))


def stacked(ref, place, group, low=0, rows=None):
    rows = ref.shape[2] if rows is None else rows
    blocks = []
    for dy, dx in group:
        y, x = moved(place, dy, dx)
        blocks.append(ref[y, x, low : low + rows])
    return blocks[0] if len(blocks) == 1 else jnp.concatenate(blocks, 0)


def store_blocks(ref, place, group, values, low=0):
    rows = values.shape[0] // len(group)
    for n, (dy, dx) in enumerate(group):
        y, x = moved(place, dy, dx)
        ref[y, x, low : low + rows] = values[n * rows : (n + 1) * rows]


def whole(ref):
    return ref[...].reshape(DEVICES * ref.shape[2], ref.shape[3])


def wide(scale):
    return jnp.broadcast_to(scale, (scale.shape[0], 128))


def first_part(
    tokens, dec_tokens, wt_in, gain_in, shift_in, wt, gs, full_h0, h0, unit0, scale0, *rest
):
    (q, k, v, xbuf, ybuf, gs_in, send, recv) = rest
    place = at_grid()
    section, _, core, partner, sibling = sections()
    links, extra = Links(send, recv, AT_GATHER[1]), Links(send, recv, AT_FIRST)
    half = wt_in.shape[0] // 2
    mine = pl.ds(core * half, half)
    x, y = tokens.at[section], dec_tokens.at[section]
    for i in range(3):
        gs_in[i : i + 1, :] = gain_in[i]
        gs_in[3 + i : 4 + i, :] = shift_in[i]
    gs_in[6:8, :] = jnp.zeros((2, x.shape[1]), F32)
    gains_copy = extra.start(gs_in, gs.at[section], partner)
    xbuf[place[0], place[1]] = x[...]
    ybuf[place[0], place[1]] = fold(y[...].astype(F32)).astype(BF16)
    passed = []

    def ready(group):
        if group == [(0, 0)]:
            passed.append(extra.start(wt_in.at[mine], wt.at[section, mine], partner))
            gs[section] = gs_in[...]
            wt[section] = wt_in[...]
            gains_copy.wait_recv()
        if group == [(1, 1), (1, 3), (3, 1), (3, 3)]:
            passed[0].wait_recv()
            theirs = wt.at[1 - section, mine]
            passed.append(extra.start(theirs, theirs, sibling))
        unit, scale = norm_parts(stacked(xbuf, place, group).astype(F32))
        rows = unit * gs[0, 0:1, :] + gs[0, 3:4, :]
        if group == [(0, 0)]:
            h0[...] = rows
            unit0[...] = unit
            scale0[...] = wide(scale)
        store_blocks(full_h0, place, group, rows.astype(BF16))

    views = [(xbuf, 0, x.shape[0]), (ybuf, 0, ybuf.shape[2])]
    run([gather(links, place, views, ready)])
    passed[1].wait_recv()
    count, width = x.shape
    for i in range(SIDE):
        rows = full_h0[i].reshape(SIDE * count, width)
        made = dot_t(rows, wt[0, 0 : 3 * HEAD, :]).astype(BF16)
        for j, ref in enumerate((q, k, v)):
            ref[i] = made[:, j * HEAD : (j + 1) * HEAD].reshape(SIDE, count, HEAD)
    links.finish()
    extra.finish()


def before(row):
    count = row.shape[1]
    place = [lax.broadcasted_iota(jnp.int32, (count, count), i) for i in range(2)]
    return (column(row)[:, 0:1] == row) & (place[1] <= place[0])


def forward_part(q, k, v, seg_e, ybuf, seg_d, h0, dec_tokens, wt, gs, ffn_in, *rest):
    (full_y, sq, sk, sv, att_d, log_d, *rest) = rest
    (ffn, full_h1, full_m, full_d1, hidden, slope, kvc, cq, d1) = rest[:9]
    (unit1, scale1, unit2, scale2, dunit0, dscale0, att_e, log_e, seg_col) = rest[9:18]
    (part, dpart, land_1, land_2, land_d, d1buf, send, recv) = rest[18:]
    place = at_grid()
    section, _, core, partner, sibling = sections()
    y = dec_tokens.at[section]
    row = own_row(seg_e)
    seg_col[...] = column(row).reshape(seg_col.shape)
    shared = Links(send, recv, AT_FFN)
    passed = [shared.start(ffn_in.at[core], ffn.at[section, core], partner)]

    def self_attention():
        rows = unfold_all(ybuf[...])
        full_y[...] = rows
        made = dot_t(rows, wt[1, 0 : 3 * HEAD, :]).astype(BF16)
        for j, ref in enumerate((sq, sk, sv)):
            ref[...] = made[:, j * HEAD : (j + 1) * HEAD]
        att, log_total = attend(sq[...], sk[...], sv[...], before(own_row(seg_d)))
        att_d[...] = att
        log_d[...] = wide(log_total)

    def chain(links, low, rows, with_dec):
        here = pl.ds(low, rows)
        at_sum, at_gather = AT_SUM[with_dec], AT_GATHER[with_dec]
        links.used = at_sum

        def attended(group):
            allowed = stacked(seg_col, place, group, low, rows)[:, 0:1] == row
            queries = stacked(q, place, group, low, rows)
            att, log_total = attend(queries, whole(k), whole(v), allowed)
            store_blocks(att_e, place, group, att, low)
            store_blocks(log_e, place, group, wide(log_total), low)
            made = dot(att, wt[0, 3 * HEAD : 4 * HEAD, :])
            store_blocks(part, place, group, made.astype(BF16), low)
            if with_dec and group == PRODUCE[0]:
                self_attention()
                dpart[...] = fold_all(dot(att_d[...], wt[1, 3 * HEAD : 4 * HEAD, :]))
            if low == 0 and group == PRODUCE[1]:
                ffn[section] = ffn_in[...]

        views = [(part, land_1, low, rows)]
        if with_dec:
            views.append((dpart, land_d, 0, dpart.shape[2]))
        sums = yield from sum_blocks(links, place, views, attended)
        unit, scale = norm_parts(h0[here] + sums[0])
        unit1[here] = unit
        scale1[here] = wide(scale)
        h1 = unit * gs[0, 1:2, :] + gs[0, 4:5, :]
        full_h1[place[0], place[1], here] = h1.astype(BF16)
        views = [(full_h1, low, rows)]
        if with_dec:
            unit, scale = norm_parts(y[...].astype(F32) + unfold(sums[1]))
            dunit0[...] = unit
            dscale0[...] = wide(scale)
            made = unit * gs[1, 0:1, :] + gs[1, 3:4, :]
            d1[...] = made
            d1buf[place[0], place[1]] = fold(made).astype(BF16)
            views.append((d1buf, 0, d1buf.shape[2]))
        if low == 0:
            passed[0].wait_recv()
            theirs = ffn.at[1 - section, core]
            passed.append(shared.start(theirs, theirs, sibling))

        def up(group):
            if group == [(0, 0)]:
                return
            if group == [(0, 1), (0, 3), (1, 0), (3, 0)]:
                if low == 0:
                    passed[1].wait_recv()
                group = [(0, 0)] + group
            made, back = gelu_parts(dot(stacked(full_h1, place, group, low, rows), ffn[0, 0]))
            store_blocks(hidden, place, group, made.astype(BF16), low)
            store_blocks(slope, place, group, back, low)

        links.used = at_gather
        yield from gather(links, place, views, up)
        links.finish(at_sum)
        if with_dec:
            made = unfold_all(d1buf[...])
            full_d1[...] = made
            cq[...] = dot_t(made, wt[1, 4 * HEAD : 5 * HEAD, :]).astype(BF16)

        def down(group):
            made = dot_t(stacked(hidden, place, group, low, rows), ffn[0, 1])
            store_blocks(part, place, group, made.astype(BF16), low)

        sums = yield from sum_blocks(links, place, [(part, land_2, low, rows)], down)
        unit, scale = norm_parts(h1 + sums[0])
        unit2[here] = unit
        scale2[here] = wide(scale)
        full_m[place[0], place[1], here] = (unit * gs[0, 2:3, :] + gs[0, 5:6, :]).astype(BF16)

        def cross(group):
            made = dot_t(stacked(full_m, place, group, low, rows), wt[0, 4 * HEAD : 6 * HEAD, :])
            store_blocks(kvc, place, group, made.astype(BF16), low)

        links.used = at_gather
        yield from gather(links, place, [(full_m, low, rows)], cross)
        links.finish()

    chains = []
    for n, (low, rows) in enumerate(CHUNKS):
        links = Links(send, recv)
        chains.append(chain(links, low, rows, n == len(CHUNKS) - 1))
    run(chains, LAG)
    shared.finish()


def decoder_part(cq, kvc, d1, cot, seg_d, seg_e, wt, ffn, gs, *rest):
    (d3, dback1, full_d2, full_db2, full_db1, hid_out, pre_out, att_out) = rest[:8]
    (cq_grad, kvc_grad, grads, ffn_grad, g_bufs, s_work, s_land, probs, send, recv) = rest[8:]
    place = at_grid()
    links = Links(send, recv, AT_SMALL)
    w5 = wt[1, 5 * HEAD : 6 * HEAD, :]
    both = whole(kvc)
    kc, vc = both[:, :HEAD], both[:, HEAD:]
    allowed = column(own_row(seg_d))[:, 0:1] == own_row(seg_e)
    scores = scores_of(cq[...], kc, allowed)
    exponent = jnp.exp(scores - jnp.max(scores, -1, keepdims=True))
    probs[...] = exponent / jnp.sum(exponent, -1, keepdims=True)
    att = dot(probs[...].astype(BF16), vc).astype(BF16)
    att_out[...] = att
    part = sum_small(links, place, s_work.at[0], s_land.at[0], dot(att, w5))
    unit1, scale1 = norm_parts(d1[...] + part)
    d2 = unit1 * gs[1, 1:2, :] + gs[1, 4:5, :]
    full = gather_small(links, place, g_bufs.at[0], d2)
    full_d2[...] = full
    hidden, slope = gelu_parts(dot(full, ffn[1, 0]))
    hidden = hidden.astype(BF16)
    hid_out[...] = hidden
    part = sum_small(links, place, s_work.at[1], s_land.at[1], dot_t(hidden, ffn[1, 1]))
    unit2, scale2 = norm_parts(d2 + part)
    d3[...] = unit2 * gs[1, 2:3, :] + gs[1, 5:6, :]
    back2, gain2, shift2 = norm_back(cot[lax.axis_index("section")].astype(F32), unit2, scale2, gs[1, 2:3, :])
    full = gather_small(links, place, g_bufs.at[1], back2)
    full_db2[...] = full
    pre = (dot(full, ffn[1, 1]) * slope).astype(BF16)
    pre_out[...] = pre

    def weights():
        count = full_d2.shape[1]
        ffn_grad[1, :count] = t_dot(pre_out[...], full_d2[...]).T.astype(BF16)
        ffn_grad[1, count:] = t_dot(hid_out[...], full_db2[...]).T.astype(BF16)

    part = dot_t(pre, ffn[1, 0])
    part = sum_small(links, place, s_work.at[2], s_land.at[2], part, weights)
    back1, gain1, shift1 = norm_back(back2 + part, unit1, scale1, gs[1, 1:2, :])
    dback1[...] = back1
    full = gather_small(links, place, g_bufs.at[2], back1)
    full_db1[...] = full
    att_grad = dot_t(full, w5).astype(BF16)
    p = probs[...]
    value_grad = t_dot(att_grad, p.astype(BF16))
    p_grad = dot_t(att_grad, vc)
    s_grad = (p * (p_grad - jnp.sum(p * p_grad, -1, keepdims=True))).astype(BF16)
    cq_grad[...] = (dot(s_grad, kc) * SCALE).astype(BF16)
    key_grad = t_dot(cq[...], s_grad) * SCALE
    both = jnp.concatenate([key_grad, value_grad], 0).T.astype(BF16)
    kvc_grad[...] = both.reshape(kvc_grad.shape)
    grads[0:1, :] = gain1
    grads[1:2, :] = gain2
    grads[2:3, :] = shift1
    grads[3:4, :] = shift2
    grads[4:8, :] = jnp.zeros((4, grads.shape[1]), F32)
    links.finish()


def backward_part(*refs):
    (kvc_grad, cq_grad, dback1, wt, gs, ffn, unit1, scale1, unit2, scale2) = refs[:10]
    (dunit0, dscale0, slope, sq, sk, sv, log_d, seg_d, full_h1, hidden) = refs[10:20]
    (full_m, full_d1, full_y, full_db1) = refs[20:24]
    (att_c, att_d, q, k, v, seg_e, seg_col, log_e) = refs[24:32]
    (full_b1, qkv_grad, kv_sum, back1, dec_grad, grads, ffn_sum, att_45) = refs[32:40]
    wt_45, att = refs[40:42]
    (full_b2, pre, part, dpart_1, dpart_2, land_1, land_2, dland_1, dland_2, dbuf) = refs[42:52]
    (ffn_grad, *pack_refs, send, recv) = refs[52:]
    kv_sum[...] = jnp.zeros(kv_sum.shape, F32)
    row = own_row(seg_e)
    place = at_grid()

    def chain(links, low, rows, with_dec):
        here = pl.ds(low, rows)
        at_sum, at_gather = AT_SUM[with_dec], AT_GATHER[with_dec]
        links.used = at_sum

        def cross(group):
            made = dot(stacked(kvc_grad, place, group, low, rows), wt[0, 4 * HEAD : 6 * HEAD, :])
            store_blocks(part, place, group, made.astype(BF16), low)
            if with_dec and group == PRODUCE[0]:
                dpart_1[...] = fold_all(dot(cq_grad[...], wt[1, 4 * HEAD : 5 * HEAD, :]))

        views = [(part, land_1, low, rows)]
        if with_dec:
            views.append((dpart_1, dland_1, 0, dpart_1.shape[2]))
        sums = yield from sum_blocks(links, place, views, cross)
        back2, gain2, shift2 = norm_back(sums[0], unit2[here], scale2[here, 0:1], gs[0, 2:3, :])
        full_b2[place[0], place[1], here] = back2.astype(BF16)
        views = [(full_b2, low, rows)]
        if with_dec:
            dback0, dgain0, dshift0 = norm_back(
                dback1[...] + unfold(sums[1]), dunit0[...], dscale0[:, 0:1], gs[1, 0:1, :]
            )
            dbuf[place[0], place[1]] = fold(dback0).astype(BF16)
            views.append((dbuf, 0, dbuf.shape[2]))

        def down(group):
            made = dot(stacked(full_b2, place, group, low, rows), ffn[0, 1])
            made = made * stacked(slope, place, group, low, rows)
            store_blocks(pre, place, group, made.astype(BF16), low)

        links.used = at_gather
        yield from gather(links, place, views, down)
        links.finish(at_sum)
        ready_rows.append(rows)
        views = [(part, land_2, low, rows)]
        if with_dec:
            full_db0 = unfold_all(dbuf[...])
            att_d_grad = dot_t(full_db0, wt[1, 3 * HEAD : 4 * HEAD, :]).astype(BF16)
            made = attend_back(
                sq[...], sk[...], sv[...], log_d[:, 0:1], before(own_row(seg_d)), att_d_grad
            )
            made = jnp.concatenate([made[0], made[1].T, made[2].T], 1).astype(BF16)
            late.extend([made, full_db0])
            dpart_2[...] = fold_all(dot(made, wt[1, 0 : 3 * HEAD, :]))
            views.append((dpart_2, dland_2, 0, dpart_2.shape[2]))

        def up(group):
            made = dot_t(stacked(pre, place, group, low, rows), ffn[0, 0])
            store_blocks(part, place, group, made.astype(BF16), low)

        sums = yield from sum_blocks(links, place, views, up)
        made, gain1, shift1 = norm_back(
            back2 + sums[0], unit1[here], scale1[here, 0:1], gs[0, 1:2, :]
        )
        back1[here] = made
        full_b1[place[0], place[1], here] = made.astype(BF16)
        totals.append((gain1, gain2, shift1, shift2))
        if with_dec:
            dec_grad[...] = dback0 + unfold(sums[1])
            grads[4:5, :] = dgain0
            grads[5:6, :] = dshift0

        pending = []

        def mixed(group):
            pending.extend(group)
            if group not in AT_ONCE:
                return
            some = lambda ref: stacked(ref, place, pending, low, rows)
            att_grad = dot_t(some(full_b1), wt[0, 3 * HEAD : 4 * HEAD, :]).astype(BF16)
            made = attend_back(
                some(q), whole(k), whole(v), some(log_e)[:, 0:1], some(seg_col)[:, 0:1] == row, att_grad
            )
            for n, (dy, dx) in enumerate(pending):
                at_y, at_x = moved(place, dy, dx)
                block = made[0][n * rows : (n + 1) * rows].astype(BF16)
                qkv_grad[at_y, at_x, here, 0:HEAD] = block
            kv_sum[...] += jnp.concatenate(made[1:], 0)
            pending.clear()

        links.used = at_gather
        yield from gather(links, place, [(full_b1, low, rows)], mixed)
        links.finish()

    def weight_chain(links):
        def put(layer, first, rows):
            ref, first = (wt_45, first - 4) if first >= 4 else (att, first)
            ref[layer, first * HEAD : first * HEAD + rows.shape[0], :] = rows.astype(BF16)

        count = full_h1.shape[3]
        yield
        put(0, 4, t_dot(whole(kvc_grad), whole(full_m)))
        yield
        put(1, 4, t_dot(cq_grad[...], full_d1[...]))
        put(1, 5, t_dot(att_c[...], full_db1[...]))
        yield from pack_sum(Links(send, recv, AT_45_PACK), wt_45, att_45, pack_refs[4:])
        while len(ready_rows) < len(CHUNKS):
            yield
        ffn_grad[0, :count] = t_dot(whole(pre), whole(full_h1)).T.astype(BF16)
        yield
        ffn_grad[0, count:] = t_dot(whole(hidden), whole(full_b2)).T.astype(BF16)
        adding = pack_sum(links, ffn_grad, ffn_sum, pack_refs[:4])
        next(adding)
        put(1, 0, t_dot(late[0], full_y[...]))
        put(1, 3, t_dot(att_d[...], late[1]))
        yield
        yield from adding

    late = []
    totals, chains, ready_rows = [], [], []
    for n, (low, rows) in enumerate(CHUNKS):
        links = Links(send, recv)
        chains.append(chain(links, low, rows, n == len(CHUNKS) - 1))
    background = weight_chain(Links(send, recv, AT_FFN_PACK))
    run(chains, LAG, background)
    for i in range(4):
        grads[i : i + 1, :] = sum(total[i] for total in totals)
    grads[6:8, :] = jnp.zeros((2, grads.shape[1]), F32)
    return background


def last_part(background, kv_sum, qkv_grad, att_e, full_b1, full_h0, *refs):
    (wt, gs, back1, unit0, scale0, small_b, small_d, out3, dec, *rest) = refs
    (att_out, small_out, enc_out, out3_out, dec_out, part, land, *pack_refs) = rest[:11]
    (fin, core_s, y_s, x_s, z_s, late, late_t, late_p) = rest[11:19]
    (enc, give_e, give_d, land_e, land_d, att, small, send, recv) = rest[19:]
    place = at_grid()
    section, zh, core, sibling, _, plus, minus = pack_places()
    other = 1 - section
    partner = {"section": other}
    far = {"dp": (1 - zh) * 2 + core}
    columns = [device_at(moved(place, d, 0)) for d in (1, 2, 3)]
    rows = [device_at(moved(place, 0, d)) for d in (1, 2, 3)]
    tensor, packs = tensor_peers(place), pack_peers()
    width = enc.shape[1] // 2
    there = pl.ds(pl.multiple_of(other * width, width), width)
    here = pl.ds(pl.multiple_of(section * width, width), width)

    small[...] = jnp.zeros(small.shape, F32)
    for layer, to, source, frm in (
        (0, 1, small_b, 0), (0, 2, small_b, 1), (0, 4, small_b, 2), (0, 5, small_b, 3),
        (1, 0, small_b, 4), (1, 3, small_b, 5),
        (1, 1, small_d, 0), (1, 2, small_d, 1), (1, 4, small_d, 2), (1, 5, small_d, 3),
    ):
        small[layer, to : to + 1, :] = source[frm : frm + 1, :]

    def early(links):
        give_d[...] = jnp.concatenate([out3[:, there], dec[:, there]], 0).astype(BF16)
        swap = links.start(give_d, land_d, partner)
        one = links.start(small.at[1 - core], core_s, sibling)
        yield
        one.wait_recv()
        fin[core] = small[core] + core_s[...]
        for land_s, devices in ((y_s, columns), (x_s, rows), (z_s, [plus, minus, far])):
            copies = [links.start(fin.at[core], land_s.at[n], d) for n, d in enumerate(devices)]
            yield
            for copy in copies:
                copy.wait_recv()
            links.finish()
            fin[core] = fin[core] + land_s[0] + land_s[1] + land_s[2]
        five = links.start(fin.at[core], fin.at[core], sibling)
        yield
        five.wait_recv()
        swap.wait_recv()
        links.finish()

    def weights(links):
        made = t_dot(whole(qkv_grad), whole(full_h0))
        att[0, 0 : 3 * HEAD, :] = made.astype(BF16)
        matrix = wt[0, 0 : 3 * HEAD, :].astype(F32)
        sums = jnp.sum(whole(qkv_grad).astype(F32), 0, keepdims=True)
        shift0 = jnp.sum(matrix * column(sums)[:, 0:1], 0, keepdims=True)
        gain0 = (jnp.sum(matrix * made, 0, keepdims=True) - shift0 * gs[0, 3:4, :]) / gs[0, 0:1, :]
        gain0 = gain0 + jnp.sum(back1[...] * unit0[...], 0, keepdims=True)
        shift0 = shift0 + jnp.sum(back1[...], 0, keepdims=True)
        quarter = width // 2
        both = [row[:, i * quarter : (i + 1) * quarter] for row in (gain0, shift0) for i in range(4)]
        late[...] = jnp.concatenate(both, 0)
        att[0, 3 * HEAD : 4 * HEAD, :] = t_dot(whole(att_e), whole(full_b1)).astype(BF16)
        yield from pack_sum(links, att, att_out, pack_refs)

    both = kv_sum[...].T.astype(BF16)
    rows_each = qkv_grad.shape[2]
    qkv_grad[:, :, :, HEAD : 3 * HEAD] = both.reshape(SIDE, SIDE, rows_each, 2 * HEAD)

    def rest_of(links, low, rows):
        band = pl.ds(low, rows)

        def heads(group):
            made = dot(stacked(qkv_grad, place, group, low, rows), wt[0, 0 : 3 * HEAD, :])
            store_blocks(part, place, group, made.astype(BF16), low)

        (sum_e,) = yield from sum_blocks(links, place, [(part, land, low, rows)], heads)
        made, _, _ = norm_back(
            back1[band] + sum_e, unit0[band], scale0[band, 0:1], gs[0, 0:1, :]
        )
        enc[band] = made
        give_e[band] = enc[band, there].astype(BF16)
        swap = links.start(give_e.at[band], land_e.at[band], partner)
        enc_out[section, band] = enc[band, here]
        yield
        swap.wait_recv()
        links.finish()

    def two_rows(links):
        copies = [links.start(late, late_t.at[n], d) for n, d in enumerate(tensor)]
        yield
        for copy in copies:
            copy.wait_recv()
        links.finish()
        late[...] = late[...] + jnp.sum(late_t[...], 0)
        copies = [links.start(late, late_p.at[n], d) for n, d in enumerate(packs)]
        yield
        for copy in copies:
            copy.wait_recv()
        links.finish()

    chains = [
        *(rest_of(Links(send, recv, AT_SUM[n]), *rows) for n, rows in enumerate(LAST_CHUNKS)),
        early(Links(send, recv, AT_EARLY)),
        weights(Links(send, recv, AT_ATT_PACK)),
        two_rows(Links(send, recv, AT_LATE)),
        background,
    ]
    run(chains)
    enc_out[other] = land_e[...].astype(F32)
    got = land_d[...].astype(F32)
    count = out3.shape[0]
    out3_out[section] = out3[:, here]
    out3_out[other] = got[:count]
    dec_out[section] = dec[:, here]
    dec_out[other] = got[count:]
    small_out[...] = fin[section]
    total = late[...] + jnp.sum(late_p[...], 0)
    quarter = width // 2
    for i in range(8):
        row = 0 if i < 4 else 3
        cols = slice((i % 4) * quarter, (i % 4 + 1) * quarter)
        added = jnp.where(section == 0, total[i : i + 1], 0.0)
        small_out[row : row + 1, cols] = small_out[row : row + 1, cols] + added


def layers_kernel(names, *refs):
    r = types.SimpleNamespace(**dict(zip(names, refs)))
    more = refs[len(names) :]
    ffn_pack, att_pack, copies = more[:8], more[8:12], more[12:]
    place = at_grid()
    greet(tensor_peers(place) + pack_peers())

    first_part(
        r.tokens, r.dec_tokens, r.wt_in, r.gain_in, r.shift_in, r.wt, r.gs, r.full_h0, r.h0, r.unit0, r.scale0,
        r.q, r.k, r.v, r.part, r.dbuf_0, r.gs_in, *copies,
    )
    forward_part(
        r.q, r.k, r.v, r.seg_e, r.dbuf_0, r.seg_d, r.h0, r.dec_tokens, r.wt, r.gs, r.ffn_in,
        r.full_y, r.sq, r.sk, r.sv, r.att_d, r.log_d,
        r.ffn, r.full_h1, r.full_m, r.full_d1, r.hidden, r.slope, r.kvc, r.cq, r.d1,
        r.unit1, r.scale1, r.unit2, r.scale2, r.dunit0, r.dscale0, r.att_e, r.log_e, r.seg_col,
        r.part, r.dpart_0, r.land_1, r.land_2, r.dland_0, r.dbuf_1, *copies,
    )
    decoder_part(
        r.cq, r.kvc, r.d1, r.cot, r.seg_d, r.seg_e, r.wt, r.ffn, r.gs,
        r.d3, r.dback1, r.full_d2, r.full_db2, r.full_db1, r.dhidden, r.dpre, r.att_c,
        r.cq_grad, r.kvc_grad, r.small_d, r.ffn_grad, r.g_bufs, r.s_work, r.s_land, r.probs, *copies,
    )
    background = backward_part(
        r.kvc_grad, r.cq_grad, r.dback1, r.wt, r.gs, r.ffn, r.unit1, r.scale1, r.unit2, r.scale2,
        r.dunit0, r.dscale0, r.slope, r.sq, r.sk, r.sv, r.log_d, r.seg_d, r.full_h1, r.hidden,
        r.full_m, r.full_d1, r.full_y, r.full_db1, r.att_c, r.att_d,
        r.q, r.k, r.v, r.seg_e, r.seg_col, r.log_e, r.full_b1, r.qkv_grad, r.kv_sum, r.back1, r.dec_grad, r.small_b, r.ffn_sum, r.att_45, r.wt_45, r.att,
        r.full_b2, r.pre, r.part, r.dpart_1, r.dpart_2, r.land_1, r.land_2, r.dland_1, r.dland_2, r.dbuf_2,
        r.ffn_grad, *ffn_pack, *copies,
    )
    last_part(
        background, r.kv_sum, r.qkv_grad, r.att_e, r.full_b1, r.full_h0,
        r.wt, r.gs, r.back1, r.unit0, r.scale0, r.small_b, r.small_d, r.d3, r.dec_grad,
        r.att_out, r.small_out, r.enc_out, r.out3_out, r.dec_out,
        r.part, r.land_1, *att_pack,
        r.fin, r.core_s, r.y_s, r.x_s, r.z_s, r.late, r.late_t, r.late_p,
        r.enc, r.give_e, r.give_d, r.land_e, r.land_d, r.att, r.small, *copies,
    )


def layers_call(args, collective_id):
    tokens, dec_tokens, ffn = args["tokens"], args["dec_tokens"], args["ffn_in"]
    (_, rows, width), count, inner = tokens.shape, dec_tokens.shape[1], ffn.shape[2]
    half, full, grid = width // 2, count * DEVICES, (SIDE, SIDE)
    low, wide_rows, head = (*grid, rows, width), (*grid, rows, 128), (*grid, rows, HEAD)
    small_block = (*grid, 2 * count, half)
    outs = dict(
        att_out=((2, 2 * HEAD, width), BF16),
        small_out=((8, width), F32),
        enc_out=((2, rows, half), F32),
        out3_out=((2, count, half), F32),
        dec_out=((2, count, half), F32),
        ffn_sum=((2, width, inner), BF16),
        att_45=((2, HEAD, width), BF16),
    )
    kept = dict(
        wt=((2, 6 * HEAD, width), BF16),
        gs=((2, 8, width), F32),
        ffn=((2, 2, width, inner), BF16),
    )
    kept |= dict(full_h0=(low, BF16), full_h1=(low, BF16), full_m=(low, BF16), full_b1=(low, BF16), full_b2=(low, BF16), part=(low, BF16))
    kept |= dict(h0=((rows, width), F32), unit0=((rows, width), F32), unit1=((rows, width), F32), unit2=((rows, width), F32), back1=((rows, width), F32), enc=((rows, width), F32))
    kept |= dict(scale0=((rows, 128), F32), scale1=((rows, 128), F32), scale2=((rows, 128), F32))
    kept |= dict(full_y=((full, width), BF16), full_d1=((full, width), BF16), full_d2=((full, width), BF16), full_db1=((full, width), BF16), full_db2=((full, width), BF16))
    kept |= dict(q=(head, BF16), k=(head, BF16), v=(head, BF16), att_e=(head, BF16))
    kept |= dict(sq=((full, HEAD), BF16), sk=((full, HEAD), BF16), sv=((full, HEAD), BF16), att_d=((full, HEAD), BF16), cq=((full, HEAD), BF16), att_c=((full, HEAD), BF16), cq_grad=((full, HEAD), BF16))
    kept |= dict(d1=((8, width), F32), dunit0=((8, width), F32), d3=((8, width), F32), dback1=((8, width), F32), dec_grad=((8, width), F32), small_b=((8, width), F32), small_d=((8, width), F32), gs_in=((8, width), F32))
    kept |= dict(dbuf_0=(small_block, BF16), dbuf_1=(small_block, BF16), dbuf_2=(small_block, BF16), dpart_0=(small_block, BF16), dpart_1=(small_block, BF16), dpart_2=(small_block, BF16))
    kept |= dict(land_1=((30, rows, half), BF16), land_2=((30, rows, half), BF16))
    kept |= dict(dland_0=((30, 2 * count, half // 2), BF16), dland_1=((30, 2 * count, half // 2), BF16), dland_2=((30, 2 * count, half // 2), BF16))
    kept |= dict(hidden=((*grid, rows, inner), BF16), pre=((*grid, rows, inner), BF16))
    kept |= dict(kvc=((*grid, rows, 2 * HEAD), BF16), kvc_grad=((*grid, rows, 2 * HEAD), BF16))
    kept |= dict(dhidden=((full, inner), BF16), dpre=((full, inner), BF16))
    kept |= dict(wt_45=((2, 2 * HEAD, width), BF16), att=((2, 4 * HEAD, width), BF16))
    kept |= dict(y_s=((3, 8, width), F32), x_s=((3, 8, width), F32), z_s=((3, 8, width), F32))
    kept |= dict(fin=((2, 8, width), F32), small=((2, 8, width), F32))
    kept |= dict(give_e=((rows, half), BF16), land_e=((rows, half), BF16))
    kept |= dict(give_d=((2 * count, half), BF16), land_d=((2 * count, half), BF16))
    kept |= dict(
        slope=((*grid, rows, inner), F32),
        log_e=(wide_rows, F32),
        seg_col=(wide_rows, F32),
        log_d=((full, 128), F32),
        dscale0=((count, 128), F32),
        g_bufs=((3, *small_block), BF16),
        s_work=((3, *small_block), BF16),
        s_land=((3, DEVICES - 1, 2 * count, half), BF16),
        probs=((full, DEVICES * rows), F32),
        ffn_grad=((2, 2 * width, inner), BF16),
        core_s=((8, width), F32),
        late=((8, width // 4), F32),
        late_t=((DEVICES - 1, 8, width // 4), F32),
        late_p=((7, 8, width // 4), F32),
        qkv_grad=((*grid, rows, 3 * HEAD), BF16),
        kv_sum=((2 * HEAD, DEVICES * rows), F32),
    )
    scratch = {name: pltpu.VMEM(dims, kind) for name, (dims, kind) in kept.items()}
    ffn_pack = [*pack_scratch(2 * width, inner), *pack_scratch(2 * HEAD, width)]
    att_pack = pack_scratch(4 * HEAD, width)
    more = [*ffn_pack, *att_pack, *sems(ALL_COPIES)]
    return pl.pallas_call(
        functools.partial(layers_kernel, [*args, *outs, *scratch]),
        out_shape=[shape(*spec) for spec in outs.values()],
        in_specs=[VM] * len(args),
        out_specs=[VM] * len(outs),
        scratch_shapes=[*scratch.values(), *more],
        compiler_params=pltpu.CompilerParams(
            collective_id=collective_id, has_side_effects=True, vmem_limit_bytes=VMEM_BYTES
        ),
    )(*args.values())


def results_kernel(att, ffn, small, enc, out3, dec, att_45, *outs):
    (att_out, ffn_out, gain_out, shift_out, enc_out, out3_out, dec_out) = outs
    many, few = 2 * HEAD, HEAD
    for i in range(2):
        att_out[i * many : (i + 1) * many] = att[i].astype(F32)
        start = 2 * many + i * few
        att_out[start : start + few] = att_45[i].astype(F32)
    ffn_out[...] = ffn[...].astype(F32)
    for i in range(3):
        gain_out[i] = small[i : i + 1, :]
        shift_out[i] = small[3 + i : 4 + i, :]
    enc_out[...] = enc[...]
    out3_out[...] = out3[...].astype(BF16)
    dec_out[...] = dec[...]


def results_call(att, ffn, small, enc, out3, dec, att_45):
    width = small.shape[1]
    return pl.pallas_call(
        results_kernel,
        out_shape=[
            shape((6 * HEAD, width), F32),
            shape(ffn.shape, F32),
            shape((3, 1, width), F32),
            shape((3, 1, width), F32),
            shape(enc.shape, F32),
            shape(out3.shape, BF16),
            shape(dec.shape, F32),
        ],
        in_specs=[VM] * 7,
        out_specs=[VM] * 7,
        compiler_params=pltpu.CompilerParams(vmem_limit_bytes=VMEM_BYTES),
    )(att, ffn, small, enc, out3, dec, att_45)


def on_device(
    encoder_tokens,
    encoder_segments,
    decoder_tokens,
    decoder_segments,
    cotangent,
    attention_weight,
    feedforward_weight,
    norm_gain,
    norm_shift,
):
    width = encoder_tokens.shape[2]
    own_wt = jnp.swapaxes(attention_weight[0], 1, 2).reshape(6 * HEAD, width)
    args = dict(
        tokens=encoder_tokens,
        dec_tokens=decoder_tokens,
        cot=cotangent,
        seg_e=encoder_segments,
        seg_d=decoder_segments,
        wt_in=own_wt,
        gain_in=jnp.swapaxes(norm_gain, 0, 1),
        shift_in=jnp.swapaxes(norm_shift, 0, 1),
        ffn_in=feedforward_weight[0],
    )
    att_sum, small_sum, enc_out, d3_out, dec_out, ffn_sum, att_45 = layers_call(args, 1)
    att_out, ffn_out, gain_out, shift_out, enc_out, d3_out, dec_out = results_call(
        att_sum, ffn_sum, small_sum, enc_out, d3_out, dec_out, att_45
    )
    return (
        d3_out,
        enc_out,
        dec_out,
        jnp.swapaxes(att_out.reshape(6, HEAD, width), 1, 2)[None],
        ffn_out.reshape(feedforward_weight.shape),
        jnp.swapaxes(gain_out, 0, 1),
        jnp.swapaxes(shift_out, 0, 1),
    )


def solution(mesh):
    in_specs = (
        P("dp", "tensor", None),
        P("dp", None),
        P("dp", "tensor", None),
        P("dp", None),
        P("dp", "tensor", None),
        P("section", None, None, "tensor"),
        P("section", None, None, "tensor"),
        P("section", None, None),
        P("section", None, None),
    )
    out_specs = (
        P("dp", "tensor", "section"),
        P("dp", "tensor", "section"),
        P("dp", "tensor", "section"),
        P("section", None, None, "tensor"),
        P("section", None, None, "tensor"),
        P("section", None, None),
        P("section", None, None),
    )
    return jax.shard_map(
        on_device, mesh=mesh, in_specs=in_specs, out_specs=out_specs, check_vma=False
    )
```

```python
import functools
import types

import jax
import jax.numpy as jnp
from jax import lax
from jax.experimental import pallas as pl
from jax.experimental.pallas import tpu as pltpu
from jax.sharding import PartitionSpec as P

HEAD = 64
EPSILON = 1e-05
MASKED = -1000000000.0
SCALE = HEAD ** (-0.5)
F32 = jnp.float32
BF16 = jnp.bfloat16
MESH = pl.DeviceIdType.MESH
VM = pl.BlockSpec(memory_space=pltpu.VMEM)
SIDE = 4
DEVICES = SIDE * SIDE
UP = (0, 2)
DOWN = (1, 3)
RING_COPIES = 30
CHUNKS = ((0, 48), (48, 32))
LAST_CHUNKS = ((0, 32), (32, 48))
PAUSES = (1, 1, 2, 1)
LAG = 0
VMEM_BYTES = 60 << 20
AT_FFN, AT_FIRST, AT_FFN_PACK, AT_ATT_PACK, AT_EARLY, AT_LATE, AT_SMALL = 0, 2, 5, 13, 21, 33, 55
AT_45_PACK = 266
AT_SUM, AT_GATHER, ALL_COPIES = (85, 146), (116, 206), 271
RING = True
INV_SQRT2 = 0.7071067811865476
INV_SQRT_2PI = 0.3989422804014327
FAR_FIRST = (10, 2, 8, 6, 14, 11, 9, 7, 13, 5, 15, 1, 3, 4, 12)


def norm_parts(values):
    center = values - jnp.mean(values, -1, keepdims=True)
    scale = lax.rsqrt(jnp.mean(center * center, -1, keepdims=True) + EPSILON)
    return center * scale, scale


def norm_back(grad, unit, scale, gains):
    inner = grad * gains
    back = scale * (
        inner
        - jnp.mean(inner, -1, keepdims=True)
        - unit * jnp.mean(inner * unit, -1, keepdims=True)
    )
    return back, jnp.sum(grad * unit, 0, keepdims=True), jnp.sum(grad, 0, keepdims=True)


def gelu_parts(u):
    cdf = 0.5 * (1.0 + lax.erf(u * INV_SQRT2))
    return u * cdf, cdf + u * (INV_SQRT_2PI * jnp.exp(-0.5 * u * u))


def dot(a, b):
    return jnp.dot(a, b, preferred_element_type=F32)


def dot_t(a, b):
    return lax.dot_general(a, b, (((1,), (1,)), ((), ())), preferred_element_type=F32)


def t_dot(a, b):
    return lax.dot_general(a, b, (((0,), (0,)), ((), ())), preferred_element_type=F32)


def scores_of(queries, key_rows, allowed):
    return jnp.where(allowed, dot_t(queries, key_rows) * SCALE, MASKED)


def attend(queries, key_rows, value_rows, allowed):
    scores = scores_of(queries, key_rows, allowed)
    row_max = jnp.max(scores, -1, keepdims=True)
    exponent = jnp.exp(scores - row_max)
    row_sum = jnp.sum(exponent, -1, keepdims=True)
    probs_low = (exponent / row_sum).astype(BF16)
    return dot(probs_low, value_rows).astype(BF16), row_max + jnp.log(row_sum)


def attend_back(queries, key_rows, value_rows, log_total, allowed, attended_grad):
    probs = jnp.exp(scores_of(queries, key_rows, allowed) - log_total)
    value_grad = t_dot(attended_grad, probs.astype(BF16))
    probs_grad = dot_t(attended_grad, value_rows)
    scores_grad = (probs * (probs_grad - jnp.sum(probs * probs_grad, -1, keepdims=True))).astype(
        BF16
    )
    return dot(scores_grad, key_rows) * SCALE, t_dot(queries, scores_grad) * SCALE, value_grad


def at_grid():
    index = lax.axis_index("tensor")
    return lax.div(index, SIDE), lax.rem(index, SIDE)


def moved(place, dy, dx):
    return lax.rem(place[0] + dy % SIDE, SIDE), lax.rem(place[1] + dx % SIDE, SIDE)


def along(axis, steps):
    return (steps, 0) if axis == 0 else (0, steps)


def device_at(place):
    return {"tensor": place[0] * SIDE + place[1]}


def tensor_peers(place):
    return [device_at(moved(place, d // SIDE, d % SIDE)) for d in FAR_FIRST]


def pack_peers():
    mine = lax.axis_index("section") * 4 + lax.axis_index("dp")
    others = [lax.rem(mine + d, 8) for d in range(1, 8)]
    return [{"section": lax.div(n, 4), "dp": lax.rem(n, 4)} for n in others]


def greet(devices):
    barrier = pltpu.get_barrier_semaphore()
    for device in devices:
        pl.semaphore_signal(barrier, inc=1, device_id=device, device_id_type=MESH)
    pl.semaphore_wait(barrier, len(devices))


def sections():
    section, dp = lax.axis_index("section"), lax.axis_index("dp")
    zh, core = lax.div(dp, 2), lax.rem(dp, 2)
    return section, zh, core, {"section": 1 - section}, {"dp": zh * 2 + 1 - core}


class Links:
    def __init__(self, send_sems, recv_sems, used=0):
        self.send, self.recv, self.used, self.started = send_sems, recv_sems, used, []

    def start(self, source, target, device):
        n = self.used
        self.used += 1
        copy = pltpu.make_async_remote_copy(
            src_ref=source,
            dst_ref=target,
            send_sem=self.send.at[n],
            recv_sem=self.recv.at[n],
            device_id=device,
            device_id_type=MESH,
        )
        copy.start()
        self.started.append(copy)
        return copy

    def finish(self, used=None):
        for copy in self.started:
            copy.wait_send()
        self.started = []
        self.used = self.used if used is None else used


def sems(n):
    return [pltpu.SemaphoreType.DMA((n,)), pltpu.SemaphoreType.DMA((n,))]


def shape(dims, kind):
    return jax.ShapeDtypeStruct(tuple(dims), kind)


def fold(rows):
    half = rows.shape[1] // 2
    return jnp.concatenate([rows[:, :half], rows[:, half:]], 0)


def unfold(rows):
    count = rows.shape[0] // 2
    return jnp.concatenate([rows[:count], rows[count:]], 1)


def unfold_all(blocks):
    count, half = blocks.shape[2] // 2, blocks.shape[3]
    split = blocks.astype(F32).reshape(DEVICES, 2, count, half)
    low = split[:, 0].reshape(DEVICES * count, half)
    high = split[:, 1].reshape(DEVICES * count, half)
    return jnp.concatenate([low, high], 1).astype(BF16)


def fold_all(part):
    count, half = part.shape[0] // DEVICES, part.shape[1] // 2
    split = part.reshape(DEVICES, count, 2 * half)
    both = jnp.concatenate([split[:, :, :half], split[:, :, half:]], 1)
    return both.astype(BF16).reshape(SIDE, SIDE, 2 * count, half)


def own_row(ref):
    return jnp.where(lax.axis_index("section") == 0, ref[0:1, :], ref[1:2, :]).astype(F32)


def column(row):
    return jnp.broadcast_to(row, (128, row.shape[1])).T


def gather(links, place, views, ready=None):
    jobs = []
    for buf, low, rows in views:
        half = buf.shape[-1] // 2
        for h in range(2):
            jobs.append((buf, 1 - h, h, h * half, half, pl.ds(low, rows)))
    ready = ready or (lambda group: None)

    def send(job, axis, steps, r, s):
        buf, a, b, start, size, rows = job
        y, x = moved(moved(place, *along(a, r)), *along(b, s))
        ref = buf.at[y, x, rows, pl.ds(start, size)]
        return links.start(ref, ref, device_at(moved(place, *along(axis, steps))))

    first, spread, ahead = [], [], []
    for job in jobs:
        first.append({-d % SIDE: send(job, job[1], d, 0, 0) for d in (1, 3, 2)})
    paths = ((1, 3), (3, 1)) if RING else ((2, 2), (1, 3), (3, 1))
    for job in jobs:
        spread.append({0: {s: send(job, job[2], d, 0, 0) for d, s in paths}})
    ready([(0, 0)])
    yield
    for r in (3, 1, 2):
        for i, job in enumerate(jobs):
            first[i][r].wait_recv()
            spread[i][r] = {s: send(job, job[2], d, r, 0) for d, s in paths}
    if RING:
        for i, job in enumerate(jobs):
            spread[i][0][3].wait_recv()
            ahead.append({0: send(job, job[2], 1, 0, 3)})
            spread[i][0][1].wait_recv()
    else:
        for i, job in enumerate(jobs):
            spread[i][0][3].wait_recv()
            spread[i][0][1].wait_recv()
            ahead.append({r: spread[i][r][2] for r in range(SIDE)})
    ready([(0, 1), (0, 3), (1, 0), (3, 0)])
    yield
    if RING:
        for r in DOWN:
            for i, job in enumerate(jobs):
                spread[i][r][1].wait_recv()
                ahead[i][r] = send(job, job[2], -1, r, 1)
        for i, job in enumerate(jobs):
            spread[i][2][3].wait_recv()
            ahead[i][2] = send(job, job[2], 1, 2, 3)
        for r in DOWN:
            for i, job in enumerate(jobs):
                spread[i][r][3].wait_recv()
    else:
        for r in DOWN:
            for i, job in enumerate(jobs):
                spread[i][r][1].wait_recv()
                spread[i][r][3].wait_recv()
    ready([(1, 1), (1, 3), (3, 1), (3, 3)])
    for i, job in enumerate(jobs):
        ahead[i][0].wait_recv()
    ready([(0, 2), (2, 0)])
    yield
    for i, job in enumerate(jobs):
        if not RING:
            spread[i][2][3].wait_recv()
        spread[i][2][1].wait_recv()
        ahead[i][1].wait_recv()
        ahead[i][3].wait_recv()
    ready([(1, 2), (3, 2), (2, 1), (2, 3)])
    for i, job in enumerate(jobs):
        ahead[i][2].wait_recv()
    ready([(2, 2)])


AT_ONCE = ([(0, 1), (0, 3), (1, 0), (3, 0)], [(0, 2), (2, 0)], [(2, 2)])
PRODUCE = (
    [(2, 2), (2, 3), (2, 1), (3, 2), (1, 2), (2, 0), (0, 2)],
    [(3, 3), (3, 1), (1, 3), (1, 1), (3, 0), (1, 0), (0, 3), (0, 1), (0, 0)],
)


def sum_blocks(links, place, views, produce=None):
    produce = produce or (lambda group: None)
    jobs = []
    for part, land, low, rows in views:
        half = part.shape[-1] // 2
        for h in range(2):
            jobs.append((part, land, 15 * h, 1 - h, h, h * half, half, pl.ds(low, rows)))

    def block(job, r, s):
        part, _, _, a, b, start, size, rows = job
        y, x = moved(moved(place, *along(a, r)), *along(b, s))
        return part.at[y, x, rows, pl.ds(start, size)]

    def landing(job, n):
        return job[1].at[job[2] + n, job[7]]

    def start(source, target, axis, steps):
        return links.start(source, target, device_at(moved(place, *along(axis, steps))))

    def add(target, *others):
        total = target[...].astype(F32)
        for other in others:
            total = total + other[...].astype(F32)
        return total

    def near_slot(job, r, steps):
        return landing(job, 4 + 2 * r + (0 if steps == 1 else 1))

    order = (2, 3, 1, 0)
    produce(PRODUCE[0])
    near = [{r: [] for r in order} for _ in jobs]
    if RING:
        far = [{} for _ in jobs]
        for r in order:
            for i, job in enumerate(jobs):
                far[i][r] = start(
                    block(job, r, 2), landing(job, r), job[4], 1 if r in UP else -1
                )
        produce(PRODUCE[1])
        for r in order:
            for i, job in enumerate(jobs):
                steps = -1 if r in UP else 1
                near[i][r].append(
                    start(block(job, r, steps), near_slot(job, r, steps), job[4], steps)
                )
        yield
        for r in order:
            for i, job in enumerate(jobs):
                steps = 1 if r in UP else -1
                far[i][r].wait_recv()
                ref = block(job, r, steps)
                ref[...] = add(ref, landing(job, r)).astype(BF16)
                near[i][r].append(start(ref, near_slot(job, r, steps), job[4], steps))
    else:
        for s in (2, 1, 3):
            for r in order:
                for i, job in enumerate(jobs):
                    slot = landing(job, 4 * (s - 1) + r)
                    near[i][r].append(start(block(job, r, s), slot, job[4], s))
            if s == 2:
                produce(PRODUCE[1])
    yield
    last = [{} for _ in jobs]
    results = []
    for r in order:
        if r == 0:
            yield
        for i, job in enumerate(jobs):
            for copy in near[i][r]:
                copy.wait_recv()
            ref = block(job, r, 0)
            if RING:
                total = add(ref, landing(job, 4 + 2 * r), landing(job, 5 + 2 * r))
            else:
                total = add(ref, landing(job, r), landing(job, 4 + r), landing(job, 8 + r))
            if r == 0:
                results.append(total)
            else:
                ref[...] = total.astype(BF16)
                last[i][r] = start(ref, landing(job, 11 + r), job[3], r)
    for i, job in enumerate(jobs):
        for r in order[:3]:
            last[i][r].wait_recv()
            results[i] = results[i] + landing(job, 11 + r)[...].astype(F32)
    return [jnp.concatenate(results[i : i + 2], 1) for i in range(0, len(results), 2)]


def run(chains, lag=0, background=None):
    turn, active = 0, list(enumerate(chains))
    while active:
        for n, chain in list(active):
            if turn >= n * lag:
                try:
                    next(chain)
                except StopIteration:
                    active.remove((n, chain))
        if background is not None:
            next(background, None)
        turn += 1


def pack_places():
    section, zh, core, partner, sibling = sections()
    zh_plus = lax.rem(zh + section, 2)
    plus = {"section": 1 - section, "dp": zh_plus * 2 + core}
    minus = {"section": 1 - section, "dp": (1 - zh_plus) * 2 + core}
    return section, zh, core, sibling, zh_plus, plus, minus


PACK_COPIES = 8


def pack_scratch(rows, cols):
    half, quarter = rows // 2, rows // 4
    return [
        pltpu.VMEM((2, half, cols), BF16),
        pltpu.VMEM((2, half, cols), BF16),
        pltpu.VMEM((2, quarter, cols), BF16),
        pltpu.VMEM((half, cols), BF16),
    ]


def pause(n):
    for _ in range(n):
        yield


def pack_sum(links, grad, out, scratch):
    work, core_land, side, over = scratch
    section, zh, core, sibling, zh_plus, plus, minus = pack_places()
    other = 1 - section
    half = grad.shape[1] // 2
    quarter = half // 2
    first = links.start(grad.at[:, pl.ds((1 - core) * half, half)], core_land, sibling)
    yield from pause(PAUSES[0])
    first.wait_recv()
    work[...] = (
        grad[:, pl.ds(core * half, half)].astype(F32) + core_land[...].astype(F32)
    ).astype(BF16)
    second = [
        links.start(work.at[other, pl.ds(h * quarter, quarter)], side.at[n], d)
        for n, (h, d) in enumerate(((zh_plus, plus), (1 - zh_plus, minus)))
    ]
    yield from pause(PAUSES[1])
    for copy in second:
        copy.wait_recv()
    mine = work.at[section, pl.ds(zh * quarter, quarter)]
    mine[...] = (mine[...].astype(F32) + side[0].astype(F32) + side[1].astype(F32)).astype(BF16)
    third = links.start(work.at[section], over, {"dp": (1 - zh) * 2 + core})
    yield from pause(PAUSES[2])
    third.wait_recv()
    out[core] = (work[section].astype(F32) + over[...].astype(F32)).astype(BF16)
    last = links.start(out.at[core], out.at[core], sibling)
    yield from pause(PAUSES[3])
    last.wait_recv()
    links.finish()


def gather_small(links, place, buf, rows):
    y, x = place
    buf[y, x] = fold(rows).astype(BF16)
    links.finish(AT_SMALL + DEVICES - 1)
    copies = []
    for d in FAR_FIRST:
        target = device_at(moved(place, d // SIDE, d % SIDE))
        copies.append(links.start(buf.at[y, x], buf.at[y, x], target))
    for copy in copies:
        copy.wait_recv()
    return unfold_all(buf[...])


def sum_small(links, place, work, land, part, meanwhile=None):
    work[...] = fold_all(part)
    links.finish(AT_SMALL + 0)
    copies = []
    for n, d in enumerate(FAR_FIRST):
        there = moved(place, d // SIDE, d % SIDE)
        copies.append(links.start(work.at[there[0], there[1]], land.at[n], device_at(there)))
    if meanwhile is not None:
        meanwhile()
    total = work[place[0], place[1]].astype(F32)
    for copy in copies:
        copy.wait_recv()
    return unfold(total + jnp.sum(land[...].astype(F32), 0))


def stacked(ref, place, group, low=0, rows=None):
    rows = ref.shape[2] if rows is None else rows
    blocks = []
    for dy, dx in group:
        y, x = moved(place, dy, dx)
        blocks.append(ref[y, x, low : low + rows])
    return blocks[0] if len(blocks) == 1 else jnp.concatenate(blocks, 0)


def store_blocks(ref, place, group, values, low=0):
    rows = values.shape[0] // len(group)
    for n, (dy, dx) in enumerate(group):
        y, x = moved(place, dy, dx)
        ref[y, x, low : low + rows] = values[n * rows : (n + 1) * rows]


def whole(ref):
    return ref[...].reshape(DEVICES * ref.shape[2], ref.shape[3])


def wide(scale):
    return jnp.broadcast_to(scale, (scale.shape[0], 128))


def first_part(
    tokens, dec_tokens, wt_in, gain_in, shift_in, wt, gs, full_h0, h0, unit0, scale0, *rest
):
    (q, k, v, xbuf, ybuf, gs_in, send, recv) = rest
    place = at_grid()
    section, _, core, partner, sibling = sections()
    links, extra = Links(send, recv, AT_GATHER[1]), Links(send, recv, AT_FIRST)
    half = wt_in.shape[0] // 2
    mine = pl.ds(core * half, half)
    x, y = tokens.at[section], dec_tokens.at[section]
    for i in range(3):
        gs_in[i : i + 1, :] = gain_in[i]
        gs_in[3 + i : 4 + i, :] = shift_in[i]
    gs_in[6:8, :] = jnp.zeros((2, x.shape[1]), F32)
    gains_copy = extra.start(gs_in, gs.at[section], partner)
    xbuf[place[0], place[1]] = x[...]
    ybuf[place[0], place[1]] = fold(y[...].astype(F32)).astype(BF16)
    passed = []

    def ready(group):
        if group == [(0, 0)]:
            passed.append(extra.start(wt_in.at[mine], wt.at[section, mine], partner))
            gs[section] = gs_in[...]
            wt[section] = wt_in[...]
            gains_copy.wait_recv()
        if group == [(1, 1), (1, 3), (3, 1), (3, 3)]:
            passed[0].wait_recv()
            theirs = wt.at[1 - section, mine]
            passed.append(extra.start(theirs, theirs, sibling))
        unit, scale = norm_parts(stacked(xbuf, place, group).astype(F32))
        rows = unit * gs[0, 0:1, :] + gs[0, 3:4, :]
        if group == [(0, 0)]:
            h0[...] = rows
            unit0[...] = unit
            scale0[...] = wide(scale)
        store_blocks(full_h0, place, group, rows.astype(BF16))

    views = [(xbuf, 0, x.shape[0]), (ybuf, 0, ybuf.shape[2])]
    run([gather(links, place, views, ready)])
    passed[1].wait_recv()
    count, width = x.shape
    for i in range(SIDE):
        rows = full_h0[i].reshape(SIDE * count, width)
        made = dot_t(rows, wt[0, 0 : 3 * HEAD, :]).astype(BF16)
        for j, ref in enumerate((q, k, v)):
            ref[i] = made[:, j * HEAD : (j + 1) * HEAD].reshape(SIDE, count, HEAD)
    links.finish()
    extra.finish()


def before(row):
    count = row.shape[1]
    place = [lax.broadcasted_iota(jnp.int32, (count, count), i) for i in range(2)]
    return (column(row)[:, 0:1] == row) & (place[1] <= place[0])


def forward_part(q, k, v, seg_e, ybuf, seg_d, h0, dec_tokens, wt, gs, ffn_in, *rest):
    (full_y, sq, sk, sv, att_d, log_d, *rest) = rest
    (ffn, full_h1, full_m, full_d1, hidden, slope, kvc, cq, d1) = rest[:9]
    (unit1, scale1, unit2, scale2, dunit0, dscale0, att_e, log_e, seg_col) = rest[9:18]
    (part, dpart, land_1, land_2, land_d, d1buf, send, recv) = rest[18:]
    place = at_grid()
    section, _, core, partner, sibling = sections()
    y = dec_tokens.at[section]
    row = own_row(seg_e)
    seg_col[...] = column(row).reshape(seg_col.shape)
    shared = Links(send, recv, AT_FFN)
    passed = [shared.start(ffn_in.at[core], ffn.at[section, core], partner)]

    def self_attention():
        rows = unfold_all(ybuf[...])
        full_y[...] = rows
        made = dot_t(rows, wt[1, 0 : 3 * HEAD, :]).astype(BF16)
        for j, ref in enumerate((sq, sk, sv)):
            ref[...] = made[:, j * HEAD : (j + 1) * HEAD]
        att, log_total = attend(sq[...], sk[...], sv[...], before(own_row(seg_d)))
        att_d[...] = att
        log_d[...] = wide(log_total)

    def chain(links, low, rows, with_dec):
        here = pl.ds(low, rows)
        at_sum, at_gather = AT_SUM[with_dec], AT_GATHER[with_dec]
        links.used = at_sum

        def attended(group):
            allowed = stacked(seg_col, place, group, low, rows)[:, 0:1] == row
            queries = stacked(q, place, group, low, rows)
            att, log_total = attend(queries, whole(k), whole(v), allowed)
            store_blocks(att_e, place, group, att, low)
            store_blocks(log_e, place, group, wide(log_total), low)
            made = dot(att, wt[0, 3 * HEAD : 4 * HEAD, :])
            store_blocks(part, place, group, made.astype(BF16), low)
            if with_dec and group == PRODUCE[0]:
                self_attention()
                dpart[...] = fold_all(dot(att_d[...], wt[1, 3 * HEAD : 4 * HEAD, :]))
            if low == 0 and group == PRODUCE[1]:
                ffn[section] = ffn_in[...]

        views = [(part, land_1, low, rows)]
        if with_dec:
            views.append((dpart, land_d, 0, dpart.shape[2]))
        sums = yield from sum_blocks(links, place, views, attended)
        unit, scale = norm_parts(h0[here] + sums[0])
        unit1[here] = unit
        scale1[here] = wide(scale)
        h1 = unit * gs[0, 1:2, :] + gs[0, 4:5, :]
        full_h1[place[0], place[1], here] = h1.astype(BF16)
        views = [(full_h1, low, rows)]
        if with_dec:
            unit, scale = norm_parts(y[...].astype(F32) + unfold(sums[1]))
            dunit0[...] = unit
            dscale0[...] = wide(scale)
            made = unit * gs[1, 0:1, :] + gs[1, 3:4, :]
            d1[...] = made
            d1buf[place[0], place[1]] = fold(made).astype(BF16)
            views.append((d1buf, 0, d1buf.shape[2]))
        if low == 0:
            passed[0].wait_recv()
            theirs = ffn.at[1 - section, core]
            passed.append(shared.start(theirs, theirs, sibling))

        def up(group):
            if group == [(0, 0)]:
                return
            if group == [(0, 1), (0, 3), (1, 0), (3, 0)]:
                if low == 0:
                    passed[1].wait_recv()
                group = [(0, 0)] + group
            made, back = gelu_parts(dot(stacked(full_h1, place, group, low, rows), ffn[0, 0]))
            store_blocks(hidden, place, group, made.astype(BF16), low)
            store_blocks(slope, place, group, back, low)

        links.used = at_gather
        yield from gather(links, place, views, up)
        links.finish(at_sum)
        if with_dec:
            made = unfold_all(d1buf[...])
            full_d1[...] = made
            cq[...] = dot_t(made, wt[1, 4 * HEAD : 5 * HEAD, :]).astype(BF16)

        def down(group):
            made = dot_t(stacked(hidden, place, group, low, rows), ffn[0, 1])
            store_blocks(part, place, group, made.astype(BF16), low)

        sums = yield from sum_blocks(links, place, [(part, land_2, low, rows)], down)
        unit, scale = norm_parts(h1 + sums[0])
        unit2[here] = unit
        scale2[here] = wide(scale)
        full_m[place[0], place[1], here] = (unit * gs[0, 2:3, :] + gs[0, 5:6, :]).astype(BF16)

        def cross(group):
            made = dot_t(stacked(full_m, place, group, low, rows), wt[0, 4 * HEAD : 6 * HEAD, :])
            store_blocks(kvc, place, group, made.astype(BF16), low)

        links.used = at_gather
        yield from gather(links, place, [(full_m, low, rows)], cross)
        links.finish()

    chains = []
    for n, (low, rows) in enumerate(CHUNKS):
        links = Links(send, recv)
        chains.append(chain(links, low, rows, n == len(CHUNKS) - 1))
    run(chains, LAG)
    shared.finish()


def decoder_part(cq, kvc, d1, cot, seg_d, seg_e, wt, ffn, gs, *rest):
    (d3, dback1, full_d2, full_db2, full_db1, hid_out, pre_out, att_out) = rest[:8]
    (cq_grad, kvc_grad, grads, ffn_grad, g_bufs, s_work, s_land, probs, send, recv) = rest[8:]
    place = at_grid()
    links = Links(send, recv, AT_SMALL)
    w5 = wt[1, 5 * HEAD : 6 * HEAD, :]
    both = whole(kvc)
    kc, vc = both[:, :HEAD], both[:, HEAD:]
    allowed = column(own_row(seg_d))[:, 0:1] == own_row(seg_e)
    scores = scores_of(cq[...], kc, allowed)
    exponent = jnp.exp(scores - jnp.max(scores, -1, keepdims=True))
    probs[...] = exponent / jnp.sum(exponent, -1, keepdims=True)
    att = dot(probs[...].astype(BF16), vc).astype(BF16)
    att_out[...] = att
    part = sum_small(links, place, s_work.at[0], s_land.at[0], dot(att, w5))
    unit1, scale1 = norm_parts(d1[...] + part)
    d2 = unit1 * gs[1, 1:2, :] + gs[1, 4:5, :]
    full = gather_small(links, place, g_bufs.at[0], d2)
    full_d2[...] = full
    hidden, slope = gelu_parts(dot(full, ffn[1, 0]))
    hidden = hidden.astype(BF16)
    hid_out[...] = hidden
    part = sum_small(links, place, s_work.at[1], s_land.at[1], dot_t(hidden, ffn[1, 1]))
    unit2, scale2 = norm_parts(d2 + part)
    d3[...] = unit2 * gs[1, 2:3, :] + gs[1, 5:6, :]
    back2, gain2, shift2 = norm_back(cot[lax.axis_index("section")].astype(F32), unit2, scale2, gs[1, 2:3, :])
    full = gather_small(links, place, g_bufs.at[1], back2)
    full_db2[...] = full
    pre = (dot(full, ffn[1, 1]) * slope).astype(BF16)
    pre_out[...] = pre

    def weights():
        count = full_d2.shape[1]
        ffn_grad[1, :count] = t_dot(pre_out[...], full_d2[...]).T.astype(BF16)
        ffn_grad[1, count:] = t_dot(hid_out[...], full_db2[...]).T.astype(BF16)

    part = dot_t(pre, ffn[1, 0])
    part = sum_small(links, place, s_work.at[2], s_land.at[2], part, weights)
    back1, gain1, shift1 = norm_back(back2 + part, unit1, scale1, gs[1, 1:2, :])
    dback1[...] = back1
    full = gather_small(links, place, g_bufs.at[2], back1)
    full_db1[...] = full
    att_grad = dot_t(full, w5).astype(BF16)
    p = probs[...]
    value_grad = t_dot(att_grad, p.astype(BF16))
    p_grad = dot_t(att_grad, vc)
    s_grad = (p * (p_grad - jnp.sum(p * p_grad, -1, keepdims=True))).astype(BF16)
    cq_grad[...] = (dot(s_grad, kc) * SCALE).astype(BF16)
    key_grad = t_dot(cq[...], s_grad) * SCALE
    both = jnp.concatenate([key_grad, value_grad], 0).T.astype(BF16)
    kvc_grad[...] = both.reshape(kvc_grad.shape)
    grads[0:1, :] = gain1
    grads[1:2, :] = gain2
    grads[2:3, :] = shift1
    grads[3:4, :] = shift2
    grads[4:8, :] = jnp.zeros((4, grads.shape[1]), F32)
    links.finish()


def backward_part(*refs):
    (kvc_grad, cq_grad, dback1, wt, gs, ffn, unit1, scale1, unit2, scale2) = refs[:10]
    (dunit0, dscale0, slope, sq, sk, sv, log_d, seg_d, full_h1, hidden) = refs[10:20]
    (full_m, full_d1, full_y, full_db1) = refs[20:24]
    (att_c, att_d, q, k, v, seg_e, seg_col, log_e) = refs[24:32]
    (full_b1, qkv_grad, kv_sum, back1, dec_grad, grads, ffn_sum, att_45) = refs[32:40]
    wt_45, att = refs[40:42]
    (full_b2, pre, part, dpart_1, dpart_2, land_1, land_2, dland_1, dland_2, dbuf) = refs[42:52]
    (ffn_grad, *pack_refs, send, recv) = refs[52:]
    kv_sum[...] = jnp.zeros(kv_sum.shape, F32)
    row = own_row(seg_e)
    place = at_grid()

    def chain(links, low, rows, with_dec):
        here = pl.ds(low, rows)
        at_sum, at_gather = AT_SUM[with_dec], AT_GATHER[with_dec]
        links.used = at_sum

        def cross(group):
            made = dot(stacked(kvc_grad, place, group, low, rows), wt[0, 4 * HEAD : 6 * HEAD, :])
            store_blocks(part, place, group, made.astype(BF16), low)
            if with_dec and group == PRODUCE[0]:
                dpart_1[...] = fold_all(dot(cq_grad[...], wt[1, 4 * HEAD : 5 * HEAD, :]))

        views = [(part, land_1, low, rows)]
        if with_dec:
            views.append((dpart_1, dland_1, 0, dpart_1.shape[2]))
        sums = yield from sum_blocks(links, place, views, cross)
        back2, gain2, shift2 = norm_back(sums[0], unit2[here], scale2[here, 0:1], gs[0, 2:3, :])
        full_b2[place[0], place[1], here] = back2.astype(BF16)
        views = [(full_b2, low, rows)]
        if with_dec:
            dback0, dgain0, dshift0 = norm_back(
                dback1[...] + unfold(sums[1]), dunit0[...], dscale0[:, 0:1], gs[1, 0:1, :]
            )
            dbuf[place[0], place[1]] = fold(dback0).astype(BF16)
            views.append((dbuf, 0, dbuf.shape[2]))

        def down(group):
            made = dot(stacked(full_b2, place, group, low, rows), ffn[0, 1])
            made = made * stacked(slope, place, group, low, rows)
            store_blocks(pre, place, group, made.astype(BF16), low)

        links.used = at_gather
        yield from gather(links, place, views, down)
        links.finish(at_sum)
        ready_rows.append(rows)
        views = [(part, land_2, low, rows)]
        if with_dec:
            full_db0 = unfold_all(dbuf[...])
            att_d_grad = dot_t(full_db0, wt[1, 3 * HEAD : 4 * HEAD, :]).astype(BF16)
            made = attend_back(
                sq[...], sk[...], sv[...], log_d[:, 0:1], before(own_row(seg_d)), att_d_grad
            )
            made = jnp.concatenate([made[0], made[1].T, made[2].T], 1).astype(BF16)
            late.extend([made, full_db0])
            dpart_2[...] = fold_all(dot(made, wt[1, 0 : 3 * HEAD, :]))
            views.append((dpart_2, dland_2, 0, dpart_2.shape[2]))

        def up(group):
            made = dot_t(stacked(pre, place, group, low, rows), ffn[0, 0])
            store_blocks(part, place, group, made.astype(BF16), low)

        sums = yield from sum_blocks(links, place, views, up)
        made, gain1, shift1 = norm_back(
            back2 + sums[0], unit1[here], scale1[here, 0:1], gs[0, 1:2, :]
        )
        back1[here] = made
        full_b1[place[0], place[1], here] = made.astype(BF16)
        totals.append((gain1, gain2, shift1, shift2))
        if with_dec:
            dec_grad[...] = dback0 + unfold(sums[1])
            grads[4:5, :] = dgain0
            grads[5:6, :] = dshift0

        pending = []

        def mixed(group):
            pending.extend(group)
            if group not in AT_ONCE:
                return
            some = lambda ref: stacked(ref, place, pending, low, rows)
            att_grad = dot_t(some(full_b1), wt[0, 3 * HEAD : 4 * HEAD, :]).astype(BF16)
            made = attend_back(
                some(q), whole(k), whole(v), some(log_e)[:, 0:1], some(seg_col)[:, 0:1] == row, att_grad
            )
            for n, (dy, dx) in enumerate(pending):
                at_y, at_x = moved(place, dy, dx)
                block = made[0][n * rows : (n + 1) * rows].astype(BF16)
                qkv_grad[at_y, at_x, here, 0:HEAD] = block
            kv_sum[...] += jnp.concatenate(made[1:], 0)
            pending.clear()

        links.used = at_gather
        yield from gather(links, place, [(full_b1, low, rows)], mixed)
        links.finish()

    def weight_chain(links):
        def put(layer, first, rows):
            ref, first = (wt_45, first - 4) if first >= 4 else (att, first)
            ref[layer, first * HEAD : first * HEAD + rows.shape[0], :] = rows.astype(BF16)

        count = full_h1.shape[3]
        yield
        put(0, 4, t_dot(whole(kvc_grad), whole(full_m)))
        yield
        put(1, 4, t_dot(cq_grad[...], full_d1[...]))
        put(1, 5, t_dot(att_c[...], full_db1[...]))
        yield from pack_sum(Links(send, recv, AT_45_PACK), wt_45, att_45, pack_refs[4:])
        while len(ready_rows) < len(CHUNKS):
            yield
        ffn_grad[0, :count] = t_dot(whole(pre), whole(full_h1)).T.astype(BF16)
        yield
        ffn_grad[0, count:] = t_dot(whole(hidden), whole(full_b2)).T.astype(BF16)
        adding = pack_sum(links, ffn_grad, ffn_sum, pack_refs[:4])
        next(adding)
        put(1, 0, t_dot(late[0], full_y[...]))
        put(1, 3, t_dot(att_d[...], late[1]))
        yield
        yield from adding

    late = []
    totals, chains, ready_rows = [], [], []
    for n, (low, rows) in enumerate(CHUNKS):
        links = Links(send, recv)
        chains.append(chain(links, low, rows, n == len(CHUNKS) - 1))
    background = weight_chain(Links(send, recv, AT_FFN_PACK))
    run(chains, LAG, background)
    for i in range(4):
        grads[i : i + 1, :] = sum(total[i] for total in totals)
    grads[6:8, :] = jnp.zeros((2, grads.shape[1]), F32)
    return background


def last_part(background, kv_sum, qkv_grad, att_e, full_b1, full_h0, *refs):
    (wt, gs, back1, unit0, scale0, small_b, small_d, out3, dec, *rest) = refs
    (att_out, small_out, enc_out, out3_out, dec_out, part, land, *pack_refs) = rest[:11]
    (fin, core_s, y_s, x_s, z_s, late, late_t, late_p) = rest[11:19]
    (enc, give_e, give_d, land_e, land_d, att, small, send, recv) = rest[19:]
    place = at_grid()
    section, zh, core, sibling, _, plus, minus = pack_places()
    other = 1 - section
    partner = {"section": other}
    far = {"dp": (1 - zh) * 2 + core}
    columns = [device_at(moved(place, d, 0)) for d in (1, 2, 3)]
    rows = [device_at(moved(place, 0, d)) for d in (1, 2, 3)]
    tensor, packs = tensor_peers(place), pack_peers()
    width = enc.shape[1] // 2
    there = pl.ds(pl.multiple_of(other * width, width), width)
    here = pl.ds(pl.multiple_of(section * width, width), width)

    small[...] = jnp.zeros(small.shape, F32)
    for layer, to, source, frm in (
        (0, 1, small_b, 0), (0, 2, small_b, 1), (0, 4, small_b, 2), (0, 5, small_b, 3),
        (1, 0, small_b, 4), (1, 3, small_b, 5),
        (1, 1, small_d, 0), (1, 2, small_d, 1), (1, 4, small_d, 2), (1, 5, small_d, 3),
    ):
        small[layer, to : to + 1, :] = source[frm : frm + 1, :]

    def early(links):
        give_d[...] = jnp.concatenate([out3[:, there], dec[:, there]], 0).astype(BF16)
        swap = links.start(give_d, land_d, partner)
        one = links.start(small.at[1 - core], core_s, sibling)
        yield
        one.wait_recv()
        fin[core] = small[core] + core_s[...]
        for land_s, devices in ((y_s, columns), (x_s, rows), (z_s, [plus, minus, far])):
            copies = [links.start(fin.at[core], land_s.at[n], d) for n, d in enumerate(devices)]
            yield
            for copy in copies:
                copy.wait_recv()
            links.finish()
            fin[core] = fin[core] + land_s[0] + land_s[1] + land_s[2]
        five = links.start(fin.at[core], fin.at[core], sibling)
        yield
        five.wait_recv()
        swap.wait_recv()
        links.finish()

    def weights(links):
        made = t_dot(whole(qkv_grad), whole(full_h0))
        att[0, 0 : 3 * HEAD, :] = made.astype(BF16)
        matrix = wt[0, 0 : 3 * HEAD, :].astype(F32)
        sums = jnp.sum(whole(qkv_grad).astype(F32), 0, keepdims=True)
        shift0 = jnp.sum(matrix * column(sums)[:, 0:1], 0, keepdims=True)
        gain0 = (jnp.sum(matrix * made, 0, keepdims=True) - shift0 * gs[0, 3:4, :]) / gs[0, 0:1, :]
        gain0 = gain0 + jnp.sum(back1[...] * unit0[...], 0, keepdims=True)
        shift0 = shift0 + jnp.sum(back1[...], 0, keepdims=True)
        quarter = width // 2
        both = [row[:, i * quarter : (i + 1) * quarter] for row in (gain0, shift0) for i in range(4)]
        late[...] = jnp.concatenate(both, 0)
        att[0, 3 * HEAD : 4 * HEAD, :] = t_dot(whole(att_e), whole(full_b1)).astype(BF16)
        yield from pack_sum(links, att, att_out, pack_refs)

    both = kv_sum[...].T.astype(BF16)
    rows_each = qkv_grad.shape[2]
    qkv_grad[:, :, :, HEAD : 3 * HEAD] = both.reshape(SIDE, SIDE, rows_each, 2 * HEAD)

    def rest_of(links, low, rows):
        band = pl.ds(low, rows)

        def heads(group):
            made = dot(stacked(qkv_grad, place, group, low, rows), wt[0, 0 : 3 * HEAD, :])
            store_blocks(part, place, group, made.astype(BF16), low)

        (sum_e,) = yield from sum_blocks(links, place, [(part, land, low, rows)], heads)
        made, _, _ = norm_back(
            back1[band] + sum_e, unit0[band], scale0[band, 0:1], gs[0, 0:1, :]
        )
        enc[band] = made
        give_e[band] = enc[band, there].astype(BF16)
        swap = links.start(give_e.at[band], land_e.at[band], partner)
        enc_out[section, band] = enc[band, here]
        yield
        swap.wait_recv()
        links.finish()

    def two_rows(links):
        copies = [links.start(late, late_t.at[n], d) for n, d in enumerate(tensor)]
        yield
        for copy in copies:
            copy.wait_recv()
        links.finish()
        late[...] = late[...] + jnp.sum(late_t[...], 0)
        copies = [links.start(late, late_p.at[n], d) for n, d in enumerate(packs)]
        yield
        for copy in copies:
            copy.wait_recv()
        links.finish()

    chains = [
        *(rest_of(Links(send, recv, AT_SUM[n]), *rows) for n, rows in enumerate(LAST_CHUNKS)),
        early(Links(send, recv, AT_EARLY)),
        weights(Links(send, recv, AT_ATT_PACK)),
        two_rows(Links(send, recv, AT_LATE)),
        background,
    ]
    run(chains)
    enc_out[other] = land_e[...].astype(F32)
    got = land_d[...].astype(F32)
    count = out3.shape[0]
    out3_out[section] = out3[:, here]
    out3_out[other] = got[:count]
    dec_out[section] = dec[:, here]
    dec_out[other] = got[count:]
    small_out[...] = fin[section]
    total = late[...] + jnp.sum(late_p[...], 0)
    quarter = width // 2
    for i in range(8):
        row = 0 if i < 4 else 3
        cols = slice((i % 4) * quarter, (i % 4 + 1) * quarter)
        added = jnp.where(section == 0, total[i : i + 1], 0.0)
        small_out[row : row + 1, cols] = small_out[row : row + 1, cols] + added


def layers_kernel(names, *refs):
    r = types.SimpleNamespace(**dict(zip(names, refs)))
    more = refs[len(names) :]
    ffn_pack, att_pack, copies = more[:8], more[8:12], more[12:]
    place = at_grid()
    greet(tensor_peers(place) + pack_peers())

    first_part(
        r.tokens, r.dec_tokens, r.wt_in, r.gain_in, r.shift_in, r.wt, r.gs, r.full_h0, r.h0, r.unit0, r.scale0,
        r.q, r.k, r.v, r.part, r.dbuf_0, r.gs_in, *copies,
    )
    forward_part(
        r.q, r.k, r.v, r.seg_e, r.dbuf_0, r.seg_d, r.h0, r.dec_tokens, r.wt, r.gs, r.ffn_in,
        r.full_y, r.sq, r.sk, r.sv, r.att_d, r.log_d,
        r.ffn, r.full_h1, r.full_m, r.full_d1, r.hidden, r.slope, r.kvc, r.cq, r.d1,
        r.unit1, r.scale1, r.unit2, r.scale2, r.dunit0, r.dscale0, r.att_e, r.log_e, r.seg_col,
        r.part, r.dpart_0, r.land_1, r.land_2, r.dland_0, r.dbuf_1, *copies,
    )
    decoder_part(
        r.cq, r.kvc, r.d1, r.cot, r.seg_d, r.seg_e, r.wt, r.ffn, r.gs,
        r.d3, r.dback1, r.full_d2, r.full_db2, r.full_db1, r.dhidden, r.dpre, r.att_c,
        r.cq_grad, r.kvc_grad, r.small_d, r.ffn_grad, r.g_bufs, r.s_work, r.s_land, r.probs, *copies,
    )
    background = backward_part(
        r.kvc_grad, r.cq_grad, r.dback1, r.wt, r.gs, r.ffn, r.unit1, r.scale1, r.unit2, r.scale2,
        r.dunit0, r.dscale0, r.slope, r.sq, r.sk, r.sv, r.log_d, r.seg_d, r.full_h1, r.hidden,
        r.full_m, r.full_d1, r.full_y, r.full_db1, r.att_c, r.att_d,
        r.q, r.k, r.v, r.seg_e, r.seg_col, r.log_e, r.full_b1, r.qkv_grad, r.kv_sum, r.back1, r.dec_grad, r.small_b, r.ffn_sum, r.att_45, r.wt_45, r.att,
        r.full_b2, r.pre, r.part, r.dpart_1, r.dpart_2, r.land_1, r.land_2, r.dland_1, r.dland_2, r.dbuf_2,
        r.ffn_grad, *ffn_pack, *copies,
    )
    last_part(
        background, r.kv_sum, r.qkv_grad, r.att_e, r.full_b1, r.full_h0,
        r.wt, r.gs, r.back1, r.unit0, r.scale0, r.small_b, r.small_d, r.d3, r.dec_grad,
        r.att_out, r.small_out, r.enc_out, r.out3_out, r.dec_out,
        r.part, r.land_1, *att_pack,
        r.fin, r.core_s, r.y_s, r.x_s, r.z_s, r.late, r.late_t, r.late_p,
        r.enc, r.give_e, r.give_d, r.land_e, r.land_d, r.att, r.small, *copies,
    )


def layers_call(args, collective_id):
    tokens, dec_tokens, ffn = args["tokens"], args["dec_tokens"], args["ffn_in"]
    (_, rows, width), count, inner = tokens.shape, dec_tokens.shape[1], ffn.shape[2]
    half, full, grid = width // 2, count * DEVICES, (SIDE, SIDE)
    low, wide_rows, head = (*grid, rows, width), (*grid, rows, 128), (*grid, rows, HEAD)
    small_block = (*grid, 2 * count, half)
    outs = dict(
        att_out=((2, 2 * HEAD, width), BF16),
        small_out=((8, width), F32),
        enc_out=((2, rows, half), F32),
        out3_out=((2, count, half), F32),
        dec_out=((2, count, half), F32),
        ffn_sum=((2, width, inner), BF16),
        att_45=((2, HEAD, width), BF16),
    )
    kept = dict(
        wt=((2, 6 * HEAD, width), BF16),
        gs=((2, 8, width), F32),
        ffn=((2, 2, width, inner), BF16),
    )
    kept |= dict(full_h0=(low, BF16), full_h1=(low, BF16), full_m=(low, BF16), full_b1=(low, BF16), full_b2=(low, BF16), part=(low, BF16))
    kept |= dict(h0=((rows, width), F32), unit0=((rows, width), F32), unit1=((rows, width), F32), unit2=((rows, width), F32), back1=((rows, width), F32), enc=((rows, width), F32))
    kept |= dict(scale0=((rows, 128), F32), scale1=((rows, 128), F32), scale2=((rows, 128), F32))
    kept |= dict(full_y=((full, width), BF16), full_d1=((full, width), BF16), full_d2=((full, width), BF16), full_db1=((full, width), BF16), full_db2=((full, width), BF16))
    kept |= dict(q=(head, BF16), k=(head, BF16), v=(head, BF16), att_e=(head, BF16))
    kept |= dict(sq=((full, HEAD), BF16), sk=((full, HEAD), BF16), sv=((full, HEAD), BF16), att_d=((full, HEAD), BF16), cq=((full, HEAD), BF16), att_c=((full, HEAD), BF16), cq_grad=((full, HEAD), BF16))
    kept |= dict(d1=((8, width), F32), dunit0=((8, width), F32), d3=((8, width), F32), dback1=((8, width), F32), dec_grad=((8, width), F32), small_b=((8, width), F32), small_d=((8, width), F32), gs_in=((8, width), F32))
    kept |= dict(dbuf_0=(small_block, BF16), dbuf_1=(small_block, BF16), dbuf_2=(small_block, BF16), dpart_0=(small_block, BF16), dpart_1=(small_block, BF16), dpart_2=(small_block, BF16))
    kept |= dict(land_1=((30, rows, half), BF16), land_2=((30, rows, half), BF16))
    kept |= dict(dland_0=((30, 2 * count, half // 2), BF16), dland_1=((30, 2 * count, half // 2), BF16), dland_2=((30, 2 * count, half // 2), BF16))
    kept |= dict(hidden=((*grid, rows, inner), BF16), pre=((*grid, rows, inner), BF16))
    kept |= dict(kvc=((*grid, rows, 2 * HEAD), BF16), kvc_grad=((*grid, rows, 2 * HEAD), BF16))
    kept |= dict(dhidden=((full, inner), BF16), dpre=((full, inner), BF16))
    kept |= dict(wt_45=((2, 2 * HEAD, width), BF16), att=((2, 4 * HEAD, width), BF16))
    kept |= dict(y_s=((3, 8, width), F32), x_s=((3, 8, width), F32), z_s=((3, 8, width), F32))
    kept |= dict(fin=((2, 8, width), F32), small=((2, 8, width), F32))
    kept |= dict(give_e=((rows, half), BF16), land_e=((rows, half), BF16))
    kept |= dict(give_d=((2 * count, half), BF16), land_d=((2 * count, half), BF16))
    kept |= dict(
        slope=((*grid, rows, inner), F32),
        log_e=(wide_rows, F32),
        seg_col=(wide_rows, F32),
        log_d=((full, 128), F32),
        dscale0=((count, 128), F32),
        g_bufs=((3, *small_block), BF16),
        s_work=((3, *small_block), BF16),
        s_land=((3, DEVICES - 1, 2 * count, half), BF16),
        probs=((full, DEVICES * rows), F32),
        ffn_grad=((2, 2 * width, inner), BF16),
        core_s=((8, width), F32),
        late=((8, width // 4), F32),
        late_t=((DEVICES - 1, 8, width // 4), F32),
        late_p=((7, 8, width // 4), F32),
        qkv_grad=((*grid, rows, 3 * HEAD), BF16),
        kv_sum=((2 * HEAD, DEVICES * rows), F32),
    )
    scratch = {name: pltpu.VMEM(dims, kind) for name, (dims, kind) in kept.items()}
    ffn_pack = [*pack_scratch(2 * width, inner), *pack_scratch(2 * HEAD, width)]
    att_pack = pack_scratch(4 * HEAD, width)
    more = [*ffn_pack, *att_pack, *sems(ALL_COPIES)]
    return pl.pallas_call(
        functools.partial(layers_kernel, [*args, *outs, *scratch]),
        out_shape=[shape(*spec) for spec in outs.values()],
        in_specs=[VM] * len(args),
        out_specs=[VM] * len(outs),
        scratch_shapes=[*scratch.values(), *more],
        compiler_params=pltpu.CompilerParams(
            collective_id=collective_id, has_side_effects=True, vmem_limit_bytes=VMEM_BYTES
        ),
    )(*args.values())


def results_kernel(att, ffn, small, enc, out3, dec, att_45, *outs):
    (att_out, ffn_out, gain_out, shift_out, enc_out, out3_out, dec_out) = outs
    many, few = 2 * HEAD, HEAD
    for i in range(2):
        att_out[i * many : (i + 1) * many] = att[i].astype(F32)
        start = 2 * many + i * few
        att_out[start : start + few] = att_45[i].astype(F32)
    ffn_out[...] = ffn[...].astype(F32)
    for i in range(3):
        gain_out[i] = small[i : i + 1, :]
        shift_out[i] = small[3 + i : 4 + i, :]
    enc_out[...] = enc[...]
    out3_out[...] = out3[...].astype(BF16)
    dec_out[...] = dec[...]


def results_call(att, ffn, small, enc, out3, dec, att_45):
    width = small.shape[1]
    return pl.pallas_call(
        results_kernel,
        out_shape=[
            shape((6 * HEAD, width), F32),
            shape(ffn.shape, F32),
            shape((3, 1, width), F32),
            shape((3, 1, width), F32),
            shape(enc.shape, F32),
            shape(out3.shape, BF16),
            shape(dec.shape, F32),
        ],
        in_specs=[VM] * 7,
        out_specs=[VM] * 7,
        compiler_params=pltpu.CompilerParams(vmem_limit_bytes=VMEM_BYTES),
    )(att, ffn, small, enc, out3, dec, att_45)


def on_device(
    encoder_tokens,
    encoder_segments,
    decoder_tokens,
    decoder_segments,
    cotangent,
    attention_weight,
    feedforward_weight,
    norm_gain,
    norm_shift,
):
    width = encoder_tokens.shape[2]
    own_wt = jnp.swapaxes(attention_weight[0], 1, 2).reshape(6 * HEAD, width)
    args = dict(
        tokens=encoder_tokens,
        dec_tokens=decoder_tokens,
        cot=cotangent,
        seg_e=encoder_segments,
        seg_d=decoder_segments,
        wt_in=own_wt,
        gain_in=jnp.swapaxes(norm_gain, 0, 1),
        shift_in=jnp.swapaxes(norm_shift, 0, 1),
        ffn_in=feedforward_weight[0],
    )
    att_sum, small_sum, enc_out, d3_out, dec_out, ffn_sum, att_45 = layers_call(args, 1)
    att_out, ffn_out, gain_out, shift_out, enc_out, d3_out, dec_out = results_call(
        att_sum, ffn_sum, small_sum, enc_out, d3_out, dec_out, att_45
    )
    return (
        d3_out,
        enc_out,
        dec_out,
        jnp.swapaxes(att_out.reshape(6, HEAD, width), 1, 2)[None],
        ffn_out.reshape(feedforward_weight.shape),
        jnp.swapaxes(gain_out, 0, 1),
        jnp.swapaxes(shift_out, 0, 1),
    )


def solution(mesh):
    in_specs = (
        P("dp", "tensor", None),
        P("dp", None),
        P("dp", "tensor", None),
        P("dp", None),
        P("dp", "tensor", None),
        P("section", None, None, "tensor"),
        P("section", None, None, "tensor"),
        P("section", None, None),
        P("section", None, None),
    )
    out_specs = (
        P("dp", "tensor", "section"),
        P("dp", "tensor", "section"),
        P("dp", "tensor", "section"),
        P("section", None, None, "tensor"),
        P("section", None, None, "tensor"),
        P("section", None, None),
        P("section", None, None),
    )
    return jax.shard_map(
        on_device, mesh=mesh, in_specs=in_specs, out_specs=out_specs, check_vma=False
    )
```
